32 devices in a mesh: seq: 8 (over y, x, core), tp: 4 (over z).
Axes of the slice: x: 2, y: 2, z: 4, core: 2. Of those that a mesh axis runs over, the one named last changes fastest.
Arguments:
- tokens: bfloat16 [2, 16384, 768], P(None, ('seq', 'tp')), may hold values from -6 to 6
- doc_lengths: int32 [2, 18], replicated, may hold values from 8 to 64, as said below
- rand_blocks: int32 [2, 256, 12, 3], P(None, 'seq', 'tp'), may hold values from 0 to 255, as said below
- query_weight: bfloat16 [768, 768], P(None, 'tp'), may hold values from -0.21875 to 0.21875
- key_weight: bfloat16 [768, 768], P(None, 'tp'), may hold values from -0.21875 to 0.21875
- value_weight: bfloat16 [768, 768], P(None, 'tp'), may hold values from -0.21875 to 0.21875
- query_bias: bfloat16 [768], P('tp'), may hold values from -3 to 3
- value_bias: bfloat16 [768], P('tp'), may hold values from -0.59765625 to 0.59765625
- proj_weight: bfloat16 [768, 768], P('tp'), may hold values from -1.75 to 1.75
- proj_bias: bfloat16 [768], replicated, may hold values from -2 to 2
- first_gain: bfloat16 [768], replicated, may hold values from 0.5 to 1.5
- first_bias: bfloat16 [768], replicated, may hold values from -1.1953125 to 1.1953125
- second_gain: bfloat16 [768], replicated, may hold values from 0.5 to 1.5
- second_bias: bfloat16 [768], replicated, may hold values from -1.1953125 to 1.1953125
- inner_weight: bfloat16 [768, 3072], P(None, 'tp'), may hold values from -0.21875 to 0.21875
- inner_bias: bfloat16 [3072], P('tp'), may hold values from -3 to 3
- outer_weight: bfloat16 [3072, 768], P('tp'), may hold values from -0.109375 to 0.109375
- outer_bias: bfloat16 [768], replicated, may hold values from -2 to 2
- out_grad: bfloat16 [2, 16384, 768], P(None, ('seq', 'tp')), may hold values from -6 to 6
Outputs:
- output: bfloat16 [2, 16384, 768], P(None, ('seq', 'tp'))
- input_grad: float32 [2, 16384, 768], P(None, ('seq', 'tp'))
- query_weight_grad: float32 [768, 768], P(None, 'tp')
- key_weight_grad: float32 [768, 768], P(None, 'tp')
- value_weight_grad: float32 [768, 768], P(None, 'tp')
- query_bias_grad: float32 [768], P('tp')
- value_bias_grad: float32 [768], P('tp')
- proj_weight_grad: float32 [768, 768], P('tp')
- proj_bias_grad: float32 [768], replicated
- first_gain_grad: float32 [768], replicated
- first_bias_grad: float32 [768], replicated
- second_gain_grad: float32 [768], replicated
- second_bias_grad: float32 [768], replicated
- inner_weight_grad: float32 [768, 3072], P(None, 'tp')
- inner_bias_grad: float32 [3072], P('tp')
- outer_weight_grad: float32 [3072, 768], P('tp')
- outer_bias_grad: float32 [768], replicated
The draws below stay inside these ranges and needn't reach their ends.
Inputs may be any that keep to these rules, and one draw needn't show every extreme that they name: `doc_lengths`: each row holds exactly 2 entries 64 and 16 entries 8, in an order drawn from the seed; they sum to 256. `rand_blocks`: every entry is a block of the same window as its query block (the block of the second index), by doc_lengths of the same micro-batch.
All inputs are finite; a program needn't handle non-finite values.
Results may differ from the reference program's by a relative error of at most 0.017.
Values may be sent and summed in bfloat16 or wider, within the bound.
A program may use at most 320 MiB of HBM per device.

```python
import math
import jax
import jax.numpy as jnp
from jax import lax

D = 768
HEADS = 12
HEAD = 64
FF = 3072
BLOCK = 64
RANDS = 3
LONG_BLK = 64
SHORT_BLK = 8
MICRO = 2
TOTAL_BLK = 256
TOKENS = 16384
LONG_DOCS = 2
SHORT_DOCS = 16
NDOCS = 18


def doc_table(key):
    table_key = jax.random.fold_in(key, 17)
    pattern = jnp.concatenate([jnp.full((LONG_DOCS,), LONG_BLK, jnp.int32), jnp.full((SHORT_DOCS,), SHORT_BLK, jnp.int32)])

    def one_order(sub_key):
        return jax.random.permutation(sub_key, pattern)
    return jax.vmap(one_order)(jax.random.split(table_key, MICRO))


def draw_doc_lengths(key, part):
    return doc_table(key)


def draw_rand_blocks(key, part):
    doc_sizes = doc_table(key)
    own_key = jax.random.fold_in(key, 3)
    doc_ends = jnp.cumsum(doc_sizes, axis=1).astype(jnp.int32)
    doc_starts = doc_ends - doc_sizes
    blocks = jnp.arange(TOTAL_BLK, dtype=jnp.int32)
    doc_owner = jnp.sum((blocks[None, :, None] >= doc_ends[:, None, :]).astype(jnp.int32), axis=2)
    doc_hit = doc_owner[:, :, None] == jnp.arange(NDOCS, dtype=jnp.int32)[None, None, :]
    doc_size = jnp.sum(jnp.where(doc_hit, doc_sizes[:, None, :], 0), axis=2).astype(jnp.int32)
    doc_first = jnp.sum(jnp.where(doc_hit, doc_starts[:, None, :], 0), axis=2).astype(jnp.int32)
    offsets = jax.random.randint(own_key, (MICRO, TOTAL_BLK, HEADS, RANDS), 0, 1 << 20, dtype=jnp.int32)
    return (doc_first[:, :, None, None] + offsets % doc_size[:, :, None, None]).astype(jnp.int32)


def block_scale(rng, dims, pieces, low, largest):
    def one(dim, blocks):
        heights = jax.random.uniform(jax.random.fold_in(jax.random.fold_in(rng, 6), dim), (blocks,), jnp.float32, low / len(pieces), largest / len(pieces))
        return jnp.repeat(jnp.exp(heights), dims[dim] // blocks).reshape((-1,) + (1,) * (len(dims) - dim - 1))

    gain = one(*pieces[0])
    for cut in pieces[1:]:
        gain = gain * one(*cut)
    return gain


def noise(stream_key, shape, deviation, limit, cuts=(), kind=jnp.bfloat16):
    factor_of = block_scale(stream_key, shape, cuts, -0.22, 0.18) if cuts else 1.0
    drawn = jax.random.normal(stream_key, shape, jnp.float32) * deviation * factor_of
    return jnp.minimum(jnp.maximum(drawn, -limit), limit).astype(kind)


def setup_inputs(seed: int = 0) -> dict:
    key_list = jax.random.split(jax.random.key(seed), 20)
    tokens = noise(key_list[0], (MICRO, TOKENS, D), 1.0, 6.0, ((1, 32),))
    doc_lengths = draw_doc_lengths(jax.random.fold_in(key_list[19], 71), 0)
    rand_blocks = draw_rand_blocks(jax.random.fold_in(key_list[19], 71), 0)
    query_weight = noise(key_list[3], (D, D), D ** -0.5, 0.21875, ((1, 4),))
    key_weight = noise(key_list[4], (D, D), D ** -0.5, 0.21875, ((1, 4),))
    value_weight = noise(key_list[5], (D, D), D ** -0.5, 0.21875, ((1, 4),))
    query_bias = noise(key_list[6], (D,), 0.5, 3.0, ((0, 4),))
    value_bias = noise(key_list[7], (D,), 0.1, 0.59765625, ((0, 4),))
    proj_weight = noise(key_list[8], (D, D), (D // 64) ** -0.5, 1.75, ((0, 4),))
    proj_bias = noise(key_list[9], (D,), 0.3, 2.0)
    first_gain = jnp.clip(1.0 + 0.1 * jax.random.normal(key_list[10], (D,), jnp.float32), 0.5, 1.5).astype(jnp.bfloat16)
    first_bias = noise(key_list[11], (D,), 0.2, 1.1953125)
    second_gain = jnp.clip(1.0 + 0.1 * jax.random.normal(key_list[12], (D,), jnp.float32), 0.5, 1.5).astype(jnp.bfloat16)
    second_bias = noise(key_list[13], (D,), 0.2, 1.1953125)
    inner_weight = noise(key_list[14], (D, FF), D ** -0.5, 0.21875, ((1, 4),))
    inner_bias = noise(key_list[15], (FF,), 0.5, 3.0, ((0, 4),))
    outer_weight = noise(key_list[16], (FF, D), FF ** -0.5, 0.109375, ((0, 4),))
    outer_bias = noise(key_list[17], (D,), 0.3, 2.0)
    out_grad = noise(key_list[18], (MICRO, TOKENS, D), 1.0, 6.0, ((1, 32),))
    return {"tokens": tokens, "doc_lengths": doc_lengths, "rand_blocks": rand_blocks, "query_weight": query_weight, "key_weight": key_weight, "value_weight": value_weight, "query_bias": query_bias, "value_bias": value_bias, "proj_weight": proj_weight, "proj_bias": proj_bias, "first_gain": first_gain, "first_bias": first_bias, "second_gain": second_gain, "second_bias": second_bias, "inner_weight": inner_weight, "inner_bias": inner_bias, "outer_weight": outer_weight, "outer_bias": outer_bias, "out_grad": out_grad}


NORM_EPS = 1e-05
MASKED = -1000000000.0
PRECISE = lax.Precision.HIGHEST

@jax.custom_vjp
def low(v):
    return lax.optimization_barrier(v.astype(jnp.bfloat16)).astype(jnp.float32)

@jax.custom_vjp
def low_back(v):
    return v

def low_keep(v):
    return (low(v), None)

def low_pass(kept, grad):
    return (grad,)

def back_keep(v):
    return (v, None)

def back_low(kept, grad):
    return (low(grad),)
low.defvjp(low_keep, low_pass)
low_back.defvjp(back_keep, back_low)

def matmul(left, right):
    return jnp.dot(left, right, precision=PRECISE)

def gelu_exact(values):
    return 0.5 * values * (1.0 + lax.erf(values / math.sqrt(2.0)))

def layer_norm(values, norm_gain, norm_shift):
    row_mean = lax.optimization_barrier(jnp.mean(values, axis=-1, keepdims=True))
    centred = values - row_mean
    inverse = lax.rsqrt(lax.optimization_barrier(jnp.mean(centred * centred, axis=-1, keepdims=True)) + NORM_EPS)
    return centred * inverse * norm_gain + norm_shift

def block_keys(lengths, randoms, blocks, top_block):
    doc_ends = jnp.cumsum(lengths).astype(jnp.int32)
    doc_starts = (doc_ends - lengths).astype(jnp.int32)
    doc_owner = lax.optimization_barrier(jnp.sum((blocks[:, None] >= doc_ends[None, :]).astype(jnp.int32), axis=1)).astype(jnp.int32)
    doc_ids = jnp.arange(lengths.shape[0], dtype=jnp.int32)
    doc_hit = doc_owner[:, None] == doc_ids[None, :]
    doc_first = lax.optimization_barrier(jnp.sum(jnp.where(doc_hit, doc_starts[None, :], 0), axis=1)).astype(jnp.int32)
    doc_final = lax.optimization_barrier(jnp.sum(jnp.where(doc_hit, doc_ends[None, :], 0), axis=1)).astype(jnp.int32)
    fixed_keys = jnp.stack([jnp.maximum(blocks - 1, 0), blocks, jnp.minimum(blocks + 1, top_block), doc_first, doc_first + 1], axis=1).astype(jnp.int32)
    block_count = randoms.shape[0]
    head_count = randoms.shape[1]
    key_index = jnp.concatenate([jnp.broadcast_to(fixed_keys[:, None, :], (block_count, head_count, 5)), randoms.astype(jnp.int32)], axis=2)
    always_on = blocks >= 0
    key_valid = jnp.stack([blocks > doc_first, always_on, blocks + 1 < doc_final, always_on, always_on, always_on, always_on, always_on], axis=1)
    return (key_index, key_valid)

def attend(queries, keys_in, values_in, key_index, key_valid):
    query_blocks = queries.transpose(0, 2, 1, 3).reshape(TOTAL_BLK // 8, 8, HEADS, BLOCK, HEAD)
    keys_all = keys_in.transpose(2, 0, 1, 3)
    values_all = values_in.transpose(2, 0, 1, 3)
    head_ids = jnp.arange(HEADS, dtype=jnp.int32)[None, :, None]

    def one_step(operands):
        query_part, index_part, valid_part = operands
        keys_part = keys_all[head_ids, index_part].reshape(8, HEADS, -1, HEAD)
        values_part = values_all[head_ids, index_part].reshape(8, HEADS, -1, HEAD)
        scores = low_back(jnp.einsum('ghqd,ghkd->ghqk', query_part, keys_part, precision=PRECISE))
        key_mask = jnp.repeat(valid_part, BLOCK, axis=1)[:, None, None, :]
        scores = jnp.where(key_mask, scores, MASKED)
        row_top = lax.optimization_barrier(jnp.max(scores, axis=-1, keepdims=True))
        raised = jnp.exp(scores - row_top)
        weights = raised / lax.optimization_barrier(jnp.sum(raised, axis=-1, keepdims=True))
        return jnp.einsum('ghqk,ghkd->ghqd', low(weights), values_part, precision=PRECISE)
    context = lax.map(jax.checkpoint(one_step), (query_blocks, key_index.reshape(TOTAL_BLK // 8, 8, HEADS, -1), key_valid.reshape(TOTAL_BLK // 8, 8, -1)))
    return context.reshape(TOTAL_BLK, HEADS, BLOCK, HEAD).transpose(0, 2, 1, 3).reshape(TOKENS, D)

def forward(inputs, weight_list, key_index, key_valid):
    query_weight, key_weight, value_weight, query_bias, value_bias, proj_weight, proj_bias, first_gain, first_bias, second_gain, second_bias, inner_weight, inner_bias, outer_weight, outer_bias = weight_list
    score_scale = 1.0 / math.sqrt(HEAD)
    normed_one = low(layer_norm(inputs, first_gain, first_bias))
    queries = low(low_back((matmul(normed_one, query_weight) + query_bias) * score_scale))
    keys_now = low(low_back(matmul(normed_one, key_weight)))
    values_now = low(low_back(matmul(normed_one, value_weight) + value_bias))
    block_shape = (TOTAL_BLK, BLOCK, HEADS, HEAD)
    context = low(low_back(attend(queries.reshape(block_shape), keys_now.reshape(block_shape), values_now.reshape(block_shape), key_index, key_valid)))
    hidden = inputs + low_back(matmul(context, proj_weight) + proj_bias)
    normed_two = low(layer_norm(hidden, second_gain, second_bias))
    before = low_back(matmul(normed_two, inner_weight) + inner_bias)
    active = low(gelu_exact(before))
    return hidden + matmul(active, outer_weight) + outer_bias

def reference(tokens, doc_lengths, rand_blocks, query_weight, key_weight, value_weight, query_bias, value_bias, proj_weight, proj_bias, first_gain, first_bias, second_gain, second_bias, inner_weight, inner_bias, outer_weight, outer_bias, out_grad):
    params = tuple((weight_arg.astype(jnp.float32) for weight_arg in (query_weight, key_weight, value_weight, query_bias, value_bias, proj_weight, proj_bias, first_gain, first_bias, second_gain, second_bias, inner_weight, inner_bias, outer_weight, outer_bias)))
    grad_sums = tuple((jnp.zeros_like(weight_arg) for weight_arg in params))
    outputs = []
    input_grads = []
    all_blocks = jnp.arange(TOTAL_BLK, dtype=jnp.int32)
    for micro_index in range(MICRO):
        key_index, key_valid = block_keys(doc_lengths[micro_index], rand_blocks[micro_index], all_blocks, TOTAL_BLK - 1)

        def layer_fn(inputs, *weight_list):
            return forward(inputs, weight_list, key_index, key_valid)
        result, pull_back = jax.vjp(layer_fn, tokens[micro_index].astype(jnp.float32), *params)
        grad_list = pull_back(out_grad[micro_index].astype(jnp.float32))
        outputs.append(result.astype(jnp.bfloat16))
        input_grads.append(grad_list[0])
        grad_sums = jax.tree.map(jnp.add, grad_sums, tuple(grad_list[1:]))
    return (jnp.stack(outputs), jnp.stack(input_grads), grad_sums[0], grad_sums[1], grad_sums[2], grad_sums[3], grad_sums[4], grad_sums[5], grad_sums[6], grad_sums[7], grad_sums[8], grad_sums[9], grad_sums[10], grad_sums[11], grad_sums[12], grad_sums[13], grad_sums[14])
```

```python
import functools
import math

import jax
import jax.numpy as jnp
from jax import lax
from jax.experimental import pallas as pl
from jax.experimental.pallas import tpu as pltpu
from jax.sharding import PartitionSpec as P

BLOCK = 64
LONG_BLK = 64
PAIR = 2 * BLOCK
UNROLL = 4

NORM_EPS = 1e-05
MASKED = -1000000000.0

f32 = jnp.float32
bf16 = jnp.bfloat16

NN = (((1,), (0,)), ((), ()))
NT = (((1,), (1,)), ((), ()))
TN = (((0,), (0,)), ((), ()))


def contract(left, right, dims):
    return lax.dot_general(left, right, dims, preferred_element_type=f32)


def from_behind(block, axis, distance):
    devices = range(lax.axis_size(axis))
    route = [(i - distance, i) for i in devices if i - distance in devices]
    return lax.ppermute(block, axis, route)


def gelu_exact(values):
    return 0.5 * values * (1.0 + lax.erf(values / math.sqrt(2.0)))


def gelu_grad(values, grad_rows):
    _, pull_back = jax.vjp(gelu_exact, values)
    return pull_back(grad_rows)[0]


def layer_stats(values, norm_gain, norm_shift):
    row_mean = jnp.mean(values, axis=-1, keepdims=True)
    centred = values - row_mean
    inverse = lax.rsqrt(jnp.mean(centred * centred, axis=-1, keepdims=True) + NORM_EPS)
    normed = centred * inverse
    return (normed * norm_gain + norm_shift, normed, inverse)


def layer_back(grad_rows, normed, inverse, norm_gain):
    scaled = grad_rows * norm_gain
    inner_term = (
        scaled
        - jnp.mean(scaled, axis=-1, keepdims=True)
        - normed * jnp.mean(scaled * normed, axis=-1, keepdims=True)
    )
    return (inverse * inner_term, jnp.sum(grad_rows * normed, axis=0), jnp.sum(grad_rows, axis=0))


def block_keys(lengths, randoms, blocks, top_block):
    doc_ends = jnp.cumsum(lengths)
    doc_starts = doc_ends - lengths
    doc_owner = jnp.sum((blocks[:, None] >= doc_ends[None, :]).astype(jnp.int32), axis=1)
    doc_ids = jnp.arange(lengths.shape[0], dtype=jnp.int32)
    doc_hit = doc_owner[:, None] == doc_ids[None, :]
    doc_first = jnp.sum(jnp.where(doc_hit, doc_starts[None, :], 0), axis=1)
    doc_final = jnp.sum(jnp.where(doc_hit, doc_ends[None, :], 0), axis=1)
    fixed_keys = jnp.stack(
        [
            jnp.maximum(blocks - 1, 0),
            jnp.minimum(blocks + 1, top_block),
            blocks,
            doc_first,
            doc_first + 1,
        ],
        axis=1,
    )
    block_count = randoms.shape[0]
    head_count = randoms.shape[1]
    key_index = jnp.concatenate(
        [jnp.broadcast_to(fixed_keys[:, None, :], (block_count, head_count, 5)), randoms], axis=2
    )
    key_valid = jnp.stack([blocks > doc_first, blocks + 1 < doc_final], axis=1)
    return (key_index, key_valid.astype(jnp.int32))


def block_rows(block):
    return pl.ds(pl.multiple_of(block * BLOCK, BLOCK), BLOCK)


def listed_blocks(index_ref, store, base, slots):
    return jnp.concatenate(
        [store[block_rows(index_ref[base + slot]), :] for slot in range(slots)], axis=0
    )


def mask_scores(scores, valid_ref, block):
    lane = lax.broadcasted_iota(jnp.int32, (1, PAIR), 1)
    keep = jnp.where(lane < BLOCK, valid_ref[2 * block], valid_ref[2 * block + 1]) > 0
    return jnp.concatenate([jnp.where(keep, scores[:, :PAIR], MASKED), scores[:, PAIR:]], axis=1)


def forward_kernel(slots, index_ref, valid_ref, query_ref, *refs):
    *pieces, context_ref, logsum_ref, store = refs
    rows = query_ref.shape[0]
    blocks = rows // BLOCK
    head = pl.program_id(0)
    for place, piece in enumerate(pieces):
        store[place * rows : (place + 1) * rows, :] = piece[...]

    def step(group, carry):
        ids = [group * UNROLL + unit for unit in range(UNROLL)]
        listed = [
            listed_blocks(index_ref, store, (head * blocks + block) * slots, slots)
            for block in ids
        ]
        scores = [
            mask_scores(contract(query_ref[block_rows(block), :], pairs, NT), valid_ref, block)
            for block, pairs in zip(ids, listed)
        ]
        probs = []
        for block, score in zip(ids, scores):
            top = jnp.max(score, axis=1, keepdims=True)
            raised = jnp.exp(score - top)
            total = jnp.sum(raised, axis=1, keepdims=True)
            probs.append((raised * (1.0 / total)).astype(bf16))
            logsum_ref[block_rows(block), :] = jnp.broadcast_to(
                top + jnp.log(total), (BLOCK, PAIR)
            )
        for block, prob, pairs in zip(ids, probs, listed):
            context_ref[block_rows(block), :] = contract(prob, pairs, NN).astype(bf16)
        return carry

    lax.fori_loop(0, blocks // UNROLL, step, 0)


def backward_kernel(slots, count, index_ref, valid_ref, both_ref, logsum_ref, *refs):
    pieces = refs[:count]
    grad_query_ref = refs[count]
    grad_pieces = refs[count + 1 : 2 * count + 1]
    store, sums = refs[2 * count + 1 :]
    rows = both_ref.shape[0]
    blocks = rows // BLOCK
    head = pl.program_id(0)
    for place, piece in enumerate(pieces):
        store[place * rows : (place + 1) * rows, :] = piece[...]
    sums[...] = jnp.zeros_like(sums)
    lane = lax.broadcasted_iota(jnp.int32, (BLOCK, PAIR), 1)

    def step(group, carry):
        ids = [group * UNROLL + unit for unit in range(UNROLL)]
        listed = [
            listed_blocks(index_ref, store, (head * blocks + block) * slots, slots)
            for block in ids
        ]
        lefts = []
        for block in ids:
            both = both_ref[block_rows(block), :]
            lefts.append(
                jnp.concatenate(
                    [
                        jnp.where(lane < BLOCK, both, 0).astype(bf16),
                        jnp.where(lane < BLOCK, 0, both).astype(bf16),
                    ],
                    axis=0,
                )
            )
        products = [contract(left, pairs, NT) for left, pairs in zip(lefts, listed)]
        mixes = []
        for block, product in zip(ids, products):
            score = mask_scores(product[:BLOCK], valid_ref, block)
            grad_prob = product[BLOCK:]
            logsum = jnp.concatenate([logsum_ref[block_rows(block), :]] * (slots // 2), axis=1)
            prob = jnp.exp(score - logsum)
            delta = jnp.sum(prob * grad_prob, axis=1, keepdims=True)
            grad_score = prob * (grad_prob - delta)
            mixes.append(jnp.concatenate([grad_score.astype(bf16), prob.astype(bf16)], axis=0))
        for block, mix, pairs in zip(ids, mixes, listed):
            grad_query_ref[block_rows(block), :] = contract(mix[:BLOCK], pairs, NN).astype(bf16)
        terms = [contract(mix, left, TN) for mix, left in zip(mixes, lefts)]
        for block, term in zip(ids, terms):
            base = (head * blocks + block) * slots
            for slot in range(slots):
                sums[block_rows(index_ref[base + slot]), :] += term[
                    slot * BLOCK : (slot + 1) * BLOCK
                ]
        return carry

    lax.fori_loop(0, blocks // UNROLL, step, 0)
    for place, grad_piece in enumerate(grad_pieces):
        grad_piece[...] = sums[place * rows : (place + 1) * rows, :].astype(bf16)


def attend_forward(index, valid, queries, pieces, heads, slots):
    rows = queries.shape[0]
    spec = pl.BlockSpec((rows, PAIR), lambda head, *_: (0, head))
    work = heads * rows * slots * BLOCK
    return pl.pallas_call(
        functools.partial(forward_kernel, slots),
        grid_spec=pltpu.PrefetchScalarGridSpec(
            num_scalar_prefetch=2,
            grid=(heads,),
            in_specs=[spec] * (1 + len(pieces)),
            out_specs=[spec, spec],
            scratch_shapes=[pltpu.VMEM((rows * len(pieces), PAIR), bf16)],
        ),
        out_shape=[
            jax.ShapeDtypeStruct((rows, heads * PAIR), bf16),
            jax.ShapeDtypeStruct((rows, heads * PAIR), f32),
        ],
        compiler_params=pltpu.CompilerParams(vmem_limit_bytes=40 * 2**20),
        cost_estimate=pl.CostEstimate(
            flops=work * PAIR * 4, bytes_accessed=rows * heads * PAIR * 18, transcendentals=work
        ),
    )(index, valid, queries, *pieces)


def attend_backward(index, valid, both, logsum, pieces, heads, slots):
    rows = both.shape[0]
    count = len(pieces)
    spec = pl.BlockSpec((rows, PAIR), lambda head, *_: (0, head))
    work = heads * rows * slots * BLOCK
    return pl.pallas_call(
        functools.partial(backward_kernel, slots, count),
        grid_spec=pltpu.PrefetchScalarGridSpec(
            num_scalar_prefetch=2,
            grid=(heads,),
            in_specs=[spec] * (2 + count),
            out_specs=[spec] * (1 + count),
            scratch_shapes=[
                pltpu.VMEM((rows * count, PAIR), bf16),
                pltpu.VMEM((rows * count, PAIR), f32),
            ],
        ),
        out_shape=[jax.ShapeDtypeStruct((rows, heads * PAIR), bf16)] * (1 + count),
        compiler_params=pltpu.CompilerParams(vmem_limit_bytes=50 * 2**20),
        cost_estimate=pl.CostEstimate(
            flops=work * PAIR * 10, bytes_accessed=rows * heads * PAIR * 28, transcendentals=work
        ),
    )(index, valid, both, logsum, *pieces)


def body(
    tokens,
    doc_lengths,
    rand_blocks,
    query_weight,
    key_weight,
    value_weight,
    query_bias,
    value_bias,
    proj_weight,
    proj_bias,
    first_gain,
    first_bias,
    second_gain,
    second_bias,
    inner_weight,
    inner_bias,
    outer_weight,
    outer_bias,
    out_grad,
):
    micro_count, local_rows, model_width = tokens.shape
    seq_count = lax.axis_size("seq")
    tp_count = lax.axis_size("tp")
    seq_place = lax.axis_index("seq")
    tp_place = lax.axis_index("tp")
    block_dev = rand_blocks.shape[1]
    heads = rand_blocks.shape[2]
    local_width = query_weight.shape[1]
    head_size = local_width // heads
    hidden_units = inner_weight.shape[1]
    group_rows = block_dev * BLOCK
    reach_dev = (block_dev + LONG_BLK - 2) // block_dev
    window = 2 * reach_dev + 1
    score_scale = 1.0 / math.sqrt(head_size)
    lowest = (seq_place - reach_dev) * block_dev
    blocks = seq_place * block_dev + jnp.arange(block_dev, dtype=jnp.int32)
    top_block = block_dev * seq_count - 1

    held = jnp.concatenate([inner_weight.T, outer_weight, proj_weight, inner_bias[None]], axis=0)
    used_rows = held.shape[0]
    piece_rows = -(-used_rows // (16 * seq_count)) * 16
    held_rows = piece_rows * seq_count
    held = jnp.pad(held, ((0, held_rows - used_rows), (0, 0)))
    share = lax.dynamic_slice_in_dim(held, seq_place * piece_rows, piece_rows, axis=0)
    spread = lax.all_gather(share, ("tp", "seq"), axis=0, tiled=True)
    spread = spread.reshape(tp_count, held_rows, model_width)
    cuts = [0, hidden_units, 2 * hidden_units, 2 * hidden_units + local_width, used_rows]
    inner_full = spread[:, cuts[0] : cuts[1]].reshape(-1, model_width)
    outer_full = spread[:, cuts[1] : cuts[2]].reshape(-1, model_width)
    proj_full = spread[:, cuts[2] : cuts[3]].reshape(-1, model_width)
    inner_bias_full = spread[:, cuts[3] : cuts[4]].reshape(-1)

    def by_head(weight):
        return weight.reshape(weight.shape[:-1] + (heads, head_size))

    def side_by_side(first, second):
        paired = jnp.concatenate([by_head(first), by_head(second)], axis=-1)
        return paired.reshape(paired.shape[:-2] + (heads * PAIR,))

    query_wide = side_by_side(query_weight, jnp.zeros_like(query_weight))
    query_wide_bias = side_by_side(query_bias, jnp.zeros_like(query_bias))
    pair_wide = side_by_side(key_weight, value_weight)
    pair_wide_bias = side_by_side(jnp.zeros_like(value_bias), value_bias)

    stage = [{} for _ in range(micro_count)]
    for micro, held_in in enumerate(stage):
        inputs = tokens[micro].astype(f32)
        shifted, stats, inverse = layer_stats(inputs, first_gain, first_bias)
        held_in["inputs"], held_in["stats_one"], held_in["inverse_one"] = inputs, stats, inverse
        held_in["one"] = lax.all_gather(shifted.astype(bf16), "tp", axis=0, tiled=True)

    for micro, held_in in enumerate(stage):
        one = held_in["one"]
        pair_rows = (contract(one, pair_wide, NN) + pair_wide_bias).astype(bf16)
        pieces = [
            pair_rows if offset == 0 else from_behind(pair_rows, "seq", -offset)
            for offset in range(-reach_dev, reach_dev + 1)
        ]
        queries = ((contract(one, query_wide, NN) + query_wide_bias) * score_scale).astype(bf16)
        key_index, key_valid = block_keys(
            doc_lengths[micro], rand_blocks[micro], blocks, top_block
        )
        slots = key_index.shape[2]
        slot_index = jnp.clip(key_index - lowest, 0, window * block_dev - 1)
        held_in["index"] = slot_index.transpose(1, 0, 2).reshape(-1)
        held_in["valid"] = key_valid.reshape(-1)
        held_in["queries"], held_in["pieces"] = queries, pieces

    for held_in in stage:
        wide_context, held_in["logsum"] = attend_forward(
            held_in["index"],
            held_in["valid"],
            held_in["queries"],
            held_in["pieces"],
            heads,
            slots,
        )
        context = wide_context.reshape(group_rows, heads, PAIR)[:, :, head_size:]
        held_in["context"] = lax.all_to_all(
            context.reshape(group_rows, local_width), "tp", split_axis=0, concat_axis=1, tiled=True
        )

    outputs = []
    for micro, held_in in enumerate(stage):
        context = held_in["context"]
        hidden = held_in["inputs"] + contract(context, proj_full, NN) + proj_bias
        shifted, stats, inverse = layer_stats(hidden, second_gain, second_bias)
        two = shifted.astype(bf16)
        before = contract(two, inner_full, NT) + inner_bias_full
        active = gelu_exact(before).astype(bf16)
        result = hidden + contract(active, outer_full, NN) + outer_bias
        outputs.append(result.astype(bf16))
        grad_out = out_grad[micro]
        grad_float = grad_out.astype(f32)
        grad_active = contract(grad_out, outer_full, NT)
        grad_before = gelu_grad(before, grad_active).astype(bf16)
        grad_two = contract(grad_before, inner_full, NN)
        back, gain_sum, shift_sum = layer_back(grad_two, stats, inverse, second_gain)
        grad_hidden = grad_float + back
        branch = grad_hidden.astype(bf16)
        grad_context = contract(branch, proj_full, NT).astype(bf16)
        held_in["grad_context"] = lax.all_to_all(
            grad_context, "tp", split_axis=1, concat_axis=0, tiled=True
        )
        held_in["grad_hidden"] = grad_hidden
        held_in["dense"] = (two, grad_before, active, grad_out, context, branch)
        held_in["row_sums"] = (
            jnp.sum(grad_before.astype(f32), axis=0),
            gain_sum,
            shift_sum,
            jnp.sum(branch.astype(f32), axis=0),
            jnp.sum(grad_float, axis=0),
        )

    two, grad_before, active, grad_out, context, branch = (
        jnp.concatenate(group, axis=0) for group in zip(*(h["dense"] for h in stage))
    )
    inner_part = contract(grad_before, two, TN).astype(bf16)
    outer_part = contract(active, grad_out, TN).astype(bf16)
    proj_part = contract(context, branch, TN).astype(bf16)
    grad_rows = 2 * hidden_units + local_width
    grad_piece = -(-grad_rows // (16 * seq_count)) * 16
    grad_held = grad_piece * seq_count
    parts = jnp.concatenate(
        [
            inner_part.reshape(tp_count, hidden_units, model_width),
            outer_part.reshape(tp_count, hidden_units, model_width),
            proj_part.reshape(tp_count, local_width, model_width),
            jnp.zeros((tp_count, grad_held - grad_rows, model_width), bf16),
        ],
        axis=1,
    ).reshape(tp_count * grad_held, model_width)
    own_part = lax.psum_scatter(parts, ("tp", "seq"), scatter_dimension=0, tiled=True)
    dense_sum = lax.all_gather(own_part, "seq", axis=0, tiled=True).astype(f32)
    inner_weight_grad = dense_sum[cuts[0] : cuts[1]].T
    outer_weight_grad = dense_sum[cuts[1] : cuts[2]]
    proj_weight_grad = dense_sum[cuts[2] : cuts[3]]

    for held_in in stage:
        queries = held_in["queries"].reshape(group_rows, heads, PAIR)[:, :, :head_size]
        both = jnp.concatenate([queries, by_head(held_in["grad_context"])], axis=-1)
        held_in["grad_query"], *grad_pieces = attend_backward(
            held_in["index"],
            held_in["valid"],
            both.reshape(group_rows, heads * PAIR),
            held_in["logsum"],
            held_in["pieces"],
            heads,
            slots,
        )
        returned = grad_pieces[reach_dev].astype(f32)
        for offset in range(-reach_dev, reach_dev + 1):
            if offset != 0:
                returned = returned + from_behind(
                    grad_pieces[offset + reach_dev], "seq", offset
                ).astype(f32)
        held_in["grad_pair"] = returned.astype(bf16)

    scaled_wide = (query_wide * score_scale).astype(bf16)
    input_grads = []
    query_sum = pair_sum = 0.0
    query_bias_sum = pair_bias_sum = 0.0
    first_gain_sum = first_bias_sum = 0.0
    for held_in in stage:
        grad_query, grad_pair, one = held_in["grad_query"], held_in["grad_pair"], held_in["one"]
        rows = contract(grad_query, scaled_wide, NT) + contract(grad_pair, pair_wide, NT)
        grad_one = lax.psum_scatter(
            rows.astype(bf16), "tp", scatter_dimension=0, tiled=True
        ).astype(f32)
        query_sum = query_sum + contract(one, grad_query, TN)
        pair_sum = pair_sum + contract(one, grad_pair, TN)
        query_bias_sum = query_bias_sum + jnp.sum(grad_query.astype(f32), axis=0)
        pair_bias_sum = pair_bias_sum + jnp.sum(grad_pair.astype(f32), axis=0)
        back, gain_sum, shift_sum = layer_back(
            grad_one, held_in["stats_one"], held_in["inverse_one"], first_gain
        )
        first_gain_sum = first_gain_sum + gain_sum
        first_bias_sum = first_bias_sum + shift_sum
        input_grads.append(held_in["grad_hidden"] + back)

    def low_half(wide):
        return wide.reshape(wide.shape[:-1] + (heads, PAIR))[..., :head_size].reshape(
            wide.shape[:-1] + (local_width,)
        )

    def high_half(wide):
        return wide.reshape(wide.shape[:-1] + (heads, PAIR))[..., head_size:].reshape(
            wide.shape[:-1] + (local_width,)
        )

    query_grad, key_grad, value_grad = lax.psum(
        (low_half(query_sum) * score_scale, low_half(pair_sum), high_half(pair_sum)), "seq"
    )
    inner_bias_sum, second_gain_sum, second_bias_sum, proj_bias_sum, outer_bias_sum = (
        sum(group) for group in zip(*(h["row_sums"] for h in stage))
    )

    def own_columns(values):
        wide = jnp.zeros((tp_count, local_width), f32)
        return lax.dynamic_update_slice_in_dim(wide, values[None], tp_place, axis=0).reshape(-1)

    early = lax.psum(
        jnp.concatenate(
            [
                inner_bias_sum,
                second_gain_sum,
                second_bias_sum,
                proj_bias_sum,
                outer_bias_sum,
            ]
        ),
        ("seq", "tp"),
    )
    late = lax.psum(
        jnp.concatenate(
            [
                first_gain_sum,
                first_bias_sum,
                own_columns(low_half(query_bias_sum) * score_scale),
                own_columns(high_half(pair_bias_sum)),
            ]
        ),
        ("seq", "tp"),
    )
    inner_bias_all = early[: tp_count * hidden_units].reshape(tp_count, hidden_units)
    early_rows = early[tp_count * hidden_units :].reshape(-1, model_width)
    late_rows = late.reshape(-1, model_width)

    def my_columns(row):
        return lax.dynamic_slice_in_dim(row, tp_place * local_width, local_width)

    return (
        jnp.stack(outputs),
        jnp.stack(input_grads),
        query_grad,
        key_grad,
        value_grad,
        my_columns(late_rows[2]),
        my_columns(late_rows[3]),
        proj_weight_grad,
        early_rows[2],
        late_rows[0],
        late_rows[1],
        early_rows[0],
        early_rows[1],
        inner_weight_grad,
        lax.dynamic_index_in_dim(inner_bias_all, tp_place, axis=0, keepdims=False),
        outer_weight_grad,
        early_rows[3],
    )


def solution(mesh):
    return jax.shard_map(
        body,
        mesh=mesh,
        in_specs=(
            P(None, ("seq", "tp"), None),
            P(),
            P(None, "seq", "tp", None),
            P(None, "tp"),
            P(None, "tp"),
            P(None, "tp"),
            P("tp"),
            P("tp"),
            P("tp", None),
            P(),
            P(),
            P(),
            P(),
            P(),
            P(None, "tp"),
            P("tp"),
            P("tp", None),
            P(),
            P(None, ("seq", "tp"), None),
        ),
        out_specs=(
            P(None, ("seq", "tp"), None),
            P(None, ("seq", "tp"), None),
            P(None, "tp"),
            P(None, "tp"),
            P(None, "tp"),
            P("tp"),
            P("tp"),
            P("tp", None),
            P(),
            P(),
            P(),
            P(),
            P(),
            P(None, "tp"),
            P("tp"),
            P("tp", None),
            P(),
        ),
        check_vma=False,
    )
```

```python
import functools
import math

import jax
import jax.numpy as jnp
from jax import lax
from jax.experimental import pallas as pl
from jax.experimental.pallas import tpu as pltpu
from jax.sharding import PartitionSpec as P

BLOCK = 64
LONG_BLK = 64
SHORT_BLK = 8
PAIR = 2 * BLOCK
UNROLL = 4
SEQ = "seq"
TP = "tp"

NORM_EPS = 1e-05
MASKED = -1000000000.0

f32 = jnp.float32
bf16 = jnp.bfloat16

NN = (((1,), (0,)), ((), ()))
NT = (((1,), (1,)), ((), ()))
TN = (((0,), (0,)), ((), ()))


def contract(left, right, dims):
    return lax.dot_general(left, right, dims, preferred_element_type=f32)


def from_behind(block, axis, distance):
    devices = range(lax.axis_size(axis))
    route = [(i - distance, i) for i in devices if i - distance in devices]
    return lax.ppermute(block, axis, route)


def gelu_exact(values):
    return 0.5 * values * (1.0 + lax.erf(values / math.sqrt(2.0)))


def gelu_grad(values, grad_rows):
    _, pull_back = jax.vjp(gelu_exact, values)
    return pull_back(grad_rows)[0]


def layer_stats(values, norm_gain, norm_shift):
    row_mean = jnp.mean(values, axis=-1, keepdims=True)
    centred = values - row_mean
    inverse = lax.rsqrt(jnp.mean(centred * centred, axis=-1, keepdims=True) + NORM_EPS)
    normed = centred * inverse
    return (normed * norm_gain + norm_shift, normed, inverse)


def layer_back(grad_rows, normed, inverse, norm_gain):
    scaled = grad_rows * norm_gain
    inner_term = (
        scaled
        - jnp.mean(scaled, axis=-1, keepdims=True)
        - normed * jnp.mean(scaled * normed, axis=-1, keepdims=True)
    )
    return (inverse * inner_term, jnp.sum(grad_rows * normed, axis=0), jnp.sum(grad_rows, axis=0))


def block_keys(lengths, randoms, blocks):
    doc_ends = jnp.cumsum(lengths)
    doc_starts = doc_ends - lengths
    doc_owner = jnp.sum((blocks[:, None] >= doc_ends[None, :]).astype(jnp.int32), axis=1)
    doc_ids = jnp.arange(lengths.shape[0], dtype=jnp.int32)
    doc_hit = doc_owner[:, None] == doc_ids[None, :]
    doc_first = jnp.sum(jnp.where(doc_hit, doc_starts[None, :], 0), axis=1)
    doc_final = jnp.sum(jnp.where(doc_hit, doc_ends[None, :], 0), axis=1)
    fixed_keys = jnp.stack(
        [
            jnp.maximum(blocks - 1, doc_first),
            jnp.minimum(blocks + 1, doc_final - 1),
            blocks,
            doc_first,
            doc_first + 1,
        ],
        axis=1,
    )
    block_count = randoms.shape[0]
    head_count = randoms.shape[1]
    key_index = jnp.concatenate(
        [jnp.broadcast_to(fixed_keys[:, None, :], (block_count, head_count, 5)), randoms], axis=2
    )
    key_valid = jnp.stack([blocks > doc_first, blocks + 1 < doc_final], axis=1)
    return (key_index, key_valid.astype(jnp.int32))


def block_rows(block):
    return pl.ds(pl.multiple_of(block * BLOCK, BLOCK), BLOCK)


def listed_blocks(index_ref, store, base, slots):
    return jnp.concatenate(
        [store[block_rows(index_ref[base + slot]), :] for slot in range(slots)], axis=0
    )


def mask_scores(scores, valid_ref, block):
    lane = lax.broadcasted_iota(jnp.int32, (1, PAIR), 1)
    keep = jnp.where(lane < BLOCK, valid_ref[2 * block], valid_ref[2 * block + 1]) > 0
    return jnp.concatenate([jnp.where(keep, scores[:, :PAIR], MASKED), scores[:, PAIR:]], axis=1)


def fill_store(store, pieces):
    place = 0
    for piece in pieces:
        store[place : place + piece.shape[0], :] = piece[...]
        place += piece.shape[0]


def each_head(heads, work):
    for head in range(heads):

        @pl.when(pl.program_id(0) == head)
        def _():
            work(slice(head * BLOCK, (head + 1) * BLOCK))


def forward_kernel(slots, heads, index_ref, valid_ref, query_ref, *refs):
    *pieces, context_ref, logsum_ref, store, wide_query, wide_context = refs
    rows = query_ref.shape[0]
    blocks = rows // BLOCK
    head = pl.program_id(0)
    fill_store(store, pieces)

    def take_query(columns):
        query = query_ref[:, columns]
        wide_query[...] = jnp.concatenate([query, jnp.zeros_like(query)], axis=1)

    each_head(heads, take_query)

    def step(group, carry):
        ids = [group * UNROLL + unit for unit in range(UNROLL)]
        listed = [
            listed_blocks(index_ref, store, (head * blocks + block) * slots, slots)
            for block in ids
        ]
        scores = [
            mask_scores(contract(wide_query[block_rows(block), :], pairs, NT), valid_ref, block)
            for block, pairs in zip(ids, listed)
        ]
        probs = []
        for block, score in zip(ids, scores):
            top = jnp.max(score, axis=1, keepdims=True)
            raised = jnp.exp(score - top)
            total = jnp.sum(raised, axis=1, keepdims=True)
            probs.append((raised * (1.0 / total)).astype(bf16))
            logsum_ref[block_rows(block), :] = jnp.broadcast_to(
                top + jnp.log(total), (BLOCK, PAIR)
            )
        for block, prob, pairs in zip(ids, probs, listed):
            wide_context[block_rows(block), :] = contract(prob, pairs, NN).astype(bf16)
        return carry

    lax.fori_loop(0, blocks // UNROLL, step, 0)

    def give_context(columns):
        context_ref[:, columns] = wide_context[:, BLOCK:]

    each_head(heads, give_context)


def backward_kernel(slots, heads, count, index_ref, valid_ref, query_ref, grad_ref, logsum_ref, *refs):
    pieces = refs[:count]
    grad_query_ref = refs[count]
    grad_pieces = refs[count + 1 : 2 * count + 1]
    store, sums, both_rows, wide_grad = refs[2 * count + 1 :]
    rows = query_ref.shape[0]
    blocks = rows // BLOCK
    head = pl.program_id(0)
    fill_store(store, pieces)
    sums[...] = jnp.zeros_like(sums)
    lane = lax.broadcasted_iota(jnp.int32, (BLOCK, PAIR), 1)

    def take_both(columns):
        both_rows[...] = jnp.concatenate([query_ref[:, columns], grad_ref[:, columns]], axis=1)

    each_head(heads, take_both)

    def step(group, carry):
        ids = [group * UNROLL + unit for unit in range(UNROLL)]
        listed = [
            listed_blocks(index_ref, store, (head * blocks + block) * slots, slots)
            for block in ids
        ]
        lefts = []
        for block in ids:
            both = both_rows[block_rows(block), :]
            lefts.append(
                jnp.concatenate(
                    [
                        jnp.where(lane < BLOCK, both, 0).astype(bf16),
                        jnp.where(lane < BLOCK, 0, both).astype(bf16),
                    ],
                    axis=0,
                )
            )
        products = [contract(left, pairs, NT) for left, pairs in zip(lefts, listed)]
        mixes = []
        for block, product in zip(ids, products):
            score = mask_scores(product[:BLOCK], valid_ref, block)
            grad_prob = product[BLOCK:]
            logsum = jnp.concatenate([logsum_ref[block_rows(block), :]] * (slots // 2), axis=1)
            prob = jnp.exp(score - logsum)
            delta = jnp.sum(prob * grad_prob, axis=1, keepdims=True)
            grad_score = prob * (grad_prob - delta)
            mixes.append(jnp.concatenate([grad_score.astype(bf16), prob.astype(bf16)], axis=0))
        for block, mix, pairs in zip(ids, mixes, listed):
            wide_grad[block_rows(block), :] = contract(mix[:BLOCK], pairs, NN).astype(bf16)
        terms = [contract(mix, left, TN) for mix, left in zip(mixes, lefts)]
        for block, term in zip(ids, terms):
            base = (head * blocks + block) * slots
            for slot in range(slots):
                sums[block_rows(index_ref[base + slot]), :] += term[
                    slot * BLOCK : (slot + 1) * BLOCK
                ]
        return carry

    lax.fori_loop(0, blocks // UNROLL, step, 0)
    place = 0
    for grad_piece in grad_pieces:
        grad_piece[...] = sums[place : place + grad_piece.shape[0], :].astype(bf16)
        place += grad_piece.shape[0]

    def give_grad(columns):
        grad_query_ref[:, columns] = wide_grad[:, :BLOCK]

    each_head(heads, give_grad)


def lasting(microseconds):
    return pl.CostEstimate(
        flops=0, bytes_accessed=int(microseconds * 3.69e6), transcendentals=0
    )


def per_head(array):
    return pl.BlockSpec((array.shape[0], PAIR), lambda head, *_: (0, head))


def whole(array):
    return pl.BlockSpec(array.shape, lambda head, *_: (0, 0))


def attend_forward(index, valid, queries, pieces, heads, slots):
    rows = queries.shape[0]
    stored = sum(piece.shape[0] for piece in pieces)
    logsum = jax.ShapeDtypeStruct((rows, heads * PAIR), f32)
    return pl.pallas_call(
        functools.partial(forward_kernel, slots, heads),
        grid_spec=pltpu.PrefetchScalarGridSpec(
            num_scalar_prefetch=2,
            grid=(heads,),
            in_specs=[whole(queries)] + [per_head(piece) for piece in pieces],
            out_specs=[whole(queries), per_head(logsum)],
            scratch_shapes=[
                pltpu.VMEM((stored, PAIR), bf16),
                pltpu.VMEM((rows, PAIR), bf16),
                pltpu.VMEM((rows, PAIR), bf16),
            ],
        ),
        out_shape=[jax.ShapeDtypeStruct(queries.shape, bf16), logsum],
        compiler_params=pltpu.CompilerParams(vmem_limit_bytes=40 * 2**20),
        cost_estimate=lasting(18),
    )(index, valid, queries, *pieces)


def attend_backward(index, valid, queries, grads, logsum, pieces, heads, slots):
    rows = queries.shape[0]
    stored = sum(piece.shape[0] for piece in pieces)
    piece_specs = [per_head(piece) for piece in pieces]
    return pl.pallas_call(
        functools.partial(backward_kernel, slots, heads, len(pieces)),
        grid_spec=pltpu.PrefetchScalarGridSpec(
            num_scalar_prefetch=2,
            grid=(heads,),
            in_specs=[whole(queries), whole(grads), per_head(logsum)] + piece_specs,
            out_specs=[whole(queries)] + piece_specs,
            scratch_shapes=[
                pltpu.VMEM((stored, PAIR), bf16),
                pltpu.VMEM((stored, PAIR), f32),
                pltpu.VMEM((rows, PAIR), bf16),
                pltpu.VMEM((rows, PAIR), bf16),
            ],
        ),
        out_shape=[jax.ShapeDtypeStruct(queries.shape, bf16)]
        + [jax.ShapeDtypeStruct(piece.shape, bf16) for piece in pieces],
        compiler_params=pltpu.CompilerParams(vmem_limit_bytes=50 * 2**20),
        cost_estimate=lasting(25),
    )(index, valid, queries, grads, logsum, *pieces)


def plane_exchange(values, split_axis, concat_axis):
    count = lax.axis_size(SEQ)
    groups = [list(range(place, count, 2)) for place in range(2)]
    return lax.all_to_all(
        values,
        SEQ,
        split_axis=split_axis,
        concat_axis=concat_axis,
        axis_index_groups=groups,
        tiled=True,
    )


def plane_gather(values):
    count = lax.axis_size(SEQ) // 2
    return plane_exchange(jnp.concatenate([values] * count, axis=0), 0, 0)


def core_swap(block):
    route = [(place, place ^ 1) for place in range(lax.axis_size(SEQ))]
    return lax.ppermute(block, SEQ, route)


def column_shift(block, step):
    count = lax.axis_size(TP)
    return lax.ppermute(block, TP, [(place, (place + step) % count) for place in range(count)])


def column_gather(values):
    count = lax.axis_size(TP)
    place = lax.axis_index(TP)
    spread = jnp.zeros((count,) + values.shape, values.dtype)
    spread = lax.dynamic_update_index_in_dim(spread, values, place, axis=0)
    for step in range(1, count):
        spread = lax.dynamic_update_index_in_dim(
            spread, column_shift(values, step), (place - step) % count, axis=0
        )
    return spread


def after(values, *earlier):
    return lax.optimization_barrier((values, earlier))[0]


def sum_parts(parts):
    total = parts[0].astype(f32)
    for place in range(1, len(parts)):
        total = total + parts[place].astype(f32)
    return total


def partner_of(place):
    return place + 1 - 2 * (place % 2)


def enter(neighbours):
    barrier = pltpu.get_barrier_semaphore()
    count = 0
    for exists, device in neighbours:

        @pl.when(exists)
        def _():
            pl.semaphore_signal(
                barrier, inc=1, device_id=device, device_id_type=pl.DeviceIdType.MESH
            )

        count = count + jnp.where(exists, 1, 0)
    pl.semaphore_wait(barrier, count)


def remote(source, target, send, receive, device):
    return pltpu.make_async_remote_copy(
        src_ref=source,
        dst_ref=target,
        send_sem=send,
        recv_sem=receive,
        device_id=device,
        device_id_type=pl.DeviceIdType.MESH,
    )


def column_reduce_kernel(
    parts,
    near_ref,
    far_ref,
    out_ref,
    sums,
    given,
    came,
    load_sem,
    send_far,
    recv_far,
    send_z,
    recv_z,
):
    count = lax.axis_size(TP)
    place = lax.axis_index(TP)
    other = {SEQ: partner_of(lax.axis_index(SEQ))}
    rows = out_ref.shape[0] // parts
    step_rows = 128
    load = pltpu.make_async_copy(near_ref, sums, load_sem)
    load.start()
    enter(
        [
            (place >= 0, other),
            (place < count - 1, {TP: place + 1}),
            (place > 0, {TP: place - 1}),
        ]
    )

    def cut(part):
        return pl.ds(part * rows, rows)

    def across(owner):
        return remote(
            far_ref.at[owner], given.at[owner], send_far.at[owner], recv_far.at[owner], other
        )

    def along(way, owner, part):
        return remote(
            sums.at[owner, cut(part)],
            came.at[way, owner, cut(part)],
            send_z.at[way, owner, part],
            recv_z.at[way, owner, part],
            {TP: place - 1 if way == 0 else place + 1},
        )

    def add(owner, source, part):
        @pl.loop(0, rows // step_rows)
        def _(step):
            at = pl.ds(pl.multiple_of(part * rows + step * step_rows, step_rows), step_rows)
            total = sums[owner, at, :].astype(f32) + source[at, :].astype(f32)
            sums[owner, at, :] = total.astype(sums.dtype)

    order = []
    for step in range(count):
        for owner in (step, count - 1 - step):
            if owner not in order:
                order.append(owner)
    for owner in order:
        across(owner).start()
    load.wait()
    for owner in order:
        across(owner).wait_recv()
        for part in range(parts):
            add(owner, given.at[owner], part)
            for way in range(2):
                passes = place > owner if way == 0 else place < owner
                takes = (place < count - 1) if way == 0 else (place > 0)

                @pl.when(passes)
                def _():
                    @pl.when(takes)
                    def _():
                        along(way, owner, part).wait_recv()
                        add(owner, came.at[way, owner], part)

                    along(way, owner, part).start()

    for part in range(parts):
        for way in range(2):
            for owner in range(count):
                takes = (place < count - 1) if way == 0 else (place > 0)

                @pl.when((place == owner) & takes)
                def _():
                    along(way, owner, part).wait_recv()
                    add(owner, came.at[way, owner], part)

    for owner in range(count):

        @pl.when(place == owner)
        def _():
            out_ref[...] = sums[owner]

        across(owner).wait_send()
        for part in range(parts):
            for way in range(2):

                @pl.when(place > owner if way == 0 else place < owner)
                def _():
                    along(way, owner, part).wait_send()


def column_reduce_both(near, far, collective_id, parts=2):
    count = lax.axis_size(TP)
    block = near.shape[1:]
    return pl.pallas_call(
        functools.partial(column_reduce_kernel, parts),
        out_shape=jax.ShapeDtypeStruct(block, near.dtype),
        in_specs=[pl.BlockSpec(memory_space=pl.ANY), pl.BlockSpec(memory_space=pltpu.VMEM)],
        out_specs=pl.BlockSpec(memory_space=pltpu.VMEM),
        scratch_shapes=[
            pltpu.VMEM((count,) + block, near.dtype),
            pltpu.VMEM((count,) + block, near.dtype),
            pltpu.VMEM((2, count) + block, near.dtype),
            pltpu.SemaphoreType.DMA,
            pltpu.SemaphoreType.DMA((count,)),
            pltpu.SemaphoreType.DMA((count,)),
            pltpu.SemaphoreType.DMA((2, count, parts)),
            pltpu.SemaphoreType.DMA((2, count, parts)),
        ],
        compiler_params=pltpu.CompilerParams(
            collective_id=collective_id, has_side_effects=True, vmem_limit_bytes=32 * 2**20
        ),
        cost_estimate=lasting(55),
    )(near, far)


def plane_ids():
    seq_place = lax.axis_index(SEQ)
    chip, core = seq_place // 2, seq_place % 2
    beside = chip + 1 - 2 * (chip % 2)
    above = chip + 2 - 4 * (chip // 2)
    facing = 3 - chip
    return chip, core, beside, above, facing


def column_way(place, way, distance):
    return place - distance if way == 0 else place + distance


class ColumnSpread:

    def __init__(self, parts, own, near, far, other, keep_sem, along_sems, across_sems):
        self.parts, self.own, self.near, self.far = parts, own, near, far
        self.other, self.keep_sem = other, keep_sem
        self.along_sems, self.across_sems = along_sems, across_sems
        self.count = lax.axis_size(TP)
        self.place = lax.axis_index(TP)
        self.rows = own.shape[0] // parts

    def cut(self, part):
        return pl.ds(part * self.rows, self.rows)

    def block(self, way, distance, part):
        if distance == 0:
            return self.own.at[self.cut(part)]
        return self.near.at[column_way(self.place, way, distance), self.cut(part)]

    def along(self, way, distance, part):
        return remote(
            self.block(way, distance, part),
            self.near.at[column_way(self.place, way, distance), self.cut(part)],
            self.along_sems[0].at[way, distance, part],
            self.along_sems[1].at[way, distance, part],
            {TP: self.place + 1 if way == 0 else self.place - 1},
        )

    def landed(self, way, distance, part):
        block = self.near.at[column_way(self.place, way, distance), self.cut(part)]
        return remote(
            block,
            block,
            self.along_sems[0].at[way, distance, part],
            self.along_sems[1].at[way, distance - 1, part],
            self.other,
        )

    def across(self, way, distance, part):
        return remote(
            self.block(way, distance, part),
            self.far.at[column_way(self.place, way, distance), self.cut(part)],
            self.across_sems[0].at[way, distance, part],
            self.across_sems[1].at[way, distance, part],
            self.other,
        )

    def keep(self):
        return pltpu.make_async_copy(self.own, self.near.at[self.place], self.keep_sem)

    def goes_on(self, way):
        return self.place < self.count - 1 if way == 0 else self.place > 0

    def has_come(self, way, distance):
        if way == 0:
            return self.place >= distance
        return self.place + distance < self.count

    def start(self):
        for part in range(self.parts):
            for way in range(2):

                @pl.when(self.goes_on(way))
                def _():
                    self.along(way, 0, part).start()

        if self.far is not None:
            for part in range(self.parts):
                self.across(0, 0, part).start()
        self.keep().start()

    def step(self, distance, part):
        for way in range(2):

            @pl.when(self.has_come(way, distance))
            def _():
                self.landed(way, distance, part).wait_recv()
                if distance < self.count - 1:

                    @pl.when(self.goes_on(way))
                    def _():
                        self.along(way, distance, part).start()

                if self.far is not None:
                    self.across(way, distance, part).start()

    def finish(self):
        self.keep().wait()
        for part in range(self.parts):
            if self.far is not None:
                self.across(0, 0, part).wait()
            for way in range(2):

                @pl.when(self.goes_on(way))
                def _():
                    self.along(way, 0, part).wait_send()

        for distance in range(1, self.count):
            for part in range(self.parts):
                for way in range(2):

                    @pl.when(self.has_come(way, distance))
                    def _():
                        if distance < self.count - 1:

                            @pl.when(self.goes_on(way))
                            def _():
                                self.along(way, distance, part).wait_send()

                        if self.far is not None:
                            self.across(way, distance, part).wait()


class PlaneSpread:

    def __init__(self, own, out, sems):
        self.own, self.out = own, out
        self.send_row, self.recv_row, self.send_on, self.recv_on = sems
        self.chip, core, beside, above, self.facing = plane_ids()
        self.ways = ({SEQ: 2 * beside + core}, {SEQ: 2 * above + core})
        self.chips = (beside, above)

    def first(self, way, part):
        return remote(
            self.own(part),
            self.out(self.chip, part),
            self.send_row.at[way, part],
            self.recv_row.at[way, part],
            self.ways[way],
        )

    def second(self, way):
        return remote(
            self.out(self.chips[way], way),
            self.out(self.chips[way], way),
            self.send_on.at[way],
            self.recv_on.at[way],
            self.ways[1 - way],
        )

    def start(self):
        self.first(0, 0).start()
        self.first(1, 1).start()

    def forward(self):
        for way in range(2):
            self.first(way, way).wait_recv()
            self.second(way).start()
        for way in range(2):
            self.first(way, 1 - way).start()

    def arrive(self):
        for way in range(2):
            self.first(way, 1 - way).wait_recv()
        for way in range(2):
            self.second(way).wait_recv()

    def finish(self):
        for way in range(2):
            self.second(way).wait_send()
            for part in range(2):
                self.first(way, part).wait_send()


def plane_sems():
    dma = pltpu.SemaphoreType.DMA
    return [dma((2, 2)), dma((2, 2)), dma((2,)), dma((2,))]


def column_sems(parts):
    sems = pltpu.SemaphoreType.DMA((2, 4, parts))
    return [sems, sems, sems, sems]


def halves_of(own, out, keep_sem):
    half = own.shape[0] // 2
    chip = plane_ids()[0]
    return (
        lambda part: own.at[pl.ds(part * half, half)],
        lambda place, part: out.at[place, pl.ds(part * half, half)],
        pltpu.make_async_copy(own, out.at[chip], keep_sem),
    )


def neighbours(facing_too, column_too):
    chip, core, beside, above, facing = plane_ids()
    count = lax.axis_size(TP)
    place = lax.axis_index(TP)
    always = place >= 0
    devices = [(always, {SEQ: 2 * chip + 1 - core})]
    devices += [(always, {SEQ: 2 * beside + core}), (always, {SEQ: 2 * above + core})]
    if facing_too:
        devices.append((always, {SEQ: 2 * facing + core}))
    if column_too:
        for step in range(1, count):
            devices.append((always, {TP: lax.rem(place + step, count)}))
    else:
        devices.append((place < count - 1, {TP: place + 1}))
        devices.append((place > 0, {TP: place - 1}))
    return devices


def first_kernel(
    parts,
    own_ref,
    weight_ref,
    share_ref,
    random_ref,
    out_ref,
    spread_ref,
    column_ref,
    random_out_ref,
    randoms,
    own_sem,
    send_row,
    recv_row,
    send_on,
    recv_on,
    send_z,
    recv_z,
    send_far,
    recv_far,
    send_random,
    recv_random,
    send_column,
    recv_column,
    send_share,
    recv_share,
):
    chip, core, beside, above, facing = plane_ids()
    tp_count = lax.axis_size(TP)
    place = lax.axis_index(TP)
    other = {SEQ: 2 * chip + 1 - core}
    weight_rows = weight_ref.shape[0] // (2 * parts)
    column = [{TP: lax.rem(place + step, tp_count)} for step in range(1, tp_count)]
    enter(neighbours(True, True))
    own, out, keep_rows = halves_of(own_ref, out_ref, own_sem.at[0])
    rows = PlaneSpread(own, out, (send_row, recv_row, send_on, recv_on))
    shares = ColumnSpread(
        1, share_ref, column_ref, None, other, own_sem.at[2], (send_share, recv_share), None
    )

    def weight_cut(part, holder):
        return pl.ds((holder * parts + part) * weight_rows, weight_rows)

    def weight_along(source, way, part):
        at = weight_cut(part, core)
        return remote(
            source.at[at],
            spread_ref.at[at],
            send_z.at[way, part],
            recv_z.at[part],
            {TP: place + 1 if way == 0 else place - 1},
        )

    def weight_across(part):
        at = weight_cut(part, core)
        return remote(
            spread_ref.at[at], spread_ref.at[at], send_far.at[part], recv_far.at[part], other
        )

    def goes_on(way):
        if way == 0:
            return (place >= chip) & (place < tp_count - 1)
        return (place <= chip) & (place > 0)

    def random_to_holder(sender):
        return remote(
            random_ref,
            randoms.at[sender],
            send_random,
            recv_random.at[sender],
            {SEQ: 2 * place + core},
        )

    def random_along(step):
        return remote(
            randoms,
            random_out_ref,
            send_column.at[step],
            recv_column,
            column[step],
        )

    rows.start()

    @pl.when(place != chip)
    def _():
        random_to_holder(chip).start()

    for part in range(parts):
        for way in range(2):

            @pl.when((place == chip) & goes_on(way))
            def _():
                weight_along(weight_ref, way, part).start()

    shares.start()
    keep_rows.start()

    @pl.when(place == chip)
    def _():
        keep = pltpu.make_async_copy(weight_ref, spread_ref, own_sem.at[1])
        keep.start()
        keep.wait()
        randoms[chip] = random_ref[...]
        for step in range(1, tp_count):
            random_to_holder(lax.rem(chip + step, tp_count)).wait_recv()
        random_out_ref[...] = randoms[...]
        for step in range(tp_count - 1):
            random_along(step).start()

    rows.forward()
    for part in range(parts):

        @pl.when(place != chip)
        def _():
            weight_along(spread_ref, 0, part).wait_recv()
            for way in range(2):

                @pl.when(goes_on(way))
                def _():
                    weight_along(spread_ref, way, part).start()

            weight_across(part).start()

    for distance in range(1, tp_count):
        shares.step(distance, 0)
    rows.arrive()
    rows.finish()
    shares.finish()
    keep_rows.wait()

    @pl.when(place != chip)
    def _():
        random_to_holder(chip).wait_send()
        random_along(0).wait_recv()

    @pl.when(place == chip)
    def _():
        for step in range(tp_count - 1):
            random_along(step).wait_send()

    for part in range(parts):

        @pl.when(place != chip)
        def _():
            weight_across(part).wait()

        for way in range(2):

            @pl.when(goes_on(way))
            def _():
                weight_along(spread_ref, way, part).wait_send()


def first_exchange(own, weight, share, randoms, collective_id, parts=2):
    chips = lax.axis_size(SEQ) // 2
    count = lax.axis_size(TP)
    resident = pl.BlockSpec(memory_space=pltpu.VMEM)
    dma = pltpu.SemaphoreType.DMA
    return pl.pallas_call(
        functools.partial(first_kernel, parts),
        out_shape=[
            jax.ShapeDtypeStruct((chips,) + own.shape, own.dtype),
            jax.ShapeDtypeStruct(weight.shape, weight.dtype),
            jax.ShapeDtypeStruct((count,) + share.shape, share.dtype),
            jax.ShapeDtypeStruct((chips,) + randoms.shape, randoms.dtype),
        ],
        in_specs=[resident] * 4,
        out_specs=[resident] * 4,
        scratch_shapes=[pltpu.VMEM((chips,) + randoms.shape, randoms.dtype), dma((3,))]
        + plane_sems()
        + [
            dma((2, parts)),
            dma((parts,)),
            dma((parts,)),
            dma((parts,)),
            dma,
            dma((chips,)),
            dma((chips - 1,)),
            dma,
        ]
        + column_sems(1)[:2],
        compiler_params=pltpu.CompilerParams(
            collective_id=collective_id, has_side_effects=True, vmem_limit_bytes=32 * 2**20
        ),
        cost_estimate=lasting(30),
    )(own, weight, share, randoms)


def second_kernel(parts, longs_ref, own_ref, near_ref, far_ref, out_ref, keep_sem, *sems):
    chip, core = plane_ids()[:2]
    enter(neighbours(False, False))
    other = {SEQ: 2 * chip + 1 - core}
    longs = ColumnSpread(
        parts, longs_ref, near_ref, far_ref, other, keep_sem.at[0], sems[:2], sems[2:4]
    )
    own, out, keep_rows = halves_of(own_ref, out_ref, keep_sem.at[1])
    rows = PlaneSpread(own, out, sems[4:])
    longs.start()
    rows.start()
    keep_rows.start()
    rows.forward()
    for distance in range(1, longs.count):
        for part in range(parts):
            longs.step(distance, part)
    rows.arrive()
    rows.finish()
    longs.finish()
    keep_rows.wait()


def second_exchange(longs, own, collective_id, parts=2):
    chips = lax.axis_size(SEQ) // 2
    near = jax.ShapeDtypeStruct((lax.axis_size(TP),) + longs.shape, longs.dtype)
    resident = pl.BlockSpec(memory_space=pltpu.VMEM)
    return pl.pallas_call(
        functools.partial(second_kernel, parts),
        out_shape=[near, near, jax.ShapeDtypeStruct((chips,) + own.shape, own.dtype)],
        in_specs=[resident] * 2,
        out_specs=[resident] * 3,
        scratch_shapes=[pltpu.SemaphoreType.DMA((2,))] + column_sems(parts) + plane_sems(),
        compiler_params=pltpu.CompilerParams(
            collective_id=collective_id, has_side_effects=True, vmem_limit_bytes=32 * 2**20
        ),
        cost_estimate=lasting(55),
    )(longs, own)


def third_kernel(parts, cuts, longs_ref, column_ref, near_ref, far_ref, *refs):
    count = len(cuts) - 1
    outs, refs = refs[:count], refs[count:]
    keep_sem, cross_sems, sems = refs[0], refs[1:3], refs[3:]
    chip, core, beside, above, facing = plane_ids()
    enter(neighbours(False, False))
    other = {SEQ: 2 * chip + 1 - core}
    longs = ColumnSpread(
        parts, longs_ref, near_ref, far_ref, other, keep_sem.at[0], sems[:2], sems[2:4]
    )
    half = column_ref.shape[0] // 2
    weights = []
    keeps = []
    for place in range(count):
        rows = pl.ds(cuts[place], cuts[place + 1] - cuts[place])
        out = outs[place]
        weights.append(
            PlaneSpread(
                lambda part, rows=rows: column_ref.at[pl.ds(part * half, half), rows],
                lambda where, part, out=out: out.at[core, where, pl.ds(part * half, half)],
                [sem.at[place] for sem in sems[4:]],
            )
        )
        keeps.append(
            pltpu.make_async_copy(
                column_ref.at[:, rows], out.at[core, chip], keep_sem.at[1 + place]
            )
        )

    def across(place, where):
        block = outs[place].at[core, (chip, beside, above, facing)[where]]
        return remote(
            block, block, cross_sems[0].at[place, where], cross_sems[1].at[place, where], other
        )

    longs.start()
    for weight, keep in zip(weights, keeps):
        weight.start()
        keep.start()
    for part in range(parts):
        longs.step(1, part)
    for place in range(count):
        weights[place].forward()
        keeps[place].wait()
        across(place, 0).start()
    for part in range(parts):
        longs.step(2, part)
    for place in range(count):
        weights[place].arrive()
        for where in range(1, 4):
            across(place, where).start()
    for part in range(parts):
        longs.step(3, part)
    longs.finish()
    for place in range(count):
        weights[place].finish()
        for where in range(4):
            across(place, where).wait()


def third_exchange(longs, column, cuts, collective_id, parts=2):
    chips = lax.axis_size(SEQ) // 2
    tp_count, _, width = column.shape
    near = jax.ShapeDtypeStruct((tp_count,) + longs.shape, longs.dtype)
    count = len(cuts) - 1
    outs = [
        jax.ShapeDtypeStruct((2, chips, tp_count, last - first, width), column.dtype)
        for first, last in zip(cuts, cuts[1:])
    ]
    resident = pl.BlockSpec(memory_space=pltpu.VMEM)
    dma = pltpu.SemaphoreType.DMA
    return pl.pallas_call(
        functools.partial(third_kernel, parts, cuts),
        out_shape=[near, near] + outs,
        in_specs=[resident] * 2,
        out_specs=[resident] * (2 + count),
        scratch_shapes=[dma((1 + count,)), dma((count, 4)), dma((count, 4))]
        + column_sems(parts)
        + [dma((count, 2, 2)), dma((count, 2, 2)), dma((count, 2)), dma((count, 2))],
        compiler_params=pltpu.CompilerParams(
            collective_id=collective_id, has_side_effects=True, vmem_limit_bytes=48 * 2**20
        ),
        cost_estimate=lasting(55),
    )(longs, column)


def plane_reduce_kernel(
    parts_ref, out_ref, came, facing_came, sent, last, send_near, recv_near, send_far, recv_far, send_on, recv_on
):
    chip, core, beside, above, facing = plane_ids()
    ways = ({SEQ: 2 * beside + core}, {SEQ: 2 * above + core})
    chips = (beside, above)
    half = out_ref.shape[0] // 2
    always = lax.axis_index(TP) >= 0
    enter([(always, ways[0]), (always, ways[1])])

    def rows_of(way):
        return pl.ds(way * half, half)

    def facing_term(way):
        return remote(
            parts_ref.at[facing, rows_of(way)],
            facing_came.at[way],
            send_far.at[way],
            recv_far.at[way],
            ways[way],
        )

    def near_term(way):
        return remote(
            parts_ref.at[chips[way], rows_of(way)],
            came.at[way],
            send_near.at[way],
            recv_near.at[way],
            ways[way],
        )

    def summed(way):
        return remote(
            sent.at[way], last.at[way], send_on.at[way], recv_on.at[way], ways[1 - way]
        )

    for way in range(2):
        facing_term(way).start()
    for way in range(2):
        near_term(way).start()
    step_rows = 64

    def each_step(work):
        @pl.loop(0, half // step_rows)
        def _(step):
            work(pl.multiple_of(step * step_rows, step_rows))

    for way in range(2):
        facing_term(way).wait_recv()

        def add_term(start):
            total = parts_ref[
                chips[1 - way], pl.ds(way * half + start, step_rows), :
            ].astype(f32) + facing_came[way, pl.ds(start, step_rows), :].astype(f32)
            sent[way, pl.ds(start, step_rows), :] = total.astype(sent.dtype)

        each_step(add_term)
        summed(way).start()
    for way in range(2):
        near_term(way).wait_recv()

        def add_near(start):
            at = pl.ds(way * half + start, step_rows)
            out_ref[at, :] = parts_ref[chip, at, :].astype(f32) + came[
                way, pl.ds(start, step_rows), :
            ].astype(f32)

        each_step(add_near)
    for way in range(2):
        summed(way).wait_recv()

        def add_last(start):
            out_ref[pl.ds(way * half + start, step_rows), :] += last[
                way, pl.ds(start, step_rows), :
            ].astype(f32)

        each_step(add_last)
    for way in range(2):
        facing_term(way).wait_send()
        near_term(way).wait_send()
        summed(way).wait_send()


def plane_reduce_now(parts, collective_id):
    chips, rows, width = parts.shape
    half = pltpu.VMEM((2, rows // 2, width), parts.dtype)
    dma = pltpu.SemaphoreType.DMA((2,))
    return pl.pallas_call(
        plane_reduce_kernel,
        out_shape=jax.ShapeDtypeStruct((rows, width), f32),
        in_specs=[pl.BlockSpec(memory_space=pltpu.VMEM)],
        out_specs=pl.BlockSpec(memory_space=pltpu.VMEM),
        scratch_shapes=[half] * 4 + [dma] * 6,
        compiler_params=pltpu.CompilerParams(
            collective_id=collective_id, has_side_effects=True, vmem_limit_bytes=32 * 2**20
        ),
        cost_estimate=lasting(28),
    )(parts)


def all_sum_kernel(rows_ref, out_ref, sums, came, send, receive):
    chip, core, beside, above, facing = plane_ids()
    place = lax.axis_index(TP)
    peers = [
        {SEQ: 2 * chip + 1 - core},
        {SEQ: 2 * beside + core},
        {SEQ: 2 * above + core},
        {TP: place + 1 - 2 * (place % 2)},
        {TP: place + 2 - 4 * (place // 2)},
    ]
    enter([(place >= 0, peer) for peer in peers])
    sums[0] = rows_ref[...]
    for step, peer in enumerate(peers):
        copy = remote(sums.at[step], came.at[step], send.at[step], receive.at[step], peer)
        copy.start()
        copy.wait()
        sums[step + 1] = sums[step] + came[step]
    out_ref[...] = sums[len(peers)]


def all_sum(rows, collective_id):
    steps = 5
    return pl.pallas_call(
        all_sum_kernel,
        out_shape=jax.ShapeDtypeStruct(rows.shape, rows.dtype),
        in_specs=[pl.BlockSpec(memory_space=pltpu.VMEM)],
        out_specs=pl.BlockSpec(memory_space=pltpu.VMEM),
        scratch_shapes=[
            pltpu.VMEM((steps + 1,) + rows.shape, rows.dtype),
            pltpu.VMEM((steps,) + rows.shape, rows.dtype),
            pltpu.SemaphoreType.DMA((steps,)),
            pltpu.SemaphoreType.DMA((steps,)),
        ],
        compiler_params=pltpu.CompilerParams(
            collective_id=collective_id, has_side_effects=True
        ),
        cost_estimate=lasting(12),
    )(rows)


def holder_sum_kernel(
    parts,
    terms_ref,
    out_ref,
    sums,
    given,
    came,
    send_far,
    recv_far,
    send_z,
    recv_z,
    send_plane,
    recv_plane,
    send_on,
    send_back,
    recv_back,
):
    chip, core, beside, above, facing = plane_ids()
    count = lax.axis_size(TP)
    place = lax.axis_index(TP)
    other = {SEQ: 2 * chip + 1 - core}
    ways = ({SEQ: 2 * beside + core}, {SEQ: 2 * above + core})
    rows = sums.shape[0]
    part_rows = rows // parts
    always = place >= 0
    holds = place == chip
    enter(
        [
            (always, other),
            (always, ways[0]),
            (always, ways[1]),
            (place < count - 1, {TP: place + 1}),
            (place > 0, {TP: place - 1}),
        ]
    )

    def cut(part):
        return pl.ds(part * part_rows, part_rows)

    def own_cut(part):
        return pl.ds(pl.multiple_of(core * rows + part * part_rows, 16), part_rows)

    across = remote(
        terms_ref.at[pl.ds(pl.multiple_of((1 - core) * rows, 16), rows)], given, send_far, recv_far, other
    )
    across.start()

    def along(way, part):
        return remote(
            sums.at[cut(part)],
            came.at[way, cut(part)],
            send_z.at[way, part],
            recv_z.at[way, part],
            {TP: place - 1 if way == 0 else place + 1},
        )

    def add(source, part):
        total = sums[cut(part), :].astype(f32) + source[cut(part), :].astype(f32)
        sums[cut(part), :] = total.astype(sums.dtype)

    def to_plane(way, part):
        return remote(
            out_ref.at[own_cut(part)],
            out_ref.at[own_cut(part)],
            send_plane.at[way, part],
            recv_plane.at[part],
            ways[way],
        )

    def onward(part):
        return remote(
            out_ref.at[own_cut(part)],
            out_ref.at[own_cut(part)],
            send_on,
            recv_plane.at[part],
            ways[1 - part],
        )

    def back(part):
        return remote(
            out_ref.at[own_cut(part)],
            out_ref.at[own_cut(part)],
            send_back.at[part],
            recv_back.at[part],
            other,
        )

    across.wait_recv()
    for part in range(parts):
        sums[cut(part), :] = terms_ref[own_cut(part), :]
        add(given, part)
        for way in range(2):
            passes = place > chip if way == 0 else place < chip
            takes = place < count - 1 if way == 0 else place > 0

            @pl.when(passes)
            def _():
                @pl.when(takes)
                def _():
                    along(way, part).wait_recv()
                    add(came.at[way], part)

                along(way, part).start()

    for part in range(parts):
        for way in range(2):
            takes = place < count - 1 if way == 0 else place > 0

            @pl.when(holds & takes)
            def _():
                along(way, part).wait_recv()
                add(came.at[way], part)

        @pl.when(holds)
        def _():
            out_ref[own_cut(part), :] = sums[cut(part), :]
            for way in range(2):
                to_plane(way, part).start()
            back(part).start()

    for part in range(parts):

        @pl.when(place != chip)
        def _():
            to_plane(0, part).wait_recv()

        @pl.when((beside if part == 0 else above) == place)
        def _():
            onward(part).start()

        @pl.when(place != chip)
        def _():
            back(part).start()

    across.wait_send()
    for part in range(parts):
        back(part).wait()

        @pl.when((beside if part == 0 else above) == place)
        def _():
            onward(part).wait_send()

        for way in range(2):

            @pl.when(holds)
            def _():
                to_plane(way, part).wait_send()

            @pl.when(place > chip if way == 0 else place < chip)
            def _():
                along(way, part).wait_send()


def holder_sum(terms, collective_id):
    parts = 2
    rows = terms.shape[0] // 2
    half = (rows,) + terms.shape[1:]
    dma = pltpu.SemaphoreType.DMA
    resident = pl.BlockSpec(memory_space=pltpu.VMEM)
    return pl.pallas_call(
        functools.partial(holder_sum_kernel, parts),
        out_shape=jax.ShapeDtypeStruct(terms.shape, terms.dtype),
        in_specs=[resident],
        out_specs=resident,
        scratch_shapes=[
            pltpu.VMEM(half, terms.dtype),
            pltpu.VMEM(half, terms.dtype),
            pltpu.VMEM((2,) + half, terms.dtype),
            dma,
            dma,
            dma((2, parts)),
            dma((2, parts)),
            dma((2, parts)),
            dma((parts,)),
            dma,
            dma((parts,)),
            dma((parts,)),
        ],
        compiler_params=pltpu.CompilerParams(
            collective_id=collective_id, has_side_effects=True, vmem_limit_bytes=32 * 2**20
        ),
        cost_estimate=lasting(35),
    )(terms)


def plane_applies(mesh, blocks, docs):
    seq_count, tp_count = mesh.shape[SEQ], mesh.shape[TP]
    groups = seq_count * tp_count
    return (
        tp_count == 4
        and seq_count == 2 * tp_count
        and blocks == groups * SHORT_BLK
        and 2 * tp_count * SHORT_BLK == LONG_BLK
        and blocks - SHORT_BLK * docs == 2 * (LONG_BLK - SHORT_BLK)
    )


class Micro:
    pass


def plane_body(
    tokens,
    doc_lengths,
    rand_blocks,
    query_weight,
    key_weight,
    value_weight,
    query_bias,
    value_bias,
    proj_weight,
    proj_bias,
    first_gain,
    first_bias,
    second_gain,
    second_bias,
    inner_weight,
    inner_bias,
    outer_weight,
    outer_bias,
    out_grad,
):
    micro_count, own_rows, model_width = tokens.shape
    seq_count = lax.axis_size(SEQ)
    tp_count = lax.axis_size(TP)
    chips = seq_count // 2
    seq_place = lax.axis_index(SEQ)
    tp_place = lax.axis_index(TP)
    chip = seq_place // 2
    core = seq_place % 2
    heads = rand_blocks.shape[2]
    rands = rand_blocks.shape[3]
    local_width = query_weight.shape[1]
    head_size = local_width // heads
    pair_width = heads * PAIR
    hidden_units = inner_weight.shape[1]
    classes = 2 * tp_count
    own_class = core * tp_count + tp_place
    long_docs = 2
    slots = 5 + rands
    group_rows = chips * own_rows
    score_scale = 1.0 / math.sqrt(head_size)

    def by_head(values):
        return values.reshape(values.shape[:-1] + (heads, -1))

    def side_by_side(first, second):
        paired = jnp.concatenate([by_head(first), by_head(second)], axis=-1)
        return paired.reshape(paired.shape[:-2] + (pair_width,))

    def low_half(wide):
        return by_head(wide)[..., :head_size].reshape(wide.shape[:-1] + (local_width,))

    def high_half(wide):
        return by_head(wide)[..., head_size:].reshape(wide.shape[:-1] + (local_width,))

    def slot_rows(values, slot):
        return values[slot * own_rows : (slot + 1) * own_rows]

    stage = [Micro() for _ in range(micro_count)]
    spare_rows = 64
    packed = jnp.concatenate([side_by_side(key_weight, value_weight), query_weight], axis=1)
    packed_bias = jnp.concatenate(
        [side_by_side(jnp.zeros_like(value_bias), value_bias), query_bias]
    )
    packed = jnp.concatenate([packed, packed_bias[None]], axis=0)
    packed = jnp.pad(packed, ((0, spare_rows - 1), (0, -packed.shape[1] % 128)))
    randoms = rand_blocks.reshape(-1)
    random_count = randoms.shape[0]
    randoms = jnp.pad(randoms, (0, -random_count % 1024)).reshape(-1, 128)
    for micro, held in enumerate(stage):
        held.inputs = tokens[micro].astype(f32)
        shifted, held.stats_one, held.inverse_one = layer_stats(
            held.inputs, first_gain, first_bias
        )
        held.low = shifted.astype(bf16)
    unit_cut = hidden_units // seq_count
    proj_cut = local_width // seq_count
    rest_rows = -(-(proj_cut + 1) // 16) * 16
    cuts = (0, rest_rows, rest_rows + unit_cut, rest_rows + 2 * unit_cut)

    def padded(row_values):
        return jnp.pad(row_values, [(0, 0)] * (row_values.ndim - 1) + [(0, model_width - unit_cut)])

    share = jnp.concatenate(
        [
            lax.dynamic_slice_in_dim(proj_weight, seq_place * proj_cut, proj_cut, axis=0),
            padded(lax.dynamic_slice_in_dim(inner_bias, seq_place * unit_cut, unit_cut)[None]),
            jnp.zeros((rest_rows - proj_cut - 1, model_width), bf16),
            lax.dynamic_slice_in_dim(inner_weight, seq_place * unit_cut, unit_cut, axis=1).T,
            lax.dynamic_slice_in_dim(outer_weight, seq_place * unit_cut, unit_cut, axis=0),
        ],
        axis=0,
    )
    one, packed, column, randoms = first_exchange(stage[0].low, packed, share, randoms, 1)
    stage[0].one = one.reshape(group_rows, model_width)
    pair_wide = packed[:model_width, :pair_width]
    pair_wide_bias = packed[model_width, :pair_width]
    query_part = packed[:model_width, pair_width : pair_width + local_width]
    query_part_bias = packed[model_width, pair_width : pair_width + local_width]

    starts = jnp.cumsum(doc_lengths, axis=1) - doc_lengths
    is_long = doc_lengths == LONG_BLK
    long_firsts = jnp.min(jnp.where(is_long, starts, jnp.iinfo(jnp.int32).max), axis=1)
    long_lasts = jnp.max(jnp.where(is_long, starts, -1), axis=1)
    randoms = randoms.reshape(chips, -1)[:, :random_count]
    randoms = randoms.reshape(chips, micro_count, tp_count, SHORT_BLK, heads, rands)
    randoms = lax.dynamic_index_in_dim(randoms, tp_place, axis=2, keepdims=False)
    randoms = jnp.pad(randoms.transpose(1, 3, 0, 2, 4), [(0, 0)] * 4 + [(slots - rands, 0)])
    shape = (heads, chips, SHORT_BLK, slots)
    slot, block, entry = (lax.broadcasted_iota(jnp.int32, shape, axis) for axis in (1, 2, 3))
    for micro, held in enumerate(stage):
        group = slot * classes + own_class
        number = group * SHORT_BLK + block
        in_long = [
            (number >= start[micro]) & (number < start[micro] + LONG_BLK)
            for start in (long_firsts, long_lasts)
        ]
        window_first = jnp.where(
            in_long[0],
            long_firsts[micro],
            jnp.where(in_long[1], long_lasts[micro], group * SHORT_BLK),
        )
        any_long = in_long[0] | in_long[1]
        window_final = window_first + jnp.where(any_long, LONG_BLK, SHORT_BLK)
        key = randoms[micro]
        for place, value in enumerate(
            (
                jnp.maximum(number - 1, window_first),
                jnp.minimum(number + 1, window_final - 1),
                number,
                window_first,
                window_first + 1,
            )
        ):
            key = jnp.where(entry == place, value, key)
        inside = key % SHORT_BLK
        key_class = (key // SHORT_BLK) % classes
        piece = key_class % tp_count + jnp.where(key_class // tp_count == core, 0, tp_count)
        long_place = piece * long_docs + jnp.where(in_long[1], 1, 0)
        short_place = classes * long_docs + slot
        held.index = (jnp.where(any_long, long_place, short_place) * SHORT_BLK + inside).reshape(-1)
        counts = jnp.where(entry == 0, number > window_first, number + 1 < window_final)
        held.valid = counts[0, :, :, :2].astype(jnp.int32).reshape(-1)
        held.long_rows = []
        for start in (long_firsts[micro], long_lasts[micro]):
            first_group = start // SHORT_BLK
            own_group = first_group + (own_class - first_group) % classes
            held.long_rows.append((own_group // classes) * own_rows)

    def long_blocks(micro):
        held = stage[micro]
        pair_rows = (contract(held.one, pair_wide, NN) + pair_wide_bias).astype(bf16)
        longs = jnp.concatenate(
            [
                lax.dynamic_slice_in_dim(pair_rows, start, own_rows, axis=0)
                for start in held.long_rows
            ],
            axis=0,
        )
        return pair_rows, longs

    def keep_pieces(micro, near, far, pair_rows):
        stage[micro].pieces = [
            near.reshape(-1, pair_width), far.reshape(-1, pair_width), pair_rows
        ]

    def attend(micro):
        held = stage[micro]
        one = held.one
        if micro:
            one = after(one, stage[micro - 1].grad_context_sent)
        held.queries = (
            (contract(one, query_part, NN) + query_part_bias) * score_scale
        ).astype(bf16)
        held.context_sent, held.logsum = attend_forward(
            held.index, held.valid, held.queries, held.pieces, heads, slots
        )
        held.context = plane_exchange(held.context_sent, 0, 1)

    def feed_forward(micro):
        held = stage[micro]
        if micro:
            held.context = after(
                held.context, stage[micro - 1].grad_query, stage[micro - 1].long_sum_sent
            )
        else:
            held.context = after(held.context, stage[1].pieces[0])
        hidden = held.inputs + contract(held.context, proj_full, NN) + proj_bias
        shifted, stats, inverse = layer_stats(hidden, second_gain, second_bias)
        held.two = shifted.astype(bf16)
        before = contract(held.two, inner_full, NT) + inner_bias_full
        held.active = gelu_exact(before).astype(bf16)
        result = hidden + contract(held.active, outer_full, NN) + outer_bias
        held.output = result.astype(bf16)
        held.grad_out = out_grad[micro]
        grad_float = held.grad_out.astype(f32)
        grad_active = contract(held.grad_out, outer_full, NT)
        held.grad_before = gelu_grad(before, grad_active).astype(bf16)
        grad_two = contract(held.grad_before, inner_full, NN)
        back, gain_sum, shift_sum = layer_back(grad_two, stats, inverse, second_gain)
        held.grad_hidden = grad_float + back
        held.branch = held.grad_hidden.astype(bf16)
        held.grad_context_sent = jnp.stack(
            [
                contract(
                    held.branch, proj_full[part * local_width : (part + 1) * local_width], NT
                ).astype(bf16)
                for part in range(chips)
            ]
        )
        held.grad_context = plane_exchange(held.grad_context_sent, 0, 0).reshape(
            group_rows, local_width
        )
        held.unit_sum = jnp.sum(held.grad_before.astype(f32), axis=0)
        held.row_sums = jnp.stack(
            [
                gain_sum,
                shift_sum,
                jnp.sum(held.branch.astype(f32), axis=0),
                jnp.sum(grad_float, axis=0),
            ]
        )

    def attend_back(micro, *earlier):
        held = stage[micro]
        held.grad_query, near, far, held.grad_pair = attend_backward(
            held.index,
            held.valid,
            held.queries,
            after(held.grad_context, *earlier),
            held.logsum,
            held.pieces,
            heads,
            slots,
        )
        return near, far

    def input_rows(micro, long_sum):
        held = stage[micro]
        for doc, start in enumerate(held.long_rows):
            held.grad_pair = lax.dynamic_update_slice_in_dim(
                held.grad_pair, slot_rows(long_sum, doc), start, axis=0
            )
        rows = contract(held.grad_query, query_part * score_scale, NT) + contract(
            held.grad_pair, pair_wide, NT
        )
        return rows.astype(bf16).reshape(chips, own_rows, model_width)

    def input_back(micro, grad_one):
        held = stage[micro]
        back, gain_sum, shift_sum = layer_back(
            grad_one, held.stats_one, held.inverse_one, first_gain
        )
        held.input_grad = held.grad_hidden + back
        held.first_sums = jnp.stack([gain_sum, shift_sum])

    pair_rows, longs = long_blocks(0)
    near, far, one = second_exchange(longs, stage[1].low, 2)
    stage[1].one = one.reshape(group_rows, model_width)
    keep_pieces(0, near, far, pair_rows)
    attend(0)
    pair_rows, longs = long_blocks(1)
    near, far, rest, inner_full, outer_full = third_exchange(
        after(longs, stage[0].context_sent), column, cuts, 7
    )
    keep_pieces(1, near, far, pair_rows)
    inner_full = inner_full.reshape(-1, model_width)
    outer_full = outer_full.reshape(-1, model_width)
    inner_bias_full = rest[:, :, :, proj_cut, :unit_cut].reshape(-1)
    proj_full = rest[:, :, :, :proj_cut].transpose(2, 1, 0, 3, 4)
    proj_full = proj_full.reshape(tp_count * local_width, model_width)
    feed_forward(0)
    attend(1)
    near, far = attend_back(0, stage[1].logsum, stage[1].context_sent)
    stage[0].long_sum_sent = sum_parts([near, core_swap(far)]).astype(bf16)
    long_sum = lax.psum_scatter(stage[0].long_sum_sent, TP, scatter_dimension=0, tiled=True)
    feed_forward(1)

    two, grad_before, active, grad_out, context, branch = (
        jnp.concatenate(group, axis=0)
        for group in zip(
            *((h.two, h.grad_before, h.active, h.grad_out, h.context, h.branch) for h in stage)
        )
    )
    two, active, context = after((two, active, context), stage[1].grad_context_sent)
    proj_part = contract(context, branch, TN).astype(bf16)
    proj_part = proj_part.reshape(tp_count, chips, 2, proj_cut, model_width)
    unit_shape = (2, chips, tp_count)
    unit_sum = sum(h.unit_sum for h in stage).astype(bf16)
    rest_part = jnp.concatenate(
        [
            proj_part.transpose(2, 1, 0, 3, 4),
            padded(unit_sum.reshape(unit_shape + (1, unit_cut))),
            jnp.zeros(unit_shape + (rest_rows - proj_cut - 1, model_width), bf16),
        ],
        axis=3,
    )
    halves = []
    for part in (
        contract(grad_before, two, TN).astype(bf16),
        contract(active, grad_out, TN).astype(bf16),
        rest_part,
    ):
        part = part.reshape(2, chips, -1, model_width)
        kept = lax.dynamic_index_in_dim(part, core, axis=0, keepdims=False)
        given = lax.dynamic_index_in_dim(part, 1 - core, axis=0, keepdims=False)
        halves.append(sum_parts([kept, core_swap(given)]).astype(bf16))
    halves = jnp.concatenate(halves, axis=1)
    by_chip = plane_exchange(halves, 0, 0)

    rows = input_rows(0, after(long_sum, stage[1].grad_context_sent))
    grad_one = [lax.dynamic_index_in_dim(rows, chip, axis=0, keepdims=False)]
    for step in range(1, chips):
        part = lax.dynamic_index_in_dim(rows, chip ^ step, axis=0, keepdims=False)
        route = [(place, place ^ (2 * step)) for place in range(seq_count)]
        grad_one.append(lax.ppermute(part, SEQ, route))
    near, far = attend_back(1, halves, rows)

    query_sum = sum(contract(h.one, h.grad_query, TN) for h in stage) * score_scale
    query_sum = query_sum.astype(bf16)
    half_rows = model_width // 2
    kept = lax.dynamic_slice_in_dim(query_sum, core * half_rows, half_rows, axis=0)
    given = core_swap(
        lax.dynamic_slice_in_dim(query_sum, (1 - core) * half_rows, half_rows, axis=0)
    )
    near = after(near, query_sum)
    column_shape = (tp_count, long_docs * own_rows, pair_width)
    long_sum = column_reduce_both(near.reshape(column_shape), far.reshape(column_shape), 3)
    input_back(0, sum_parts(after(grad_one, long_sum)))
    rows = input_rows(1, long_sum)

    half = sum_parts([kept, given]).astype(bf16)
    came = [
        lax.ppermute(
            after(half, rows),
            (SEQ, TP),
            [
                (place * tp_count + (place // 2 + step) % tp_count, place * tp_count + place // 2)
                for place in range(seq_count)
            ],
        )
        for step in range(1, tp_count)
    ]
    quarters = jnp.sum(after(by_chip, rows).astype(f32), axis=0).astype(bf16)
    cuts = [0, tp_count * unit_cut, 2 * tp_count * unit_cut, quarters.shape[0]]
    quarters = jnp.concatenate(
        [
            quarters[first:last].reshape(tp_count, -1, model_width)
            for first, last in zip(cuts, cuts[1:])
        ],
        axis=1,
    )
    by_column = lax.all_to_all(quarters, TP, split_axis=0, concat_axis=0, tiled=True)
    grad_one = plane_reduce_now(after(rows, quarters, half), 4)
    input_back(1, grad_one)

    ones = after([h.one for h in stage], grad_one)
    pair_sum = sum(contract(one, h.grad_pair, TN) for one, h in zip(ones, stage)).astype(bf16)
    half = sum_parts([half] + after(came, grad_one)).astype(bf16)
    came = [
        lax.ppermute(
            half,
            (SEQ, TP),
            [
                (place * tp_count + place // 2, (place ^ (2 * step)) * tp_count + place // 2)
                for place in range(seq_count)
            ],
        )
        for step in range(1, chips)
    ]
    own_sum = jnp.sum(after(by_column, grad_one).astype(f32), axis=0).astype(bf16)
    other_sum = core_swap(own_sum)
    pair_sum = holder_sum(after(pair_sum, half, own_sum), 6).astype(f32)
    key_grad = low_half(pair_sum)
    value_grad = high_half(pair_sum)

    other_sum = after(other_sum, pair_sum)
    chip_sum = jnp.where(
        core == 0, jnp.stack([own_sum, other_sum]), jnp.stack([other_sum, own_sum])
    )
    dense_sum = plane_gather(chip_sum)
    near = jnp.where(tp_place == chip, half, sum(after(came, pair_sum)))
    far = core_swap(near)

    def own_columns(values):
        wide = jnp.zeros((chips, local_width), f32)
        return lax.dynamic_update_slice_in_dim(wide, values[None], chip, axis=0).reshape(-1)

    query_bias_sum = sum(jnp.sum(h.grad_query.astype(f32), axis=0) for h in stage)
    pair_bias_sum = sum(jnp.sum(h.grad_pair.astype(f32), axis=0) for h in stage)
    all_rows = all_sum(
        after(
            jnp.concatenate(
                [
                    sum(h.row_sums for h in stage),
                    sum(h.first_sums for h in stage),
                    own_columns(query_bias_sum * score_scale)[None],
                    own_columns(high_half(pair_bias_sum))[None],
                ],
                axis=0,
            ),
            near,
            chip_sum,
        ),
        5,
    )
    query_grad = jnp.where(
        core == 0, jnp.concatenate([near, far], axis=0), jnp.concatenate([far, near], axis=0)
    ).astype(f32)
    dense_sum = dense_sum.reshape(seq_count, -1, model_width).astype(f32)
    inner_weight_grad = dense_sum[:, :unit_cut].reshape(hidden_units, model_width).T
    outer_weight_grad = dense_sum[:, unit_cut : 2 * unit_cut].reshape(hidden_units, model_width)
    rest = dense_sum[:, 2 * unit_cut :]
    proj_weight_grad = rest[:, :proj_cut].reshape(local_width, model_width)
    inner_bias_grad = rest[:, proj_cut, :unit_cut].reshape(hidden_units)

    def my_columns(row):
        return lax.dynamic_slice_in_dim(row, tp_place * local_width, local_width)

    return (
        jnp.stack([h.output for h in stage]),
        jnp.stack([h.input_grad for h in stage]),
        query_grad,
        key_grad,
        value_grad,
        my_columns(all_rows[6]),
        my_columns(all_rows[7]),
        proj_weight_grad,
        all_rows[2],
        all_rows[4],
        all_rows[5],
        all_rows[0],
        all_rows[1],
        inner_weight_grad,
        inner_bias_grad,
        outer_weight_grad,
        all_rows[3],
    )


def general_body(
    tokens,
    doc_lengths,
    rand_blocks,
    query_weight,
    key_weight,
    value_weight,
    query_bias,
    value_bias,
    proj_weight,
    proj_bias,
    first_gain,
    first_bias,
    second_gain,
    second_bias,
    inner_weight,
    inner_bias,
    outer_weight,
    outer_bias,
    out_grad,
):
    micro_count, local_rows, model_width = tokens.shape
    seq_count = lax.axis_size(SEQ)
    tp_count = lax.axis_size(TP)
    seq_place = lax.axis_index(SEQ)
    tp_place = lax.axis_index(TP)
    block_dev = rand_blocks.shape[1]
    heads = rand_blocks.shape[2]
    local_width = query_weight.shape[1]
    head_size = local_width // heads
    hidden_units = inner_weight.shape[1]
    group_rows = block_dev * BLOCK
    reach_dev = (block_dev + LONG_BLK - 2) // block_dev
    window = 2 * reach_dev + 1
    score_scale = 1.0 / math.sqrt(head_size)
    lowest = (seq_place - reach_dev) * block_dev
    blocks = seq_place * block_dev + jnp.arange(block_dev, dtype=jnp.int32)

    held = jnp.concatenate([inner_weight.T, outer_weight, proj_weight, inner_bias[None]], axis=0)
    used_rows = held.shape[0]
    piece_rows = -(-used_rows // (16 * seq_count)) * 16
    held_rows = piece_rows * seq_count
    held = jnp.pad(held, ((0, held_rows - used_rows), (0, 0)))
    share = lax.dynamic_slice_in_dim(held, seq_place * piece_rows, piece_rows, axis=0)
    spread = lax.all_gather(share, (TP, SEQ), axis=0, tiled=True)
    spread = spread.reshape(tp_count, held_rows, model_width)
    cuts = [0, hidden_units, 2 * hidden_units, 2 * hidden_units + local_width, used_rows]
    inner_full = spread[:, cuts[0] : cuts[1]].reshape(-1, model_width)
    outer_full = spread[:, cuts[1] : cuts[2]].reshape(-1, model_width)
    proj_full = spread[:, cuts[2] : cuts[3]].reshape(-1, model_width)
    inner_bias_full = spread[:, cuts[3] : cuts[4]].reshape(-1)

    def by_head(weight):
        return weight.reshape(weight.shape[:-1] + (heads, head_size))

    def side_by_side(first, second):
        paired = jnp.concatenate([by_head(first), by_head(second)], axis=-1)
        return paired.reshape(paired.shape[:-2] + (heads * PAIR,))

    pair_wide = side_by_side(key_weight, value_weight)
    pair_wide_bias = side_by_side(jnp.zeros_like(value_bias), value_bias)

    stage = [Micro() for _ in range(micro_count)]
    for micro, held in enumerate(stage):
        inputs = tokens[micro].astype(f32)
        shifted, stats, inverse = layer_stats(inputs, first_gain, first_bias)
        held.inputs, held.stats_one, held.inverse_one = inputs, stats, inverse
        held.one = lax.all_gather(shifted.astype(bf16), TP, axis=0, tiled=True)

    for micro, held in enumerate(stage):
        one = held.one
        pair_rows = (contract(one, pair_wide, NN) + pair_wide_bias).astype(bf16)
        pieces = [
            pair_rows if offset == 0 else from_behind(pair_rows, SEQ, -offset)
            for offset in range(-reach_dev, reach_dev + 1)
        ]
        queries = ((contract(one, query_weight, NN) + query_bias) * score_scale).astype(bf16)
        key_index, key_valid = block_keys(doc_lengths[micro], rand_blocks[micro], blocks)
        slots = key_index.shape[2]
        slot_index = jnp.clip(key_index - lowest, 0, window * block_dev - 1)
        held.index = slot_index.transpose(1, 0, 2).reshape(-1)
        held.valid = key_valid.reshape(-1)
        held.queries, held.pieces = queries, pieces

    for held in stage:
        context, held.logsum = attend_forward(
            held.index,
            held.valid,
            held.queries,
            held.pieces,
            heads,
            slots,
        )
        held.context = lax.all_to_all(context, TP, split_axis=0, concat_axis=1, tiled=True)

    outputs = []
    for micro, held in enumerate(stage):
        context = held.context
        hidden = held.inputs + contract(context, proj_full, NN) + proj_bias
        shifted, stats, inverse = layer_stats(hidden, second_gain, second_bias)
        two = shifted.astype(bf16)
        before = contract(two, inner_full, NT) + inner_bias_full
        active = gelu_exact(before).astype(bf16)
        result = hidden + contract(active, outer_full, NN) + outer_bias
        outputs.append(result.astype(bf16))
        grad_out = out_grad[micro]
        grad_float = grad_out.astype(f32)
        grad_active = contract(grad_out, outer_full, NT)
        grad_before = gelu_grad(before, grad_active).astype(bf16)
        grad_two = contract(grad_before, inner_full, NN)
        back, gain_sum, shift_sum = layer_back(grad_two, stats, inverse, second_gain)
        grad_hidden = grad_float + back
        branch = grad_hidden.astype(bf16)
        grad_context = contract(branch, proj_full, NT).astype(bf16)
        held.grad_context = lax.all_to_all(
            grad_context, TP, split_axis=1, concat_axis=0, tiled=True
        )
        held.grad_hidden = grad_hidden
        held.dense = (two, grad_before, active, grad_out, context, branch)
        held.row_sums = (
            jnp.sum(grad_before.astype(f32), axis=0),
            gain_sum,
            shift_sum,
            jnp.sum(branch.astype(f32), axis=0),
            jnp.sum(grad_float, axis=0),
        )

    two, grad_before, active, grad_out, context, branch = (
        jnp.concatenate(group, axis=0) for group in zip(*(h.dense for h in stage))
    )
    inner_part = contract(grad_before, two, TN).astype(bf16)
    outer_part = contract(active, grad_out, TN).astype(bf16)
    proj_part = contract(context, branch, TN).astype(bf16)
    grad_rows = 2 * hidden_units + local_width
    grad_piece = -(-grad_rows // (16 * seq_count)) * 16
    grad_held = grad_piece * seq_count
    parts = jnp.concatenate(
        [
            inner_part.reshape(tp_count, hidden_units, model_width),
            outer_part.reshape(tp_count, hidden_units, model_width),
            proj_part.reshape(tp_count, local_width, model_width),
            jnp.zeros((tp_count, grad_held - grad_rows, model_width), bf16),
        ],
        axis=1,
    ).reshape(tp_count * grad_held, model_width)
    own_part = lax.psum_scatter(parts, (TP, SEQ), scatter_dimension=0, tiled=True)
    dense_sum = lax.all_gather(own_part, SEQ, axis=0, tiled=True).astype(f32)
    inner_weight_grad = dense_sum[cuts[0] : cuts[1]].T
    outer_weight_grad = dense_sum[cuts[1] : cuts[2]]
    proj_weight_grad = dense_sum[cuts[2] : cuts[3]]

    for held in stage:
        held.grad_query, *grad_pieces = attend_backward(
            held.index,
            held.valid,
            held.queries,
            held.grad_context,
            held.logsum,
            held.pieces,
            heads,
            slots,
        )
        returned = grad_pieces[reach_dev].astype(f32)
        for offset in range(-reach_dev, reach_dev + 1):
            if offset != 0:
                returned = returned + from_behind(
                    grad_pieces[offset + reach_dev], SEQ, offset
                ).astype(f32)
        held.grad_pair = returned.astype(bf16)

    input_grads = []
    query_sum = pair_sum = 0.0
    query_bias_sum = pair_bias_sum = 0.0
    first_gain_sum = first_bias_sum = 0.0
    for held in stage:
        grad_query, grad_pair, one = held.grad_query, held.grad_pair, held.one
        rows = contract(grad_query, query_weight * score_scale, NT) + contract(grad_pair, pair_wide, NT)
        grad_one = lax.psum_scatter(
            rows.astype(bf16), TP, scatter_dimension=0, tiled=True
        ).astype(f32)
        query_sum = query_sum + contract(one, grad_query, TN)
        pair_sum = pair_sum + contract(one, grad_pair, TN)
        query_bias_sum = query_bias_sum + jnp.sum(grad_query.astype(f32), axis=0)
        pair_bias_sum = pair_bias_sum + jnp.sum(grad_pair.astype(f32), axis=0)
        back, gain_sum, shift_sum = layer_back(
            grad_one, held.stats_one, held.inverse_one, first_gain
        )
        first_gain_sum = first_gain_sum + gain_sum
        first_bias_sum = first_bias_sum + shift_sum
        input_grads.append(held.grad_hidden + back)

    def low_half(wide):
        return wide.reshape(wide.shape[:-1] + (heads, PAIR))[..., :head_size].reshape(
            wide.shape[:-1] + (local_width,)
        )

    def high_half(wide):
        return wide.reshape(wide.shape[:-1] + (heads, PAIR))[..., head_size:].reshape(
            wide.shape[:-1] + (local_width,)
        )

    query_grad, key_grad, value_grad = lax.psum(
        (query_sum * score_scale, low_half(pair_sum), high_half(pair_sum)), SEQ
    )
    inner_bias_sum, second_gain_sum, second_bias_sum, proj_bias_sum, outer_bias_sum = (
        sum(group) for group in zip(*(h.row_sums for h in stage))
    )

    def own_columns(values):
        wide = jnp.zeros((tp_count, local_width), f32)
        return lax.dynamic_update_slice_in_dim(wide, values[None], tp_place, axis=0).reshape(-1)

    early = lax.psum(
        jnp.concatenate(
            [
                inner_bias_sum,
                second_gain_sum,
                second_bias_sum,
                proj_bias_sum,
                outer_bias_sum,
            ]
        ),
        (SEQ, TP),
    )
    late = lax.psum(
        jnp.concatenate(
            [
                first_gain_sum,
                first_bias_sum,
                own_columns(query_bias_sum * score_scale),
                own_columns(high_half(pair_bias_sum)),
            ]
        ),
        (SEQ, TP),
    )
    inner_bias_all = early[: tp_count * hidden_units].reshape(tp_count, hidden_units)
    early_rows = early[tp_count * hidden_units :].reshape(-1, model_width)
    late_rows = late.reshape(-1, model_width)

    def my_columns(row):
        return lax.dynamic_slice_in_dim(row, tp_place * local_width, local_width)

    return (
        jnp.stack(outputs),
        jnp.stack(input_grads),
        query_grad,
        key_grad,
        value_grad,
        my_columns(late_rows[2]),
        my_columns(late_rows[3]),
        proj_weight_grad,
        early_rows[2],
        late_rows[0],
        late_rows[1],
        early_rows[0],
        early_rows[1],
        inner_weight_grad,
        lax.dynamic_index_in_dim(inner_bias_all, tp_place, axis=0, keepdims=False),
        outer_weight_grad,
        early_rows[3],
    )


def solution(mesh):
    def choose(tokens, doc_lengths, rand_blocks, *rest):
        blocks = rand_blocks.shape[1] * mesh.shape[SEQ]
        if plane_applies(mesh, blocks, doc_lengths.shape[1]):
            return plane_body(tokens, doc_lengths, rand_blocks, *rest)
        return general_body(tokens, doc_lengths, rand_blocks, *rest)

    return jax.shard_map(
        choose,
        mesh=mesh,
        in_specs=(
            P(None, (SEQ, TP), None),
            P(),
            P(None, SEQ, TP, None),
            P(None, TP),
            P(None, TP),
            P(None, TP),
            P(TP),
            P(TP),
            P(TP, None),
            P(),
            P(),
            P(),
            P(),
            P(),
            P(None, TP),
            P(TP),
            P(TP, None),
            P(),
            P(None, (SEQ, TP), None),
        ),
        out_specs=(
            P(None, (SEQ, TP), None),
            P(None, (SEQ, TP), None),
            P(None, TP),
            P(None, TP),
            P(None, TP),
            P(TP),
            P(TP),
            P(TP, None),
            P(),
            P(),
            P(),
            P(),
            P(),
            P(None, TP),
            P(TP),
            P(TP, None),
            P(),
        ),
        check_vma=False,
    )
```

```python
import functools
import math

import jax
import jax.numpy as jnp
import numpy as np
from jax import lax
from jax.experimental import pallas as pl
from jax.experimental.pallas import tpu as pltpu
from jax.sharding import PartitionSpec as P

BLOCK = 64
LONG_BLK = 64
SHORT_BLK = 8
PAIR = 2 * BLOCK
UNROLL = 4
SEQ = "seq"
TP = "tp"

NORM_EPS = 1e-05
MASKED = -1000000000.0

f32 = jnp.float32
bf16 = jnp.bfloat16

NN = (((1,), (0,)), ((), ()))
NT = (((1,), (1,)), ((), ()))
TN = (((0,), (0,)), ((), ()))


def contract(left, right, dims):
    return lax.dot_general(left, right, dims, preferred_element_type=f32)


def from_behind(block, axis, distance):
    devices = range(lax.axis_size(axis))
    route = [(i - distance, i) for i in devices if i - distance in devices]
    return lax.ppermute(block, axis, route)


def gelu_exact(values):
    return 0.5 * values * (1.0 + lax.erf(values / math.sqrt(2.0)))


def gelu_grad(values, grad_rows):
    _, pull_back = jax.vjp(gelu_exact, values)
    return pull_back(grad_rows)[0]


def layer_stats(values, norm_gain, norm_shift):
    row_mean = jnp.mean(values, axis=-1, keepdims=True)
    centred = values - row_mean
    inverse = lax.rsqrt(jnp.mean(centred * centred, axis=-1, keepdims=True) + NORM_EPS)
    normed = centred * inverse
    return (normed * norm_gain + norm_shift, normed, inverse)


def layer_back(grad_rows, normed, inverse, norm_gain):
    scaled = grad_rows * norm_gain
    inner_term = (
        scaled
        - jnp.mean(scaled, axis=-1, keepdims=True)
        - normed * jnp.mean(scaled * normed, axis=-1, keepdims=True)
    )
    return (inverse * inner_term, jnp.sum(grad_rows * normed, axis=0), jnp.sum(grad_rows, axis=0))


def block_keys(lengths, randoms, blocks):
    doc_ends = jnp.cumsum(lengths)
    doc_starts = doc_ends - lengths
    doc_owner = jnp.sum((blocks[:, None] >= doc_ends[None, :]).astype(jnp.int32), axis=1)
    doc_ids = jnp.arange(lengths.shape[0], dtype=jnp.int32)
    doc_hit = doc_owner[:, None] == doc_ids[None, :]
    doc_first = jnp.sum(jnp.where(doc_hit, doc_starts[None, :], 0), axis=1)
    doc_final = jnp.sum(jnp.where(doc_hit, doc_ends[None, :], 0), axis=1)
    fixed_keys = jnp.stack(
        [
            jnp.maximum(blocks - 1, doc_first),
            jnp.minimum(blocks + 1, doc_final - 1),
            blocks,
            doc_first,
            doc_first + 1,
        ],
        axis=1,
    )
    block_count = randoms.shape[0]
    head_count = randoms.shape[1]
    key_index = jnp.concatenate(
        [jnp.broadcast_to(fixed_keys[:, None, :], (block_count, head_count, 5)), randoms], axis=2
    )
    key_valid = jnp.stack([blocks > doc_first, blocks + 1 < doc_final], axis=1)
    return (key_index, key_valid.astype(jnp.int32))


def block_rows(block):
    return pl.ds(pl.multiple_of(block * BLOCK, BLOCK), BLOCK)


def listed_blocks(index_ref, store, base, slots):
    return jnp.concatenate(
        [store[block_rows(index_ref[base + slot]), :] for slot in range(slots)], axis=0
    )


def mask_scores(scores, valid_ref, block):
    lane = lax.broadcasted_iota(jnp.int32, (1, PAIR), 1)
    keep = jnp.where(lane < BLOCK, valid_ref[2 * block], valid_ref[2 * block + 1]) > 0
    return jnp.concatenate([jnp.where(keep, scores[:, :PAIR], MASKED), scores[:, PAIR:]], axis=1)


def fill_store(store, pieces):
    place = 0
    for piece in pieces:
        store[place : place + piece.shape[0], :] = piece[...]
        place += piece.shape[0]


def each_head(heads, work):
    for head in range(heads):

        @pl.when(pl.program_id(0) == head)
        def _():
            work(slice(head * BLOCK, (head + 1) * BLOCK))


def forward_kernel(slots, heads, index_ref, valid_ref, query_ref, *refs):
    *pieces, context_ref, logsum_ref, store, wide_query, wide_context = refs
    rows = query_ref.shape[0]
    blocks = rows // BLOCK
    head = pl.program_id(0)
    fill_store(store, pieces)

    def take_query(columns):
        query = query_ref[:, columns]
        wide_query[...] = jnp.concatenate([query, jnp.zeros_like(query)], axis=1)

    each_head(heads, take_query)

    def step(group, carry):
        ids = [group * UNROLL + unit for unit in range(UNROLL)]
        listed = [
            listed_blocks(index_ref, store, (head * blocks + block) * slots, slots)
            for block in ids
        ]
        scores = [
            mask_scores(contract(wide_query[block_rows(block), :], pairs, NT), valid_ref, block)
            for block, pairs in zip(ids, listed)
        ]
        probs = []
        for block, score in zip(ids, scores):
            top = jnp.max(score, axis=1, keepdims=True)
            raised = jnp.exp(score - top)
            total = jnp.sum(raised, axis=1, keepdims=True)
            probs.append((raised * (1.0 / total)).astype(bf16))
            logsum_ref[block_rows(block), :] = jnp.broadcast_to(
                top + jnp.log(total), (BLOCK, PAIR)
            )
        for block, prob, pairs in zip(ids, probs, listed):
            wide_context[block_rows(block), :] = contract(prob, pairs, NN).astype(bf16)
        return carry

    lax.fori_loop(0, blocks // UNROLL, step, 0)

    def give_context(columns):
        context_ref[:, columns] = wide_context[:, BLOCK:]

    each_head(heads, give_context)


def backward_kernel(slots, heads, count, index_ref, valid_ref, query_ref, grad_ref, logsum_ref, *refs):
    pieces = refs[:count]
    grad_query_ref = refs[count]
    grad_pieces = refs[count + 1 : 2 * count + 1]
    store, sums, both_rows, wide_grad = refs[2 * count + 1 :]
    rows = query_ref.shape[0]
    blocks = rows // BLOCK
    head = pl.program_id(0)
    fill_store(store, pieces)
    sums[...] = jnp.zeros_like(sums)
    lane = lax.broadcasted_iota(jnp.int32, (BLOCK, PAIR), 1)

    def take_both(columns):
        both_rows[...] = jnp.concatenate([query_ref[:, columns], grad_ref[:, columns]], axis=1)

    each_head(heads, take_both)

    def step(group, carry):
        ids = [group * UNROLL + unit for unit in range(UNROLL)]
        listed = [
            listed_blocks(index_ref, store, (head * blocks + block) * slots, slots)
            for block in ids
        ]
        lefts = []
        for block in ids:
            both = both_rows[block_rows(block), :]
            lefts.append(
                jnp.concatenate(
                    [
                        jnp.where(lane < BLOCK, both, 0).astype(bf16),
                        jnp.where(lane < BLOCK, 0, both).astype(bf16),
                    ],
                    axis=0,
                )
            )
        products = [contract(left, pairs, NT) for left, pairs in zip(lefts, listed)]
        mixes = []
        for block, product in zip(ids, products):
            score = mask_scores(product[:BLOCK], valid_ref, block)
            grad_prob = product[BLOCK:]
            logsum = jnp.concatenate([logsum_ref[block_rows(block), :]] * (slots // 2), axis=1)
            prob = jnp.exp(score - logsum)
            delta = jnp.sum(prob * grad_prob, axis=1, keepdims=True)
            grad_score = prob * (grad_prob - delta)
            mixes.append(jnp.concatenate([grad_score.astype(bf16), prob.astype(bf16)], axis=0))
        for block, mix, pairs in zip(ids, mixes, listed):
            wide_grad[block_rows(block), :] = contract(mix[:BLOCK], pairs, NN).astype(bf16)
        terms = [contract(mix, left, TN) for mix, left in zip(mixes, lefts)]
        for block, term in zip(ids, terms):
            base = (head * blocks + block) * slots
            for slot in range(slots):
                sums[block_rows(index_ref[base + slot]), :] += term[
                    slot * BLOCK : (slot + 1) * BLOCK
                ]
        return carry

    lax.fori_loop(0, blocks // UNROLL, step, 0)
    place = 0
    for grad_piece in grad_pieces:
        grad_piece[...] = sums[place : place + grad_piece.shape[0], :].astype(bf16)
        place += grad_piece.shape[0]

    def give_grad(columns):
        grad_query_ref[:, columns] = wide_grad[:, :BLOCK]

    each_head(heads, give_grad)


def lasting(microseconds):
    return pl.CostEstimate(
        flops=0, bytes_accessed=int(microseconds * 3.69e6), transcendentals=0
    )


def per_head(array):
    return pl.BlockSpec((array.shape[0], PAIR), lambda head, *_: (0, head))


def whole(array):
    return pl.BlockSpec(array.shape, lambda head, *_: (0, 0))


def attend_forward(index, valid, queries, pieces, heads, slots):
    rows = queries.shape[0]
    stored = sum(piece.shape[0] for piece in pieces)
    logsum = jax.ShapeDtypeStruct((rows, heads * PAIR), f32)
    return pl.pallas_call(
        functools.partial(forward_kernel, slots, heads),
        grid_spec=pltpu.PrefetchScalarGridSpec(
            num_scalar_prefetch=2,
            grid=(heads,),
            in_specs=[whole(queries)] + [per_head(piece) for piece in pieces],
            out_specs=[whole(queries), per_head(logsum)],
            scratch_shapes=[
                pltpu.VMEM((stored, PAIR), bf16),
                pltpu.VMEM((rows, PAIR), bf16),
                pltpu.VMEM((rows, PAIR), bf16),
            ],
        ),
        out_shape=[jax.ShapeDtypeStruct(queries.shape, bf16), logsum],
        compiler_params=pltpu.CompilerParams(vmem_limit_bytes=40 * 2**20),
        cost_estimate=lasting(18),
    )(index, valid, queries, *pieces)


def attend_backward(index, valid, queries, grads, logsum, pieces, heads, slots):
    rows = queries.shape[0]
    stored = sum(piece.shape[0] for piece in pieces)
    piece_specs = [per_head(piece) for piece in pieces]
    return pl.pallas_call(
        functools.partial(backward_kernel, slots, heads, len(pieces)),
        grid_spec=pltpu.PrefetchScalarGridSpec(
            num_scalar_prefetch=2,
            grid=(heads,),
            in_specs=[whole(queries), whole(grads), per_head(logsum)] + piece_specs,
            out_specs=[whole(queries)] + piece_specs,
            scratch_shapes=[
                pltpu.VMEM((stored, PAIR), bf16),
                pltpu.VMEM((stored, PAIR), f32),
                pltpu.VMEM((rows, PAIR), bf16),
                pltpu.VMEM((rows, PAIR), bf16),
            ],
        ),
        out_shape=[jax.ShapeDtypeStruct(queries.shape, bf16)]
        + [jax.ShapeDtypeStruct(piece.shape, bf16) for piece in pieces],
        compiler_params=pltpu.CompilerParams(vmem_limit_bytes=50 * 2**20),
        cost_estimate=lasting(25),
    )(index, valid, queries, grads, logsum, *pieces)


def plane_exchange(values, split_axis, concat_axis):
    count = lax.axis_size(SEQ)
    groups = [list(range(place, count, 2)) for place in range(2)]
    return lax.all_to_all(
        values,
        SEQ,
        split_axis=split_axis,
        concat_axis=concat_axis,
        axis_index_groups=groups,
        tiled=True,
    )


def plane_gather(values):
    count = lax.axis_size(SEQ) // 2
    return plane_exchange(jnp.concatenate([values] * count, axis=0), 0, 0)


def core_swap(block):
    route = [(place, place ^ 1) for place in range(lax.axis_size(SEQ))]
    return lax.ppermute(block, SEQ, route)


def column_shift(block, step):
    count = lax.axis_size(TP)
    return lax.ppermute(block, TP, [(place, (place + step) % count) for place in range(count)])


def column_gather(values):
    count = lax.axis_size(TP)
    place = lax.axis_index(TP)
    spread = jnp.zeros((count,) + values.shape, values.dtype)
    spread = lax.dynamic_update_index_in_dim(spread, values, place, axis=0)
    for step in range(1, count):
        spread = lax.dynamic_update_index_in_dim(
            spread, column_shift(values, step), (place - step) % count, axis=0
        )
    return spread


def after(values, *earlier):
    return lax.optimization_barrier((values, earlier))[0]


def sum_parts(parts):
    total = parts[0].astype(f32)
    for place in range(1, len(parts)):
        total = total + parts[place].astype(f32)
    return total


def partner_of(place):
    return place + 1 - 2 * (place % 2)


def enter(neighbours):
    barrier = pltpu.get_barrier_semaphore()
    count = 0
    for exists, device in neighbours:

        @pl.when(exists)
        def _():
            pl.semaphore_signal(
                barrier, inc=1, device_id=device, device_id_type=pl.DeviceIdType.MESH
            )

        count = count + jnp.where(exists, 1, 0)
    pl.semaphore_wait(barrier, count)


def remote(source, target, send, receive, device):
    return pltpu.make_async_remote_copy(
        src_ref=source,
        dst_ref=target,
        send_sem=send,
        recv_sem=receive,
        device_id=device,
        device_id_type=pl.DeviceIdType.MESH,
    )


def plane_ids():
    seq_place = lax.axis_index(SEQ)
    chip, core = seq_place // 2, seq_place % 2
    beside = chip + 1 - 2 * (chip % 2)
    above = chip + 2 - 4 * (chip // 2)
    facing = 3 - chip
    return chip, core, beside, above, facing


def column_way(place, way, distance):
    return place - distance if way == 0 else place + distance


class ColumnSpread:

    def __init__(self, parts, own, near, far, other, keep_sem, along_sems, across_sems):
        self.parts, self.own, self.near, self.far = parts, own, near, far
        self.other, self.keep_sem = other, keep_sem
        self.along_sems, self.across_sems = along_sems, across_sems
        self.count = lax.axis_size(TP)
        self.place = lax.axis_index(TP)
        self.rows = own.shape[0] // parts

    def cut(self, part):
        return pl.ds(part * self.rows, self.rows)

    def block(self, way, distance, part):
        if distance == 0:
            return self.own.at[self.cut(part)]
        return self.near.at[column_way(self.place, way, distance), self.cut(part)]

    def along(self, way, distance, part):
        return remote(
            self.block(way, distance, part),
            self.near.at[column_way(self.place, way, distance), self.cut(part)],
            self.along_sems[0].at[way, distance, part],
            self.along_sems[1].at[way, distance, part],
            {TP: self.place + 1 if way == 0 else self.place - 1},
        )

    def landed(self, way, distance, part):
        block = self.near.at[column_way(self.place, way, distance), self.cut(part)]
        return remote(
            block,
            block,
            self.along_sems[0].at[way, distance, part],
            self.along_sems[1].at[way, distance - 1, part],
            self.other,
        )

    def across(self, way, distance, part):
        return remote(
            self.block(way, distance, part),
            self.far.at[column_way(self.place, way, distance), self.cut(part)],
            self.across_sems[0].at[way, distance, part],
            self.across_sems[1].at[way, distance, part],
            self.other,
        )

    def keep(self):
        return pltpu.make_async_copy(self.own, self.near.at[self.place], self.keep_sem)

    def goes_on(self, way):
        return self.place < self.count - 1 if way == 0 else self.place > 0

    def has_come(self, way, distance):
        if way == 0:
            return self.place >= distance
        return self.place + distance < self.count

    def start(self):
        for part in range(self.parts):
            for way in range(2):

                @pl.when(self.goes_on(way))
                def _():
                    self.along(way, 0, part).start()

        if self.far is not None:
            for part in range(self.parts):
                self.across(0, 0, part).start()
        self.keep().start()

    def step(self, distance, part):
        for way in range(2):

            @pl.when(self.has_come(way, distance))
            def _():
                self.landed(way, distance, part).wait_recv()
                if distance < self.count - 1:

                    @pl.when(self.goes_on(way))
                    def _():
                        self.along(way, distance, part).start()

                if self.far is not None:
                    self.across(way, distance, part).start()

    def finish(self):
        self.keep().wait()
        for part in range(self.parts):
            if self.far is not None:
                self.across(0, 0, part).wait()
            for way in range(2):

                @pl.when(self.goes_on(way))
                def _():
                    self.along(way, 0, part).wait_send()

        for distance in range(1, self.count):
            for part in range(self.parts):
                for way in range(2):

                    @pl.when(self.has_come(way, distance))
                    def _():
                        if distance < self.count - 1:

                            @pl.when(self.goes_on(way))
                            def _():
                                self.along(way, distance, part).wait_send()

                        if self.far is not None:
                            self.across(way, distance, part).wait()


class PlaneSpread:

    def __init__(self, own, out, sems):
        self.own, self.out = own, out
        self.send_row, self.recv_row, self.send_on, self.recv_on = sems
        self.chip, core, beside, above, self.facing = plane_ids()
        self.ways = ({SEQ: 2 * beside + core}, {SEQ: 2 * above + core})
        self.chips = (beside, above)

    def first(self, way, part):
        return remote(
            self.own(part),
            self.out(self.chip, part),
            self.send_row.at[way, part],
            self.recv_row.at[way, part],
            self.ways[way],
        )

    def second(self, way):
        return remote(
            self.out(self.chips[way], way),
            self.out(self.chips[way], way),
            self.send_on.at[way],
            self.recv_on.at[way],
            self.ways[1 - way],
        )

    def start(self):
        self.first(0, 0).start()
        self.first(1, 1).start()

    def forward(self):
        for way in range(2):
            self.first(way, way).wait_recv()
            self.second(way).start()
        for way in range(2):
            self.first(way, 1 - way).start()

    def arrive(self):
        for way in range(2):
            self.first(way, 1 - way).wait_recv()
        for way in range(2):
            self.second(way).wait_recv()

    def finish(self):
        for way in range(2):
            self.second(way).wait_send()
            for part in range(2):
                self.first(way, part).wait_send()


def plane_sems():
    dma = pltpu.SemaphoreType.DMA
    return [dma((2, 2)), dma((2, 2)), dma((2,)), dma((2,))]


def column_sems(parts):
    sems = pltpu.SemaphoreType.DMA((2, 4, parts))
    return [sems, sems, sems, sems]


def halves_of(own, out, keep_sem):
    half = own.shape[0] // 2
    chip = plane_ids()[0]
    return (
        lambda part: own.at[pl.ds(part * half, half)],
        lambda place, part: out.at[place, pl.ds(part * half, half)],
        pltpu.make_async_copy(own, out.at[chip], keep_sem),
    )


def neighbours(facing_too, column_too):
    chip, core, beside, above, facing = plane_ids()
    count = lax.axis_size(TP)
    place = lax.axis_index(TP)
    always = place >= 0
    devices = [(always, {SEQ: 2 * chip + 1 - core})]
    devices += [(always, {SEQ: 2 * beside + core}), (always, {SEQ: 2 * above + core})]
    if facing_too:
        devices.append((always, {SEQ: 2 * facing + core}))
    if column_too:
        for step in range(1, count):
            devices.append((always, {TP: lax.rem(place + step, count)}))
    else:
        devices.append((place < count - 1, {TP: place + 1}))
        devices.append((place > 0, {TP: place - 1}))
    return devices


def first_kernel(
    parts,
    own_ref,
    weight_ref,
    share_ref,
    random_ref,
    out_ref,
    spread_ref,
    column_ref,
    random_out_ref,
    randoms,
    own_sem,
    send_row,
    recv_row,
    send_on,
    recv_on,
    send_z,
    recv_z,
    send_far,
    recv_far,
    send_random,
    recv_random,
    send_column,
    recv_column,
    send_share,
    recv_share,
):
    chip, core, beside, above, facing = plane_ids()
    tp_count = lax.axis_size(TP)
    place = lax.axis_index(TP)
    other = {SEQ: 2 * chip + 1 - core}
    weight_rows = weight_ref.shape[0] // (2 * parts)
    column = [{TP: lax.rem(place + step, tp_count)} for step in range(1, tp_count)]
    enter(neighbours(True, True))
    own, out, keep_rows = halves_of(own_ref, out_ref, own_sem.at[0])
    rows = PlaneSpread(own, out, (send_row, recv_row, send_on, recv_on))
    shares = ColumnSpread(
        2, share_ref, column_ref, None, other, own_sem.at[2], (send_share, recv_share), None
    )

    def weight_cut(part, holder):
        return pl.ds((holder * parts + part) * weight_rows, weight_rows)

    def weight_along(source, way, part):
        at = weight_cut(part, core)
        return remote(
            source.at[at],
            spread_ref.at[at],
            send_z.at[way, part],
            recv_z.at[part],
            {TP: place + 1 if way == 0 else place - 1},
        )

    def weight_across(part):
        at = weight_cut(part, core)
        return remote(
            spread_ref.at[at], spread_ref.at[at], send_far.at[part], recv_far.at[part], other
        )

    def goes_on(way):
        if way == 0:
            return (place >= chip) & (place < tp_count - 1)
        return (place <= chip) & (place > 0)

    def random_to_holder(sender):
        return remote(
            random_ref,
            randoms.at[sender],
            send_random,
            recv_random.at[sender],
            {SEQ: 2 * place + core},
        )

    def random_along(step):
        return remote(
            randoms,
            random_out_ref,
            send_column.at[step],
            recv_column,
            column[step],
        )

    rows.start()

    @pl.when(place != chip)
    def _():
        random_to_holder(chip).start()

    for part in range(parts):
        for way in range(2):

            @pl.when((place == chip) & goes_on(way))
            def _():
                weight_along(weight_ref, way, part).start()

    shares.start()
    keep_rows.start()

    @pl.when(place == chip)
    def _():
        keep = pltpu.make_async_copy(weight_ref, spread_ref, own_sem.at[1])
        keep.start()
        keep.wait()
        randoms[chip] = random_ref[...]
        for step in range(1, tp_count):
            random_to_holder(lax.rem(chip + step, tp_count)).wait_recv()
        random_out_ref[...] = randoms[...]
        for step in range(tp_count - 1):
            random_along(step).start()

    rows.forward()
    for part in range(parts):

        @pl.when(place != chip)
        def _():
            weight_along(spread_ref, 0, part).wait_recv()
            for way in range(2):

                @pl.when(goes_on(way))
                def _():
                    weight_along(spread_ref, way, part).start()

            weight_across(part).start()

    for distance in range(1, tp_count):
        for part in range(2):
            shares.step(distance, part)
    rows.arrive()
    rows.finish()
    shares.finish()
    keep_rows.wait()

    @pl.when(place != chip)
    def _():
        random_to_holder(chip).wait_send()
        random_along(0).wait_recv()

    @pl.when(place == chip)
    def _():
        for step in range(tp_count - 1):
            random_along(step).wait_send()

    for part in range(parts):

        @pl.when(place != chip)
        def _():
            weight_across(part).wait()

        for way in range(2):

            @pl.when(goes_on(way))
            def _():
                weight_along(spread_ref, way, part).wait_send()


def first_exchange(own, weight, share, randoms, collective_id, parts=4):
    chips = lax.axis_size(SEQ) // 2
    count = lax.axis_size(TP)
    resident = pl.BlockSpec(memory_space=pltpu.VMEM)
    dma = pltpu.SemaphoreType.DMA
    return pl.pallas_call(
        functools.partial(first_kernel, parts),
        out_shape=[
            jax.ShapeDtypeStruct((chips,) + own.shape, own.dtype),
            jax.ShapeDtypeStruct(weight.shape, weight.dtype),
            jax.ShapeDtypeStruct((count,) + share.shape, share.dtype),
            jax.ShapeDtypeStruct((chips,) + randoms.shape, randoms.dtype),
        ],
        in_specs=[resident] * 4,
        out_specs=[resident] * 4,
        scratch_shapes=[pltpu.VMEM((chips,) + randoms.shape, randoms.dtype), dma((3,))]
        + plane_sems()
        + [
            dma((2, parts)),
            dma((parts,)),
            dma((parts,)),
            dma((parts,)),
            dma,
            dma((chips,)),
            dma((chips - 1,)),
            dma,
        ]
        + column_sems(2)[:2],
        compiler_params=pltpu.CompilerParams(
            collective_id=collective_id, has_side_effects=True, vmem_limit_bytes=32 * 2**20
        ),
        cost_estimate=lasting(30),
    )(own, weight, share, randoms)


def second_kernel(parts, longs_ref, own_ref, near_ref, far_ref, out_ref, keep_sem, *sems):
    chip, core = plane_ids()[:2]
    enter(neighbours(False, False))
    other = {SEQ: 2 * chip + 1 - core}
    longs = ColumnSpread(
        parts, longs_ref, near_ref, far_ref, other, keep_sem.at[0], sems[:2], sems[2:4]
    )
    own, out, keep_rows = halves_of(own_ref, out_ref, keep_sem.at[1])
    rows = PlaneSpread(own, out, sems[4:])
    longs.start()
    rows.start()
    keep_rows.start()
    rows.forward()
    for distance in range(1, longs.count):
        for part in range(parts):
            longs.step(distance, part)
    rows.arrive()
    rows.finish()
    longs.finish()
    keep_rows.wait()


def second_exchange(longs, own, collective_id, parts=2):
    chips = lax.axis_size(SEQ) // 2
    near = jax.ShapeDtypeStruct((lax.axis_size(TP),) + longs.shape, longs.dtype)
    resident = pl.BlockSpec(memory_space=pltpu.VMEM)
    return pl.pallas_call(
        functools.partial(second_kernel, parts),
        out_shape=[near, near, jax.ShapeDtypeStruct((chips,) + own.shape, own.dtype)],
        in_specs=[resident] * 2,
        out_specs=[resident] * 3,
        scratch_shapes=[pltpu.SemaphoreType.DMA((2,))] + column_sems(parts) + plane_sems(),
        compiler_params=pltpu.CompilerParams(
            collective_id=collective_id, has_side_effects=True, vmem_limit_bytes=32 * 2**20
        ),
        cost_estimate=lasting(55),
    )(longs, own)


def third_kernel(
    parts, cuts, longs_ref, column_ref, sent_ref, near_ref, far_ref, context_ref, *refs
):
    count = len(cuts) - 1
    outs, refs = refs[:count], refs[count:]
    keep_sem, cross_sems, block_sems, sems = refs[0], refs[1:3], refs[3:5], refs[5:]
    chip, core, beside, above, facing = plane_ids()
    enter(neighbours(True, False))
    other = {SEQ: 2 * chip + 1 - core}
    longs = ColumnSpread(
        parts, longs_ref, near_ref, far_ref, other, keep_sem.at[0], sems[:2], sems[2:4]
    )
    half = column_ref.shape[0] // 2
    weights = []
    keeps = []
    for place in range(count):
        rows = pl.ds(cuts[place], cuts[place + 1] - cuts[place])
        out = outs[place]
        weights.append(
            PlaneSpread(
                lambda part, rows=rows: column_ref.at[pl.ds(part * half, half), rows],
                lambda where, part, out=out: out.at[core, where, pl.ds(part * half, half)],
                [sem.at[place] for sem in sems[4:]],
            )
        )
        keeps.append(
            pltpu.make_async_copy(
                column_ref.at[:, rows], out.at[core, chip], keep_sem.at[1 + place]
            )
        )

    def across(place, where, part):
        block = outs[place].at[
            core, (chip, beside, above, facing)[where], pl.ds(part * half, half)
        ]
        at = (place, where, part)
        return remote(block, block, cross_sems[0].at[at], cross_sems[1].at[at], other)

    def send_block(index):
        target = (beside, above, facing)[index]
        return remote(
            sent_ref.at[target],
            context_ref.at[chip],
            block_sems[0].at[index],
            block_sems[1].at[index],
            {SEQ: 2 * target + core},
        )

    keep_block = pltpu.make_async_copy(
        sent_ref.at[chip], context_ref.at[chip], keep_sem.at[1 + count]
    )
    longs.start()
    for weight, keep in zip(weights, keeps):
        weight.start()
        keep.start()
    for index in range(3):
        send_block(index).start()
    keep_block.start()
    for part in range(parts):
        longs.step(1, part)
    for place in range(count):
        weights[place].forward()
        keeps[place].wait()
        for where, part in ((0, 0), (0, 1), (1, 0), (2, 1)):
            across(place, where, part).start()
    for part in range(parts):
        longs.step(2, part)
    for place in range(count):
        weights[place].arrive()
        for where, part in ((1, 1), (2, 0), (3, 0), (3, 1)):
            across(place, where, part).start()
    for part in range(parts):
        longs.step(3, part)
    longs.finish()
    for place in range(count):
        weights[place].finish()
        for where in range(4):
            for part in range(2):
                across(place, where, part).wait()
    for index in range(3):
        send_block(index).wait()
    keep_block.wait()


def third_exchange(longs, column, sent, cuts, collective_id, parts=2):
    chips = lax.axis_size(SEQ) // 2
    tp_count, _, width = column.shape
    near = jax.ShapeDtypeStruct((tp_count,) + longs.shape, longs.dtype)
    count = len(cuts) - 1
    outs = [
        jax.ShapeDtypeStruct((2, chips, tp_count, last - first, width), column.dtype)
        for first, last in zip(cuts, cuts[1:])
    ]
    resident = pl.BlockSpec(memory_space=pltpu.VMEM)
    dma = pltpu.SemaphoreType.DMA
    return pl.pallas_call(
        functools.partial(third_kernel, parts, cuts),
        out_shape=[near, near, jax.ShapeDtypeStruct(sent.shape, sent.dtype)] + outs,
        in_specs=[resident] * 3,
        out_specs=[resident] * (3 + count),
        scratch_shapes=[dma((2 + count,)), dma((count, 4, 2)), dma((count, 4, 2)), dma((3,)), dma((3,))]
        + column_sems(parts)
        + [dma((count, 2, 2)), dma((count, 2, 2)), dma((count, 2)), dma((count, 2))],
        compiler_params=pltpu.CompilerParams(
            collective_id=collective_id, has_side_effects=True, vmem_limit_bytes=48 * 2**20
        ),
        cost_estimate=lasting(55),
    )(longs, column, sent)


class ColumnReduce:

    def __init__(self, parts, step_rows, sums, came, sems):
        self.parts, self.step_rows = parts, step_rows
        self.sums, self.came, self.sems = sums, came, sems
        self.count = lax.axis_size(TP)
        self.place = lax.axis_index(TP)
        self.rows = sums.shape[1] // parts
        self.order = []
        for step in range(self.count):
            for owner in (step, self.count - 1 - step):
                if owner not in self.order:
                    self.order.append(owner)

    def along(self, way, owner, part):
        at = pl.ds(part * self.rows, self.rows)
        return remote(
            self.sums.at[owner, at],
            self.came.at[way, owner, at],
            self.sems[0].at[way, owner, part],
            self.sems[1].at[way, owner, part],
            {TP: self.place - 1 if way == 0 else self.place + 1},
        )

    def add(self, owner, source, part):
        @pl.loop(0, self.rows // self.step_rows)
        def _(step):
            start = pl.multiple_of(part * self.rows + step * self.step_rows, self.step_rows)
            at = pl.ds(start, self.step_rows)
            total = self.sums[owner, at, :].astype(f32) + source[at, :].astype(f32)
            self.sums[owner, at, :] = total.astype(self.sums.dtype)

    def takes(self, way):
        return self.place < self.count - 1 if way == 0 else self.place > 0

    def passes(self, way, owner):
        return self.place > owner if way == 0 else self.place < owner

    def begin(self, owner, part):
        for way in range(2):

            @pl.when(self.passes(way, owner) & ~self.takes(way))
            def _():
                self.along(way, owner, part).start()

    def move(self, way, owner, part):
        @pl.when(self.passes(way, owner) & self.takes(way))
        def _():
            self.along(way, owner, part).wait_recv()
            self.add(owner, self.came.at[way, owner], part)
            self.along(way, owner, part).start()

    def end(self):
        for part in range(self.parts):
            for way in range(2):
                for owner in range(self.count):

                    @pl.when((self.place == owner) & self.takes(way))
                    def _():
                        self.along(way, owner, part).wait_recv()
                        self.add(owner, self.came.at[way, owner], part)

    def finish(self):
        for owner in range(self.count):
            for part in range(self.parts):
                for way in range(2):

                    @pl.when(self.passes(way, owner))
                    def _():
                        self.along(way, owner, part).wait_send()

    def give(self, out):
        for owner in range(self.count):

            @pl.when(self.place == owner)
            def _():
                out[...] = self.sums[owner]


class PlaneReduce:

    def __init__(self, step_rows, terms, out, buffers, sems):
        self.step_rows, self.terms, self.out = step_rows, terms, out
        self.came, self.facing_came, self.sent, self.last = buffers
        self.sems = sems
        self.chip, core, beside, above, self.facing = plane_ids()
        self.ways = ({SEQ: 2 * beside + core}, {SEQ: 2 * above + core})
        self.chips = (beside, above)
        self.half = terms.shape[1] // 2

    def copy(self, kind, way, source, target, device):
        return remote(
            source, target.at[way], self.sems[0].at[kind, way], self.sems[1].at[kind, way], device
        )

    def pieces(self, way):
        return pl.ds(way * self.half, self.half)

    def facing_term(self, way):
        source = self.terms.at[self.facing, self.pieces(way)]
        return self.copy(0, way, source, self.facing_came, self.ways[way])

    def near_term(self, way):
        source = self.terms.at[self.chips[way], self.pieces(way)]
        return self.copy(1, way, source, self.came, self.ways[way])

    def summed(self, way):
        return self.copy(2, way, self.sent.at[way], self.last, self.ways[1 - way])

    def each_step(self, work):
        steps = self.terms.shape[2] // self.step_rows

        @pl.loop(0, self.half * steps)
        def _(step):
            start = pl.multiple_of((step % steps) * self.step_rows, self.step_rows)
            work(step // steps, pl.ds(start, self.step_rows))

    def start(self):
        for way in range(2):
            self.facing_term(way).start()
        for way in range(2):
            self.near_term(way).start()

    def move(self):
        for way in range(2):
            self.facing_term(way).wait_recv()

            def add_term(piece, at):
                total = self.terms[self.chips[1 - way], way * self.half + piece, at, :].astype(f32)
                total = total + self.facing_came[way, piece, at, :].astype(f32)
                self.sent[way, piece, at, :] = total.astype(self.sent.dtype)

            self.each_step(add_term)
            self.summed(way).start()

    def end(self):
        for way in range(2):
            self.near_term(way).wait_recv()
            self.summed(way).wait_recv()

            def add_last(piece, at):
                total = self.terms[self.chip, way * self.half + piece, at, :].astype(f32)
                total = total + self.came[way, piece, at, :].astype(f32)
                total = total + self.last[way, piece, at, :].astype(f32)
                self.out[way * self.half + piece, at, :] = total.astype(self.out.dtype)

            self.each_step(add_last)

    def finish(self):
        for way in range(2):
            self.facing_term(way).wait_send()
            self.near_term(way).wait_send()
            self.summed(way).wait_send()


def reduce_scratch(shape, dtype):
    half = pltpu.VMEM((2, shape[1] // 2) + shape[2:], dtype)
    sems = pltpu.SemaphoreType.DMA((3, 2))
    return [half] * 4 + [sems, sems]


def fourth_kernel(parts, cuts, near_ref, far_ref, rows_ref, *refs):
    count = len(cuts) - 1
    terms, givens, refs = refs[:count], refs[count : 2 * count], refs[2 * count :]
    out_ref, dense_ref, rows_out_ref, sums, given, came, dense, more = refs[:8]
    load_sem, send_far, recv_far, send_z, recv_z = refs[8:13]
    buffers, sems = refs[13:17], refs[17:19]
    row_buffers, row_sems = refs[19:23], refs[23:25]
    place = lax.axis_index(TP)
    chip, core = plane_ids()[:2]
    other = {SEQ: 2 * chip + 1 - core}
    loads = [pltpu.make_async_copy(near_ref, sums, load_sem.at[0])]
    for index in range(count):
        rows = pl.ds(cuts[index], cuts[index + 1] - cuts[index])
        loads.append(
            pltpu.make_async_copy(
                terms[index].at[core], dense.at[:, :, rows], load_sem.at[1 + 2 * index]
            )
        )
        loads.append(
            pltpu.make_async_copy(givens[index], more.at[:, :, rows], load_sem.at[2 + 2 * index])
        )
    for load in loads:
        load.start()
    enter(neighbours(False, False))
    column = ColumnReduce(parts, 128, sums, came, (send_z, recv_z))
    plane = PlaneReduce(32, dense, dense_ref, buffers, sems)
    rows = PlaneReduce(64, rows_ref, rows_out_ref, row_buffers, row_sems)

    def across(owner):
        return remote(
            far_ref.at[owner], given.at[owner], send_far.at[owner], recv_far.at[owner], other
        )

    def move(steps):
        for part in range(parts):
            for way, owner in steps:
                column.move(way, owner, part)

    rows.start()
    for owner in column.order:
        across(owner).start()
    for load in loads:
        load.wait()
    pieces, steps = dense.shape[1], dense.shape[2] // 32

    @pl.loop(0, dense.shape[0] * pieces * steps)
    def _(step):
        at = pl.ds(pl.multiple_of((step % steps) * 32, 32), 32)
        piece = (step // steps) % pieces
        where = step // (steps * pieces)
        total = dense[where, piece, at, :].astype(f32) + more[where, piece, at, :].astype(f32)
        dense[where, piece, at, :] = total.astype(dense.dtype)

    plane.start()
    for owner in column.order:
        across(owner).wait_recv()
        for part in range(parts):
            column.add(owner, given.at[owner], part)
            column.begin(owner, part)
    rows.move()
    last = column.count - 1

    @pl.when(place == last - 1)
    def _():
        move([(0, 0)])

    @pl.when(place == 1)
    def _():
        move([(1, last)])

    plane.move()

    @pl.when(place == last - 1)
    def _():
        move([(0, 1), (1, last)])

    @pl.when(place == 1)
    def _():
        move([(1, last - 1), (0, 0)])

    rows.end()
    column.end()
    column.give(out_ref)
    plane.end()
    column.finish()
    plane.finish()
    rows.finish()
    for owner in column.order:
        across(owner).wait_send()


def fourth_exchange(near, far, rows, terms, givens, cuts, collective_id, parts=2):
    count = lax.axis_size(TP)
    block = near.shape[1:]
    chips = givens[0].shape[0]
    width = givens[0].shape[-1]
    dense = (chips, count, cuts[-1], width)
    resident = pl.BlockSpec(memory_space=pltpu.VMEM)
    anywhere = pl.BlockSpec(memory_space=pl.ANY)
    dma = pltpu.SemaphoreType.DMA
    pieces = len(cuts) - 1
    return pl.pallas_call(
        functools.partial(fourth_kernel, parts, cuts),
        out_shape=[
            jax.ShapeDtypeStruct(block, near.dtype),
            jax.ShapeDtypeStruct(dense[1:], near.dtype),
            jax.ShapeDtypeStruct(rows.shape[1:], f32),
        ],
        in_specs=[anywhere, resident, resident] + [anywhere] * (2 * pieces),
        out_specs=[resident] * 3,
        scratch_shapes=[
            pltpu.VMEM((count,) + block, near.dtype),
            pltpu.VMEM((count,) + block, near.dtype),
            pltpu.VMEM((2, count) + block, near.dtype),
            pltpu.VMEM(dense, near.dtype),
            pltpu.VMEM(dense, near.dtype),
            dma((1 + 2 * pieces,)),
            dma((count,)),
            dma((count,)),
            dma((2, count, parts)),
            dma((2, count, parts)),
        ]
        + reduce_scratch(dense, near.dtype)
        + reduce_scratch(rows.shape, rows.dtype),
        compiler_params=pltpu.CompilerParams(
            collective_id=collective_id, has_side_effects=True, vmem_limit_bytes=52 * 2**20
        ),
        cost_estimate=lasting(62),
    )(near, far, rows, *terms, *givens)


def fifth_kernel(rows_ref, dense_ref, out_ref, own_ref, came, send_z, recv_z, *refs):
    buffers, sems = refs[:4], refs[4:6]
    count = lax.axis_size(TP)
    place = lax.axis_index(TP)
    enter(neighbours(False, True))
    plane = PlaneReduce(64, rows_ref, out_ref, buffers, sems)

    def to_owner(step):
        owner = lax.rem(place + step, count)
        return remote(
            dense_ref.at[owner], came.at[step - 1], send_z.at[step], recv_z.at[step], {TP: owner}
        )

    plane.start()
    for step in range(1, count):
        to_owner(step).start()
    plane.move()
    plane.end()
    for step in range(1, count):
        to_owner(step).wait()

    @pl.loop(0, own_ref.shape[0] // 32)
    def _(step):
        at = pl.ds(pl.multiple_of(step * 32, 32), 32)
        total = dense_ref[place, at, :].astype(f32)
        for other in range(count - 1):
            total = total + came[other, at, :].astype(f32)
        own_ref[at, :] = total.astype(own_ref.dtype)

    plane.finish()


def fifth_exchange(rows, dense, collective_id):
    count = lax.axis_size(TP)
    resident = pl.BlockSpec(memory_space=pltpu.VMEM)
    dma = pltpu.SemaphoreType.DMA
    return pl.pallas_call(
        fifth_kernel,
        out_shape=[
            jax.ShapeDtypeStruct(rows.shape[1:], f32),
            jax.ShapeDtypeStruct(dense.shape[1:], dense.dtype),
        ],
        in_specs=[resident] * 2,
        out_specs=[resident] * 2,
        scratch_shapes=[
            pltpu.VMEM((count - 1,) + dense.shape[1:], dense.dtype),
            dma((count,)),
            dma((count,)),
        ]
        + reduce_scratch(rows.shape, rows.dtype),
        compiler_params=pltpu.CompilerParams(
            collective_id=collective_id, has_side_effects=True, vmem_limit_bytes=48 * 2**20
        ),
        cost_estimate=lasting(30),
    )(rows, dense)


def sixth_kernel(
    parts,
    terms_ref,
    own_ref,
    rows_ref,
    out_ref,
    dense_ref,
    all_ref,
    sums,
    given,
    came,
    send_far,
    recv_far,
    send_z,
    recv_z,
    send_plane,
    recv_plane,
    send_on,
    send_back,
    recv_back,
    keep_sem,
    send_row,
    recv_row,
    send_next,
    recv_next,
    send_dense,
    recv_dense,
    column_came,
    plane_came,
    send_all,
    recv_all,
):
    chip, core, beside, above, facing = plane_ids()
    count = lax.axis_size(TP)
    place = lax.axis_index(TP)
    other = {SEQ: 2 * chip + 1 - core}
    ways = ({SEQ: 2 * beside + core}, {SEQ: 2 * above + core})
    rows = sums.shape[0]
    part_rows = rows // parts
    always = place >= 0
    holds = place == chip
    far_column = [
        (always, {SEQ: 2 * chip + 1 - core, TP: lax.rem(place + step, count)})
        for step in range(1, count)
    ]
    enter(neighbours(True, True) + far_column)
    half = own_ref.shape[0] // 2
    dense = PlaneSpread(
        lambda part: own_ref.at[pl.ds(part * half, half)],
        lambda where, part: dense_ref.at[where, core, pl.ds(part * half, half)],
        (send_row, recv_row, send_next, recv_next),
    )
    keep = pltpu.make_async_copy(own_ref, dense_ref.at[chip, core], keep_sem)

    def dense_across(where):
        block = dense_ref.at[(chip, beside, above, facing)[where], core]
        return remote(block, block, send_dense.at[where], recv_dense.at[where], other)

    mine = core * count + place

    def column_copy(index):
        peer = lax.rem(mine + index, 2 * count)
        return remote(
            rows_ref,
            column_came.at[mine],
            send_all.at[index],
            recv_all.at[index],
            {SEQ: 2 * chip + peer // count, TP: lax.rem(peer, count)},
        )

    def column_landed(index):
        sender = lax.rem(mine + 2 * count - index, 2 * count)
        block = column_came.at[sender]
        return remote(block, block, send_all.at[index], recv_all.at[index], other)

    def plane_copy(index):
        return remote(
            plane_came.at[chip],
            plane_came.at[chip],
            send_all.at[2 * count + index],
            recv_all.at[2 * count + index],
            {SEQ: 2 * (beside, above, facing)[index] + core},
        )

    dense.start()
    keep.start()
    column_came[mine] = rows_ref[...]
    for index in range(1, 2 * count):
        column_copy(index).start()

    def cut(part):
        return pl.ds(part * part_rows, part_rows)

    def own_cut(part):
        return pl.ds(pl.multiple_of(core * rows + part * part_rows, 16), part_rows)

    across = remote(
        terms_ref.at[pl.ds(pl.multiple_of((1 - core) * rows, 16), rows)], given, send_far, recv_far, other
    )
    across.start()

    def along(way, part):
        return remote(
            sums.at[cut(part)],
            came.at[way, cut(part)],
            send_z.at[way, part],
            recv_z.at[way, part],
            {TP: place - 1 if way == 0 else place + 1},
        )

    def add(source, part):
        total = sums[cut(part), :].astype(f32) + source[cut(part), :].astype(f32)
        sums[cut(part), :] = total.astype(sums.dtype)

    def to_plane(way, part):
        return remote(
            out_ref.at[own_cut(part)],
            out_ref.at[own_cut(part)],
            send_plane.at[way, part],
            recv_plane.at[part],
            ways[way],
        )

    def onward(part):
        return remote(
            out_ref.at[own_cut(part)],
            out_ref.at[own_cut(part)],
            send_on.at[part],
            recv_plane.at[part],
            ways[1 - part // (parts // 2)],
        )

    def back(part):
        return remote(
            out_ref.at[own_cut(part)],
            out_ref.at[own_cut(part)],
            send_back.at[part],
            recv_back.at[part],
            other,
        )

    across.wait_recv()
    keep.wait()
    dense_across(0).start()
    for part in range(parts):
        sums[cut(part), :] = terms_ref[own_cut(part), :]
        add(given, part)
        for way in range(2):
            passes = place > chip if way == 0 else place < chip
            takes = place < count - 1 if way == 0 else place > 0

            @pl.when(passes)
            def _():
                @pl.when(takes)
                def _():
                    along(way, part).wait_recv()
                    add(came.at[way], part)

                along(way, part).start()

    dense.forward()
    for part in range(parts):
        for way in range(2):
            takes = place < count - 1 if way == 0 else place > 0

            @pl.when(holds & takes)
            def _():
                along(way, part).wait_recv()
                add(came.at[way], part)

        @pl.when(holds)
        def _():
            out_ref[own_cut(part), :] = sums[cut(part), :]
            for way in range(2):
                to_plane(way, part).start()
            back(part).start()

    for index in range(1, 2 * count):
        column_landed(index).wait_recv()
    total = column_came[0]
    for index in range(1, 2 * count):
        total = total + column_came[index]
    plane_came[chip] = total
    for index in range(3):
        plane_copy(index).start()
    dense.arrive()
    for where in range(1, 4):
        dense_across(where).start()
    for part in range(parts):

        @pl.when(place != chip)
        def _():
            to_plane(0, part).wait_recv()

        @pl.when((beside if part < parts // 2 else above) == place)
        def _():
            onward(part).start()

        @pl.when(place != chip)
        def _():
            back(part).start()

    for index in range(1, 2 * count):
        column_copy(index).wait_send()
    for index in range(3):
        plane_copy(index).wait()
    total = plane_came[0]
    for index in range(1, plane_came.shape[0]):
        total = total + plane_came[index]
    all_ref[...] = total
    across.wait_send()
    dense.finish()
    for where in range(4):
        dense_across(where).wait()
    for part in range(parts):
        back(part).wait()

        @pl.when((beside if part < parts // 2 else above) == place)
        def _():
            onward(part).wait_send()

        for way in range(2):

            @pl.when(holds)
            def _():
                to_plane(way, part).wait_send()

            @pl.when(place > chip if way == 0 else place < chip)
            def _():
                along(way, part).wait_send()


def sixth_exchange(terms, own, small, collective_id):
    parts = 4
    chips = lax.axis_size(SEQ) // 2
    column = 2 * lax.axis_size(TP)
    rows = terms.shape[0] // 2
    half = (rows,) + terms.shape[1:]
    dma = pltpu.SemaphoreType.DMA
    resident = pl.BlockSpec(memory_space=pltpu.VMEM)
    return pl.pallas_call(
        functools.partial(sixth_kernel, parts),
        out_shape=[
            jax.ShapeDtypeStruct(terms.shape, terms.dtype),
            jax.ShapeDtypeStruct((chips, 2) + own.shape, own.dtype),
            jax.ShapeDtypeStruct(small.shape, small.dtype),
        ],
        in_specs=[resident] * 3,
        out_specs=[resident] * 3,
        scratch_shapes=[
            pltpu.VMEM(half, terms.dtype),
            pltpu.VMEM(half, terms.dtype),
            pltpu.VMEM((2,) + half, terms.dtype),
            dma,
            dma,
            dma((2, parts)),
            dma((2, parts)),
            dma((2, parts)),
            dma((parts,)),
            dma((parts,)),
            dma((parts,)),
            dma((parts,)),
            dma,
        ]
        + plane_sems()
        + [
            dma((4,)),
            dma((4,)),
            pltpu.VMEM((column,) + small.shape, small.dtype),
            pltpu.VMEM((chips,) + small.shape, small.dtype),
            dma((column + 3,)),
            dma((column + 3,)),
        ],
        compiler_params=pltpu.CompilerParams(
            collective_id=collective_id, has_side_effects=True, vmem_limit_bytes=32 * 2**20
        ),
        cost_estimate=lasting(35),
    )(terms, own, small)


def plane_applies(mesh, blocks, docs):
    seq_count, tp_count = mesh.shape[SEQ], mesh.shape[TP]
    groups = seq_count * tp_count
    return (
        tp_count == 4
        and seq_count == 2 * tp_count
        and blocks == groups * SHORT_BLK
        and 2 * tp_count * SHORT_BLK == LONG_BLK
        and blocks - SHORT_BLK * docs == 2 * (LONG_BLK - SHORT_BLK)
    )


class Micro:
    pass


def plane_body(
    tokens,
    doc_lengths,
    rand_blocks,
    query_weight,
    key_weight,
    value_weight,
    query_bias,
    value_bias,
    proj_weight,
    proj_bias,
    first_gain,
    first_bias,
    second_gain,
    second_bias,
    inner_weight,
    inner_bias,
    outer_weight,
    outer_bias,
    out_grad,
):
    micro_count, own_rows, model_width = tokens.shape
    seq_count = lax.axis_size(SEQ)
    tp_count = lax.axis_size(TP)
    chips = seq_count // 2
    seq_place = lax.axis_index(SEQ)
    tp_place = lax.axis_index(TP)
    chip = lax.shift_right_logical(seq_place, 1)
    core = seq_place & 1
    heads = rand_blocks.shape[2]
    rands = rand_blocks.shape[3]
    local_width = query_weight.shape[1]
    head_size = local_width // heads
    pair_width = heads * PAIR
    hidden_units = inner_weight.shape[1]
    classes = 2 * tp_count
    class_bits = classes.bit_length() - 1
    group_bits = SHORT_BLK.bit_length() - 1
    own_class = core * tp_count + tp_place
    long_docs = 2
    slots = 5 + rands
    group_rows = chips * own_rows
    score_scale = 1.0 / math.sqrt(head_size)

    def by_head(values):
        return values.reshape(values.shape[:-1] + (heads, -1))

    def side_by_side(first, second):
        paired = jnp.concatenate([by_head(first), by_head(second)], axis=-1)
        return paired.reshape(paired.shape[:-2] + (pair_width,))

    def low_half(wide):
        return by_head(wide)[..., :head_size].reshape(wide.shape[:-1] + (local_width,))

    def high_half(wide):
        return by_head(wide)[..., head_size:].reshape(wide.shape[:-1] + (local_width,))

    def slot_rows(values, slot):
        return values[slot * own_rows : (slot + 1) * own_rows]

    stage = [Micro() for _ in range(micro_count)]
    spare_rows = 128
    packed = jnp.concatenate([side_by_side(key_weight, value_weight), query_weight], axis=1)
    packed_bias = jnp.concatenate(
        [side_by_side(jnp.zeros_like(value_bias), value_bias), query_bias]
    )
    packed = jnp.concatenate([packed, packed_bias[None]], axis=0)
    packed = jnp.pad(packed, ((0, spare_rows - 1), (0, -packed.shape[1] % 128)))
    randoms = rand_blocks.reshape(-1)
    random_count = randoms.shape[0]
    randoms = jnp.pad(randoms, (0, -random_count % 1024)).reshape(-1, 128)
    for micro, held in enumerate(stage):
        held.inputs = tokens[micro].astype(f32)
        shifted, held.stats_one, held.inverse_one = layer_stats(
            held.inputs, first_gain, first_bias
        )
        held.low = shifted.astype(bf16)
    unit_cut = hidden_units // seq_count
    proj_cut = local_width // seq_count
    rest_rows = -(-(proj_cut + 1) // 16) * 16
    cuts = (0, rest_rows, rest_rows + unit_cut, rest_rows + 2 * unit_cut)

    def padded(row_values):
        return jnp.pad(row_values, [(0, 0)] * (row_values.ndim - 1) + [(0, model_width - unit_cut)])

    share = jnp.concatenate(
        [
            lax.dynamic_slice_in_dim(proj_weight, seq_place * proj_cut, proj_cut, axis=0),
            padded(lax.dynamic_slice_in_dim(inner_bias, seq_place * unit_cut, unit_cut)[None]),
            jnp.zeros((rest_rows - proj_cut - 1, model_width), bf16),
            lax.dynamic_slice_in_dim(inner_weight, seq_place * unit_cut, unit_cut, axis=1).T,
            lax.dynamic_slice_in_dim(outer_weight, seq_place * unit_cut, unit_cut, axis=0),
        ],
        axis=0,
    )
    one, packed, column, randoms = first_exchange(stage[0].low, packed, share, randoms, 1)
    stage[0].one = one.reshape(group_rows, model_width)
    pair_wide = packed[:model_width, :pair_width]
    pair_wide_bias = packed[model_width, :pair_width]
    query_part = packed[:model_width, pair_width : pair_width + local_width]
    query_part_bias = packed[model_width, pair_width : pair_width + local_width]
    joined_weight = jnp.concatenate([pair_wide, query_part * score_scale], axis=1)

    starts = jnp.cumsum(doc_lengths, axis=1) - doc_lengths
    is_long = doc_lengths == LONG_BLK
    long_firsts = jnp.min(jnp.where(is_long, starts, jnp.iinfo(jnp.int32).max), axis=1)
    long_lasts = jnp.max(jnp.where(is_long, starts, -1), axis=1)
    first_groups = lax.shift_right_logical(jnp.stack([long_firsts, long_lasts]), group_bits)
    own_groups = first_groups + ((own_class - first_groups) & (classes - 1))
    long_rows = lax.shift_right_logical(own_groups, class_bits) * own_rows
    randoms = randoms.reshape(chips, -1)[:, :random_count]
    randoms = randoms.reshape(chips, micro_count, tp_count, SHORT_BLK, heads, rands)
    randoms = lax.dynamic_index_in_dim(randoms, tp_place, axis=2, keepdims=False)
    randoms = jnp.pad(randoms.transpose(1, 3, 0, 2, 4), [(0, 0)] * 4 + [(slots - rands, 0)])
    randoms = randoms.reshape(micro_count, -1)
    shape = (heads, chips, SHORT_BLK, slots)
    slot, block, entry = (part.reshape(-1) for part in np.indices(shape, np.int32)[1:])
    for micro, held in enumerate(stage):
        group = slot * classes + own_class
        number = group * SHORT_BLK + block
        in_long = [
            (number >= start[micro]) & (number < start[micro] + LONG_BLK)
            for start in (long_firsts, long_lasts)
        ]
        window_first = jnp.where(
            in_long[0],
            long_firsts[micro],
            jnp.where(in_long[1], long_lasts[micro], group * SHORT_BLK),
        )
        any_long = in_long[0] | in_long[1]
        window_final = window_first + jnp.where(any_long, LONG_BLK, SHORT_BLK)
        key = randoms[micro]
        for place, value in enumerate(
            (
                jnp.maximum(number - 1, window_first),
                jnp.minimum(number + 1, window_final - 1),
                number,
                window_first,
                window_first + 1,
            )
        ):
            key = jnp.where(entry == place, value, key)
        inside = key & (SHORT_BLK - 1)
        key_class = lax.shift_right_logical(key, group_bits) & (classes - 1)
        own_core = lax.shift_right_logical(key_class, class_bits - 1) == core
        piece = (key_class & (tp_count - 1)) + jnp.where(own_core, 0, tp_count)
        long_place = piece * long_docs + jnp.where(in_long[1], 1, 0)
        short_place = classes * long_docs + slot
        held.index = jnp.where(any_long, long_place, short_place) * SHORT_BLK + inside
        counts = jnp.where(entry == 0, number > window_first, number + 1 < window_final)
        counts = counts.astype(jnp.int32)[: chips * SHORT_BLK * slots]
        held.valid = counts.reshape(-1, slots)[:, :2].reshape(-1)
        held.long_rows = [long_rows[doc, micro] for doc in range(long_docs)]

    def long_blocks(micro):
        held = stage[micro]
        pair_rows = (contract(held.one, pair_wide, NN) + pair_wide_bias).astype(bf16)
        longs = jnp.concatenate(
            [
                lax.dynamic_slice_in_dim(pair_rows, start, own_rows, axis=0)
                for start in held.long_rows
            ],
            axis=0,
        )
        return pair_rows, longs

    def keep_pieces(micro, near, far, pair_rows):
        stage[micro].pieces = [
            near.reshape(-1, pair_width), far.reshape(-1, pair_width), pair_rows
        ]

    def attend(micro):
        held = stage[micro]
        one = held.one
        if micro:
            one = after(one, stage[micro - 1].grad_context_sent)
        held.queries = (
            (contract(one, query_part, NN) + query_part_bias) * score_scale
        ).astype(bf16)
        held.context_sent, held.logsum = attend_forward(
            held.index, held.valid, held.queries, held.pieces, heads, slots
        )
        if micro:
            held.context = plane_exchange(held.context_sent, 0, 1)

    def feed_forward(micro):
        held = stage[micro]
        if micro:
            held.context = after(
                held.context, stage[micro - 1].grad_query, stage[micro - 1].long_sum_sent
            )
        hidden = held.inputs + contract(held.context, proj_full, NN) + proj_bias
        shifted, stats, inverse = layer_stats(hidden, second_gain, second_bias)
        held.two = shifted.astype(bf16)
        before = contract(held.two, inner_full, NT) + inner_bias_full
        held.active = gelu_exact(before).astype(bf16)
        result = hidden + contract(held.active, outer_full, NN) + outer_bias
        held.output = result.astype(bf16)
        held.grad_out = out_grad[micro]
        grad_float = held.grad_out.astype(f32)
        grad_active = contract(held.grad_out, outer_full, NT)
        held.grad_before = gelu_grad(before, grad_active).astype(bf16)
        grad_two = contract(held.grad_before, inner_full, NN)
        back, gain_sum, shift_sum = layer_back(grad_two, stats, inverse, second_gain)
        held.grad_hidden = grad_float + back
        held.branch = held.grad_hidden.astype(bf16)
        held.grad_context_sent = jnp.stack(
            [
                contract(
                    held.branch, proj_full[part * local_width : (part + 1) * local_width], NT
                ).astype(bf16)
                for part in range(chips)
            ]
        )
        held.grad_context = plane_exchange(held.grad_context_sent, 0, 0).reshape(
            group_rows, local_width
        )
        held.unit_sum = jnp.sum(held.grad_before.astype(f32), axis=0)
        held.row_sums = jnp.stack(
            [
                gain_sum,
                shift_sum,
                jnp.sum(held.branch.astype(f32), axis=0),
                jnp.sum(grad_float, axis=0),
            ]
        )

    def attend_back(micro, *earlier):
        held = stage[micro]
        held.grad_query, near, far, held.grad_pair = attend_backward(
            held.index,
            held.valid,
            held.queries,
            after(held.grad_context, *earlier),
            held.logsum,
            held.pieces,
            heads,
            slots,
        )
        return near, far

    def input_rows(micro, long_sum):
        held = stage[micro]
        for doc, start in enumerate(held.long_rows):
            held.grad_pair = lax.dynamic_update_slice_in_dim(
                held.grad_pair, slot_rows(long_sum, doc), start, axis=0
            )
        held.grad_joined = jnp.concatenate([held.grad_pair, held.grad_query], axis=1)
        rows = contract(held.grad_joined, joined_weight, NT)
        return rows.astype(bf16).reshape(chips, own_rows, model_width)

    def input_back(micro, grad_one):
        held = stage[micro]
        back, gain_sum, shift_sum = layer_back(
            grad_one, held.stats_one, held.inverse_one, first_gain
        )
        held.input_grad = held.grad_hidden + back
        held.first_sums = jnp.stack([gain_sum, shift_sum])

    pair_rows, longs = long_blocks(0)
    near, far, one = second_exchange(longs, stage[1].low, 2)
    stage[1].one = one.reshape(group_rows, model_width)
    keep_pieces(0, near, far, pair_rows)
    attend(0)
    pair_rows, longs = long_blocks(1)
    near, far, context, rest, inner_full, outer_full = third_exchange(
        longs,
        column,
        stage[0].context_sent.reshape(chips, own_rows, local_width),
        cuts,
        7,
    )
    keep_pieces(1, near, far, pair_rows)
    stage[0].context = context.transpose(1, 0, 2).reshape(own_rows, model_width)
    inner_full = inner_full.reshape(-1, model_width)
    outer_full = outer_full.reshape(-1, model_width)
    inner_bias_full = rest[:, :, :, proj_cut, :unit_cut].reshape(-1)
    proj_full = rest[:, :, :, :proj_cut].transpose(2, 1, 0, 3, 4)
    proj_full = proj_full.reshape(tp_count * local_width, model_width)
    feed_forward(0)
    attend(1)
    near, far = attend_back(0, stage[1].logsum, stage[1].context_sent)
    stage[0].long_sum_sent = sum_parts([near, core_swap(far)]).astype(bf16)
    long_sum = lax.psum_scatter(stage[0].long_sum_sent, TP, scatter_dimension=0, tiled=True)
    feed_forward(1)

    two, grad_before, active, grad_out, context, branch = (
        jnp.concatenate(group, axis=0)
        for group in zip(
            *((h.two, h.grad_before, h.active, h.grad_out, h.context, h.branch) for h in stage)
        )
    )
    two, active, context = after((two, active, context), stage[1].grad_context_sent)
    proj_part = contract(context, branch, TN).astype(bf16)
    proj_part = proj_part.reshape(tp_count, chips, 2, proj_cut, model_width)
    unit_shape = (2, chips, tp_count)
    unit_sum = sum(h.unit_sum for h in stage).astype(bf16)
    rest_part = jnp.concatenate(
        [
            proj_part.transpose(2, 1, 0, 3, 4),
            padded(unit_sum.reshape(unit_shape + (1, unit_cut))),
            jnp.zeros(unit_shape + (rest_rows - proj_cut - 1, model_width), bf16),
        ],
        axis=3,
    )
    terms = [
        part.reshape(2, chips, tp_count, -1, model_width)
        for part in (
            contract(grad_before, two, TN).astype(bf16),
            contract(active, grad_out, TN).astype(bf16),
            rest_part,
        )
    ]
    givens = [
        core_swap(lax.dynamic_index_in_dim(part, 1 - core, axis=0, keepdims=False))
        for part in terms
    ]

    rows = input_rows(0, after(long_sum, stage[1].grad_context_sent))
    near, far = attend_back(1, rows)

    column_shape = (tp_count, long_docs * own_rows, pair_width)
    cuts = (0, unit_cut, 2 * unit_cut, 2 * unit_cut + rest_rows)
    row_shape = (chips, 2, own_rows // 2, model_width)
    long_sum, quarters, grad_one = fourth_exchange(
        near.reshape(column_shape),
        far.reshape(column_shape),
        rows.reshape(row_shape),
        terms,
        givens,
        cuts,
        3,
    )
    rows = input_rows(1, long_sum)
    grad_one_now, own_sum = fifth_exchange(rows.reshape(row_shape), quarters, 4)
    input_back(0, after(grad_one, rows).reshape(own_rows, model_width))
    input_back(1, grad_one_now.reshape(own_rows, model_width))

    ones = after([h.one for h in stage], grad_one_now)
    packed_sum = sum(contract(one, h.grad_joined, TN) for one, h in zip(ones, stage))
    packed_sum = jnp.pad(packed_sum, ((0, 0), (0, -packed_sum.shape[1] % 128))).astype(bf16)

    def own_columns(values):
        wide = jnp.zeros((chips, local_width), f32)
        return lax.dynamic_update_slice_in_dim(wide, values[None], chip, axis=0).reshape(-1)

    query_bias_sum = sum(jnp.sum(h.grad_query.astype(f32), axis=0) for h in stage)
    pair_bias_sum = sum(jnp.sum(h.grad_pair.astype(f32), axis=0) for h in stage)
    packed_sum, dense_sum, all_rows = sixth_exchange(
        packed_sum,
        own_sum,
        jnp.concatenate(
            [
                sum(h.row_sums for h in stage),
                sum(h.first_sums for h in stage),
                own_columns(query_bias_sum * score_scale)[None],
                own_columns(high_half(pair_bias_sum))[None],
            ],
            axis=0,
        ),
        6,
    )
    key_grad = low_half(packed_sum[:, :pair_width]).astype(f32)
    value_grad = high_half(packed_sum[:, :pair_width]).astype(f32)
    query_grad = packed_sum[:, pair_width : pair_width + local_width].astype(f32) * score_scale
    dense_sum = dense_sum.reshape(seq_count, -1, model_width).astype(f32)
    inner_weight_grad = dense_sum[:, :unit_cut].reshape(hidden_units, model_width).T
    outer_weight_grad = dense_sum[:, unit_cut : 2 * unit_cut].reshape(hidden_units, model_width)
    rest = dense_sum[:, 2 * unit_cut :]
    proj_weight_grad = rest[:, :proj_cut].reshape(local_width, model_width)
    inner_bias_grad = rest[:, proj_cut, :unit_cut].reshape(hidden_units)

    def my_columns(row):
        return lax.dynamic_slice_in_dim(row, tp_place * local_width, local_width)

    return (
        jnp.stack([h.output for h in stage]),
        jnp.stack([h.input_grad for h in stage]),
        query_grad,
        key_grad,
        value_grad,
        my_columns(all_rows[6]),
        my_columns(all_rows[7]),
        proj_weight_grad,
        all_rows[2],
        all_rows[4],
        all_rows[5],
        all_rows[0],
        all_rows[1],
        inner_weight_grad,
        inner_bias_grad,
        outer_weight_grad,
        all_rows[3],
    )


def general_body(
    tokens,
    doc_lengths,
    rand_blocks,
    query_weight,
    key_weight,
    value_weight,
    query_bias,
    value_bias,
    proj_weight,
    proj_bias,
    first_gain,
    first_bias,
    second_gain,
    second_bias,
    inner_weight,
    inner_bias,
    outer_weight,
    outer_bias,
    out_grad,
):
    micro_count, local_rows, model_width = tokens.shape
    seq_count = lax.axis_size(SEQ)
    tp_count = lax.axis_size(TP)
    seq_place = lax.axis_index(SEQ)
    tp_place = lax.axis_index(TP)
    block_dev = rand_blocks.shape[1]
    heads = rand_blocks.shape[2]
    local_width = query_weight.shape[1]
    head_size = local_width // heads
    hidden_units = inner_weight.shape[1]
    group_rows = block_dev * BLOCK
    reach_dev = (block_dev + LONG_BLK - 2) // block_dev
    window = 2 * reach_dev + 1
    score_scale = 1.0 / math.sqrt(head_size)
    lowest = (seq_place - reach_dev) * block_dev
    blocks = seq_place * block_dev + jnp.arange(block_dev, dtype=jnp.int32)

    held = jnp.concatenate([inner_weight.T, outer_weight, proj_weight, inner_bias[None]], axis=0)
    used_rows = held.shape[0]
    piece_rows = -(-used_rows // (16 * seq_count)) * 16
    held_rows = piece_rows * seq_count
    held = jnp.pad(held, ((0, held_rows - used_rows), (0, 0)))
    share = lax.dynamic_slice_in_dim(held, seq_place * piece_rows, piece_rows, axis=0)
    spread = lax.all_gather(share, (TP, SEQ), axis=0, tiled=True)
    spread = spread.reshape(tp_count, held_rows, model_width)
    cuts = [0, hidden_units, 2 * hidden_units, 2 * hidden_units + local_width, used_rows]
    inner_full = spread[:, cuts[0] : cuts[1]].reshape(-1, model_width)
    outer_full = spread[:, cuts[1] : cuts[2]].reshape(-1, model_width)
    proj_full = spread[:, cuts[2] : cuts[3]].reshape(-1, model_width)
    inner_bias_full = spread[:, cuts[3] : cuts[4]].reshape(-1)

    def by_head(weight):
        return weight.reshape(weight.shape[:-1] + (heads, head_size))

    def side_by_side(first, second):
        paired = jnp.concatenate([by_head(first), by_head(second)], axis=-1)
        return paired.reshape(paired.shape[:-2] + (heads * PAIR,))

    pair_wide = side_by_side(key_weight, value_weight)
    pair_wide_bias = side_by_side(jnp.zeros_like(value_bias), value_bias)

    stage = [Micro() for _ in range(micro_count)]
    for micro, held in enumerate(stage):
        inputs = tokens[micro].astype(f32)
        shifted, stats, inverse = layer_stats(inputs, first_gain, first_bias)
        held.inputs, held.stats_one, held.inverse_one = inputs, stats, inverse
        held.one = lax.all_gather(shifted.astype(bf16), TP, axis=0, tiled=True)

    for micro, held in enumerate(stage):
        one = held.one
        pair_rows = (contract(one, pair_wide, NN) + pair_wide_bias).astype(bf16)
        pieces = [
            pair_rows if offset == 0 else from_behind(pair_rows, SEQ, -offset)
            for offset in range(-reach_dev, reach_dev + 1)
        ]
        queries = ((contract(one, query_weight, NN) + query_bias) * score_scale).astype(bf16)
        key_index, key_valid = block_keys(doc_lengths[micro], rand_blocks[micro], blocks)
        slots = key_index.shape[2]
        slot_index = jnp.clip(key_index - lowest, 0, window * block_dev - 1)
        held.index = slot_index.transpose(1, 0, 2).reshape(-1)
        held.valid = key_valid.reshape(-1)
        held.queries, held.pieces = queries, pieces

    for held in stage:
        context, held.logsum = attend_forward(
            held.index,
            held.valid,
            held.queries,
            held.pieces,
            heads,
            slots,
        )
        held.context = lax.all_to_all(context, TP, split_axis=0, concat_axis=1, tiled=True)

    outputs = []
    for micro, held in enumerate(stage):
        context = held.context
        hidden = held.inputs + contract(context, proj_full, NN) + proj_bias
        shifted, stats, inverse = layer_stats(hidden, second_gain, second_bias)
        two = shifted.astype(bf16)
        before = contract(two, inner_full, NT) + inner_bias_full
        active = gelu_exact(before).astype(bf16)
        result = hidden + contract(active, outer_full, NN) + outer_bias
        outputs.append(result.astype(bf16))
        grad_out = out_grad[micro]
        grad_float = grad_out.astype(f32)
        grad_active = contract(grad_out, outer_full, NT)
        grad_before = gelu_grad(before, grad_active).astype(bf16)
        grad_two = contract(grad_before, inner_full, NN)
        back, gain_sum, shift_sum = layer_back(grad_two, stats, inverse, second_gain)
        grad_hidden = grad_float + back
        branch = grad_hidden.astype(bf16)
        grad_context = contract(branch, proj_full, NT).astype(bf16)
        held.grad_context = lax.all_to_all(
            grad_context, TP, split_axis=1, concat_axis=0, tiled=True
        )
        held.grad_hidden = grad_hidden
        held.dense = (two, grad_before, active, grad_out, context, branch)
        held.row_sums = (
            jnp.sum(grad_before.astype(f32), axis=0),
            gain_sum,
            shift_sum,
            jnp.sum(branch.astype(f32), axis=0),
            jnp.sum(grad_float, axis=0),
        )

    two, grad_before, active, grad_out, context, branch = (
        jnp.concatenate(group, axis=0) for group in zip(*(h.dense for h in stage))
    )
    inner_part = contract(grad_before, two, TN).astype(bf16)
    outer_part = contract(active, grad_out, TN).astype(bf16)
    proj_part = contract(context, branch, TN).astype(bf16)
    grad_rows = 2 * hidden_units + local_width
    grad_piece = -(-grad_rows // (16 * seq_count)) * 16
    grad_held = grad_piece * seq_count
    parts = jnp.concatenate(
        [
            inner_part.reshape(tp_count, hidden_units, model_width),
            outer_part.reshape(tp_count, hidden_units, model_width),
            proj_part.reshape(tp_count, local_width, model_width),
            jnp.zeros((tp_count, grad_held - grad_rows, model_width), bf16),
        ],
        axis=1,
    ).reshape(tp_count * grad_held, model_width)
    own_part = lax.psum_scatter(parts, (TP, SEQ), scatter_dimension=0, tiled=True)
    dense_sum = lax.all_gather(own_part, SEQ, axis=0, tiled=True).astype(f32)
    inner_weight_grad = dense_sum[cuts[0] : cuts[1]].T
    outer_weight_grad = dense_sum[cuts[1] : cuts[2]]
    proj_weight_grad = dense_sum[cuts[2] : cuts[3]]

    for held in stage:
        held.grad_query, *grad_pieces = attend_backward(
            held.index,
            held.valid,
            held.queries,
            held.grad_context,
            held.logsum,
            held.pieces,
            heads,
            slots,
        )
        returned = grad_pieces[reach_dev].astype(f32)
        for offset in range(-reach_dev, reach_dev + 1):
            if offset != 0:
                returned = returned + from_behind(
                    grad_pieces[offset + reach_dev], SEQ, offset
                ).astype(f32)
        held.grad_pair = returned.astype(bf16)

    input_grads = []
    query_sum = pair_sum = 0.0
    query_bias_sum = pair_bias_sum = 0.0
    first_gain_sum = first_bias_sum = 0.0
    for held in stage:
        grad_query, grad_pair, one = held.grad_query, held.grad_pair, held.one
        rows = contract(grad_query, query_weight * score_scale, NT) + contract(grad_pair, pair_wide, NT)
        grad_one = lax.psum_scatter(
            rows.astype(bf16), TP, scatter_dimension=0, tiled=True
        ).astype(f32)
        query_sum = query_sum + contract(one, grad_query, TN)
        pair_sum = pair_sum + contract(one, grad_pair, TN)
        query_bias_sum = query_bias_sum + jnp.sum(grad_query.astype(f32), axis=0)
        pair_bias_sum = pair_bias_sum + jnp.sum(grad_pair.astype(f32), axis=0)
        back, gain_sum, shift_sum = layer_back(
            grad_one, held.stats_one, held.inverse_one, first_gain
        )
        first_gain_sum = first_gain_sum + gain_sum
        first_bias_sum = first_bias_sum + shift_sum
        input_grads.append(held.grad_hidden + back)

    def low_half(wide):
        return wide.reshape(wide.shape[:-1] + (heads, PAIR))[..., :head_size].reshape(
            wide.shape[:-1] + (local_width,)
        )

    def high_half(wide):
        return wide.reshape(wide.shape[:-1] + (heads, PAIR))[..., head_size:].reshape(
            wide.shape[:-1] + (local_width,)
        )

    query_grad, key_grad, value_grad = lax.psum(
        (query_sum * score_scale, low_half(pair_sum), high_half(pair_sum)), SEQ
    )
    inner_bias_sum, second_gain_sum, second_bias_sum, proj_bias_sum, outer_bias_sum = (
        sum(group) for group in zip(*(h.row_sums for h in stage))
    )

    def own_columns(values):
        wide = jnp.zeros((tp_count, local_width), f32)
        return lax.dynamic_update_slice_in_dim(wide, values[None], tp_place, axis=0).reshape(-1)

    early = lax.psum(
        jnp.concatenate(
            [
                inner_bias_sum,
                second_gain_sum,
                second_bias_sum,
                proj_bias_sum,
                outer_bias_sum,
            ]
        ),
        (SEQ, TP),
    )
    late = lax.psum(
        jnp.concatenate(
            [
                first_gain_sum,
                first_bias_sum,
                own_columns(query_bias_sum * score_scale),
                own_columns(high_half(pair_bias_sum)),
            ]
        ),
        (SEQ, TP),
    )
    inner_bias_all = early[: tp_count * hidden_units].reshape(tp_count, hidden_units)
    early_rows = early[tp_count * hidden_units :].reshape(-1, model_width)
    late_rows = late.reshape(-1, model_width)

    def my_columns(row):
        return lax.dynamic_slice_in_dim(row, tp_place * local_width, local_width)

    return (
        jnp.stack(outputs),
        jnp.stack(input_grads),
        query_grad,
        key_grad,
        value_grad,
        my_columns(late_rows[2]),
        my_columns(late_rows[3]),
        proj_weight_grad,
        early_rows[2],
        late_rows[0],
        late_rows[1],
        early_rows[0],
        early_rows[1],
        inner_weight_grad,
        lax.dynamic_index_in_dim(inner_bias_all, tp_place, axis=0, keepdims=False),
        outer_weight_grad,
        early_rows[3],
    )


def solution(mesh):
    def choose(tokens, doc_lengths, rand_blocks, *rest):
        blocks = rand_blocks.shape[1] * mesh.shape[SEQ]
        if plane_applies(mesh, blocks, doc_lengths.shape[1]):
            return plane_body(tokens, doc_lengths, rand_blocks, *rest)
        return general_body(tokens, doc_lengths, rand_blocks, *rest)

    return jax.shard_map(
        choose,
        mesh=mesh,
        in_specs=(
            P(None, (SEQ, TP), None),
            P(),
            P(None, SEQ, TP, None),
            P(None, TP),
            P(None, TP),
            P(None, TP),
            P(TP),
            P(TP),
            P(TP, None),
            P(),
            P(),
            P(),
            P(),
            P(),
            P(None, TP),
            P(TP),
            P(TP, None),
            P(),
            P(None, (SEQ, TP), None),
        ),
        out_specs=(
            P(None, (SEQ, TP), None),
            P(None, (SEQ, TP), None),
            P(None, TP),
            P(None, TP),
            P(None, TP),
            P(TP),
            P(TP),
            P(TP, None),
            P(),
            P(),
            P(),
            P(),
            P(),
            P(None, TP),
            P(TP),
            P(TP, None),
            P(),
        ),
        check_vma=False,
    )
```

```python
import functools
import math

import jax
import jax.numpy as jnp
import numpy as np
from jax import lax
from jax.experimental import pallas as pl
from jax.experimental.pallas import tpu as pltpu
from jax.sharding import PartitionSpec as P

BLOCK = 64
LONG_BLK = 64
SHORT_BLK = 8
PAIR = 2 * BLOCK
UNROLL = 4
SEQ = "seq"
TP = "tp"

NORM_EPS = 1e-05
MASKED = -1000000000.0

f32 = jnp.float32
bf16 = jnp.bfloat16

NN = (((1,), (0,)), ((), ()))
NT = (((1,), (1,)), ((), ()))
TN = (((0,), (0,)), ((), ()))


def contract(left, right, dims):
    return lax.dot_general(left, right, dims, preferred_element_type=f32)


def from_behind(block, axis, distance):
    devices = range(lax.axis_size(axis))
    route = [(i - distance, i) for i in devices if i - distance in devices]
    return lax.ppermute(block, axis, route)


def gelu_exact(values):
    return 0.5 * values * (1.0 + lax.erf(values / math.sqrt(2.0)))


def gelu_grad(values, grad_rows):
    _, pull_back = jax.vjp(gelu_exact, values)
    return pull_back(grad_rows)[0]


def layer_stats(values, norm_gain, norm_shift):
    row_mean = jnp.mean(values, axis=-1, keepdims=True)
    centred = values - row_mean
    inverse = lax.rsqrt(jnp.mean(centred * centred, axis=-1, keepdims=True) + NORM_EPS)
    normed = centred * inverse
    return (normed * norm_gain + norm_shift, normed, inverse)


def layer_back(grad_rows, normed, inverse, norm_gain):
    scaled = grad_rows * norm_gain
    inner_term = (
        scaled
        - jnp.mean(scaled, axis=-1, keepdims=True)
        - normed * jnp.mean(scaled * normed, axis=-1, keepdims=True)
    )
    return (inverse * inner_term, jnp.sum(grad_rows * normed, axis=0), jnp.sum(grad_rows, axis=0))


def block_keys(lengths, randoms, blocks):
    doc_ends = jnp.cumsum(lengths)
    doc_starts = doc_ends - lengths
    doc_owner = jnp.sum((blocks[:, None] >= doc_ends[None, :]).astype(jnp.int32), axis=1)
    doc_ids = jnp.arange(lengths.shape[0], dtype=jnp.int32)
    doc_hit = doc_owner[:, None] == doc_ids[None, :]
    doc_first = jnp.sum(jnp.where(doc_hit, doc_starts[None, :], 0), axis=1)
    doc_final = jnp.sum(jnp.where(doc_hit, doc_ends[None, :], 0), axis=1)
    fixed_keys = jnp.stack(
        [
            jnp.maximum(blocks - 1, doc_first),
            jnp.minimum(blocks + 1, doc_final - 1),
            blocks,
            doc_first,
            doc_first + 1,
        ],
        axis=1,
    )
    block_count = randoms.shape[0]
    head_count = randoms.shape[1]
    key_index = jnp.concatenate(
        [jnp.broadcast_to(fixed_keys[:, None, :], (block_count, head_count, 5)), randoms], axis=2
    )
    key_valid = jnp.stack([blocks > doc_first, blocks + 1 < doc_final], axis=1)
    return (key_index, key_valid.astype(jnp.int32))


def block_rows(block):
    return pl.ds(pl.multiple_of(block * BLOCK, BLOCK), BLOCK)


def listed_blocks(index_ref, store, base, slots):
    return jnp.concatenate(
        [store[block_rows(index_ref[base + slot]), :] for slot in range(slots)], axis=0
    )


def mask_scores(scores, valid_ref, block):
    lane = lax.broadcasted_iota(jnp.int32, (1, PAIR), 1)
    keep = jnp.where(lane < BLOCK, valid_ref[2 * block], valid_ref[2 * block + 1]) > 0
    return jnp.concatenate([jnp.where(keep, scores[:, :PAIR], MASKED), scores[:, PAIR:]], axis=1)


def fill_store(store, pieces):
    place = 0
    for piece in pieces:
        store[place : place + piece.shape[0], :] = piece[...]
        place += piece.shape[0]


def each_head(heads, work):
    for head in range(heads):

        @pl.when(pl.program_id(0) == head)
        def _():
            work(head)


def head_columns(head, first=0):
    return slice(first + head * BLOCK, first + (head + 1) * BLOCK)


def forward_kernel(slots, heads, index_ref, valid_ref, query_ref, *refs):
    *pieces, context_ref, logsum_ref, store, wide_query, wide_context = refs
    rows = query_ref.shape[0]
    blocks = rows // BLOCK
    head = pl.program_id(0)
    fill_store(store, pieces)

    def take_query(own):
        query = query_ref[:, head_columns(own, heads * PAIR)]
        wide_query[...] = jnp.concatenate([query, jnp.zeros_like(query)], axis=1)

    each_head(heads, take_query)

    def step(group, carry):
        ids = [group * UNROLL + unit for unit in range(UNROLL)]
        listed = [
            listed_blocks(index_ref, store, (head * blocks + block) * slots, slots)
            for block in ids
        ]
        scores = [
            mask_scores(contract(wide_query[block_rows(block), :], pairs, NT), valid_ref, block)
            for block, pairs in zip(ids, listed)
        ]
        probs = []
        for block, score in zip(ids, scores):
            top = jnp.max(score, axis=1, keepdims=True)
            raised = jnp.exp(score - top)
            total = jnp.sum(raised, axis=1, keepdims=True)
            probs.append((raised * (1.0 / total)).astype(bf16))
            logsum_ref[block_rows(block), :] = jnp.broadcast_to(
                top + jnp.log(total), (BLOCK, PAIR)
            )
        for block, prob, pairs in zip(ids, probs, listed):
            wide_context[block_rows(block), :] = contract(prob, pairs, NN).astype(bf16)
        return carry

    lax.fori_loop(0, blocks // UNROLL, step, 0)

    def give_context(own):
        context_ref[:, head_columns(own)] = wide_context[:, BLOCK:]

    each_head(heads, give_context)


def backward_kernel(slots, heads, count, index_ref, valid_ref, query_ref, grad_ref, logsum_ref, *refs):
    pieces, refs = refs[:count], refs[count:]
    grad_pieces, joined_ref = refs[: count - 1], refs[count - 1]
    store, sums, both_rows, wide_grad = refs[count:]
    rows = query_ref.shape[0]
    blocks = rows // BLOCK
    head = pl.program_id(0)
    fill_store(store, pieces)
    sums[...] = jnp.zeros_like(sums)
    lane = lax.broadcasted_iota(jnp.int32, (BLOCK, PAIR), 1)

    def take_both(own):
        query = query_ref[:, head_columns(own, heads * PAIR)]
        both_rows[...] = jnp.concatenate([query, grad_ref[:, head_columns(own)]], axis=1)

    each_head(heads, take_both)

    def step(group, carry):
        ids = [group * UNROLL + unit for unit in range(UNROLL)]
        listed = [
            listed_blocks(index_ref, store, (head * blocks + block) * slots, slots)
            for block in ids
        ]
        lefts = []
        for block in ids:
            both = both_rows[block_rows(block), :]
            lefts.append(
                jnp.concatenate(
                    [
                        jnp.where(lane < BLOCK, both, 0).astype(bf16),
                        jnp.where(lane < BLOCK, 0, both).astype(bf16),
                    ],
                    axis=0,
                )
            )
        products = [contract(left, pairs, NT) for left, pairs in zip(lefts, listed)]
        mixes = []
        for block, product in zip(ids, products):
            score = mask_scores(product[:BLOCK], valid_ref, block)
            grad_prob = product[BLOCK:]
            logsum = jnp.concatenate([logsum_ref[block_rows(block), :]] * (slots // 2), axis=1)
            prob = jnp.exp(score - logsum)
            delta = jnp.sum(prob * grad_prob, axis=1, keepdims=True)
            grad_score = prob * (grad_prob - delta)
            mixes.append(jnp.concatenate([grad_score.astype(bf16), prob.astype(bf16)], axis=0))
        for block, mix, pairs in zip(ids, mixes, listed):
            wide_grad[block_rows(block), :] = contract(mix[:BLOCK], pairs, NN).astype(bf16)
        terms = [contract(mix, left, TN) for mix, left in zip(mixes, lefts)]
        for block, term in zip(ids, terms):
            base = (head * blocks + block) * slots
            for slot in range(slots):
                sums[block_rows(index_ref[base + slot]), :] += term[
                    slot * BLOCK : (slot + 1) * BLOCK
                ]
        return carry

    lax.fori_loop(0, blocks // UNROLL, step, 0)
    place = 0
    for grad_piece in grad_pieces:
        grad_piece[...] = sums[place : place + grad_piece.shape[0], :].astype(bf16)
        place += grad_piece.shape[0]

    def give_joined(own):
        joined_ref[:, own * PAIR : (own + 1) * PAIR] = sums[place:, :].astype(bf16)
        start = heads * PAIR + own * BLOCK
        joined_ref[:, start : start + BLOCK] = wide_grad[:, :BLOCK]

    each_head(heads, give_joined)


def lasting(microseconds):
    return pl.CostEstimate(
        flops=0, bytes_accessed=int(microseconds * 3.69e6), transcendentals=0
    )


def per_head(array):
    return pl.BlockSpec((array.shape[0], PAIR), lambda head, *_: (0, head))


def whole(array):
    return pl.BlockSpec(array.shape, lambda head, *_: (0, 0))


def attend_forward(index, valid, joined, pieces, heads, slots):
    rows = joined.shape[0]
    pieces = pieces + [joined]
    context = jax.ShapeDtypeStruct((rows, heads * BLOCK), bf16)
    stored = sum(piece.shape[0] for piece in pieces)
    logsum = jax.ShapeDtypeStruct((rows, heads * PAIR), f32)
    return pl.pallas_call(
        functools.partial(forward_kernel, slots, heads),
        grid_spec=pltpu.PrefetchScalarGridSpec(
            num_scalar_prefetch=2,
            grid=(heads,),
            in_specs=[whole(joined)] + [per_head(piece) for piece in pieces],
            out_specs=[whole(context), per_head(logsum)],
            scratch_shapes=[
                pltpu.VMEM((stored, PAIR), bf16),
                pltpu.VMEM((rows, PAIR), bf16),
                pltpu.VMEM((rows, PAIR), bf16),
            ],
        ),
        out_shape=[context, logsum],
        compiler_params=pltpu.CompilerParams(vmem_limit_bytes=40 * 2**20),
        cost_estimate=lasting(18),
    )(index, valid, joined, *pieces)


def attend_backward(index, valid, joined, grads, logsum, pieces, heads, slots):
    rows = joined.shape[0]
    pieces = pieces + [joined]
    stored = sum(piece.shape[0] for piece in pieces)
    piece_specs = [per_head(piece) for piece in pieces]
    return pl.pallas_call(
        functools.partial(backward_kernel, slots, heads, len(pieces)),
        grid_spec=pltpu.PrefetchScalarGridSpec(
            num_scalar_prefetch=2,
            grid=(heads,),
            in_specs=[whole(joined), whole(grads), per_head(logsum)] + piece_specs,
            out_specs=piece_specs[:-1] + [whole(joined)],
            scratch_shapes=[
                pltpu.VMEM((stored, PAIR), bf16),
                pltpu.VMEM((stored, PAIR), f32),
                pltpu.VMEM((rows, PAIR), bf16),
                pltpu.VMEM((rows, PAIR), bf16),
            ],
        ),
        out_shape=[jax.ShapeDtypeStruct(piece.shape, bf16) for piece in pieces],
        compiler_params=pltpu.CompilerParams(vmem_limit_bytes=50 * 2**20),
        cost_estimate=lasting(25),
    )(index, valid, joined, grads, logsum, *pieces)


def dense_kernel(core_ref, *refs):
    ins, (given_inner, given_outer, kept_inner, kept_outer, proj) = refs[:12], refs[12:]
    step = pl.program_id(0)
    half = pl.num_programs(0) // 2

    def term(first):
        total = contract(ins[first][...], ins[first + 2][...], TN)
        return (total + contract(ins[first + 1][...], ins[first + 3][...], TN)).astype(bf16)

    @pl.when(step < half)
    def _():
        given_inner[...] = term(0)
        given_outer[...] = term(4)

    @pl.when(step >= half)
    def _():
        kept_inner[...] = term(0)
        kept_outer[...] = term(4)

    @pl.when(step == 0)
    def _():
        proj[...] = term(8)


def dense_terms(core, units, rows):
    steps = 8
    hidden = units[0][0].shape[1]
    tile = hidden // steps
    width = rows[0][0].shape[1]

    def unit_tile(step, core_ref):
        owner = jnp.where(step < steps // 2, 1 - core_ref[0], core_ref[0])
        return (0, owner * (steps // 2) + step % (steps // 2))

    def whole_rows(array):
        return pl.BlockSpec(array.shape, lambda step, *_: (0, 0))

    ins, specs = [], []
    for place in range(3):
        for array in units[place]:
            ins.append(array)
            if place < 2:
                specs.append(pl.BlockSpec((array.shape[0], tile), unit_tile))
            else:
                specs.append(whole_rows(array))
        for array in rows[place]:
            ins.append(array)
            specs.append(whole_rows(array))
    half = jax.ShapeDtypeStruct((hidden // 2, width), bf16)
    proj = jax.ShapeDtypeStruct((units[2][0].shape[1], width), bf16)
    given = pl.BlockSpec((tile, width), lambda step, *_: (jnp.minimum(step, steps // 2 - 1), 0))
    kept = pl.BlockSpec((tile, width), lambda step, *_: (jnp.maximum(step - steps // 2, 0), 0))
    return pl.pallas_call(
        dense_kernel,
        grid_spec=pltpu.PrefetchScalarGridSpec(
            num_scalar_prefetch=1,
            grid=(steps,),
            in_specs=specs,
            out_specs=[given, given, kept, kept, whole_rows(proj)],
        ),
        out_shape=[half] * 4 + [proj],
        compiler_params=pltpu.CompilerParams(vmem_limit_bytes=40 * 2**20),
        cost_estimate=lasting(15),
    )(core.reshape(1), *ins)


def plane_exchange(values, split_axis, concat_axis):
    count = lax.axis_size(SEQ)
    groups = [list(range(place, count, 2)) for place in range(2)]
    return lax.all_to_all(
        values,
        SEQ,
        split_axis=split_axis,
        concat_axis=concat_axis,
        axis_index_groups=groups,
        tiled=True,
    )


def plane_gather(values):
    count = lax.axis_size(SEQ) // 2
    return plane_exchange(jnp.concatenate([values] * count, axis=0), 0, 0)


def core_swap(block):
    route = [(place, place ^ 1) for place in range(lax.axis_size(SEQ))]
    return lax.ppermute(block, SEQ, route)


def column_shift(block, step):
    count = lax.axis_size(TP)
    return lax.ppermute(block, TP, [(place, (place + step) % count) for place in range(count)])


def column_gather(values):
    count = lax.axis_size(TP)
    place = lax.axis_index(TP)
    spread = jnp.zeros((count,) + values.shape, values.dtype)
    spread = lax.dynamic_update_index_in_dim(spread, values, place, axis=0)
    for step in range(1, count):
        spread = lax.dynamic_update_index_in_dim(
            spread, column_shift(values, step), (place - step) % count, axis=0
        )
    return spread


def after(values, *earlier):
    return lax.optimization_barrier((values, earlier))[0]


def sum_parts(parts):
    total = parts[0].astype(f32)
    for place in range(1, len(parts)):
        total = total + parts[place].astype(f32)
    return total


def partner_of(place):
    return place + 1 - 2 * (place % 2)


def enter(neighbours):
    barrier = pltpu.get_barrier_semaphore()
    count = 0
    for exists, device in neighbours:

        @pl.when(exists)
        def _():
            pl.semaphore_signal(
                barrier, inc=1, device_id=device, device_id_type=pl.DeviceIdType.MESH
            )

        count = count + jnp.where(exists, 1, 0)
    pl.semaphore_wait(barrier, count)


def remote(source, target, send, receive, device):
    return pltpu.make_async_remote_copy(
        src_ref=source,
        dst_ref=target,
        send_sem=send,
        recv_sem=receive,
        device_id=device,
        device_id_type=pl.DeviceIdType.MESH,
    )


def plane_ids():
    seq_place = lax.axis_index(SEQ)
    chip, core = seq_place // 2, seq_place % 2
    beside = chip + 1 - 2 * (chip % 2)
    above = chip + 2 - 4 * (chip // 2)
    facing = 3 - chip
    return chip, core, beside, above, facing


def column_way(place, way, distance):
    return place - distance if way == 0 else place + distance


class ColumnSpread:

    def __init__(self, parts, own, near, far, other, keep_sem, along_sems, across_sems):
        self.parts, self.own, self.near, self.far = parts, own, near, far
        self.other, self.keep_sem = other, keep_sem
        self.along_sems, self.across_sems = along_sems, across_sems
        self.count = lax.axis_size(TP)
        self.place = lax.axis_index(TP)
        self.rows = own.shape[0] // parts

    def cut(self, part):
        return pl.ds(part * self.rows, self.rows)

    def block(self, way, distance, part):
        if distance == 0:
            return self.own.at[self.cut(part)]
        return self.near.at[column_way(self.place, way, distance), self.cut(part)]

    def along(self, way, distance, part):
        return remote(
            self.block(way, distance, part),
            self.near.at[column_way(self.place, way, distance), self.cut(part)],
            self.along_sems[0].at[way, distance, part],
            self.along_sems[1].at[way, distance, part],
            {TP: self.place + 1 if way == 0 else self.place - 1},
        )

    def landed(self, way, distance, part):
        block = self.near.at[column_way(self.place, way, distance), self.cut(part)]
        return remote(
            block,
            block,
            self.along_sems[0].at[way, distance, part],
            self.along_sems[1].at[way, distance - 1, part],
            self.other,
        )

    def across(self, way, distance, part):
        return remote(
            self.block(way, distance, part),
            self.far.at[column_way(self.place, way, distance), self.cut(part)],
            self.across_sems[0].at[way, distance, part],
            self.across_sems[1].at[way, distance, part],
            self.other,
        )

    def keep(self):
        return pltpu.make_async_copy(self.own, self.near.at[self.place], self.keep_sem)

    def goes_on(self, way):
        return self.place < self.count - 1 if way == 0 else self.place > 0

    def has_come(self, way, distance):
        if way == 0:
            return self.place >= distance
        return self.place + distance < self.count

    def start(self):
        for part in range(self.parts):
            for way in range(2):

                @pl.when(self.goes_on(way))
                def _():
                    self.along(way, 0, part).start()

        if self.far is not None:
            for part in range(self.parts):
                self.across(0, 0, part).start()
        self.keep().start()

    def step(self, distance, part):
        for way in range(2):

            @pl.when(self.has_come(way, distance))
            def _():
                self.landed(way, distance, part).wait_recv()
                if distance < self.count - 1:

                    @pl.when(self.goes_on(way))
                    def _():
                        self.along(way, distance, part).start()

                if self.far is not None:
                    self.across(way, distance, part).start()

    def finish(self):
        self.keep().wait()
        for part in range(self.parts):
            if self.far is not None:
                self.across(0, 0, part).wait()
            for way in range(2):

                @pl.when(self.goes_on(way))
                def _():
                    self.along(way, 0, part).wait_send()

        for distance in range(1, self.count):
            for part in range(self.parts):
                for way in range(2):

                    @pl.when(self.has_come(way, distance))
                    def _():
                        if distance < self.count - 1:

                            @pl.when(self.goes_on(way))
                            def _():
                                self.along(way, distance, part).wait_send()

                        if self.far is not None:
                            self.across(way, distance, part).wait()


class PlaneSpread:

    def __init__(self, own, out, sems):
        self.own, self.out = own, out
        self.send_row, self.recv_row, self.send_on, self.recv_on = sems
        self.chip, core, beside, above, self.facing = plane_ids()
        self.ways = ({SEQ: 2 * beside + core}, {SEQ: 2 * above + core})
        self.chips = (beside, above)

    def first(self, way, part):
        return remote(
            self.own(part),
            self.out(self.chip, part),
            self.send_row.at[way, part],
            self.recv_row.at[way, part],
            self.ways[way],
        )

    def second(self, way):
        return remote(
            self.out(self.chips[way], way),
            self.out(self.chips[way], way),
            self.send_on.at[way],
            self.recv_on.at[way],
            self.ways[1 - way],
        )

    def start(self):
        self.first(0, 0).start()
        self.first(1, 1).start()

    def forward(self):
        for way in range(2):
            self.first(way, way).wait_recv()
            self.second(way).start()
        for way in range(2):
            self.first(way, 1 - way).start()

    def arrive(self):
        for way in range(2):
            self.first(way, 1 - way).wait_recv()
        for way in range(2):
            self.second(way).wait_recv()

    def finish(self):
        for way in range(2):
            self.second(way).wait_send()
            for part in range(2):
                self.first(way, part).wait_send()


def plane_sems():
    dma = pltpu.SemaphoreType.DMA
    return [dma((2, 2)), dma((2, 2)), dma((2,)), dma((2,))]


def column_sems(parts):
    sems = pltpu.SemaphoreType.DMA((2, 4, parts))
    return [sems, sems, sems, sems]


def halves_of(own, out, keep_sem):
    half = own.shape[0] // 2
    chip = plane_ids()[0]
    return (
        lambda part: own.at[pl.ds(part * half, half)],
        lambda place, part: out.at[place, pl.ds(part * half, half)],
        pltpu.make_async_copy(own, out.at[chip], keep_sem),
    )


def neighbours(facing_too, column_too):
    chip, core, beside, above, facing = plane_ids()
    count = lax.axis_size(TP)
    place = lax.axis_index(TP)
    always = place >= 0
    devices = [(always, {SEQ: 2 * chip + 1 - core})]
    devices += [(always, {SEQ: 2 * beside + core}), (always, {SEQ: 2 * above + core})]
    if facing_too:
        devices.append((always, {SEQ: 2 * facing + core}))
    if column_too:
        for step in range(1, count):
            devices.append((always, {TP: lax.rem(place + step, count)}))
    else:
        devices.append((place < count - 1, {TP: place + 1}))
        devices.append((place > 0, {TP: place - 1}))
    return devices


def first_kernel(
    parts,
    own_ref,
    weight_ref,
    share_ref,
    random_ref,
    out_ref,
    spread_ref,
    column_ref,
    random_out_ref,
    randoms,
    own_sem,
    send_row,
    recv_row,
    send_on,
    recv_on,
    send_z,
    recv_z,
    send_far,
    recv_far,
    send_random,
    recv_random,
    send_column,
    recv_column,
    send_share,
    recv_share,
):
    chip, core, beside, above, facing = plane_ids()
    tp_count = lax.axis_size(TP)
    place = lax.axis_index(TP)
    other = {SEQ: 2 * chip + 1 - core}
    weight_rows = weight_ref.shape[0] // (2 * parts)
    column = [{TP: lax.rem(place + step, tp_count)} for step in range(1, tp_count)]
    enter(neighbours(True, True))
    own, out, keep_rows = halves_of(own_ref, out_ref, own_sem.at[0])
    rows = PlaneSpread(own, out, (send_row, recv_row, send_on, recv_on))
    shares = ColumnSpread(
        2, share_ref, column_ref, None, other, own_sem.at[2], (send_share, recv_share), None
    )

    def weight_cut(part, holder):
        return pl.ds((holder * parts + part) * weight_rows, weight_rows)

    def weight_along(source, way, part):
        at = weight_cut(part, core)
        return remote(
            source.at[at],
            spread_ref.at[at],
            send_z.at[way, part],
            recv_z.at[part],
            {TP: place + 1 if way == 0 else place - 1},
        )

    def weight_across(part):
        at = weight_cut(part, core)
        return remote(
            spread_ref.at[at], spread_ref.at[at], send_far.at[part], recv_far.at[part], other
        )

    def goes_on(way):
        if way == 0:
            return (place >= chip) & (place < tp_count - 1)
        return (place <= chip) & (place > 0)

    def random_to_holder(sender):
        return remote(
            random_ref,
            randoms.at[sender],
            send_random,
            recv_random.at[sender],
            {SEQ: 2 * place + core},
        )

    def random_along(step):
        return remote(
            randoms,
            random_out_ref,
            send_column.at[step],
            recv_column,
            column[step],
        )

    rows.start()

    @pl.when(place != chip)
    def _():
        random_to_holder(chip).start()

    for part in range(parts):
        for way in range(2):

            @pl.when((place == chip) & goes_on(way))
            def _():
                weight_along(weight_ref, way, part).start()

    shares.start()
    keep_rows.start()

    @pl.when(place == chip)
    def _():
        keep = pltpu.make_async_copy(weight_ref, spread_ref, own_sem.at[1])
        keep.start()
        keep.wait()
        randoms[chip] = random_ref[...]
        for step in range(1, tp_count):
            random_to_holder(lax.rem(chip + step, tp_count)).wait_recv()
        random_out_ref[...] = randoms[...]
        for step in range(tp_count - 1):
            random_along(step).start()

    rows.forward()
    for part in range(parts):

        @pl.when(place != chip)
        def _():
            weight_along(spread_ref, 0, part).wait_recv()
            for way in range(2):

                @pl.when(goes_on(way))
                def _():
                    weight_along(spread_ref, way, part).start()

            weight_across(part).start()

    for distance in range(1, tp_count):
        for part in range(2):
            shares.step(distance, part)
    rows.arrive()
    rows.finish()
    shares.finish()
    keep_rows.wait()

    @pl.when(place != chip)
    def _():
        random_to_holder(chip).wait_send()
        random_along(0).wait_recv()

    @pl.when(place == chip)
    def _():
        for step in range(tp_count - 1):
            random_along(step).wait_send()

    for part in range(parts):

        @pl.when(place != chip)
        def _():
            weight_across(part).wait()

        for way in range(2):

            @pl.when(goes_on(way))
            def _():
                weight_along(spread_ref, way, part).wait_send()


def first_exchange(own, weight, share, randoms, collective_id, parts=4):
    chips = lax.axis_size(SEQ) // 2
    count = lax.axis_size(TP)
    resident = pl.BlockSpec(memory_space=pltpu.VMEM)
    dma = pltpu.SemaphoreType.DMA
    return pl.pallas_call(
        functools.partial(first_kernel, parts),
        out_shape=[
            jax.ShapeDtypeStruct((chips,) + own.shape, own.dtype),
            jax.ShapeDtypeStruct(weight.shape, weight.dtype),
            jax.ShapeDtypeStruct((count,) + share.shape, share.dtype),
            jax.ShapeDtypeStruct((chips,) + randoms.shape, randoms.dtype),
        ],
        in_specs=[resident] * 4,
        out_specs=[resident] * 4,
        scratch_shapes=[pltpu.VMEM((chips,) + randoms.shape, randoms.dtype), dma((3,))]
        + plane_sems()
        + [
            dma((2, parts)),
            dma((parts,)),
            dma((parts,)),
            dma((parts,)),
            dma,
            dma((chips,)),
            dma((chips - 1,)),
            dma,
        ]
        + column_sems(2)[:2],
        compiler_params=pltpu.CompilerParams(
            collective_id=collective_id, has_side_effects=True, vmem_limit_bytes=32 * 2**20
        ),
        cost_estimate=lasting(30),
    )(own, weight, share, randoms)


class WeightSpread:

    def __init__(self, column, rows, out, keep_sem, cross_sems, plane_sems):
        self.out, self.cross_sems = out, cross_sems
        self.chip, self.core, self.beside, self.above, self.facing = plane_ids()
        self.other = {SEQ: 2 * self.chip + 1 - self.core}
        self.half = column.shape[0] // 2
        self.plane = PlaneSpread(
            lambda part: column.at[pl.ds(part * self.half, self.half), rows],
            lambda where, part: out.at[self.core, where, pl.ds(part * self.half, self.half)],
            plane_sems,
        )
        self.keep = pltpu.make_async_copy(
            column.at[:, rows], out.at[self.core, self.chip], keep_sem
        )

    def across(self, where, part):
        chip = (self.chip, self.beside, self.above, self.facing)[where]
        block = self.out.at[self.core, chip, pl.ds(part * self.half, self.half)]
        at = (where, part)
        return remote(
            block, block, self.cross_sems[0].at[at], self.cross_sems[1].at[at], self.other
        )

    def start(self):
        self.plane.start()
        self.keep.start()

    def forward(self):
        self.plane.forward()
        self.keep.wait()
        for where, part in ((0, 0), (0, 1), (1, 0), (2, 1)):
            self.across(where, part).start()

    def arrive(self):
        self.plane.arrive()
        for where, part in ((1, 1), (2, 0), (3, 0), (3, 1)):
            self.across(where, part).start()

    def finish(self):
        self.plane.finish()
        for where in range(4):
            for part in range(2):
                self.across(where, part).wait()


def weight_sems():
    dma = pltpu.SemaphoreType.DMA
    return [dma, dma((4, 2)), dma((4, 2))] + plane_sems()


def weight_shape(column, rows):
    tp_count, _, width = column.shape
    chips = lax.axis_size(SEQ) // 2
    return jax.ShapeDtypeStruct((2, chips, tp_count, rows[1] - rows[0], width), column.dtype)


def second_kernel(
    parts,
    rows,
    longs_ref,
    own_ref,
    column_ref,
    near_ref,
    far_ref,
    out_ref,
    weight_ref,
    keep_sem,
    *sems,
):
    chip, core = plane_ids()[:2]
    enter(neighbours(False, False))
    other = {SEQ: 2 * chip + 1 - core}
    longs = ColumnSpread(
        parts, longs_ref, near_ref, far_ref, other, keep_sem.at[0], sems[:2], sems[2:4]
    )
    own, out, keep_rows = halves_of(own_ref, out_ref, keep_sem.at[1])
    plane = PlaneSpread(own, out, sems[4:8])
    weight = WeightSpread(
        column_ref, pl.ds(rows[0], rows[1] - rows[0]), weight_ref, sems[8], sems[9:11], sems[11:15]
    )
    longs.start()
    plane.start()
    weight.start()
    keep_rows.start()
    for part in range(parts):
        longs.step(1, part)
    plane.forward()
    weight.forward()
    for part in range(parts):
        longs.step(2, part)
    plane.arrive()
    weight.arrive()
    for part in range(parts):
        longs.step(3, part)
    plane.finish()
    weight.finish()
    longs.finish()
    keep_rows.wait()


def second_exchange(longs, own, column, rows, collective_id, parts=2):
    chips = lax.axis_size(SEQ) // 2
    near = jax.ShapeDtypeStruct((lax.axis_size(TP),) + longs.shape, longs.dtype)
    resident = pl.BlockSpec(memory_space=pltpu.VMEM)
    return pl.pallas_call(
        functools.partial(second_kernel, parts, rows),
        out_shape=[
            near,
            near,
            jax.ShapeDtypeStruct((chips,) + own.shape, own.dtype),
            weight_shape(column, rows),
        ],
        in_specs=[resident] * 3,
        out_specs=[resident] * 4,
        scratch_shapes=[pltpu.SemaphoreType.DMA((2,))]
        + column_sems(parts)
        + plane_sems()
        + weight_sems(),
        compiler_params=pltpu.CompilerParams(
            collective_id=collective_id, has_side_effects=True, vmem_limit_bytes=48 * 2**20
        ),
        cost_estimate=lasting(58),
    )(longs, own, column)


def third_kernel(
    parts,
    cuts,
    longs_ref,
    column_ref,
    sent_ref,
    near_ref,
    far_ref,
    context_ref,
    *refs,
):
    count = len(cuts)
    outs, refs = refs[:count], refs[count:]
    keep_sem, block_sems, sems = refs[0], refs[1:3], refs[3:7]
    chip, core, beside, above, facing = plane_ids()
    enter(neighbours(True, False))
    other = {SEQ: 2 * chip + 1 - core}
    longs = ColumnSpread(
        parts, longs_ref, near_ref, far_ref, other, keep_sem.at[0], sems[:2], sems[2:4]
    )
    weights = []
    for index, (first, last) in enumerate(cuts):
        own = refs[7 + 7 * index : 14 + 7 * index]
        weights.append(
            WeightSpread(
                column_ref, pl.ds(first, last - first), outs[index], own[0], own[1:3], own[3:7]
            )
        )

    def send_block(index):
        target = (beside, above, facing)[index]
        return remote(
            sent_ref.at[target],
            context_ref.at[chip],
            block_sems[0].at[index],
            block_sems[1].at[index],
            {SEQ: 2 * target + core},
        )

    keep_block = pltpu.make_async_copy(sent_ref.at[chip], context_ref.at[chip], keep_sem.at[1])
    longs.start()
    for weight in weights:
        weight.start()
    for index in range(3):
        send_block(index).start()
    keep_block.start()
    for part in range(parts):
        longs.step(1, part)
    for weight in weights:
        weight.forward()
    for part in range(parts):
        longs.step(2, part)
    for weight in weights:
        weight.arrive()
    for part in range(parts):
        longs.step(3, part)
    longs.finish()
    for weight in weights:
        weight.finish()
    for index in range(3):
        send_block(index).wait()
    keep_block.wait()


def third_exchange(longs, column, sent, cuts, collective_id, parts=2):
    near = jax.ShapeDtypeStruct((column.shape[0],) + longs.shape, longs.dtype)
    resident = pl.BlockSpec(memory_space=pltpu.VMEM)
    dma = pltpu.SemaphoreType.DMA
    sems = [sem for _ in cuts for sem in weight_sems()]
    return pl.pallas_call(
        functools.partial(third_kernel, parts, cuts),
        out_shape=[near, near, jax.ShapeDtypeStruct(sent.shape, sent.dtype)]
        + [weight_shape(column, rows) for rows in cuts],
        in_specs=[resident] * 3,
        out_specs=[resident] * (3 + len(cuts)),
        scratch_shapes=[dma((2,)), dma((3,)), dma((3,))] + column_sems(parts) + sems,
        compiler_params=pltpu.CompilerParams(
            collective_id=collective_id, has_side_effects=True, vmem_limit_bytes=48 * 2**20
        ),
        cost_estimate=lasting(58),
    )(longs, column, sent)


class ColumnReduce:

    def __init__(self, parts, step_rows, sums, came, sems):
        self.parts, self.step_rows = parts, step_rows
        self.sums, self.came, self.sems = sums, came, sems
        self.count = lax.axis_size(TP)
        self.place = lax.axis_index(TP)
        self.rows = sums.shape[1] // parts
        self.order = []
        for step in range(self.count):
            for owner in (step, self.count - 1 - step):
                if owner not in self.order:
                    self.order.append(owner)

    def along(self, way, owner, part):
        at = pl.ds(part * self.rows, self.rows)
        return remote(
            self.sums.at[owner, at],
            self.came.at[way, owner, at],
            self.sems[0].at[way, owner, part],
            self.sems[1].at[way, owner, part],
            {TP: self.place - 1 if way == 0 else self.place + 1},
        )

    def add(self, owner, source, part):
        @pl.loop(0, self.rows // self.step_rows)
        def _(step):
            start = pl.multiple_of(part * self.rows + step * self.step_rows, self.step_rows)
            at = pl.ds(start, self.step_rows)
            total = self.sums[owner, at, :].astype(f32) + source[at, :].astype(f32)
            self.sums[owner, at, :] = total.astype(self.sums.dtype)

    def takes(self, way):
        return self.place < self.count - 1 if way == 0 else self.place > 0

    def passes(self, way, owner):
        return self.place > owner if way == 0 else self.place < owner

    def begin(self, owner, part):
        for way in range(2):

            @pl.when(self.passes(way, owner) & ~self.takes(way))
            def _():
                self.along(way, owner, part).start()

    def move(self, way, owner, part):
        @pl.when(self.passes(way, owner) & self.takes(way))
        def _():
            self.along(way, owner, part).wait_recv()
            self.add(owner, self.came.at[way, owner], part)
            self.along(way, owner, part).start()

    def end(self):
        for part in range(self.parts):
            for way in range(2):
                for owner in range(self.count):

                    @pl.when((self.place == owner) & self.takes(way))
                    def _():
                        self.along(way, owner, part).wait_recv()
                        self.add(owner, self.came.at[way, owner], part)

    def finish(self):
        for owner in range(self.count):
            for part in range(self.parts):
                for way in range(2):

                    @pl.when(self.passes(way, owner))
                    def _():
                        self.along(way, owner, part).wait_send()

    def give(self, out):
        for owner in range(self.count):

            @pl.when(self.place == owner)
            def _():
                out[...] = self.sums[owner]


class PlaneReduce:

    def __init__(self, step_rows, terms, out, buffers, sems):
        self.step_rows, self.terms, self.out = step_rows, terms, out
        self.came, self.facing_came, self.sent, self.last = buffers
        self.sems = sems
        self.chip, core, beside, above, self.facing = plane_ids()
        self.ways = ({SEQ: 2 * beside + core}, {SEQ: 2 * above + core})
        self.chips = (beside, above)
        self.half = terms.shape[1] // 2

    def copy(self, kind, way, source, target, device):
        return remote(
            source, target.at[way], self.sems[0].at[kind, way], self.sems[1].at[kind, way], device
        )

    def pieces(self, way):
        return pl.ds(way * self.half, self.half)

    def facing_term(self, way):
        source = self.terms.at[self.facing, self.pieces(way)]
        return self.copy(0, way, source, self.facing_came, self.ways[way])

    def near_term(self, way):
        source = self.terms.at[self.chips[way], self.pieces(way)]
        return self.copy(1, way, source, self.came, self.ways[way])

    def summed(self, way):
        return self.copy(2, way, self.sent.at[way], self.last, self.ways[1 - way])

    def each_step(self, work):
        steps = self.terms.shape[2] // self.step_rows

        @pl.loop(0, self.half * steps)
        def _(step):
            start = pl.multiple_of((step % steps) * self.step_rows, self.step_rows)
            work(step // steps, pl.ds(start, self.step_rows))

    def start(self):
        for way in range(2):
            self.facing_term(way).start()
        for way in range(2):
            self.near_term(way).start()

    def move(self):
        for way in range(2):
            self.facing_term(way).wait_recv()

            def add_term(piece, at):
                total = self.terms[self.chips[1 - way], way * self.half + piece, at, :].astype(f32)
                total = total + self.facing_came[way, piece, at, :].astype(f32)
                self.sent[way, piece, at, :] = total.astype(self.sent.dtype)

            self.each_step(add_term)
            self.summed(way).start()

    def end(self):
        for way in range(2):
            self.near_term(way).wait_recv()
            self.summed(way).wait_recv()

            def add_last(piece, at):
                total = self.terms[self.chip, way * self.half + piece, at, :].astype(f32)
                total = total + self.came[way, piece, at, :].astype(f32)
                total = total + self.last[way, piece, at, :].astype(f32)
                self.out[way * self.half + piece, at, :] = total.astype(self.out.dtype)

            self.each_step(add_last)

    def finish(self):
        for way in range(2):
            self.facing_term(way).wait_send()
            self.near_term(way).wait_send()
            self.summed(way).wait_send()


def reduce_scratch(shape, dtype):
    half = pltpu.VMEM((2, shape[1] // 2) + shape[2:], dtype)
    sems = pltpu.SemaphoreType.DMA((3, 2))
    return [half] * 4 + [sems, sems]


def fourth_kernel(parts, cuts, near_ref, far_ref, *refs):
    count = len(cuts) - 1
    terms, givens, refs = refs[:count], refs[count : 2 * count], refs[2 * count :]
    out_ref, dense_ref, sums, given, came, dense, more = refs[:7]
    load_sem, send_far, recv_far, send_z, recv_z = refs[7:12]
    buffers, sems = refs[12:16], refs[16:18]
    place = lax.axis_index(TP)
    chip, core = plane_ids()[:2]
    other = {SEQ: 2 * chip + 1 - core}
    loads = [pltpu.make_async_copy(near_ref, sums, load_sem.at[0])]
    for index in range(count):
        rows = pl.ds(cuts[index], cuts[index + 1] - cuts[index])
        loads.append(
            pltpu.make_async_copy(
                terms[index], dense.at[:, :, rows], load_sem.at[1 + 2 * index]
            )
        )
        loads.append(
            pltpu.make_async_copy(givens[index], more.at[:, :, rows], load_sem.at[2 + 2 * index])
        )
    for load in loads:
        load.start()
    enter(neighbours(False, False))
    step_rows = dense.shape[2] // 2
    column = ColumnReduce(parts, sums.shape[1] // parts // 2, sums, came, (send_z, recv_z))
    plane = PlaneReduce(step_rows, dense, dense_ref, buffers, sems)

    def across(owner):
        return remote(
            far_ref.at[owner], given.at[owner], send_far.at[owner], recv_far.at[owner], other
        )

    def move(steps):
        for part in range(parts):
            for way, owner in steps:
                column.move(way, owner, part)

    for owner in column.order:
        across(owner).start()
    for load in loads:
        load.wait()
    pieces, steps = dense.shape[1], dense.shape[2] // step_rows

    @pl.loop(0, dense.shape[0] * pieces * steps)
    def _(step):
        at = pl.ds(pl.multiple_of((step % steps) * step_rows, step_rows), step_rows)
        piece = (step // steps) % pieces
        where = step // (steps * pieces)
        total = dense[where, piece, at, :].astype(f32) + more[where, piece, at, :].astype(f32)
        dense[where, piece, at, :] = total.astype(dense.dtype)

    plane.start()
    for owner in column.order:
        across(owner).wait_recv()
        for part in range(parts):
            column.add(owner, given.at[owner], part)
            column.begin(owner, part)
    last = column.count - 1

    @pl.when(place == last - 1)
    def _():
        move([(0, 0)])

    @pl.when(place == 1)
    def _():
        move([(1, last)])

    plane.move()

    @pl.when(place == last - 1)
    def _():
        move([(0, 1), (1, last)])

    @pl.when(place == 1)
    def _():
        move([(1, last - 1), (0, 0)])

    column.end()
    column.give(out_ref)
    plane.end()
    column.finish()
    plane.finish()
    for owner in column.order:
        across(owner).wait_send()


def fourth_exchange(near, far, terms, givens, cuts, collective_id, parts=2):
    count = lax.axis_size(TP)
    block = near.shape[1:]
    chips = givens[0].shape[0]
    width = givens[0].shape[-1]
    dense = (chips, count, cuts[-1], width)
    resident = pl.BlockSpec(memory_space=pltpu.VMEM)
    anywhere = pl.BlockSpec(memory_space=pl.ANY)
    dma = pltpu.SemaphoreType.DMA
    pieces = len(cuts) - 1
    return pl.pallas_call(
        functools.partial(fourth_kernel, parts, cuts),
        out_shape=[
            jax.ShapeDtypeStruct(block, near.dtype),
            jax.ShapeDtypeStruct(dense[1:], near.dtype),
        ],
        in_specs=[anywhere, resident] + [anywhere] * (2 * pieces),
        out_specs=[resident] * 2,
        scratch_shapes=[
            pltpu.VMEM((count,) + block, near.dtype),
            pltpu.VMEM((count,) + block, near.dtype),
            pltpu.VMEM((2, count) + block, near.dtype),
            pltpu.VMEM(dense, near.dtype),
            pltpu.VMEM(dense, near.dtype),
            dma((1 + 2 * pieces,)),
            dma((count,)),
            dma((count,)),
            dma((2, count, parts)),
            dma((2, count, parts)),
        ]
        + reduce_scratch(dense, near.dtype),
        compiler_params=pltpu.CompilerParams(
            collective_id=collective_id, has_side_effects=True, vmem_limit_bytes=52 * 2**20
        ),
        cost_estimate=lasting(62),
    )(near, far, *terms, *givens)


def fifth_kernel(rows_ref, dense_ref, out_ref, own_ref, came, send_z, recv_z, *refs):
    buffers, sems = refs[:4], refs[4:6]
    count = lax.axis_size(TP)
    place = lax.axis_index(TP)
    enter(neighbours(False, True))
    plane = PlaneReduce(rows_ref.shape[2] // 2, rows_ref, out_ref, buffers, sems)

    def to_owner(step):
        owner = lax.rem(place + step, count)
        return remote(
            dense_ref.at[owner], came.at[step - 1], send_z.at[step], recv_z.at[step], {TP: owner}
        )

    plane.start()
    for step in range(1, count):
        to_owner(step).start()
    plane.move()
    plane.end()
    for step in range(1, count):
        to_owner(step).wait()

    step_rows = own_ref.shape[0] // 2

    @pl.loop(0, 2)
    def _(step):
        at = pl.ds(pl.multiple_of(step * step_rows, step_rows), step_rows)
        total = dense_ref[place, at, :].astype(f32)
        for other in range(count - 1):
            total = total + came[other, at, :].astype(f32)
        own_ref[at, :] = total.astype(own_ref.dtype)

    plane.finish()


def fifth_exchange(rows, dense, collective_id):
    count = lax.axis_size(TP)
    resident = pl.BlockSpec(memory_space=pltpu.VMEM)
    dma = pltpu.SemaphoreType.DMA
    return pl.pallas_call(
        fifth_kernel,
        out_shape=[
            jax.ShapeDtypeStruct(rows.shape[1:], f32),
            jax.ShapeDtypeStruct(dense.shape[1:], dense.dtype),
        ],
        in_specs=[resident] * 2,
        out_specs=[resident] * 2,
        scratch_shapes=[
            pltpu.VMEM((count - 1,) + dense.shape[1:], dense.dtype),
            dma((count,)),
            dma((count,)),
        ]
        + reduce_scratch(rows.shape, rows.dtype),
        compiler_params=pltpu.CompilerParams(
            collective_id=collective_id, has_side_effects=True, vmem_limit_bytes=48 * 2**20
        ),
        cost_estimate=lasting(30),
    )(rows, dense)


def sixth_kernel(
    parts,
    terms_ref,
    own_ref,
    rows_ref,
    out_ref,
    dense_ref,
    all_ref,
    sums,
    given,
    came,
    send_far,
    recv_far,
    send_z,
    recv_z,
    send_plane,
    recv_plane,
    send_on,
    send_back,
    recv_back,
    keep_sem,
    send_row,
    recv_row,
    send_next,
    recv_next,
    send_dense,
    recv_dense,
    column_came,
    plane_came,
    send_all,
    recv_all,
):
    chip, core, beside, above, facing = plane_ids()
    count = lax.axis_size(TP)
    place = lax.axis_index(TP)
    other = {SEQ: 2 * chip + 1 - core}
    ways = ({SEQ: 2 * beside + core}, {SEQ: 2 * above + core})
    rows = sums.shape[0]
    part_rows = rows // parts
    always = place >= 0
    holds = place == chip
    far_column = [
        (always, {SEQ: 2 * chip + 1 - core, TP: lax.rem(place + step, count)})
        for step in range(1, count)
    ]
    enter(neighbours(True, True) + far_column)
    half = own_ref.shape[0] // 2
    dense = PlaneSpread(
        lambda part: own_ref.at[pl.ds(part * half, half)],
        lambda where, part: dense_ref.at[where, core, pl.ds(part * half, half)],
        (send_row, recv_row, send_next, recv_next),
    )
    keep = pltpu.make_async_copy(own_ref, dense_ref.at[chip, core], keep_sem)

    def dense_across(where):
        block = dense_ref.at[(chip, beside, above, facing)[where], core]
        return remote(block, block, send_dense.at[where], recv_dense.at[where], other)

    mine = core * count + place

    def column_copy(index):
        peer = lax.rem(mine + index, 2 * count)
        return remote(
            rows_ref,
            column_came.at[mine],
            send_all.at[index],
            recv_all.at[index],
            {SEQ: 2 * chip + peer // count, TP: lax.rem(peer, count)},
        )

    def column_landed(index):
        sender = lax.rem(mine + 2 * count - index, 2 * count)
        block = column_came.at[sender]
        return remote(block, block, send_all.at[index], recv_all.at[index], other)

    def plane_copy(index):
        return remote(
            plane_came.at[chip],
            plane_came.at[chip],
            send_all.at[2 * count + index],
            recv_all.at[2 * count + index],
            {SEQ: 2 * (beside, above, facing)[index] + core},
        )

    dense.start()
    keep.start()
    column_came[mine] = rows_ref[...]
    for index in range(1, 2 * count):
        column_copy(index).start()

    def cut(part):
        return pl.ds(part * part_rows, part_rows)

    def own_cut(part):
        return pl.ds(pl.multiple_of(core * rows + part * part_rows, 16), part_rows)

    across = remote(
        terms_ref.at[pl.ds(pl.multiple_of((1 - core) * rows, 16), rows)], given, send_far, recv_far, other
    )
    across.start()

    def along(way, part):
        return remote(
            sums.at[cut(part)],
            came.at[way, cut(part)],
            send_z.at[way, part],
            recv_z.at[way, part],
            {TP: place - 1 if way == 0 else place + 1},
        )

    def add(source, part):
        total = sums[cut(part), :].astype(f32) + source[cut(part), :].astype(f32)
        sums[cut(part), :] = total.astype(sums.dtype)

    def to_plane(way, part):
        return remote(
            out_ref.at[own_cut(part)],
            out_ref.at[own_cut(part)],
            send_plane.at[way, part],
            recv_plane.at[part],
            ways[way],
        )

    def onward(part):
        return remote(
            out_ref.at[own_cut(part)],
            out_ref.at[own_cut(part)],
            send_on.at[part],
            recv_plane.at[part],
            ways[1 - part // (parts // 2)],
        )

    def back(part):
        return remote(
            out_ref.at[own_cut(part)],
            out_ref.at[own_cut(part)],
            send_back.at[part],
            recv_back.at[part],
            other,
        )

    across.wait_recv()
    keep.wait()
    dense_across(0).start()
    for part in range(parts):
        sums[cut(part), :] = terms_ref[own_cut(part), :]
        add(given, part)
        for way in range(2):
            passes = place > chip if way == 0 else place < chip
            takes = place < count - 1 if way == 0 else place > 0

            @pl.when(passes)
            def _():
                @pl.when(takes)
                def _():
                    along(way, part).wait_recv()
                    add(came.at[way], part)

                along(way, part).start()

    dense.forward()
    for part in range(parts):
        for way in range(2):
            takes = place < count - 1 if way == 0 else place > 0

            @pl.when(holds & takes)
            def _():
                along(way, part).wait_recv()
                add(came.at[way], part)

        @pl.when(holds)
        def _():
            out_ref[own_cut(part), :] = sums[cut(part), :]
            for way in range(2):
                to_plane(way, part).start()
            back(part).start()

    for index in range(1, 2 * count):
        column_landed(index).wait_recv()
    total = column_came[0]
    for index in range(1, 2 * count):
        total = total + column_came[index]
    plane_came[chip] = total
    for index in range(3):
        plane_copy(index).start()
    dense.arrive()
    for where in range(1, 4):
        dense_across(where).start()
    for part in range(parts):

        @pl.when(place != chip)
        def _():
            to_plane(0, part).wait_recv()

        @pl.when((beside if part < parts // 2 else above) == place)
        def _():
            onward(part).start()

        @pl.when(place != chip)
        def _():
            back(part).start()

    for index in range(1, 2 * count):
        column_copy(index).wait_send()
    for index in range(3):
        plane_copy(index).wait()
    total = plane_came[0]
    for index in range(1, plane_came.shape[0]):
        total = total + plane_came[index]
    all_ref[...] = total
    across.wait_send()
    dense.finish()
    for where in range(4):
        dense_across(where).wait()
    for part in range(parts):
        back(part).wait()

        @pl.when((beside if part < parts // 2 else above) == place)
        def _():
            onward(part).wait_send()

        for way in range(2):

            @pl.when(holds)
            def _():
                to_plane(way, part).wait_send()

            @pl.when(place > chip if way == 0 else place < chip)
            def _():
                along(way, part).wait_send()


def sixth_exchange(terms, own, small, collective_id):
    parts = 4
    chips = lax.axis_size(SEQ) // 2
    column = 2 * lax.axis_size(TP)
    rows = terms.shape[0] // 2
    half = (rows,) + terms.shape[1:]
    dma = pltpu.SemaphoreType.DMA
    resident = pl.BlockSpec(memory_space=pltpu.VMEM)
    return pl.pallas_call(
        functools.partial(sixth_kernel, parts),
        out_shape=[
            jax.ShapeDtypeStruct(terms.shape, terms.dtype),
            jax.ShapeDtypeStruct((chips, 2) + own.shape, own.dtype),
            jax.ShapeDtypeStruct(small.shape, small.dtype),
        ],
        in_specs=[resident] * 3,
        out_specs=[resident] * 3,
        scratch_shapes=[
            pltpu.VMEM(half, terms.dtype),
            pltpu.VMEM(half, terms.dtype),
            pltpu.VMEM((2,) + half, terms.dtype),
            dma,
            dma,
            dma((2, parts)),
            dma((2, parts)),
            dma((2, parts)),
            dma((parts,)),
            dma((parts,)),
            dma((parts,)),
            dma((parts,)),
            dma,
        ]
        + plane_sems()
        + [
            dma((4,)),
            dma((4,)),
            pltpu.VMEM((column,) + small.shape, small.dtype),
            pltpu.VMEM((chips,) + small.shape, small.dtype),
            dma((column + 3,)),
            dma((column + 3,)),
        ],
        compiler_params=pltpu.CompilerParams(
            collective_id=collective_id, has_side_effects=True, vmem_limit_bytes=32 * 2**20
        ),
        cost_estimate=lasting(35),
    )(terms, own, small)


def plane_applies(mesh, blocks, docs):
    seq_count, tp_count = mesh.shape[SEQ], mesh.shape[TP]
    groups = seq_count * tp_count
    return (
        tp_count == 4
        and seq_count == 2 * tp_count
        and blocks == groups * SHORT_BLK
        and 2 * tp_count * SHORT_BLK == LONG_BLK
        and blocks - SHORT_BLK * docs == 2 * (LONG_BLK - SHORT_BLK)
    )


class Micro:
    pass


def plane_body(
    tokens,
    doc_lengths,
    rand_blocks,
    query_weight,
    key_weight,
    value_weight,
    query_bias,
    value_bias,
    proj_weight,
    proj_bias,
    first_gain,
    first_bias,
    second_gain,
    second_bias,
    inner_weight,
    inner_bias,
    outer_weight,
    outer_bias,
    out_grad,
):
    micro_count, own_rows, model_width = tokens.shape
    seq_count = lax.axis_size(SEQ)
    tp_count = lax.axis_size(TP)
    chips = seq_count // 2
    seq_place = lax.axis_index(SEQ)
    tp_place = lax.axis_index(TP)
    chip = lax.shift_right_logical(seq_place, 1)
    core = seq_place & 1
    heads = rand_blocks.shape[2]
    rands = rand_blocks.shape[3]
    local_width = query_weight.shape[1]
    head_size = local_width // heads
    pair_width = heads * PAIR
    hidden_units = inner_weight.shape[1]
    classes = 2 * tp_count
    class_bits = classes.bit_length() - 1
    group_bits = SHORT_BLK.bit_length() - 1
    own_class = core * tp_count + tp_place
    long_docs = 2
    slots = 5 + rands
    group_rows = chips * own_rows
    score_scale = 1.0 / math.sqrt(head_size)

    def by_head(values):
        return values.reshape(values.shape[:-1] + (heads, -1))

    def side_by_side(first, second):
        paired = jnp.concatenate([by_head(first), by_head(second)], axis=-1)
        return paired.reshape(paired.shape[:-2] + (pair_width,))

    def low_half(wide):
        return by_head(wide)[..., :head_size].reshape(wide.shape[:-1] + (local_width,))

    def high_half(wide):
        return by_head(wide)[..., head_size:].reshape(wide.shape[:-1] + (local_width,))

    def slot_rows(values, slot):
        return values[slot * own_rows : (slot + 1) * own_rows]

    stage = [Micro() for _ in range(micro_count)]
    spare_rows = 128
    packed = jnp.concatenate([side_by_side(key_weight, value_weight), query_weight], axis=1)
    packed_bias = jnp.concatenate(
        [side_by_side(jnp.zeros_like(value_bias), value_bias), query_bias]
    )
    packed = jnp.concatenate([packed, packed_bias[None]], axis=0)
    packed = jnp.pad(packed, ((0, spare_rows - 1), (0, -packed.shape[1] % 128)))
    randoms = rand_blocks.reshape(-1)
    random_count = randoms.shape[0]
    randoms = jnp.pad(randoms, (0, -random_count % 1024)).reshape(-1, 128)
    for micro, held in enumerate(stage):
        held.inputs = tokens[micro].astype(f32)
        shifted, held.stats_one, held.inverse_one = layer_stats(
            held.inputs, first_gain, first_bias
        )
        held.low = shifted.astype(bf16)
    unit_cut = hidden_units // seq_count
    proj_cut = local_width // seq_count
    rest_rows = -(-(proj_cut + 1) // 16) * 16
    cuts = (0, rest_rows, rest_rows + unit_cut, rest_rows + 2 * unit_cut)

    def padded(row_values):
        return jnp.pad(row_values, [(0, 0)] * (row_values.ndim - 1) + [(0, model_width - unit_cut)])

    share = jnp.concatenate(
        [
            lax.dynamic_slice_in_dim(proj_weight, seq_place * proj_cut, proj_cut, axis=0),
            padded(lax.dynamic_slice_in_dim(inner_bias, seq_place * unit_cut, unit_cut)[None]),
            jnp.zeros((rest_rows - proj_cut - 1, model_width), bf16),
            lax.dynamic_slice_in_dim(inner_weight, seq_place * unit_cut, unit_cut, axis=1).T,
            lax.dynamic_slice_in_dim(outer_weight, seq_place * unit_cut, unit_cut, axis=0),
        ],
        axis=0,
    )
    one, packed, column, randoms = first_exchange(stage[0].low, packed, share, randoms, 1)
    stage[0].one = one.reshape(group_rows, model_width)
    pair_wide = packed[:model_width, :pair_width]
    pair_wide_bias = packed[model_width, :pair_width]
    query_part = packed[:model_width, pair_width : pair_width + local_width]
    query_part_bias = packed[model_width, pair_width : pair_width + local_width]
    joined_weight = jnp.concatenate([pair_wide, query_part * score_scale], axis=1)
    joined_bias = jnp.concatenate([pair_wide_bias, query_part_bias * score_scale])

    starts = jnp.cumsum(doc_lengths, axis=1) - doc_lengths
    is_long = doc_lengths == LONG_BLK
    long_firsts = jnp.min(jnp.where(is_long, starts, jnp.iinfo(jnp.int32).max), axis=1)
    long_lasts = jnp.max(jnp.where(is_long, starts, -1), axis=1)
    first_groups = lax.shift_right_logical(jnp.stack([long_firsts, long_lasts]), group_bits)
    own_groups = first_groups + ((own_class - first_groups) & (classes - 1))
    long_rows = lax.shift_right_logical(own_groups, class_bits) * own_rows
    randoms = randoms.reshape(chips, -1)[:, :random_count]
    randoms = randoms.reshape(chips, micro_count, tp_count, SHORT_BLK, heads, rands)
    randoms = lax.dynamic_index_in_dim(randoms, tp_place, axis=2, keepdims=False)
    randoms = jnp.pad(randoms.transpose(1, 3, 0, 2, 4), [(0, 0)] * 4 + [(slots - rands, 0)])
    randoms = randoms.reshape(micro_count, -1)
    shape = (heads, chips, SHORT_BLK, slots)
    slot, block, entry = (part.reshape(-1) for part in np.indices(shape, np.int32)[1:])
    for micro, held in enumerate(stage):
        group = slot * classes + own_class
        number = group * SHORT_BLK + block
        in_long = [
            (number >= start[micro]) & (number < start[micro] + LONG_BLK)
            for start in (long_firsts, long_lasts)
        ]
        window_first = jnp.where(
            in_long[0],
            long_firsts[micro],
            jnp.where(in_long[1], long_lasts[micro], group * SHORT_BLK),
        )
        any_long = in_long[0] | in_long[1]
        window_final = window_first + jnp.where(any_long, LONG_BLK, SHORT_BLK)
        key = randoms[micro]
        for place, value in enumerate(
            (
                jnp.maximum(number - 1, window_first),
                jnp.minimum(number + 1, window_final - 1),
                number,
                window_first,
                window_first + 1,
            )
        ):
            key = jnp.where(entry == place, value, key)
        inside = key & (SHORT_BLK - 1)
        key_class = lax.shift_right_logical(key, group_bits) & (classes - 1)
        own_core = lax.shift_right_logical(key_class, class_bits - 1) == core
        piece = (key_class & (tp_count - 1)) + jnp.where(own_core, 0, tp_count)
        long_place = piece * long_docs + jnp.where(in_long[1], 1, 0)
        short_place = classes * long_docs + slot
        held.index = jnp.where(any_long, long_place, short_place) * SHORT_BLK + inside
        counts = jnp.where(entry == 0, number > window_first, number + 1 < window_final)
        counts = counts.astype(jnp.int32)[: chips * SHORT_BLK * slots]
        held.valid = counts.reshape(-1, slots)[:, :2].reshape(-1)
        held.long_rows = [long_rows[doc, micro] for doc in range(long_docs)]

    def long_blocks(micro):
        held = stage[micro]
        held.joined = (contract(held.one, joined_weight, NN) + joined_bias).astype(bf16)
        longs = jnp.concatenate(
            [
                lax.dynamic_slice(held.joined, (start, 0), (own_rows, pair_width))
                for start in held.long_rows
            ],
            axis=0,
        )
        return longs

    def keep_pieces(micro, near, far):
        stage[micro].pieces = [near.reshape(-1, pair_width), far.reshape(-1, pair_width)]

    def attend(micro):
        held = stage[micro]
        index = held.index
        if micro:
            index = after(index, stage[micro - 1].grad_context_sent)
        held.context_sent, held.logsum = attend_forward(
            index, held.valid, held.joined, held.pieces, heads, slots
        )
        if micro:
            held.context = plane_exchange(held.context_sent, 0, 1)

    def feed_forward(micro):
        held = stage[micro]
        if micro:
            held.context = after(
                held.context, stage[micro - 1].long_sum_sent
            )
        hidden = held.inputs + contract(held.context, proj_full, NN) + proj_bias
        shifted, stats, inverse = layer_stats(hidden, second_gain, second_bias)
        held.two = shifted.astype(bf16)
        before = contract(held.two, inner_full, NT) + inner_bias_full
        held.active = gelu_exact(before).astype(bf16)
        result = hidden + contract(held.active, outer_full, NN) + outer_bias
        held.output = result.astype(bf16)
        held.grad_out = out_grad[micro]
        grad_float = held.grad_out.astype(f32)
        grad_active = contract(held.grad_out, outer_full, NT)
        held.grad_before = gelu_grad(before, grad_active).astype(bf16)
        grad_two = contract(held.grad_before, inner_full, NN)
        back, gain_sum, shift_sum = layer_back(grad_two, stats, inverse, second_gain)
        held.grad_hidden = grad_float + back
        held.branch = held.grad_hidden.astype(bf16)
        held.grad_context_sent = jnp.stack(
            [
                contract(
                    held.branch, proj_full[part * local_width : (part + 1) * local_width], NT
                ).astype(bf16)
                for part in range(chips)
            ]
        )
        held.grad_context = plane_exchange(held.grad_context_sent, 0, 0).reshape(
            group_rows, local_width
        )
        held.unit_sum = jnp.sum(held.grad_before.astype(f32), axis=0)
        held.row_sums = jnp.stack(
            [
                gain_sum,
                shift_sum,
                jnp.sum(held.branch.astype(f32), axis=0),
                jnp.sum(grad_float, axis=0),
            ]
        )

    def attend_back(micro, *earlier):
        held = stage[micro]
        near, far, held.grad_joined = attend_backward(
            held.index,
            held.valid,
            held.joined,
            after(held.grad_context, *earlier),
            held.logsum,
            held.pieces,
            heads,
            slots,
        )
        return near, far

    def input_rows(micro, long_sum):
        held = stage[micro]
        shape = (chips, own_rows, pair_width + local_width)
        place, lane = np.indices(shape, np.int32, sparse=True)[::2]
        joined = held.grad_joined.reshape(shape)
        for doc, start in enumerate(held.long_rows):
            long_part = jnp.pad(slot_rows(long_sum, doc), ((0, 0), (0, local_width)))
            joined = jnp.where((place * own_rows == start) & (lane < pair_width), long_part, joined)
        held.grad_joined = joined.reshape(group_rows, -1)
        rows = contract(held.grad_joined, joined_weight, NT)
        return rows.astype(bf16).reshape(chips, own_rows, model_width)

    def input_back(micro, grad_one):
        held = stage[micro]
        back, gain_sum, shift_sum = layer_back(
            grad_one, held.stats_one, held.inverse_one, first_gain
        )
        held.input_grad = held.grad_hidden + back
        held.first_sums = jnp.stack([gain_sum, shift_sum])

    longs = long_blocks(0)
    near, far, one, outer_full = second_exchange(longs, stage[1].low, column, cuts[2:4], 2)
    stage[1].one = one.reshape(group_rows, model_width)
    keep_pieces(0, near, far)
    attend(0)
    longs = long_blocks(1)
    near, far, context, rest, inner_full = third_exchange(
        longs,
        column,
        stage[0].context_sent.reshape(chips, own_rows, local_width),
        (cuts[0:2], cuts[1:3]),
        7,
    )
    keep_pieces(1, near, far)
    stage[0].context = context.transpose(1, 0, 2).reshape(own_rows, model_width)
    inner_full = inner_full.reshape(-1, model_width)
    outer_full = outer_full.reshape(-1, model_width)
    inner_bias_full = rest[:, :, :, proj_cut, :unit_cut].reshape(-1)
    proj_full = rest[:, :, :, :proj_cut].transpose(2, 1, 0, 3, 4)
    proj_full = proj_full.reshape(tp_count * local_width, model_width)
    feed_forward(0)
    attend(1)
    near, far = attend_back(0, stage[1].logsum, stage[1].context_sent)
    stage[0].long_sum_sent = sum_parts([near, core_swap(far)]).astype(bf16)
    long_sum = lax.psum_scatter(stage[0].long_sum_sent, TP, scatter_dimension=0, tiled=True)
    feed_forward(1)

    given_inner, given_outer, kept_inner, kept_outer, proj_part = dense_terms(
        after(core, stage[1].grad_context_sent),
        [[h.grad_before for h in stage], [h.active for h in stage], [h.context for h in stage]],
        [[h.two for h in stage], [h.grad_out for h in stage], [h.branch for h in stage]],
    )
    proj_part = proj_part.reshape(tp_count, chips, 2, proj_cut, model_width)
    unit_shape = (2, chips, tp_count)
    unit_sum = sum(h.unit_sum for h in stage).astype(bf16)
    rest_part = jnp.concatenate(
        [
            proj_part.transpose(2, 1, 0, 3, 4),
            padded(unit_sum.reshape(unit_shape + (1, unit_cut))),
            jnp.zeros(unit_shape + (rest_rows - proj_cut - 1, model_width), bf16),
        ],
        axis=3,
    )
    unit_shape = (chips, tp_count, -1, model_width)
    terms = [kept_inner.reshape(unit_shape), kept_outer.reshape(unit_shape)]
    givens = [core_swap(part.reshape(unit_shape)) for part in (given_inner, given_outer)]
    terms.append(lax.dynamic_index_in_dim(rest_part, core, axis=0, keepdims=False))
    givens.append(
        core_swap(lax.dynamic_index_in_dim(rest_part, 1 - core, axis=0, keepdims=False))
    )

    rows = input_rows(0, after(long_sum, kept_inner))
    grad_one = lax.psum_scatter(
        rows.reshape(group_rows, model_width),
        SEQ,
        scatter_dimension=0,
        axis_index_groups=[list(range(place, seq_count, 2)) for place in range(2)],
        tiled=True,
    )
    near, far = attend_back(1, rows)

    column_shape = (tp_count, long_docs * own_rows, pair_width)
    cuts = (0, unit_cut, 2 * unit_cut, 2 * unit_cut + rest_rows)
    row_shape = (chips, 2, own_rows // 2, model_width)
    long_sum, quarters = fourth_exchange(
        near.reshape(column_shape), far.reshape(column_shape), terms, givens, cuts, 3
    )
    rows = input_rows(1, long_sum)
    grad_one_now, own_sum = fifth_exchange(rows.reshape(row_shape), quarters, 4)
    input_back(0, after(grad_one, rows).astype(f32))
    input_back(1, grad_one_now.reshape(own_rows, model_width))

    ones = after([h.one for h in stage], grad_one_now)
    packed_sum = sum(contract(one, h.grad_joined, TN) for one, h in zip(ones, stage))
    packed_sum = jnp.pad(packed_sum, ((0, 0), (0, -packed_sum.shape[1] % 128))).astype(bf16)

    def own_columns(values):
        wide = jnp.zeros((chips, local_width), f32)
        return lax.dynamic_update_slice_in_dim(wide, values[None], chip, axis=0).reshape(-1)

    joined_sum = sum(jnp.sum(h.grad_joined.astype(f32), axis=0) for h in stage)
    packed_sum, dense_sum, all_rows = sixth_exchange(
        packed_sum,
        own_sum,
        jnp.concatenate(
            [
                sum(h.row_sums for h in stage),
                sum(h.first_sums for h in stage),
                own_columns(joined_sum[pair_width:] * score_scale)[None],
                own_columns(high_half(joined_sum[:pair_width]))[None],
            ],
            axis=0,
        ),
        6,
    )
    key_grad = low_half(packed_sum[:, :pair_width]).astype(f32)
    value_grad = high_half(packed_sum[:, :pair_width]).astype(f32)
    query_grad = packed_sum[:, pair_width : pair_width + local_width].astype(f32) * score_scale
    dense_sum = dense_sum.reshape(seq_count, -1, model_width).astype(f32)
    inner_weight_grad = dense_sum[:, :unit_cut].reshape(hidden_units, model_width).T
    outer_weight_grad = dense_sum[:, unit_cut : 2 * unit_cut].reshape(hidden_units, model_width)
    rest = dense_sum[:, 2 * unit_cut :]
    proj_weight_grad = rest[:, :proj_cut].reshape(local_width, model_width)
    inner_bias_grad = rest[:, proj_cut, :unit_cut].reshape(hidden_units)

    def my_columns(row):
        return lax.dynamic_slice_in_dim(row, tp_place * local_width, local_width)

    return (
        jnp.stack([h.output for h in stage]),
        jnp.stack([h.input_grad for h in stage]),
        query_grad,
        key_grad,
        value_grad,
        my_columns(all_rows[6]),
        my_columns(all_rows[7]),
        proj_weight_grad,
        all_rows[2],
        all_rows[4],
        all_rows[5],
        all_rows[0],
        all_rows[1],
        inner_weight_grad,
        inner_bias_grad,
        outer_weight_grad,
        all_rows[3],
    )


def general_body(
    tokens,
    doc_lengths,
    rand_blocks,
    query_weight,
    key_weight,
    value_weight,
    query_bias,
    value_bias,
    proj_weight,
    proj_bias,
    first_gain,
    first_bias,
    second_gain,
    second_bias,
    inner_weight,
    inner_bias,
    outer_weight,
    outer_bias,
    out_grad,
):
    micro_count, local_rows, model_width = tokens.shape
    seq_count = lax.axis_size(SEQ)
    tp_count = lax.axis_size(TP)
    seq_place = lax.axis_index(SEQ)
    tp_place = lax.axis_index(TP)
    block_dev = rand_blocks.shape[1]
    heads = rand_blocks.shape[2]
    local_width = query_weight.shape[1]
    head_size = local_width // heads
    hidden_units = inner_weight.shape[1]
    group_rows = block_dev * BLOCK
    reach_dev = (block_dev + LONG_BLK - 2) // block_dev
    window = 2 * reach_dev + 1
    score_scale = 1.0 / math.sqrt(head_size)
    lowest = (seq_place - reach_dev) * block_dev
    blocks = seq_place * block_dev + jnp.arange(block_dev, dtype=jnp.int32)

    held = jnp.concatenate([inner_weight.T, outer_weight, proj_weight, inner_bias[None]], axis=0)
    used_rows = held.shape[0]
    piece_rows = -(-used_rows // (16 * seq_count)) * 16
    held_rows = piece_rows * seq_count
    held = jnp.pad(held, ((0, held_rows - used_rows), (0, 0)))
    share = lax.dynamic_slice_in_dim(held, seq_place * piece_rows, piece_rows, axis=0)
    spread = lax.all_gather(share, (TP, SEQ), axis=0, tiled=True)
    spread = spread.reshape(tp_count, held_rows, model_width)
    cuts = [0, hidden_units, 2 * hidden_units, 2 * hidden_units + local_width, used_rows]
    inner_full = spread[:, cuts[0] : cuts[1]].reshape(-1, model_width)
    outer_full = spread[:, cuts[1] : cuts[2]].reshape(-1, model_width)
    proj_full = spread[:, cuts[2] : cuts[3]].reshape(-1, model_width)
    inner_bias_full = spread[:, cuts[3] : cuts[4]].reshape(-1)

    def by_head(weight):
        return weight.reshape(weight.shape[:-1] + (heads, head_size))

    def side_by_side(first, second):
        paired = jnp.concatenate([by_head(first), by_head(second)], axis=-1)
        return paired.reshape(paired.shape[:-2] + (heads * PAIR,))

    pair_wide = side_by_side(key_weight, value_weight)
    pair_wide_bias = side_by_side(jnp.zeros_like(value_bias), value_bias)

    stage = [Micro() for _ in range(micro_count)]
    for micro, held in enumerate(stage):
        inputs = tokens[micro].astype(f32)
        shifted, stats, inverse = layer_stats(inputs, first_gain, first_bias)
        held.inputs, held.stats_one, held.inverse_one = inputs, stats, inverse
        held.one = lax.all_gather(shifted.astype(bf16), TP, axis=0, tiled=True)

    for micro, held in enumerate(stage):
        one = held.one
        pair_rows = (contract(one, pair_wide, NN) + pair_wide_bias).astype(bf16)
        offsets = [offset for offset in range(-reach_dev, reach_dev + 1) if offset != 0]
        pieces = [from_behind(pair_rows, SEQ, -offset) for offset in offsets]
        queries = ((contract(one, query_weight, NN) + query_bias) * score_scale).astype(bf16)
        held.joined = jnp.concatenate([pair_rows, queries], axis=1)
        key_index, key_valid = block_keys(doc_lengths[micro], rand_blocks[micro], blocks)
        slots = key_index.shape[2]
        slot_index = jnp.clip(key_index - lowest, 0, window * block_dev - 1)
        piece = slot_index // block_dev
        piece = jnp.where(piece == reach_dev, 2 * reach_dev, piece - (piece > reach_dev))
        slot_index = piece * block_dev + slot_index % block_dev
        held.index = slot_index.transpose(1, 0, 2).reshape(-1)
        held.valid = key_valid.reshape(-1)
        held.pieces = pieces

    for held in stage:
        context, held.logsum = attend_forward(
            held.index,
            held.valid,
            held.joined,
            held.pieces,
            heads,
            slots,
        )
        held.context = lax.all_to_all(context, TP, split_axis=0, concat_axis=1, tiled=True)

    outputs = []
    for micro, held in enumerate(stage):
        context = held.context
        hidden = held.inputs + contract(context, proj_full, NN) + proj_bias
        shifted, stats, inverse = layer_stats(hidden, second_gain, second_bias)
        two = shifted.astype(bf16)
        before = contract(two, inner_full, NT) + inner_bias_full
        active = gelu_exact(before).astype(bf16)
        result = hidden + contract(active, outer_full, NN) + outer_bias
        outputs.append(result.astype(bf16))
        grad_out = out_grad[micro]
        grad_float = grad_out.astype(f32)
        grad_active = contract(grad_out, outer_full, NT)
        grad_before = gelu_grad(before, grad_active).astype(bf16)
        grad_two = contract(grad_before, inner_full, NN)
        back, gain_sum, shift_sum = layer_back(grad_two, stats, inverse, second_gain)
        grad_hidden = grad_float + back
        branch = grad_hidden.astype(bf16)
        grad_context = contract(branch, proj_full, NT).astype(bf16)
        held.grad_context = lax.all_to_all(
            grad_context, TP, split_axis=1, concat_axis=0, tiled=True
        )
        held.grad_hidden = grad_hidden
        held.dense = (two, grad_before, active, grad_out, context, branch)
        held.row_sums = (
            jnp.sum(grad_before.astype(f32), axis=0),
            gain_sum,
            shift_sum,
            jnp.sum(branch.astype(f32), axis=0),
            jnp.sum(grad_float, axis=0),
        )

    two, grad_before, active, grad_out, context, branch = (
        jnp.concatenate(group, axis=0) for group in zip(*(h.dense for h in stage))
    )
    inner_part = contract(grad_before, two, TN).astype(bf16)
    outer_part = contract(active, grad_out, TN).astype(bf16)
    proj_part = contract(context, branch, TN).astype(bf16)
    grad_rows = 2 * hidden_units + local_width
    grad_piece = -(-grad_rows // (16 * seq_count)) * 16
    grad_held = grad_piece * seq_count
    parts = jnp.concatenate(
        [
            inner_part.reshape(tp_count, hidden_units, model_width),
            outer_part.reshape(tp_count, hidden_units, model_width),
            proj_part.reshape(tp_count, local_width, model_width),
            jnp.zeros((tp_count, grad_held - grad_rows, model_width), bf16),
        ],
        axis=1,
    ).reshape(tp_count * grad_held, model_width)
    own_part = lax.psum_scatter(parts, (TP, SEQ), scatter_dimension=0, tiled=True)
    dense_sum = lax.all_gather(own_part, SEQ, axis=0, tiled=True).astype(f32)
    inner_weight_grad = dense_sum[cuts[0] : cuts[1]].T
    outer_weight_grad = dense_sum[cuts[1] : cuts[2]]
    proj_weight_grad = dense_sum[cuts[2] : cuts[3]]

    for held in stage:
        *grad_pieces, joined = attend_backward(
            held.index,
            held.valid,
            held.joined,
            held.grad_context,
            held.logsum,
            held.pieces,
            heads,
            slots,
        )
        pair_width = heads * PAIR
        returned = joined[:, :pair_width].astype(f32)
        held.grad_query = joined[:, pair_width:]
        for offset, grad_piece in zip(offsets, grad_pieces):
            returned = returned + from_behind(grad_piece, SEQ, offset).astype(f32)
        held.grad_pair = returned.astype(bf16)

    input_grads = []
    query_sum = pair_sum = 0.0
    query_bias_sum = pair_bias_sum = 0.0
    first_gain_sum = first_bias_sum = 0.0
    for held in stage:
        grad_query, grad_pair, one = held.grad_query, held.grad_pair, held.one
        rows = contract(grad_query, query_weight * score_scale, NT) + contract(grad_pair, pair_wide, NT)
        grad_one = lax.psum_scatter(
            rows.astype(bf16), TP, scatter_dimension=0, tiled=True
        ).astype(f32)
        query_sum = query_sum + contract(one, grad_query, TN)
        pair_sum = pair_sum + contract(one, grad_pair, TN)
        query_bias_sum = query_bias_sum + jnp.sum(grad_query.astype(f32), axis=0)
        pair_bias_sum = pair_bias_sum + jnp.sum(grad_pair.astype(f32), axis=0)
        back, gain_sum, shift_sum = layer_back(
            grad_one, held.stats_one, held.inverse_one, first_gain
        )
        first_gain_sum = first_gain_sum + gain_sum
        first_bias_sum = first_bias_sum + shift_sum
        input_grads.append(held.grad_hidden + back)

    def low_half(wide):
        return wide.reshape(wide.shape[:-1] + (heads, PAIR))[..., :head_size].reshape(
            wide.shape[:-1] + (local_width,)
        )

    def high_half(wide):
        return wide.reshape(wide.shape[:-1] + (heads, PAIR))[..., head_size:].reshape(
            wide.shape[:-1] + (local_width,)
        )

    query_grad, key_grad, value_grad = lax.psum(
        (query_sum * score_scale, low_half(pair_sum), high_half(pair_sum)), SEQ
    )
    inner_bias_sum, second_gain_sum, second_bias_sum, proj_bias_sum, outer_bias_sum = (
        sum(group) for group in zip(*(h.row_sums for h in stage))
    )

    def own_columns(values):
        wide = jnp.zeros((tp_count, local_width), f32)
        return lax.dynamic_update_slice_in_dim(wide, values[None], tp_place, axis=0).reshape(-1)

    early = lax.psum(
        jnp.concatenate(
            [
                inner_bias_sum,
                second_gain_sum,
                second_bias_sum,
                proj_bias_sum,
                outer_bias_sum,
            ]
        ),
        (SEQ, TP),
    )
    late = lax.psum(
        jnp.concatenate(
            [
                first_gain_sum,
                first_bias_sum,
                own_columns(query_bias_sum * score_scale),
                own_columns(high_half(pair_bias_sum)),
            ]
        ),
        (SEQ, TP),
    )
    inner_bias_all = early[: tp_count * hidden_units].reshape(tp_count, hidden_units)
    early_rows = early[tp_count * hidden_units :].reshape(-1, model_width)
    late_rows = late.reshape(-1, model_width)

    def my_columns(row):
        return lax.dynamic_slice_in_dim(row, tp_place * local_width, local_width)

    return (
        jnp.stack(outputs),
        jnp.stack(input_grads),
        query_grad,
        key_grad,
        value_grad,
        my_columns(late_rows[2]),
        my_columns(late_rows[3]),
        proj_weight_grad,
        early_rows[2],
        late_rows[0],
        late_rows[1],
        early_rows[0],
        early_rows[1],
        inner_weight_grad,
        lax.dynamic_index_in_dim(inner_bias_all, tp_place, axis=0, keepdims=False),
        outer_weight_grad,
        early_rows[3],
    )


def solution(mesh):
    def choose(tokens, doc_lengths, rand_blocks, *rest):
        blocks = rand_blocks.shape[1] * mesh.shape[SEQ]
        if plane_applies(mesh, blocks, doc_lengths.shape[1]):
            return plane_body(tokens, doc_lengths, rand_blocks, *rest)
        return general_body(tokens, doc_lengths, rand_blocks, *rest)

    return jax.shard_map(
        choose,
        mesh=mesh,
        in_specs=(
            P(None, (SEQ, TP), None),
            P(),
            P(None, SEQ, TP, None),
            P(None, TP),
            P(None, TP),
            P(None, TP),
            P(TP),
            P(TP),
            P(TP, None),
            P(),
            P(),
            P(),
            P(),
            P(),
            P(None, TP),
            P(TP),
            P(TP, None),
            P(),
            P(None, (SEQ, TP), None),
        ),
        out_specs=(
            P(None, (SEQ, TP), None),
            P(None, (SEQ, TP), None),
            P(None, TP),
            P(None, TP),
            P(None, TP),
            P(TP),
            P(TP),
            P(TP, None),
            P(),
            P(),
            P(),
            P(),
            P(),
            P(None, TP),
            P(TP),
            P(TP, None),
            P(),
        ),
        check_vma=False,
    )
```

```python
import functools
import math

import jax
import jax.numpy as jnp
import numpy as np
from jax import lax
from jax.experimental import pallas as pl
from jax.experimental.pallas import tpu as pltpu
from jax.sharding import PartitionSpec as P

BLOCK = 64
LONG_BLK = 64
SHORT_BLK = 8
PAIR = 2 * BLOCK
UNROLL = 4
SEQ = "seq"
TP = "tp"

NORM_EPS = 1e-05
MASKED = -1000000000.0

f32 = jnp.float32
bf16 = jnp.bfloat16

NN = (((1,), (0,)), ((), ()))
NT = (((1,), (1,)), ((), ()))
TN = (((0,), (0,)), ((), ()))


def contract(left, right, dims):
    return lax.dot_general(left, right, dims, preferred_element_type=f32)


def from_behind(block, axis, distance):
    devices = range(lax.axis_size(axis))
    route = [(i - distance, i) for i in devices if i - distance in devices]
    return lax.ppermute(block, axis, route)


def gelu_exact(values):
    return 0.5 * values * (1.0 + lax.erf(values / math.sqrt(2.0)))


def gelu_grad(values, grad_rows):
    _, pull_back = jax.vjp(gelu_exact, values)
    return pull_back(grad_rows)[0]


def layer_stats(values, norm_gain, norm_shift):
    row_mean = jnp.mean(values, axis=-1, keepdims=True)
    centred = values - row_mean
    inverse = lax.rsqrt(jnp.mean(centred * centred, axis=-1, keepdims=True) + NORM_EPS)
    normed = centred * inverse
    return (normed * norm_gain + norm_shift, normed, inverse)


def layer_back(grad_rows, normed, inverse, norm_gain):
    scaled = grad_rows * norm_gain
    inner_term = (
        scaled
        - jnp.mean(scaled, axis=-1, keepdims=True)
        - normed * jnp.mean(scaled * normed, axis=-1, keepdims=True)
    )
    return (inverse * inner_term, jnp.sum(grad_rows * normed, axis=0), jnp.sum(grad_rows, axis=0))


def block_keys(lengths, randoms, blocks):
    doc_ends = jnp.cumsum(lengths)
    doc_starts = doc_ends - lengths
    doc_owner = jnp.sum((blocks[:, None] >= doc_ends[None, :]).astype(jnp.int32), axis=1)
    doc_ids = jnp.arange(lengths.shape[0], dtype=jnp.int32)
    doc_hit = doc_owner[:, None] == doc_ids[None, :]
    doc_first = jnp.sum(jnp.where(doc_hit, doc_starts[None, :], 0), axis=1)
    doc_final = jnp.sum(jnp.where(doc_hit, doc_ends[None, :], 0), axis=1)
    fixed_keys = jnp.stack(
        [
            jnp.maximum(blocks - 1, doc_first),
            jnp.minimum(blocks + 1, doc_final - 1),
            blocks,
            doc_first,
            doc_first + 1,
        ],
        axis=1,
    )
    block_count = randoms.shape[0]
    head_count = randoms.shape[1]
    key_index = jnp.concatenate(
        [jnp.broadcast_to(fixed_keys[:, None, :], (block_count, head_count, 5)), randoms], axis=2
    )
    key_valid = jnp.stack([blocks > doc_first, blocks + 1 < doc_final], axis=1)
    return (key_index, key_valid.astype(jnp.int32))


def block_rows(block):
    return pl.ds(pl.multiple_of(block * BLOCK, BLOCK), BLOCK)


def listed_blocks(index_ref, store, base, slots):
    return jnp.concatenate(
        [store[block_rows(index_ref[base + slot]), :] for slot in range(slots)], axis=0
    )


def mask_scores(scores, valid_ref, block):
    lane = lax.broadcasted_iota(jnp.int32, (1, PAIR), 1)
    keep = jnp.where(lane < BLOCK, valid_ref[2 * block], valid_ref[2 * block + 1]) > 0
    return jnp.concatenate([jnp.where(keep, scores[:, :PAIR], MASKED), scores[:, PAIR:]], axis=1)


def fill_store(store, pieces):
    place = 0
    for piece in pieces:
        store[place : place + piece.shape[0], :] = piece[...]
        place += piece.shape[0]


def each_head(heads, work):
    for head in range(heads):

        @pl.when(pl.program_id(0) == head)
        def _():
            work(head)


def head_columns(head, first=0):
    return slice(first + head * BLOCK, first + (head + 1) * BLOCK)


def forward_head(slots, head, index_ref, valid_ref, store, wide_query, wide_context, logsum_ref):
    blocks = wide_query.shape[0] // BLOCK

    def step(group, carry):
        ids = [group * UNROLL + unit for unit in range(UNROLL)]
        listed = []
        for block in ids:
            first = (head * blocks + block) * slots
            listed.append(
                jnp.concatenate([store[index_ref[first + slot]] for slot in range(slots)], axis=0)
            )
        scores = [
            mask_scores(contract(wide_query[block_rows(block), :], pairs, NT), valid_ref, block)
            for block, pairs in zip(ids, listed)
        ]
        probs = []
        for block, score in zip(ids, scores):
            top = jnp.max(score, axis=1, keepdims=True)
            raised = jnp.exp(score - top)
            total = jnp.sum(raised, axis=1, keepdims=True)
            probs.append((raised * (1.0 / total)).astype(bf16))
            logsum_ref[block_rows(block), :] = jnp.broadcast_to(
                top + jnp.log(total), (BLOCK, PAIR)
            )
        for block, prob, pairs in zip(ids, probs, listed):
            wide_context[block_rows(block), :] = contract(prob, pairs, NN).astype(bf16)
        return carry

    lax.fori_loop(0, blocks // UNROLL, step, 0)


def widen(query):
    return jnp.concatenate([query, jnp.zeros_like(query)], axis=1)


def forward_kernel(slots, heads, index_ref, valid_ref, query_ref, *refs):
    *pieces, context_ref, logsum_ref, store, wide_query, wide_context = refs
    place = 0
    for piece in pieces:
        count = piece.shape[0] // BLOCK
        store[place : place + count] = piece[...].reshape(count, BLOCK, PAIR)
        place += count

    def take_query(own):
        wide_query[...] = widen(query_ref[:, head_columns(own, heads * PAIR)])

    each_head(heads, take_query)
    forward_head(
        slots, pl.program_id(0), index_ref, valid_ref, store, wide_query, wide_context, logsum_ref
    )

    def give_context(own):
        context_ref[:, head_columns(own)] = wide_context[:, BLOCK:]

    each_head(heads, give_context)


def backward_kernel(slots, heads, count, index_ref, valid_ref, query_ref, grad_ref, logsum_ref, *refs):
    pieces, refs = refs[:count], refs[count:]
    grad_pieces, joined_ref = refs[: count - 1], refs[count - 1]
    store, sums, both_rows, wide_grad = refs[count:]
    rows = query_ref.shape[0]
    blocks = rows // BLOCK
    head = pl.program_id(0)
    fill_store(store, pieces)
    sums[...] = jnp.zeros_like(sums)
    lane = lax.broadcasted_iota(jnp.int32, (BLOCK, PAIR), 1)

    def take_both(own):
        query = query_ref[:, head_columns(own, heads * PAIR)]
        both_rows[...] = jnp.concatenate([query, grad_ref[:, head_columns(own)]], axis=1)

    each_head(heads, take_both)

    def step(group, carry):
        ids = [group * UNROLL + unit for unit in range(UNROLL)]
        listed = [
            listed_blocks(index_ref, store, (head * blocks + block) * slots, slots)
            for block in ids
        ]
        lefts = []
        for block in ids:
            both = both_rows[block_rows(block), :]
            lefts.append(
                jnp.concatenate(
                    [
                        jnp.where(lane < BLOCK, both, 0).astype(bf16),
                        jnp.where(lane < BLOCK, 0, both).astype(bf16),
                    ],
                    axis=0,
                )
            )
        products = [contract(left, pairs, NT) for left, pairs in zip(lefts, listed)]
        mixes = []
        for block, product in zip(ids, products):
            score = mask_scores(product[:BLOCK], valid_ref, block)
            grad_prob = product[BLOCK:]
            logsum = jnp.concatenate([logsum_ref[block_rows(block), :]] * (slots // 2), axis=1)
            prob = jnp.exp(score - logsum)
            delta = jnp.sum(prob * grad_prob, axis=1, keepdims=True)
            grad_score = prob * (grad_prob - delta)
            mixes.append(jnp.concatenate([grad_score.astype(bf16), prob.astype(bf16)], axis=0))
        for block, mix, pairs in zip(ids, mixes, listed):
            wide_grad[block_rows(block), :] = contract(mix[:BLOCK], pairs, NN).astype(bf16)
        terms = [contract(mix, left, TN) for mix, left in zip(mixes, lefts)]
        for block, term in zip(ids, terms):
            base = (head * blocks + block) * slots
            for slot in range(slots):
                sums[block_rows(index_ref[base + slot]), :] += term[
                    slot * BLOCK : (slot + 1) * BLOCK
                ]
        return carry

    lax.fori_loop(0, blocks // UNROLL, step, 0)
    place = 0
    for grad_piece in grad_pieces:
        grad_piece[...] = sums[place : place + grad_piece.shape[0], :].astype(bf16)
        place += grad_piece.shape[0]

    def give_joined(own):
        joined_ref[:, own * PAIR : (own + 1) * PAIR] = sums[place:, :].astype(bf16)
        start = heads * PAIR + own * BLOCK
        joined_ref[:, start : start + BLOCK] = wide_grad[:, :BLOCK]

    each_head(heads, give_joined)


def lasting(microseconds):
    return pl.CostEstimate(
        flops=0, bytes_accessed=int(microseconds * 3.69e6), transcendentals=0
    )


def per_head(array):
    return pl.BlockSpec((array.shape[0], PAIR), lambda head, *_: (0, head))


def whole(array):
    return pl.BlockSpec(array.shape, lambda head, *_: (0, 0))


def attend_forward(index, valid, joined, pieces, heads, slots):
    rows = joined.shape[0]
    pieces = pieces + [joined]
    context = jax.ShapeDtypeStruct((rows, heads * BLOCK), bf16)
    stored = sum(piece.shape[0] for piece in pieces)
    logsum = jax.ShapeDtypeStruct((rows, heads * PAIR), f32)
    return pl.pallas_call(
        functools.partial(forward_kernel, slots, heads),
        grid_spec=pltpu.PrefetchScalarGridSpec(
            num_scalar_prefetch=2,
            grid=(heads,),
            in_specs=[whole(joined)] + [per_head(piece) for piece in pieces],
            out_specs=[whole(context), per_head(logsum)],
            scratch_shapes=[
                pltpu.VMEM((stored // BLOCK, BLOCK, PAIR), bf16),
                pltpu.VMEM((rows, PAIR), bf16),
                pltpu.VMEM((rows, PAIR), bf16),
            ],
        ),
        out_shape=[context, logsum],
        compiler_params=pltpu.CompilerParams(vmem_limit_bytes=40 * 2**20),
        cost_estimate=lasting(18),
    )(index, valid, joined, *pieces)


def attend_backward(index, valid, joined, grads, logsum, pieces, heads, slots):
    rows = joined.shape[0]
    pieces = pieces + [joined]
    stored = sum(piece.shape[0] for piece in pieces)
    piece_specs = [per_head(piece) for piece in pieces]
    return pl.pallas_call(
        functools.partial(backward_kernel, slots, heads, len(pieces)),
        grid_spec=pltpu.PrefetchScalarGridSpec(
            num_scalar_prefetch=2,
            grid=(heads,),
            in_specs=[whole(joined), whole(grads), per_head(logsum)] + piece_specs,
            out_specs=piece_specs[:-1] + [whole(joined)],
            scratch_shapes=[
                pltpu.VMEM((stored, PAIR), bf16),
                pltpu.VMEM((stored, PAIR), f32),
                pltpu.VMEM((rows, PAIR), bf16),
                pltpu.VMEM((rows, PAIR), bf16),
            ],
        ),
        out_shape=[jax.ShapeDtypeStruct(piece.shape, bf16) for piece in pieces],
        compiler_params=pltpu.CompilerParams(vmem_limit_bytes=50 * 2**20),
        cost_estimate=lasting(25),
    )(index, valid, joined, grads, logsum, *pieces)


def dense_kernel(core_ref, *refs):
    ins, (given_inner, given_outer, kept_inner, kept_outer, proj) = refs[:12], refs[12:]
    step = pl.program_id(0)
    half = pl.num_programs(0) // 2

    def term(first):
        total = contract(ins[first][...], ins[first + 2][...], TN)
        return (total + contract(ins[first + 1][...], ins[first + 3][...], TN)).astype(bf16)

    @pl.when(step < half)
    def _():
        given_inner[...] = term(0)
        given_outer[...] = term(4)

    @pl.when(step >= half)
    def _():
        kept_inner[...] = term(0)
        kept_outer[...] = term(4)

    @pl.when(step == 0)
    def _():
        proj[...] = term(8)


def dense_terms(core, units, rows):
    steps = 8
    hidden = units[0][0].shape[1]
    tile = hidden // steps
    width = rows[0][0].shape[1]

    def unit_tile(step, core_ref):
        owner = jnp.where(step < steps // 2, 1 - core_ref[0], core_ref[0])
        return (0, owner * (steps // 2) + step % (steps // 2))

    def whole_rows(array):
        return pl.BlockSpec(array.shape, lambda step, *_: (0, 0))

    ins, specs = [], []
    for place in range(3):
        for array in units[place]:
            ins.append(array)
            if place < 2:
                specs.append(pl.BlockSpec((array.shape[0], tile), unit_tile))
            else:
                specs.append(whole_rows(array))
        for array in rows[place]:
            ins.append(array)
            specs.append(whole_rows(array))
    half = jax.ShapeDtypeStruct((hidden // 2, width), bf16)
    proj = jax.ShapeDtypeStruct((units[2][0].shape[1], width), bf16)
    given = pl.BlockSpec((tile, width), lambda step, *_: (jnp.minimum(step, steps // 2 - 1), 0))
    kept = pl.BlockSpec((tile, width), lambda step, *_: (jnp.maximum(step - steps // 2, 0), 0))
    return pl.pallas_call(
        dense_kernel,
        grid_spec=pltpu.PrefetchScalarGridSpec(
            num_scalar_prefetch=1,
            grid=(steps,),
            in_specs=specs,
            out_specs=[given, given, kept, kept, whole_rows(proj)],
        ),
        out_shape=[half] * 4 + [proj],
        compiler_params=pltpu.CompilerParams(vmem_limit_bytes=40 * 2**20),
        cost_estimate=lasting(15),
    )(core.reshape(1), *ins)


def plane_exchange(values, split_axis, concat_axis):
    count = lax.axis_size(SEQ)
    groups = [list(range(place, count, 2)) for place in range(2)]
    return lax.all_to_all(
        values,
        SEQ,
        split_axis=split_axis,
        concat_axis=concat_axis,
        axis_index_groups=groups,
        tiled=True,
    )


def plane_gather(values):
    count = lax.axis_size(SEQ) // 2
    return plane_exchange(jnp.concatenate([values] * count, axis=0), 0, 0)


def core_swap(block):
    route = [(place, place ^ 1) for place in range(lax.axis_size(SEQ))]
    return lax.ppermute(block, SEQ, route)


def column_shift(block, step):
    count = lax.axis_size(TP)
    return lax.ppermute(block, TP, [(place, (place + step) % count) for place in range(count)])


def column_gather(values):
    count = lax.axis_size(TP)
    place = lax.axis_index(TP)
    spread = jnp.zeros((count,) + values.shape, values.dtype)
    spread = lax.dynamic_update_index_in_dim(spread, values, place, axis=0)
    for step in range(1, count):
        spread = lax.dynamic_update_index_in_dim(
            spread, column_shift(values, step), (place - step) % count, axis=0
        )
    return spread


def after(values, *earlier):
    return lax.optimization_barrier((values, earlier))[0]


def sum_parts(parts):
    total = parts[0].astype(f32)
    for place in range(1, len(parts)):
        total = total + parts[place].astype(f32)
    return total


def partner_of(place):
    return place + 1 - 2 * (place % 2)


def enter(neighbours):
    barrier = pltpu.get_barrier_semaphore()
    count = 0
    for exists, device in neighbours:

        @pl.when(exists)
        def _():
            pl.semaphore_signal(
                barrier, inc=1, device_id=device, device_id_type=pl.DeviceIdType.MESH
            )

        count = count + jnp.where(exists, 1, 0)
    pl.semaphore_wait(barrier, count)


def remote(source, target, send, receive, device):
    return pltpu.make_async_remote_copy(
        src_ref=source,
        dst_ref=target,
        send_sem=send,
        recv_sem=receive,
        device_id=device,
        device_id_type=pl.DeviceIdType.MESH,
    )


def plane_ids():
    seq_place = lax.axis_index(SEQ)
    chip, core = seq_place // 2, seq_place % 2
    beside = chip + 1 - 2 * (chip % 2)
    above = chip + 2 - 4 * (chip // 2)
    facing = 3 - chip
    return chip, core, beside, above, facing


def column_way(place, way, distance):
    return place - distance if way == 0 else place + distance


class ColumnSpread:

    def __init__(self, parts, own, near, far, other, keep_sem, along_sems, across_sems):
        self.parts, self.own, self.near, self.far = parts, own, near, far
        self.other, self.keep_sem = other, keep_sem
        self.along_sems, self.across_sems = along_sems, across_sems
        self.count = lax.axis_size(TP)
        self.place = lax.axis_index(TP)
        self.rows = own.shape[0] // parts

    def cut(self, part):
        return pl.ds(part * self.rows, self.rows)

    def block(self, way, distance, part):
        if distance == 0:
            return self.own.at[self.cut(part)]
        return self.near.at[column_way(self.place, way, distance), self.cut(part)]

    def along(self, way, distance, part):
        return remote(
            self.block(way, distance, part),
            self.near.at[column_way(self.place, way, distance), self.cut(part)],
            self.along_sems[0].at[way, distance, part],
            self.along_sems[1].at[way, distance, part],
            {TP: self.place + 1 if way == 0 else self.place - 1},
        )

    def landed(self, way, distance, part):
        block = self.near.at[column_way(self.place, way, distance), self.cut(part)]
        return remote(
            block,
            block,
            self.along_sems[0].at[way, distance, part],
            self.along_sems[1].at[way, distance - 1, part],
            self.other,
        )

    def across(self, way, distance, part):
        return remote(
            self.block(way, distance, part),
            self.far.at[column_way(self.place, way, distance), self.cut(part)],
            self.across_sems[0].at[way, distance, part],
            self.across_sems[1].at[way, distance, part],
            self.other,
        )

    def keep(self):
        return pltpu.make_async_copy(self.own, self.near.at[self.place], self.keep_sem)

    def goes_on(self, way):
        return self.place < self.count - 1 if way == 0 else self.place > 0

    def has_come(self, way, distance):
        if way == 0:
            return self.place >= distance
        return self.place + distance < self.count

    def start(self):
        for part in range(self.parts):
            for way in range(2):

                @pl.when(self.goes_on(way))
                def _():
                    self.along(way, 0, part).start()

        if self.far is not None:
            for part in range(self.parts):
                self.across(0, 0, part).start()
        self.keep().start()

    def step(self, distance, part):
        for way in range(2):

            @pl.when(self.has_come(way, distance))
            def _():
                self.landed(way, distance, part).wait_recv()
                if distance < self.count - 1:

                    @pl.when(self.goes_on(way))
                    def _():
                        self.along(way, distance, part).start()

                if self.far is not None:
                    self.across(way, distance, part).start()

    def finish(self):
        self.keep().wait()
        for part in range(self.parts):
            if self.far is not None:
                self.across(0, 0, part).wait()
            for way in range(2):

                @pl.when(self.goes_on(way))
                def _():
                    self.along(way, 0, part).wait_send()

        for distance in range(1, self.count):
            for part in range(self.parts):
                for way in range(2):

                    @pl.when(self.has_come(way, distance))
                    def _():
                        if distance < self.count - 1:

                            @pl.when(self.goes_on(way))
                            def _():
                                self.along(way, distance, part).wait_send()

                        if self.far is not None:
                            self.across(way, distance, part).wait()


class PlaneSpread:

    def __init__(self, own, out, sems):
        self.own, self.out = own, out
        self.send_row, self.recv_row, self.send_on, self.recv_on = sems
        self.chip, core, beside, above, self.facing = plane_ids()
        self.ways = ({SEQ: 2 * beside + core}, {SEQ: 2 * above + core})
        self.chips = (beside, above)

    def first(self, way, part):
        return remote(
            self.own(part),
            self.out(self.chip, part),
            self.send_row.at[way, part],
            self.recv_row.at[way, part],
            self.ways[way],
        )

    def second(self, way):
        return remote(
            self.out(self.chips[way], way),
            self.out(self.chips[way], way),
            self.send_on.at[way],
            self.recv_on.at[way],
            self.ways[1 - way],
        )

    def start(self):
        self.first(0, 0).start()
        self.first(1, 1).start()

    def forward(self):
        for way in range(2):
            self.first(way, way).wait_recv()
            self.second(way).start()
        for way in range(2):
            self.first(way, 1 - way).start()

    def arrive(self):
        for way in range(2):
            self.first(way, 1 - way).wait_recv()
        for way in range(2):
            self.second(way).wait_recv()

    def finish(self):
        for way in range(2):
            self.second(way).wait_send()
            for part in range(2):
                self.first(way, part).wait_send()


def plane_sems():
    dma = pltpu.SemaphoreType.DMA
    return [dma((2, 2)), dma((2, 2)), dma((2,)), dma((2,))]


def column_sems(parts):
    sems = pltpu.SemaphoreType.DMA((2, 4, parts))
    return [sems, sems, sems, sems]


def halves_of(own, out, keep_sem):
    half = own.shape[0] // 2
    chip = plane_ids()[0]
    return (
        lambda part: own.at[pl.ds(part * half, half)],
        lambda place, part: out.at[place, pl.ds(part * half, half)],
        pltpu.make_async_copy(own, out.at[chip], keep_sem),
    )


def neighbours(facing_too, column_too):
    chip, core, beside, above, facing = plane_ids()
    count = lax.axis_size(TP)
    place = lax.axis_index(TP)
    always = place >= 0
    devices = [(always, {SEQ: 2 * chip + 1 - core})]
    devices += [(always, {SEQ: 2 * beside + core}), (always, {SEQ: 2 * above + core})]
    if facing_too:
        devices.append((always, {SEQ: 2 * facing + core}))
    if column_too:
        for step in range(1, count):
            devices.append((always, {TP: lax.rem(place + step, count)}))
    else:
        devices.append((place < count - 1, {TP: place + 1}))
        devices.append((place > 0, {TP: place - 1}))
    return devices


def first_kernel(
    parts,
    own_ref,
    weight_ref,
    share_ref,
    random_ref,
    out_ref,
    spread_ref,
    column_ref,
    random_out_ref,
    randoms,
    own_sem,
    send_row,
    recv_row,
    send_on,
    recv_on,
    send_z,
    recv_z,
    send_far,
    recv_far,
    send_random,
    recv_random,
    send_column,
    recv_column,
    send_share,
    recv_share,
):
    chip, core, beside, above, facing = plane_ids()
    tp_count = lax.axis_size(TP)
    place = lax.axis_index(TP)
    other = {SEQ: 2 * chip + 1 - core}
    weight_rows = weight_ref.shape[0] // (2 * parts)
    column = [{TP: lax.rem(place + step, tp_count)} for step in range(1, tp_count)]
    enter(neighbours(True, True))
    own, out, keep_rows = halves_of(own_ref, out_ref, own_sem.at[0])
    rows = PlaneSpread(own, out, (send_row, recv_row, send_on, recv_on))
    shares = ColumnSpread(
        2, share_ref, column_ref, None, other, own_sem.at[2], (send_share, recv_share), None
    )

    def weight_cut(part, holder):
        return pl.ds((holder * parts + part) * weight_rows, weight_rows)

    def weight_along(source, way, part):
        at = weight_cut(part, core)
        return remote(
            source.at[at],
            spread_ref.at[at],
            send_z.at[way, part],
            recv_z.at[part],
            {TP: place + 1 if way == 0 else place - 1},
        )

    def weight_across(part):
        at = weight_cut(part, core)
        return remote(
            spread_ref.at[at], spread_ref.at[at], send_far.at[part], recv_far.at[part], other
        )

    def goes_on(way):
        if way == 0:
            return (place >= chip) & (place < tp_count - 1)
        return (place <= chip) & (place > 0)

    def random_to_holder(sender):
        return remote(
            random_ref,
            randoms.at[sender],
            send_random,
            recv_random.at[sender],
            {SEQ: 2 * place + core},
        )

    def random_along(step):
        return remote(
            randoms,
            random_out_ref,
            send_column.at[step],
            recv_column,
            column[step],
        )

    rows.start()

    @pl.when(place != chip)
    def _():
        random_to_holder(chip).start()

    for part in range(parts):
        for way in range(2):

            @pl.when((place == chip) & goes_on(way))
            def _():
                weight_along(weight_ref, way, part).start()

    shares.start()
    keep_rows.start()

    @pl.when(place == chip)
    def _():
        keep = pltpu.make_async_copy(weight_ref, spread_ref, own_sem.at[1])
        keep.start()
        keep.wait()
        randoms[chip] = random_ref[...]
        for step in range(1, tp_count):
            random_to_holder(lax.rem(chip + step, tp_count)).wait_recv()
        random_out_ref[...] = randoms[...]
        for step in range(tp_count - 1):
            random_along(step).start()

    rows.forward()
    for part in range(parts):

        @pl.when(place != chip)
        def _():
            weight_along(spread_ref, 0, part).wait_recv()
            for way in range(2):

                @pl.when(goes_on(way))
                def _():
                    weight_along(spread_ref, way, part).start()

            weight_across(part).start()

    for distance in range(1, tp_count):
        for part in range(2):
            shares.step(distance, part)
    rows.arrive()
    rows.finish()
    shares.finish()
    keep_rows.wait()

    @pl.when(place != chip)
    def _():
        random_to_holder(chip).wait_send()
        random_along(0).wait_recv()

    @pl.when(place == chip)
    def _():
        for step in range(tp_count - 1):
            random_along(step).wait_send()

    for part in range(parts):

        @pl.when(place != chip)
        def _():
            weight_across(part).wait()

        for way in range(2):

            @pl.when(goes_on(way))
            def _():
                weight_along(spread_ref, way, part).wait_send()


def first_exchange(own, weight, share, randoms, collective_id, parts=4):
    chips = lax.axis_size(SEQ) // 2
    count = lax.axis_size(TP)
    resident = pl.BlockSpec(memory_space=pltpu.VMEM)
    dma = pltpu.SemaphoreType.DMA
    return pl.pallas_call(
        functools.partial(first_kernel, parts),
        out_shape=[
            jax.ShapeDtypeStruct((chips,) + own.shape, own.dtype),
            jax.ShapeDtypeStruct(weight.shape, weight.dtype),
            jax.ShapeDtypeStruct((count,) + share.shape, share.dtype),
            jax.ShapeDtypeStruct((chips,) + randoms.shape, randoms.dtype),
        ],
        in_specs=[resident] * 4,
        out_specs=[resident] * 4,
        scratch_shapes=[pltpu.VMEM((chips,) + randoms.shape, randoms.dtype), dma((3,))]
        + plane_sems()
        + [
            dma((2, parts)),
            dma((parts,)),
            dma((parts,)),
            dma((parts,)),
            dma,
            dma((chips,)),
            dma((chips - 1,)),
            dma,
        ]
        + column_sems(2)[:2],
        compiler_params=pltpu.CompilerParams(
            collective_id=collective_id, has_side_effects=True, vmem_limit_bytes=32 * 2**20
        ),
        cost_estimate=lasting(30),
    )(own, weight, share, randoms)


class WeightSpread:

    def __init__(self, column, rows, out, keep_sem, cross_sems, plane_sems):
        self.out, self.cross_sems = out, cross_sems
        self.chip, self.core, self.beside, self.above, self.facing = plane_ids()
        self.other = {SEQ: 2 * self.chip + 1 - self.core}
        self.half = column.shape[0] // 2
        self.plane = PlaneSpread(
            lambda part: column.at[pl.ds(part * self.half, self.half), rows],
            lambda where, part: out.at[self.core, where, pl.ds(part * self.half, self.half)],
            plane_sems,
        )
        self.keep = pltpu.make_async_copy(
            column.at[:, rows], out.at[self.core, self.chip], keep_sem
        )

    def across(self, where, part):
        chip = (self.chip, self.beside, self.above, self.facing)[where]
        block = self.out.at[self.core, chip, pl.ds(part * self.half, self.half)]
        at = (where, part)
        return remote(
            block, block, self.cross_sems[0].at[at], self.cross_sems[1].at[at], self.other
        )

    def start(self):
        self.plane.start()
        self.keep.start()

    def forward(self):
        self.plane.forward()
        self.keep.wait()
        for where, part in ((0, 0), (0, 1), (1, 0), (2, 1)):
            self.across(where, part).start()

    def arrive(self):
        self.plane.arrive()
        for where, part in ((1, 1), (2, 0), (3, 0), (3, 1)):
            self.across(where, part).start()

    def finish(self):
        self.plane.finish()
        for where in range(4):
            for part in range(2):
                self.across(where, part).wait()


def weight_sems():
    dma = pltpu.SemaphoreType.DMA
    return [dma, dma((4, 2)), dma((4, 2))] + plane_sems()


def weight_shape(column, rows):
    tp_count, _, width = column.shape
    chips = lax.axis_size(SEQ) // 2
    return jax.ShapeDtypeStruct((2, chips, tp_count, rows[1] - rows[0], width), column.dtype)


def second_kernel(
    parts,
    rows,
    longs_ref,
    own_ref,
    column_ref,
    near_ref,
    far_ref,
    out_ref,
    weight_ref,
    keep_sem,
    *sems,
):
    chip, core = plane_ids()[:2]
    enter(neighbours(False, False))
    other = {SEQ: 2 * chip + 1 - core}
    longs = ColumnSpread(
        parts, longs_ref, near_ref, far_ref, other, keep_sem.at[0], sems[:2], sems[2:4]
    )
    own, out, keep_rows = halves_of(own_ref, out_ref, keep_sem.at[1])
    plane = PlaneSpread(own, out, sems[4:8])
    weight = WeightSpread(
        column_ref, pl.ds(rows[0], rows[1] - rows[0]), weight_ref, sems[8], sems[9:11], sems[11:15]
    )
    longs.start()
    plane.start()
    weight.start()
    keep_rows.start()
    for part in range(parts):
        longs.step(1, part)
    plane.forward()
    weight.forward()
    for part in range(parts):
        longs.step(2, part)
    plane.arrive()
    weight.arrive()
    for part in range(parts):
        longs.step(3, part)
    plane.finish()
    weight.finish()
    longs.finish()
    keep_rows.wait()


def second_exchange(longs, own, column, rows, collective_id, parts=2):
    chips = lax.axis_size(SEQ) // 2
    near = jax.ShapeDtypeStruct((lax.axis_size(TP),) + longs.shape, longs.dtype)
    resident = pl.BlockSpec(memory_space=pltpu.VMEM)
    return pl.pallas_call(
        functools.partial(second_kernel, parts, rows),
        out_shape=[
            near,
            near,
            jax.ShapeDtypeStruct((chips,) + own.shape, own.dtype),
            weight_shape(column, rows),
        ],
        in_specs=[resident] * 3,
        out_specs=[resident] * 4,
        scratch_shapes=[pltpu.SemaphoreType.DMA((2,))]
        + column_sems(parts)
        + plane_sems()
        + weight_sems(),
        compiler_params=pltpu.CompilerParams(
            collective_id=collective_id, has_side_effects=True, vmem_limit_bytes=48 * 2**20
        ),
        cost_estimate=lasting(58),
    )(longs, own, column)


def third_kernel(
    parts,
    cuts,
    slots,
    heads,
    index_ref,
    valid_ref,
    longs_ref,
    column_ref,
    joined_ref,
    *refs,
):
    count = len(cuts)
    pieces, refs = refs[:3], refs[3:]
    near_ref, far_ref, context_ref, logsum_ref, refs = refs[0], refs[1], refs[2], refs[3], refs[4:]
    outs, refs = refs[:count], refs[count:]
    stores, wide_query, wide_context, sent, refs = refs[:2], refs[2], refs[3], refs[4], refs[5:]
    load_sem, keep_sem, block_sems, sems = refs[0], refs[1], refs[2:4], refs[4:8]
    chip, core, beside, above, facing = plane_ids()
    enter(neighbours(True, False))
    other = {SEQ: 2 * chip + 1 - core}
    longs = ColumnSpread(
        parts, longs_ref, near_ref, far_ref, other, keep_sem, sems[:2], sems[2:4]
    )
    weights = []
    for index, (first, last) in enumerate(cuts):
        own = refs[8 + 7 * index : 15 + 7 * index]
        weights.append(
            WeightSpread(
                column_ref, pl.ds(first, last - first), outs[index], own[0], own[1:3], own[3:7]
            )
        )

    def loads(head):
        copies, place = [], 0
        for index, piece in enumerate(pieces):
            rows = piece.shape[0]
            copies.append(
                pltpu.make_async_copy(
                    piece.at[:, :, pl.ds(head * PAIR, PAIR)],
                    stores[head % 2].at[pl.ds(place, rows)],
                    load_sem.at[head, index],
                )
            )
            place += rows
        return copies

    def load(head):
        for copy in loads(head):
            copy.start()

    def work(head):
        for copy in loads(head):
            copy.wait()
        if head + 1 < heads:
            load(head + 1)
        wide_query[...] = widen(joined_ref[:, head_columns(head, heads * PAIR)])
        forward_head(
            slots,
            head,
            index_ref,
            valid_ref,
            stores[head % 2],
            wide_query,
            wide_context,
            logsum_ref.at[:, pl.ds(head * PAIR, PAIR)],
        )
        rows = sent.shape[1]
        for place in range(sent.shape[0]):
            sent[place, :, head_columns(head)] = wide_context[
                place * rows : (place + 1) * rows, BLOCK:
            ]

    def send_block(index):
        target = (beside, above, facing)[index]
        return remote(
            sent.at[target],
            context_ref.at[chip],
            block_sems[0].at[index],
            block_sems[1].at[index],
            {SEQ: 2 * target + core},
        )

    load(0)
    longs.start()
    for weight in weights:
        weight.start()
    work(0)
    for part in range(parts):
        longs.step(1, part)
    for weight in weights:
        weight.forward()
    work(1)
    for part in range(parts):
        longs.step(2, part)
    work(2)
    for index in range(3):
        send_block(index).start()
    context_ref[chip] = sent[chip]
    for weight in weights:
        weight.arrive()
    for part in range(parts):
        longs.step(3, part)
    longs.finish()
    for weight in weights:
        weight.finish()
    for index in range(3):
        send_block(index).wait()


def third_exchange(
    longs, column, index, valid, joined, pieces, cuts, heads, slots, collective_id, parts=2
):
    near = jax.ShapeDtypeStruct((column.shape[0],) + longs.shape, longs.dtype)
    chips = lax.axis_size(SEQ) // 2
    rows = joined.shape[0]
    stored = sum(piece.shape[0] for piece in pieces) + rows
    context = jax.ShapeDtypeStruct((chips, rows // chips, heads * BLOCK), joined.dtype)
    resident = pl.BlockSpec(memory_space=pltpu.VMEM)
    scalars = pl.BlockSpec(memory_space=pltpu.SMEM)
    anywhere = pl.BlockSpec(memory_space=pl.ANY)
    dma = pltpu.SemaphoreType.DMA
    sems = [sem for _ in cuts for sem in weight_sems()]
    return pl.pallas_call(
        functools.partial(third_kernel, parts, cuts, slots, heads),
        out_shape=[near, near, context, jax.ShapeDtypeStruct((rows, heads * PAIR), f32)]
        + [weight_shape(column, cut) for cut in cuts],
        in_specs=[scalars] * 2 + [resident] * 3 + [anywhere] * 3,
        out_specs=[resident] * (4 + len(cuts)),
        scratch_shapes=[
            pltpu.VMEM((stored // BLOCK, BLOCK, PAIR), bf16),
            pltpu.VMEM((stored // BLOCK, BLOCK, PAIR), bf16),
            pltpu.VMEM((rows, PAIR), bf16),
            pltpu.VMEM((rows, PAIR), bf16),
            pltpu.VMEM(context.shape, bf16),
            dma((heads, 3)),
            dma,
            dma((3,)),
            dma((3,)),
        ]
        + column_sems(parts)
        + sems,
        compiler_params=pltpu.CompilerParams(
            collective_id=collective_id, has_side_effects=True, vmem_limit_bytes=52 * 2**20
        ),
        cost_estimate=lasting(62),
    )(
        index,
        valid,
        longs,
        column,
        joined,
        *(piece.reshape(-1, BLOCK, piece.shape[1]) for piece in pieces + [joined]),
    )


class ColumnReduce:

    def __init__(self, parts, step_rows, sums, came, sems):
        self.parts, self.step_rows = parts, step_rows
        self.sums, self.came, self.sems = sums, came, sems
        self.count = lax.axis_size(TP)
        self.place = lax.axis_index(TP)
        self.rows = sums.shape[1] // parts
        self.order = []
        for step in range(self.count):
            for owner in (step, self.count - 1 - step):
                if owner not in self.order:
                    self.order.append(owner)

    def along(self, way, owner, part):
        at = pl.ds(part * self.rows, self.rows)
        return remote(
            self.sums.at[owner, at],
            self.came.at[way, owner, at],
            self.sems[0].at[way, owner, part],
            self.sems[1].at[way, owner, part],
            {TP: self.place - 1 if way == 0 else self.place + 1},
        )

    def add(self, owner, source, part):
        @pl.loop(0, self.rows // self.step_rows)
        def _(step):
            start = pl.multiple_of(part * self.rows + step * self.step_rows, self.step_rows)
            at = pl.ds(start, self.step_rows)
            total = self.sums[owner, at, :].astype(f32) + source[at, :].astype(f32)
            self.sums[owner, at, :] = total.astype(self.sums.dtype)

    def takes(self, way):
        return self.place < self.count - 1 if way == 0 else self.place > 0

    def passes(self, way, owner):
        return self.place > owner if way == 0 else self.place < owner

    def begin(self, owner, part):
        for way in range(2):

            @pl.when(self.passes(way, owner) & ~self.takes(way))
            def _():
                self.along(way, owner, part).start()

    def move(self, way, owner, part):
        @pl.when(self.passes(way, owner) & self.takes(way))
        def _():
            self.along(way, owner, part).wait_recv()
            self.add(owner, self.came.at[way, owner], part)
            self.along(way, owner, part).start()

    def end(self):
        for part in range(self.parts):
            for way in range(2):
                for owner in range(self.count):

                    @pl.when((self.place == owner) & self.takes(way))
                    def _():
                        self.along(way, owner, part).wait_recv()
                        self.add(owner, self.came.at[way, owner], part)

    def finish(self):
        for owner in range(self.count):
            for part in range(self.parts):
                for way in range(2):

                    @pl.when(self.passes(way, owner))
                    def _():
                        self.along(way, owner, part).wait_send()

    def give(self, out):
        for owner in range(self.count):

            @pl.when(self.place == owner)
            def _():
                out[...] = self.sums[owner]


class PlaneReduce:

    def __init__(self, step_rows, terms, out, buffers, sems):
        self.step_rows, self.terms, self.out = step_rows, terms, out
        self.came, self.facing_came, self.sent, self.last = buffers
        self.sems = sems
        self.chip, core, beside, above, self.facing = plane_ids()
        self.ways = ({SEQ: 2 * beside + core}, {SEQ: 2 * above + core})
        self.chips = (beside, above)
        self.half = terms.shape[1] // 2

    def copy(self, kind, way, source, target, device):
        return remote(
            source, target.at[way], self.sems[0].at[kind, way], self.sems[1].at[kind, way], device
        )

    def pieces(self, way):
        return pl.ds(way * self.half, self.half)

    def facing_term(self, way):
        source = self.terms.at[self.facing, self.pieces(way)]
        return self.copy(0, way, source, self.facing_came, self.ways[way])

    def near_term(self, way):
        source = self.terms.at[self.chips[way], self.pieces(way)]
        return self.copy(1, way, source, self.came, self.ways[way])

    def summed(self, way):
        return self.copy(2, way, self.sent.at[way], self.last, self.ways[1 - way])

    def each_step(self, work):
        steps = self.terms.shape[2] // self.step_rows

        @pl.loop(0, self.half * steps)
        def _(step):
            start = pl.multiple_of((step % steps) * self.step_rows, self.step_rows)
            work(step // steps, pl.ds(start, self.step_rows))

    def start(self):
        for way in range(2):
            self.facing_term(way).start()
        for way in range(2):
            self.near_term(way).start()

    def move(self):
        for way in range(2):
            self.facing_term(way).wait_recv()

            def add_term(piece, at):
                total = self.terms[self.chips[1 - way], way * self.half + piece, at, :].astype(f32)
                total = total + self.facing_came[way, piece, at, :].astype(f32)
                self.sent[way, piece, at, :] = total.astype(self.sent.dtype)

            self.each_step(add_term)
            self.summed(way).start()

    def end(self):
        for way in range(2):
            self.near_term(way).wait_recv()
            self.summed(way).wait_recv()

            def add_last(piece, at):
                total = self.terms[self.chip, way * self.half + piece, at, :].astype(f32)
                total = total + self.came[way, piece, at, :].astype(f32)
                total = total + self.last[way, piece, at, :].astype(f32)
                self.out[way * self.half + piece, at, :] = total.astype(self.out.dtype)

            self.each_step(add_last)

    def finish(self):
        for way in range(2):
            self.facing_term(way).wait_send()
            self.near_term(way).wait_send()
            self.summed(way).wait_send()


def reduce_scratch(shape, dtype):
    half = pltpu.VMEM((2, shape[1] // 2) + shape[2:], dtype)
    sems = pltpu.SemaphoreType.DMA((3, 2))
    return [half] * 4 + [sems, sems]


def fourth_kernel(parts, cuts, near_ref, far_ref, *refs):
    count = len(cuts) - 1
    terms, givens, refs = refs[:count], refs[count : 2 * count], refs[2 * count :]
    out_ref, dense_ref, sums, given, came, dense, more = refs[:7]
    load_sem, send_far, recv_far, send_z, recv_z = refs[7:12]
    buffers, sems = refs[12:16], refs[16:18]
    place = lax.axis_index(TP)
    chip, core = plane_ids()[:2]
    other = {SEQ: 2 * chip + 1 - core}
    loads = [pltpu.make_async_copy(near_ref, sums, load_sem.at[0])]
    for index in range(count):
        rows = pl.ds(cuts[index], cuts[index + 1] - cuts[index])
        loads.append(
            pltpu.make_async_copy(
                terms[index], dense.at[:, :, rows], load_sem.at[1 + 2 * index]
            )
        )
        loads.append(
            pltpu.make_async_copy(givens[index], more.at[:, :, rows], load_sem.at[2 + 2 * index])
        )
    for load in loads:
        load.start()
    enter(neighbours(False, False))
    step_rows = dense.shape[2] // 2
    column = ColumnReduce(parts, sums.shape[1] // parts // 2, sums, came, (send_z, recv_z))
    plane = PlaneReduce(step_rows, dense, dense_ref, buffers, sems)

    def across(owner):
        return remote(
            far_ref.at[owner], given.at[owner], send_far.at[owner], recv_far.at[owner], other
        )

    def move(steps):
        for part in range(parts):
            for way, owner in steps:
                column.move(way, owner, part)

    for owner in column.order:
        across(owner).start()
    for load in loads:
        load.wait()
    pieces, steps = dense.shape[1], dense.shape[2] // step_rows

    @pl.loop(0, dense.shape[0] * pieces * steps)
    def _(step):
        at = pl.ds(pl.multiple_of((step % steps) * step_rows, step_rows), step_rows)
        piece = (step // steps) % pieces
        where = step // (steps * pieces)
        total = dense[where, piece, at, :].astype(f32) + more[where, piece, at, :].astype(f32)
        dense[where, piece, at, :] = total.astype(dense.dtype)

    plane.start()
    for owner in column.order:
        across(owner).wait_recv()
        for part in range(parts):
            column.add(owner, given.at[owner], part)
            column.begin(owner, part)
    last = column.count - 1

    @pl.when(place == last - 1)
    def _():
        move([(0, 0)])

    @pl.when(place == 1)
    def _():
        move([(1, last)])

    plane.move()

    @pl.when(place == last - 1)
    def _():
        move([(0, 1), (1, last)])

    @pl.when(place == 1)
    def _():
        move([(1, last - 1), (0, 0)])

    column.end()
    column.give(out_ref)
    plane.end()
    column.finish()
    plane.finish()
    for owner in column.order:
        across(owner).wait_send()


def fourth_exchange(near, far, terms, givens, cuts, collective_id, parts=2):
    count = lax.axis_size(TP)
    block = near.shape[1:]
    chips = givens[0].shape[0]
    width = givens[0].shape[-1]
    dense = (chips, count, cuts[-1], width)
    resident = pl.BlockSpec(memory_space=pltpu.VMEM)
    anywhere = pl.BlockSpec(memory_space=pl.ANY)
    dma = pltpu.SemaphoreType.DMA
    pieces = len(cuts) - 1
    return pl.pallas_call(
        functools.partial(fourth_kernel, parts, cuts),
        out_shape=[
            jax.ShapeDtypeStruct(block, near.dtype),
            jax.ShapeDtypeStruct(dense[1:], near.dtype),
        ],
        in_specs=[anywhere, resident] + [anywhere] * (2 * pieces),
        out_specs=[resident] * 2,
        scratch_shapes=[
            pltpu.VMEM((count,) + block, near.dtype),
            pltpu.VMEM((count,) + block, near.dtype),
            pltpu.VMEM((2, count) + block, near.dtype),
            pltpu.VMEM(dense, near.dtype),
            pltpu.VMEM(dense, near.dtype),
            dma((1 + 2 * pieces,)),
            dma((count,)),
            dma((count,)),
            dma((2, count, parts)),
            dma((2, count, parts)),
        ]
        + reduce_scratch(dense, near.dtype),
        compiler_params=pltpu.CompilerParams(
            collective_id=collective_id, has_side_effects=True, vmem_limit_bytes=52 * 2**20
        ),
        cost_estimate=lasting(62),
    )(near, far, *terms, *givens)


def fifth_kernel(rows_ref, dense_ref, out_ref, own_ref, came, send_z, recv_z, *refs):
    buffers, sems = refs[:4], refs[4:6]
    count = lax.axis_size(TP)
    place = lax.axis_index(TP)
    enter(neighbours(False, True))
    plane = PlaneReduce(rows_ref.shape[2] // 2, rows_ref, out_ref, buffers, sems)

    def to_owner(step):
        owner = lax.rem(place + step, count)
        return remote(
            dense_ref.at[owner], came.at[step - 1], send_z.at[step], recv_z.at[step], {TP: owner}
        )

    plane.start()
    for step in range(1, count):
        to_owner(step).start()
    plane.move()
    plane.end()
    for step in range(1, count):
        to_owner(step).wait()

    step_rows = own_ref.shape[0] // 2

    @pl.loop(0, 2)
    def _(step):
        at = pl.ds(pl.multiple_of(step * step_rows, step_rows), step_rows)
        total = dense_ref[place, at, :].astype(f32)
        for other in range(count - 1):
            total = total + came[other, at, :].astype(f32)
        own_ref[at, :] = total.astype(own_ref.dtype)

    plane.finish()


def fifth_exchange(rows, dense, collective_id):
    count = lax.axis_size(TP)
    resident = pl.BlockSpec(memory_space=pltpu.VMEM)
    dma = pltpu.SemaphoreType.DMA
    return pl.pallas_call(
        fifth_kernel,
        out_shape=[
            jax.ShapeDtypeStruct(rows.shape[1:], f32),
            jax.ShapeDtypeStruct(dense.shape[1:], dense.dtype),
        ],
        in_specs=[resident] * 2,
        out_specs=[resident] * 2,
        scratch_shapes=[
            pltpu.VMEM((count - 1,) + dense.shape[1:], dense.dtype),
            dma((count,)),
            dma((count,)),
        ]
        + reduce_scratch(rows.shape, rows.dtype),
        compiler_params=pltpu.CompilerParams(
            collective_id=collective_id, has_side_effects=True, vmem_limit_bytes=48 * 2**20
        ),
        cost_estimate=lasting(30),
    )(rows, dense)


def sixth_kernel(
    parts,
    terms_ref,
    own_ref,
    rows_ref,
    out_ref,
    dense_ref,
    all_ref,
    sums,
    given,
    came,
    send_far,
    recv_far,
    send_z,
    recv_z,
    send_plane,
    recv_plane,
    send_on,
    send_back,
    recv_back,
    keep_sem,
    send_row,
    recv_row,
    send_next,
    recv_next,
    send_dense,
    recv_dense,
    column_came,
    plane_came,
    send_all,
    recv_all,
):
    chip, core, beside, above, facing = plane_ids()
    count = lax.axis_size(TP)
    place = lax.axis_index(TP)
    other = {SEQ: 2 * chip + 1 - core}
    ways = ({SEQ: 2 * beside + core}, {SEQ: 2 * above + core})
    rows = sums.shape[0]
    part_rows = rows // parts
    always = place >= 0
    holds = place == chip
    far_column = [
        (always, {SEQ: 2 * chip + 1 - core, TP: lax.rem(place + step, count)})
        for step in range(1, count)
    ]
    enter(neighbours(True, True) + far_column)
    half = own_ref.shape[0] // 2
    dense = PlaneSpread(
        lambda part: own_ref.at[pl.ds(part * half, half)],
        lambda where, part: dense_ref.at[where, core, pl.ds(part * half, half)],
        (send_row, recv_row, send_next, recv_next),
    )
    keep = pltpu.make_async_copy(own_ref, dense_ref.at[chip, core], keep_sem)

    def dense_across(where):
        block = dense_ref.at[(chip, beside, above, facing)[where], core]
        return remote(block, block, send_dense.at[where], recv_dense.at[where], other)

    mine = core * count + place

    def column_copy(index):
        peer = lax.rem(mine + index, 2 * count)
        return remote(
            rows_ref,
            column_came.at[mine],
            send_all.at[index],
            recv_all.at[index],
            {SEQ: 2 * chip + peer // count, TP: lax.rem(peer, count)},
        )

    def column_landed(index):
        sender = lax.rem(mine + 2 * count - index, 2 * count)
        block = column_came.at[sender]
        return remote(block, block, send_all.at[index], recv_all.at[index], other)

    def plane_copy(index):
        return remote(
            plane_came.at[chip],
            plane_came.at[chip],
            send_all.at[2 * count + index],
            recv_all.at[2 * count + index],
            {SEQ: 2 * (beside, above, facing)[index] + core},
        )

    dense.start()
    keep.start()
    column_came[mine] = rows_ref[...]
    for index in range(1, 2 * count):
        column_copy(index).start()

    def cut(part):
        return pl.ds(part * part_rows, part_rows)

    def own_cut(part):
        return pl.ds(pl.multiple_of(core * rows + part * part_rows, 16), part_rows)

    across = remote(
        terms_ref.at[pl.ds(pl.multiple_of((1 - core) * rows, 16), rows)], given, send_far, recv_far, other
    )
    across.start()

    def along(way, part):
        return remote(
            sums.at[cut(part)],
            came.at[way, cut(part)],
            send_z.at[way, part],
            recv_z.at[way, part],
            {TP: place - 1 if way == 0 else place + 1},
        )

    def add(source, part):
        total = sums[cut(part), :].astype(f32) + source[cut(part), :].astype(f32)
        sums[cut(part), :] = total.astype(sums.dtype)

    def to_plane(way, part):
        return remote(
            out_ref.at[own_cut(part)],
            out_ref.at[own_cut(part)],
            send_plane.at[way, part],
            recv_plane.at[part],
            ways[way],
        )

    def onward(part):
        return remote(
            out_ref.at[own_cut(part)],
            out_ref.at[own_cut(part)],
            send_on.at[part],
            recv_plane.at[part],
            ways[1 - part // (parts // 2)],
        )

    def back(part):
        return remote(
            out_ref.at[own_cut(part)],
            out_ref.at[own_cut(part)],
            send_back.at[part],
            recv_back.at[part],
            other,
        )

    across.wait_recv()
    keep.wait()
    dense_across(0).start()
    for part in range(parts):
        sums[cut(part), :] = terms_ref[own_cut(part), :]
        add(given, part)
        for way in range(2):
            passes = place > chip if way == 0 else place < chip
            takes = place < count - 1 if way == 0 else place > 0

            @pl.when(passes)
            def _():
                @pl.when(takes)
                def _():
                    along(way, part).wait_recv()
                    add(came.at[way], part)

                along(way, part).start()

    dense.forward()
    for part in range(parts):
        for way in range(2):
            takes = place < count - 1 if way == 0 else place > 0

            @pl.when(holds & takes)
            def _():
                along(way, part).wait_recv()
                add(came.at[way], part)

        @pl.when(holds)
        def _():
            out_ref[own_cut(part), :] = sums[cut(part), :]
            for way in range(2):
                to_plane(way, part).start()
            back(part).start()

    for index in range(1, 2 * count):
        column_landed(index).wait_recv()
    total = column_came[0]
    for index in range(1, 2 * count):
        total = total + column_came[index]
    plane_came[chip] = total
    for index in range(3):
        plane_copy(index).start()
    dense.arrive()
    for where in range(1, 4):
        dense_across(where).start()
    for part in range(parts):

        @pl.when(place != chip)
        def _():
            to_plane(0, part).wait_recv()

        @pl.when((beside if part < parts // 2 else above) == place)
        def _():
            onward(part).start()

        @pl.when(place != chip)
        def _():
            back(part).start()

    for index in range(1, 2 * count):
        column_copy(index).wait_send()
    for index in range(3):
        plane_copy(index).wait()
    total = plane_came[0]
    for index in range(1, plane_came.shape[0]):
        total = total + plane_came[index]
    all_ref[...] = total
    across.wait_send()
    dense.finish()
    for where in range(4):
        dense_across(where).wait()
    for part in range(parts):
        back(part).wait()

        @pl.when((beside if part < parts // 2 else above) == place)
        def _():
            onward(part).wait_send()

        for way in range(2):

            @pl.when(holds)
            def _():
                to_plane(way, part).wait_send()

            @pl.when(place > chip if way == 0 else place < chip)
            def _():
                along(way, part).wait_send()


def sixth_exchange(terms, own, small, collective_id):
    parts = 4
    chips = lax.axis_size(SEQ) // 2
    column = 2 * lax.axis_size(TP)
    rows = terms.shape[0] // 2
    half = (rows,) + terms.shape[1:]
    dma = pltpu.SemaphoreType.DMA
    resident = pl.BlockSpec(memory_space=pltpu.VMEM)
    return pl.pallas_call(
        functools.partial(sixth_kernel, parts),
        out_shape=[
            jax.ShapeDtypeStruct(terms.shape, terms.dtype),
            jax.ShapeDtypeStruct((chips, 2) + own.shape, own.dtype),
            jax.ShapeDtypeStruct(small.shape, small.dtype),
        ],
        in_specs=[resident] * 3,
        out_specs=[resident] * 3,
        scratch_shapes=[
            pltpu.VMEM(half, terms.dtype),
            pltpu.VMEM(half, terms.dtype),
            pltpu.VMEM((2,) + half, terms.dtype),
            dma,
            dma,
            dma((2, parts)),
            dma((2, parts)),
            dma((2, parts)),
            dma((parts,)),
            dma((parts,)),
            dma((parts,)),
            dma((parts,)),
            dma,
        ]
        + plane_sems()
        + [
            dma((4,)),
            dma((4,)),
            pltpu.VMEM((column,) + small.shape, small.dtype),
            pltpu.VMEM((chips,) + small.shape, small.dtype),
            dma((column + 3,)),
            dma((column + 3,)),
        ],
        compiler_params=pltpu.CompilerParams(
            collective_id=collective_id, has_side_effects=True, vmem_limit_bytes=32 * 2**20
        ),
        cost_estimate=lasting(35),
    )(terms, own, small)


def plane_applies(mesh, blocks, docs):
    seq_count, tp_count = mesh.shape[SEQ], mesh.shape[TP]
    groups = seq_count * tp_count
    return (
        tp_count == 4
        and seq_count == 2 * tp_count
        and blocks == groups * SHORT_BLK
        and 2 * tp_count * SHORT_BLK == LONG_BLK
        and blocks - SHORT_BLK * docs == 2 * (LONG_BLK - SHORT_BLK)
    )


class Micro:
    pass


def plane_body(
    tokens,
    doc_lengths,
    rand_blocks,
    query_weight,
    key_weight,
    value_weight,
    query_bias,
    value_bias,
    proj_weight,
    proj_bias,
    first_gain,
    first_bias,
    second_gain,
    second_bias,
    inner_weight,
    inner_bias,
    outer_weight,
    outer_bias,
    out_grad,
):
    micro_count, own_rows, model_width = tokens.shape
    seq_count = lax.axis_size(SEQ)
    tp_count = lax.axis_size(TP)
    chips = seq_count // 2
    seq_place = lax.axis_index(SEQ)
    tp_place = lax.axis_index(TP)
    chip = lax.shift_right_logical(seq_place, 1)
    core = seq_place & 1
    heads = rand_blocks.shape[2]
    rands = rand_blocks.shape[3]
    local_width = query_weight.shape[1]
    head_size = local_width // heads
    pair_width = heads * PAIR
    hidden_units = inner_weight.shape[1]
    classes = 2 * tp_count
    class_bits = classes.bit_length() - 1
    group_bits = SHORT_BLK.bit_length() - 1
    own_class = core * tp_count + tp_place
    long_docs = 2
    slots = 5 + rands
    group_rows = chips * own_rows
    score_scale = 1.0 / math.sqrt(head_size)

    def by_head(values):
        return values.reshape(values.shape[:-1] + (heads, -1))

    def side_by_side(first, second):
        paired = jnp.concatenate([by_head(first), by_head(second)], axis=-1)
        return paired.reshape(paired.shape[:-2] + (pair_width,))

    def low_half(wide):
        return by_head(wide)[..., :head_size].reshape(wide.shape[:-1] + (local_width,))

    def high_half(wide):
        return by_head(wide)[..., head_size:].reshape(wide.shape[:-1] + (local_width,))

    def slot_rows(values, slot):
        return values[slot * own_rows : (slot + 1) * own_rows]

    stage = [Micro() for _ in range(micro_count)]
    spare_rows = 128
    packed = jnp.concatenate([side_by_side(key_weight, value_weight), query_weight], axis=1)
    packed_bias = jnp.concatenate(
        [side_by_side(jnp.zeros_like(value_bias), value_bias), query_bias]
    )
    packed = jnp.concatenate([packed, packed_bias[None]], axis=0)
    packed = jnp.pad(packed, ((0, spare_rows - 1), (0, -packed.shape[1] % 128)))
    randoms = rand_blocks.reshape(-1)
    random_count = randoms.shape[0]
    randoms = jnp.pad(randoms, (0, -random_count % 1024)).reshape(-1, 128)
    for micro, held in enumerate(stage):
        held.inputs = tokens[micro].astype(f32)
        shifted, held.stats_one, held.inverse_one = layer_stats(
            held.inputs, first_gain, first_bias
        )
        held.low = shifted.astype(bf16)
    unit_cut = hidden_units // seq_count
    proj_cut = local_width // seq_count
    rest_rows = -(-(proj_cut + 1) // 16) * 16
    cuts = (0, rest_rows, rest_rows + unit_cut, rest_rows + 2 * unit_cut)

    def padded(row_values):
        return jnp.pad(row_values, [(0, 0)] * (row_values.ndim - 1) + [(0, model_width - unit_cut)])

    share = jnp.concatenate(
        [
            lax.dynamic_slice_in_dim(proj_weight, seq_place * proj_cut, proj_cut, axis=0),
            padded(lax.dynamic_slice_in_dim(inner_bias, seq_place * unit_cut, unit_cut)[None]),
            jnp.zeros((rest_rows - proj_cut - 1, model_width), bf16),
            lax.dynamic_slice_in_dim(inner_weight, seq_place * unit_cut, unit_cut, axis=1).T,
            lax.dynamic_slice_in_dim(outer_weight, seq_place * unit_cut, unit_cut, axis=0),
        ],
        axis=0,
    )
    one, packed, column, randoms = first_exchange(stage[0].low, packed, share, randoms, 1)
    stage[0].one = one.reshape(group_rows, model_width)
    pair_wide = packed[:model_width, :pair_width]
    pair_wide_bias = packed[model_width, :pair_width]
    query_part = packed[:model_width, pair_width : pair_width + local_width]
    query_part_bias = packed[model_width, pair_width : pair_width + local_width]
    joined_weight = jnp.concatenate([pair_wide, query_part * score_scale], axis=1)
    joined_bias = jnp.concatenate([pair_wide_bias, query_part_bias * score_scale])

    starts = jnp.cumsum(doc_lengths, axis=1) - doc_lengths
    is_long = doc_lengths == LONG_BLK
    long_firsts = jnp.min(jnp.where(is_long, starts, jnp.iinfo(jnp.int32).max), axis=1)
    long_lasts = jnp.max(jnp.where(is_long, starts, -1), axis=1)
    first_groups = lax.shift_right_logical(jnp.stack([long_firsts, long_lasts]), group_bits)
    own_groups = first_groups + ((own_class - first_groups) & (classes - 1))
    long_rows = lax.shift_right_logical(own_groups, class_bits) * own_rows
    randoms = randoms.reshape(chips, -1)[:, :random_count]
    randoms = randoms.reshape(chips, micro_count, tp_count, SHORT_BLK, heads, rands)
    randoms = lax.dynamic_index_in_dim(randoms, tp_place, axis=2, keepdims=False)
    randoms = jnp.pad(randoms.transpose(1, 3, 0, 2, 4), [(0, 0)] * 4 + [(slots - rands, 0)])
    randoms = randoms.reshape(micro_count, -1)
    shape = (heads, chips, SHORT_BLK, slots)
    slot, block, entry = (part.reshape(-1) for part in np.indices(shape, np.int32)[1:])
    for micro, held in enumerate(stage):
        group = slot * classes + own_class
        number = group * SHORT_BLK + block
        in_long = [
            (number >= start[micro]) & (number < start[micro] + LONG_BLK)
            for start in (long_firsts, long_lasts)
        ]
        window_first = jnp.where(
            in_long[0],
            long_firsts[micro],
            jnp.where(in_long[1], long_lasts[micro], group * SHORT_BLK),
        )
        any_long = in_long[0] | in_long[1]
        window_final = window_first + jnp.where(any_long, LONG_BLK, SHORT_BLK)
        key = randoms[micro]
        for place, value in enumerate(
            (
                jnp.maximum(number - 1, window_first),
                jnp.minimum(number + 1, window_final - 1),
                number,
                window_first,
                window_first + 1,
            )
        ):
            key = jnp.where(entry == place, value, key)
        inside = key & (SHORT_BLK - 1)
        key_class = lax.shift_right_logical(key, group_bits) & (classes - 1)
        own_core = lax.shift_right_logical(key_class, class_bits - 1) == core
        piece = (key_class & (tp_count - 1)) + jnp.where(own_core, 0, tp_count)
        long_place = piece * long_docs + jnp.where(in_long[1], 1, 0)
        short_place = classes * long_docs + slot
        held.index = jnp.where(any_long, long_place, short_place) * SHORT_BLK + inside
        counts = jnp.where(entry == 0, number > window_first, number + 1 < window_final)
        counts = counts.astype(jnp.int32)[: chips * SHORT_BLK * slots]
        held.valid = counts.reshape(-1, slots)[:, :2].reshape(-1)
        held.long_rows = [long_rows[doc, micro] for doc in range(long_docs)]

    def long_blocks(micro):
        held = stage[micro]
        held.joined = (contract(held.one, joined_weight, NN) + joined_bias).astype(bf16)
        longs = jnp.concatenate(
            [
                lax.dynamic_slice(held.joined, (start, 0), (own_rows, pair_width))
                for start in held.long_rows
            ],
            axis=0,
        )
        return longs

    def keep_pieces(micro, near, far):
        stage[micro].pieces = [near.reshape(-1, pair_width), far.reshape(-1, pair_width)]

    def attend(micro):
        held = stage[micro]
        index = after(held.index, stage[micro - 1].grad_context_sent)
        held.context_sent, held.logsum = attend_forward(
            index, held.valid, held.joined, held.pieces, heads, slots
        )
        held.context = plane_exchange(held.context_sent, 0, 1)

    def feed_forward(micro):
        held = stage[micro]
        if micro:
            held.context = after(
                held.context, stage[micro - 1].long_sum_sent
            )
        hidden = held.inputs + contract(held.context, proj_full, NN) + proj_bias
        shifted, stats, inverse = layer_stats(hidden, second_gain, second_bias)
        held.two = shifted.astype(bf16)
        before = contract(held.two, inner_full, NT) + inner_bias_full
        held.active = gelu_exact(before).astype(bf16)
        result = hidden + contract(held.active, outer_full, NN) + outer_bias
        held.output = result.astype(bf16)
        held.grad_out = out_grad[micro]
        grad_float = held.grad_out.astype(f32)
        grad_active = contract(held.grad_out, outer_full, NT)
        held.grad_before = gelu_grad(before, grad_active).astype(bf16)
        grad_two = contract(held.grad_before, inner_full, NN)
        back, gain_sum, shift_sum = layer_back(grad_two, stats, inverse, second_gain)
        held.grad_hidden = grad_float + back
        held.branch = held.grad_hidden.astype(bf16)
        held.grad_context_sent = jnp.stack(
            [
                contract(
                    held.branch, proj_full[part * local_width : (part + 1) * local_width], NT
                ).astype(bf16)
                for part in range(chips)
            ]
        )
        held.grad_context = plane_exchange(held.grad_context_sent, 0, 0).reshape(
            group_rows, local_width
        )
        held.unit_sum = jnp.sum(held.grad_before.astype(f32), axis=0)
        held.row_sums = jnp.stack(
            [
                gain_sum,
                shift_sum,
                jnp.sum(held.branch.astype(f32), axis=0),
                jnp.sum(grad_float, axis=0),
            ]
        )

    def attend_back(micro, *earlier):
        held = stage[micro]
        near, far, held.grad_joined = attend_backward(
            held.index,
            held.valid,
            held.joined,
            after(held.grad_context, *earlier),
            held.logsum,
            held.pieces,
            heads,
            slots,
        )
        return near, far

    def input_rows(micro, long_sum):
        held = stage[micro]
        shape = (chips, own_rows, pair_width + local_width)
        place, lane = np.indices(shape, np.int32, sparse=True)[::2]
        joined = held.grad_joined.reshape(shape)
        for doc, start in enumerate(held.long_rows):
            long_part = jnp.pad(slot_rows(long_sum, doc), ((0, 0), (0, local_width)))
            joined = jnp.where((place * own_rows == start) & (lane < pair_width), long_part, joined)
        held.grad_joined = joined.reshape(group_rows, -1)
        rows = contract(held.grad_joined, joined_weight, NT)
        return rows.astype(bf16).reshape(chips, own_rows, model_width)

    def input_back(micro, grad_one):
        held = stage[micro]
        back, gain_sum, shift_sum = layer_back(
            grad_one, held.stats_one, held.inverse_one, first_gain
        )
        held.input_grad = held.grad_hidden + back
        held.first_sums = jnp.stack([gain_sum, shift_sum])

    longs = long_blocks(0)
    near, far, one, outer_full = second_exchange(longs, stage[1].low, column, cuts[2:4], 2)
    stage[1].one = one.reshape(group_rows, model_width)
    keep_pieces(0, near, far)
    longs = long_blocks(1)
    near, far, context, stage[0].logsum, rest, inner_full = third_exchange(
        longs,
        column,
        stage[0].index,
        stage[0].valid,
        stage[0].joined,
        stage[0].pieces,
        (cuts[0:2], cuts[1:3]),
        heads,
        slots,
        7,
    )
    keep_pieces(1, near, far)
    stage[0].context = context.transpose(1, 0, 2).reshape(own_rows, model_width)
    inner_full = inner_full.reshape(-1, model_width)
    outer_full = outer_full.reshape(-1, model_width)
    inner_bias_full = rest[:, :, :, proj_cut, :unit_cut].reshape(-1)
    proj_full = rest[:, :, :, :proj_cut].transpose(2, 1, 0, 3, 4)
    proj_full = proj_full.reshape(tp_count * local_width, model_width)
    feed_forward(0)
    attend(1)
    near, far = attend_back(0, stage[1].logsum, stage[1].context_sent)
    stage[0].long_sum_sent = sum_parts([near, core_swap(far)]).astype(bf16)
    long_sum = lax.psum_scatter(stage[0].long_sum_sent, TP, scatter_dimension=0, tiled=True)
    feed_forward(1)

    given_inner, given_outer, kept_inner, kept_outer, proj_part = dense_terms(
        after(core, stage[1].grad_context_sent),
        [[h.grad_before for h in stage], [h.active for h in stage], [h.context for h in stage]],
        [[h.two for h in stage], [h.grad_out for h in stage], [h.branch for h in stage]],
    )
    proj_part = proj_part.reshape(tp_count, chips, 2, proj_cut, model_width)
    unit_shape = (2, chips, tp_count)
    unit_sum = sum(h.unit_sum for h in stage).astype(bf16)
    rest_part = jnp.concatenate(
        [
            proj_part.transpose(2, 1, 0, 3, 4),
            padded(unit_sum.reshape(unit_shape + (1, unit_cut))),
            jnp.zeros(unit_shape + (rest_rows - proj_cut - 1, model_width), bf16),
        ],
        axis=3,
    )
    unit_shape = (chips, tp_count, -1, model_width)
    terms = [kept_inner.reshape(unit_shape), kept_outer.reshape(unit_shape)]
    givens = [core_swap(part.reshape(unit_shape)) for part in (given_inner, given_outer)]
    terms.append(lax.dynamic_index_in_dim(rest_part, core, axis=0, keepdims=False))
    givens.append(
        core_swap(lax.dynamic_index_in_dim(rest_part, 1 - core, axis=0, keepdims=False))
    )

    rows = input_rows(0, after(long_sum, kept_inner))
    grad_one = lax.psum_scatter(
        rows.reshape(group_rows, model_width),
        SEQ,
        scatter_dimension=0,
        axis_index_groups=[list(range(place, seq_count, 2)) for place in range(2)],
        tiled=True,
    )
    near, far = attend_back(1, rows)

    column_shape = (tp_count, long_docs * own_rows, pair_width)
    cuts = (0, unit_cut, 2 * unit_cut, 2 * unit_cut + rest_rows)
    row_shape = (chips, 2, own_rows // 2, model_width)
    long_sum, quarters = fourth_exchange(
        near.reshape(column_shape), far.reshape(column_shape), terms, givens, cuts, 3
    )
    rows = input_rows(1, long_sum)
    grad_one_now, own_sum = fifth_exchange(rows.reshape(row_shape), quarters, 4)
    input_back(0, after(grad_one, rows).astype(f32))
    input_back(1, grad_one_now.reshape(own_rows, model_width))

    ones = after([h.one for h in stage], grad_one_now)
    packed_sum = sum(contract(one, h.grad_joined, TN) for one, h in zip(ones, stage))
    packed_sum = jnp.pad(packed_sum, ((0, 0), (0, -packed_sum.shape[1] % 128))).astype(bf16)

    def own_columns(values):
        wide = jnp.zeros((chips, local_width), f32)
        return lax.dynamic_update_slice_in_dim(wide, values[None], chip, axis=0).reshape(-1)

    joined_sum = sum(jnp.sum(h.grad_joined.astype(f32), axis=0) for h in stage)
    packed_sum, dense_sum, all_rows = sixth_exchange(
        packed_sum,
        own_sum,
        jnp.concatenate(
            [
                sum(h.row_sums for h in stage),
                sum(h.first_sums for h in stage),
                own_columns(joined_sum[pair_width:] * score_scale)[None],
                own_columns(high_half(joined_sum[:pair_width]))[None],
            ],
            axis=0,
        ),
        6,
    )
    key_grad = low_half(packed_sum[:, :pair_width]).astype(f32)
    value_grad = high_half(packed_sum[:, :pair_width]).astype(f32)
    query_grad = packed_sum[:, pair_width : pair_width + local_width].astype(f32) * score_scale
    dense_sum = dense_sum.reshape(seq_count, -1, model_width).astype(f32)
    inner_weight_grad = dense_sum[:, :unit_cut].reshape(hidden_units, model_width).T
    outer_weight_grad = dense_sum[:, unit_cut : 2 * unit_cut].reshape(hidden_units, model_width)
    rest = dense_sum[:, 2 * unit_cut :]
    proj_weight_grad = rest[:, :proj_cut].reshape(local_width, model_width)
    inner_bias_grad = rest[:, proj_cut, :unit_cut].reshape(hidden_units)

    def my_columns(row):
        return lax.dynamic_slice_in_dim(row, tp_place * local_width, local_width)

    return (
        jnp.stack([h.output for h in stage]),
        jnp.stack([h.input_grad for h in stage]),
        query_grad,
        key_grad,
        value_grad,
        my_columns(all_rows[6]),
        my_columns(all_rows[7]),
        proj_weight_grad,
        all_rows[2],
        all_rows[4],
        all_rows[5],
        all_rows[0],
        all_rows[1],
        inner_weight_grad,
        inner_bias_grad,
        outer_weight_grad,
        all_rows[3],
    )


def general_body(
    tokens,
    doc_lengths,
    rand_blocks,
    query_weight,
    key_weight,
    value_weight,
    query_bias,
    value_bias,
    proj_weight,
    proj_bias,
    first_gain,
    first_bias,
    second_gain,
    second_bias,
    inner_weight,
    inner_bias,
    outer_weight,
    outer_bias,
    out_grad,
):
    micro_count, local_rows, model_width = tokens.shape
    seq_count = lax.axis_size(SEQ)
    tp_count = lax.axis_size(TP)
    seq_place = lax.axis_index(SEQ)
    tp_place = lax.axis_index(TP)
    block_dev = rand_blocks.shape[1]
    heads = rand_blocks.shape[2]
    local_width = query_weight.shape[1]
    head_size = local_width // heads
    hidden_units = inner_weight.shape[1]
    group_rows = block_dev * BLOCK
    reach_dev = (block_dev + LONG_BLK - 2) // block_dev
    window = 2 * reach_dev + 1
    score_scale = 1.0 / math.sqrt(head_size)
    lowest = (seq_place - reach_dev) * block_dev
    blocks = seq_place * block_dev + jnp.arange(block_dev, dtype=jnp.int32)

    held = jnp.concatenate([inner_weight.T, outer_weight, proj_weight, inner_bias[None]], axis=0)
    used_rows = held.shape[0]
    piece_rows = -(-used_rows // (16 * seq_count)) * 16
    held_rows = piece_rows * seq_count
    held = jnp.pad(held, ((0, held_rows - used_rows), (0, 0)))
    share = lax.dynamic_slice_in_dim(held, seq_place * piece_rows, piece_rows, axis=0)
    spread = lax.all_gather(share, (TP, SEQ), axis=0, tiled=True)
    spread = spread.reshape(tp_count, held_rows, model_width)
    cuts = [0, hidden_units, 2 * hidden_units, 2 * hidden_units + local_width, used_rows]
    inner_full = spread[:, cuts[0] : cuts[1]].reshape(-1, model_width)
    outer_full = spread[:, cuts[1] : cuts[2]].reshape(-1, model_width)
    proj_full = spread[:, cuts[2] : cuts[3]].reshape(-1, model_width)
    inner_bias_full = spread[:, cuts[3] : cuts[4]].reshape(-1)

    def by_head(weight):
        return weight.reshape(weight.shape[:-1] + (heads, head_size))

    def side_by_side(first, second):
        paired = jnp.concatenate([by_head(first), by_head(second)], axis=-1)
        return paired.reshape(paired.shape[:-2] + (heads * PAIR,))

    pair_wide = side_by_side(key_weight, value_weight)
    pair_wide_bias = side_by_side(jnp.zeros_like(value_bias), value_bias)

    stage = [Micro() for _ in range(micro_count)]
    for micro, held in enumerate(stage):
        inputs = tokens[micro].astype(f32)
        shifted, stats, inverse = layer_stats(inputs, first_gain, first_bias)
        held.inputs, held.stats_one, held.inverse_one = inputs, stats, inverse
        held.one = lax.all_gather(shifted.astype(bf16), TP, axis=0, tiled=True)

    for micro, held in enumerate(stage):
        one = held.one
        pair_rows = (contract(one, pair_wide, NN) + pair_wide_bias).astype(bf16)
        offsets = [offset for offset in range(-reach_dev, reach_dev + 1) if offset != 0]
        pieces = [from_behind(pair_rows, SEQ, -offset) for offset in offsets]
        queries = ((contract(one, query_weight, NN) + query_bias) * score_scale).astype(bf16)
        held.joined = jnp.concatenate([pair_rows, queries], axis=1)
        key_index, key_valid = block_keys(doc_lengths[micro], rand_blocks[micro], blocks)
        slots = key_index.shape[2]
        slot_index = jnp.clip(key_index - lowest, 0, window * block_dev - 1)
        piece = slot_index // block_dev
        piece = jnp.where(piece == reach_dev, 2 * reach_dev, piece - (piece > reach_dev))
        slot_index = piece * block_dev + slot_index % block_dev
        held.index = slot_index.transpose(1, 0, 2).reshape(-1)
        held.valid = key_valid.reshape(-1)
        held.pieces = pieces

    for held in stage:
        context, held.logsum = attend_forward(
            held.index,
            held.valid,
            held.joined,
            held.pieces,
            heads,
            slots,
        )
        held.context = lax.all_to_all(context, TP, split_axis=0, concat_axis=1, tiled=True)

    outputs = []
    for micro, held in enumerate(stage):
        context = held.context
        hidden = held.inputs + contract(context, proj_full, NN) + proj_bias
        shifted, stats, inverse = layer_stats(hidden, second_gain, second_bias)
        two = shifted.astype(bf16)
        before = contract(two, inner_full, NT) + inner_bias_full
        active = gelu_exact(before).astype(bf16)
        result = hidden + contract(active, outer_full, NN) + outer_bias
        outputs.append(result.astype(bf16))
        grad_out = out_grad[micro]
        grad_float = grad_out.astype(f32)
        grad_active = contract(grad_out, outer_full, NT)
        grad_before = gelu_grad(before, grad_active).astype(bf16)
        grad_two = contract(grad_before, inner_full, NN)
        back, gain_sum, shift_sum = layer_back(grad_two, stats, inverse, second_gain)
        grad_hidden = grad_float + back
        branch = grad_hidden.astype(bf16)
        grad_context = contract(branch, proj_full, NT).astype(bf16)
        held.grad_context = lax.all_to_all(
            grad_context, TP, split_axis=1, concat_axis=0, tiled=True
        )
        held.grad_hidden = grad_hidden
        held.dense = (two, grad_before, active, grad_out, context, branch)
        held.row_sums = (
            jnp.sum(grad_before.astype(f32), axis=0),
            gain_sum,
            shift_sum,
            jnp.sum(branch.astype(f32), axis=0),
            jnp.sum(grad_float, axis=0),
        )

    two, grad_before, active, grad_out, context, branch = (
        jnp.concatenate(group, axis=0) for group in zip(*(h.dense for h in stage))
    )
    inner_part = contract(grad_before, two, TN).astype(bf16)
    outer_part = contract(active, grad_out, TN).astype(bf16)
    proj_part = contract(context, branch, TN).astype(bf16)
    grad_rows = 2 * hidden_units + local_width
    grad_piece = -(-grad_rows // (16 * seq_count)) * 16
    grad_held = grad_piece * seq_count
    parts = jnp.concatenate(
        [
            inner_part.reshape(tp_count, hidden_units, model_width),
            outer_part.reshape(tp_count, hidden_units, model_width),
            proj_part.reshape(tp_count, local_width, model_width),
            jnp.zeros((tp_count, grad_held - grad_rows, model_width), bf16),
        ],
        axis=1,
    ).reshape(tp_count * grad_held, model_width)
    own_part = lax.psum_scatter(parts, (TP, SEQ), scatter_dimension=0, tiled=True)
    dense_sum = lax.all_gather(own_part, SEQ, axis=0, tiled=True).astype(f32)
    inner_weight_grad = dense_sum[cuts[0] : cuts[1]].T
    outer_weight_grad = dense_sum[cuts[1] : cuts[2]]
    proj_weight_grad = dense_sum[cuts[2] : cuts[3]]

    for held in stage:
        *grad_pieces, joined = attend_backward(
            held.index,
            held.valid,
            held.joined,
            held.grad_context,
            held.logsum,
            held.pieces,
            heads,
            slots,
        )
        pair_width = heads * PAIR
        returned = joined[:, :pair_width].astype(f32)
        held.grad_query = joined[:, pair_width:]
        for offset, grad_piece in zip(offsets, grad_pieces):
            returned = returned + from_behind(grad_piece, SEQ, offset).astype(f32)
        held.grad_pair = returned.astype(bf16)

    input_grads = []
    query_sum = pair_sum = 0.0
    query_bias_sum = pair_bias_sum = 0.0
    first_gain_sum = first_bias_sum = 0.0
    for held in stage:
        grad_query, grad_pair, one = held.grad_query, held.grad_pair, held.one
        rows = contract(grad_query, query_weight * score_scale, NT) + contract(grad_pair, pair_wide, NT)
        grad_one = lax.psum_scatter(
            rows.astype(bf16), TP, scatter_dimension=0, tiled=True
        ).astype(f32)
        query_sum = query_sum + contract(one, grad_query, TN)
        pair_sum = pair_sum + contract(one, grad_pair, TN)
        query_bias_sum = query_bias_sum + jnp.sum(grad_query.astype(f32), axis=0)
        pair_bias_sum = pair_bias_sum + jnp.sum(grad_pair.astype(f32), axis=0)
        back, gain_sum, shift_sum = layer_back(
            grad_one, held.stats_one, held.inverse_one, first_gain
        )
        first_gain_sum = first_gain_sum + gain_sum
        first_bias_sum = first_bias_sum + shift_sum
        input_grads.append(held.grad_hidden + back)

    def low_half(wide):
        return wide.reshape(wide.shape[:-1] + (heads, PAIR))[..., :head_size].reshape(
            wide.shape[:-1] + (local_width,)
        )

    def high_half(wide):
        return wide.reshape(wide.shape[:-1] + (heads, PAIR))[..., head_size:].reshape(
            wide.shape[:-1] + (local_width,)
        )

    query_grad, key_grad, value_grad = lax.psum(
        (query_sum * score_scale, low_half(pair_sum), high_half(pair_sum)), SEQ
    )
    inner_bias_sum, second_gain_sum, second_bias_sum, proj_bias_sum, outer_bias_sum = (
        sum(group) for group in zip(*(h.row_sums for h in stage))
    )

    def own_columns(values):
        wide = jnp.zeros((tp_count, local_width), f32)
        return lax.dynamic_update_slice_in_dim(wide, values[None], tp_place, axis=0).reshape(-1)

    early = lax.psum(
        jnp.concatenate(
            [
                inner_bias_sum,
                second_gain_sum,
                second_bias_sum,
                proj_bias_sum,
                outer_bias_sum,
            ]
        ),
        (SEQ, TP),
    )
    late = lax.psum(
        jnp.concatenate(
            [
                first_gain_sum,
                first_bias_sum,
                own_columns(query_bias_sum * score_scale),
                own_columns(high_half(pair_bias_sum)),
            ]
        ),
        (SEQ, TP),
    )
    inner_bias_all = early[: tp_count * hidden_units].reshape(tp_count, hidden_units)
    early_rows = early[tp_count * hidden_units :].reshape(-1, model_width)
    late_rows = late.reshape(-1, model_width)

    def my_columns(row):
        return lax.dynamic_slice_in_dim(row, tp_place * local_width, local_width)

    return (
        jnp.stack(outputs),
        jnp.stack(input_grads),
        query_grad,
        key_grad,
        value_grad,
        my_columns(late_rows[2]),
        my_columns(late_rows[3]),
        proj_weight_grad,
        early_rows[2],
        late_rows[0],
        late_rows[1],
        early_rows[0],
        early_rows[1],
        inner_weight_grad,
        lax.dynamic_index_in_dim(inner_bias_all, tp_place, axis=0, keepdims=False),
        outer_weight_grad,
        early_rows[3],
    )


def solution(mesh):
    def choose(tokens, doc_lengths, rand_blocks, *rest):
        blocks = rand_blocks.shape[1] * mesh.shape[SEQ]
        if plane_applies(mesh, blocks, doc_lengths.shape[1]):
            return plane_body(tokens, doc_lengths, rand_blocks, *rest)
        return general_body(tokens, doc_lengths, rand_blocks, *rest)

    return jax.shard_map(
        choose,
        mesh=mesh,
        in_specs=(
            P(None, (SEQ, TP), None),
            P(),
            P(None, SEQ, TP, None),
            P(None, TP),
            P(None, TP),
            P(None, TP),
            P(TP),
            P(TP),
            P(TP, None),
            P(),
            P(),
            P(),
            P(),
            P(),
            P(None, TP),
            P(TP),
            P(TP, None),
            P(),
            P(None, (SEQ, TP), None),
        ),
        out_specs=(
            P(None, (SEQ, TP), None),
            P(None, (SEQ, TP), None),
            P(None, TP),
            P(None, TP),
            P(None, TP),
            P(TP),
            P(TP),
            P(TP, None),
            P(),
            P(),
            P(),
            P(),
            P(),
            P(None, TP),
            P(TP),
            P(TP, None),
            P(),
        ),
        check_vma=False,
    )
```

```python
import functools
import math

import jax
import jax.numpy as jnp
import numpy as np
from jax import lax
from jax.experimental import pallas as pl
from jax.experimental.pallas import tpu as pltpu
from jax.sharding import PartitionSpec as P

BLOCK = 64
LONG_BLK = 64
SHORT_BLK = 8
PAIR = 2 * BLOCK
UNROLL = 4
SEQ = "seq"
TP = "tp"

NORM_EPS = 1e-05
MASKED = -1000000000.0

f32 = jnp.float32
bf16 = jnp.bfloat16

NN = (((1,), (0,)), ((), ()))
NT = (((1,), (1,)), ((), ()))
TN = (((0,), (0,)), ((), ()))


def contract(left, right, dims):
    return lax.dot_general(left, right, dims, preferred_element_type=f32)


def from_behind(block, axis, distance):
    devices = range(lax.axis_size(axis))
    route = [(i - distance, i) for i in devices if i - distance in devices]
    return lax.ppermute(block, axis, route)


def gelu_exact(values):
    return 0.5 * values * (1.0 + lax.erf(values / math.sqrt(2.0)))


def gelu_grad(values, grad_rows):
    _, pull_back = jax.vjp(gelu_exact, values)
    return pull_back(grad_rows)[0]


def layer_stats(values, norm_gain, norm_shift):
    row_mean = jnp.mean(values, axis=-1, keepdims=True)
    centred = values - row_mean
    inverse = lax.rsqrt(jnp.mean(centred * centred, axis=-1, keepdims=True) + NORM_EPS)
    normed = centred * inverse
    return (normed * norm_gain + norm_shift, normed, inverse)


def layer_back(grad_rows, normed, inverse, norm_gain):
    scaled = grad_rows * norm_gain
    inner_term = (
        scaled
        - jnp.mean(scaled, axis=-1, keepdims=True)
        - normed * jnp.mean(scaled * normed, axis=-1, keepdims=True)
    )
    return (inverse * inner_term, jnp.sum(grad_rows * normed, axis=0), jnp.sum(grad_rows, axis=0))


def block_keys(lengths, randoms, blocks):
    doc_ends = jnp.cumsum(lengths)
    doc_starts = doc_ends - lengths
    doc_owner = jnp.sum((blocks[:, None] >= doc_ends[None, :]).astype(jnp.int32), axis=1)
    doc_ids = jnp.arange(lengths.shape[0], dtype=jnp.int32)
    doc_hit = doc_owner[:, None] == doc_ids[None, :]
    doc_first = jnp.sum(jnp.where(doc_hit, doc_starts[None, :], 0), axis=1)
    doc_final = jnp.sum(jnp.where(doc_hit, doc_ends[None, :], 0), axis=1)
    fixed_keys = jnp.stack(
        [
            jnp.maximum(blocks - 1, doc_first),
            jnp.minimum(blocks + 1, doc_final - 1),
            blocks,
            doc_first,
            doc_first + 1,
        ],
        axis=1,
    )
    block_count = randoms.shape[0]
    head_count = randoms.shape[1]
    key_index = jnp.concatenate(
        [jnp.broadcast_to(fixed_keys[:, None, :], (block_count, head_count, 5)), randoms], axis=2
    )
    key_valid = jnp.stack([blocks > doc_first, blocks + 1 < doc_final], axis=1)
    return (key_index, key_valid.astype(jnp.int32))


def block_rows(block):
    return pl.ds(pl.multiple_of(block * BLOCK, BLOCK), BLOCK)


def listed_blocks(index_ref, store, base, slots):
    return jnp.concatenate(
        [store[block_rows(index_ref[base + slot]), :] for slot in range(slots)], axis=0
    )


def mask_scores(scores, valid_ref, block):
    lane = lax.broadcasted_iota(jnp.int32, (1, PAIR), 1)
    keep = jnp.where(lane < BLOCK, valid_ref[2 * block], valid_ref[2 * block + 1]) > 0
    return jnp.concatenate([jnp.where(keep, scores[:, :PAIR], MASKED), scores[:, PAIR:]], axis=1)


def fill_store(store, pieces):
    place = 0
    for piece in pieces:
        store[place : place + piece.shape[0], :] = piece[...]
        place += piece.shape[0]


def each_head(heads, work):
    for head in range(heads):

        @pl.when(pl.program_id(0) == head)
        def _():
            work(head)


def head_columns(head, first=0):
    return slice(first + head * BLOCK, first + (head + 1) * BLOCK)


def forward_head(slots, head, index_ref, valid_ref, store, wide_query, wide_context, logsum_ref):
    blocks = wide_query.shape[0] // BLOCK

    def step(group, carry):
        ids = [group * UNROLL + unit for unit in range(UNROLL)]
        listed = []
        for block in ids:
            first = (head * blocks + block) * slots
            listed.append(
                jnp.concatenate([store[index_ref[first + slot]] for slot in range(slots)], axis=0)
            )
        scores = [
            mask_scores(contract(wide_query[block_rows(block), :], pairs, NT), valid_ref, block)
            for block, pairs in zip(ids, listed)
        ]
        probs = []
        for block, score in zip(ids, scores):
            top = jnp.max(score, axis=1, keepdims=True)
            raised = jnp.exp(score - top)
            total = jnp.sum(raised, axis=1, keepdims=True)
            probs.append((raised * (1.0 / total)).astype(bf16))
            logsum_ref[block_rows(block), :] = jnp.broadcast_to(
                top + jnp.log(total), (BLOCK, PAIR)
            )
        for block, prob, pairs in zip(ids, probs, listed):
            wide_context[block_rows(block), :] = contract(prob, pairs, NN).astype(bf16)
        return carry

    lax.fori_loop(0, blocks // UNROLL, step, 0)


def widen(query):
    return jnp.concatenate([query, jnp.zeros_like(query)], axis=1)


def forward_kernel(slots, heads, index_ref, valid_ref, query_ref, *refs):
    *pieces, context_ref, logsum_ref, store, wide_query, wide_context = refs
    place = 0
    for piece in pieces:
        count = piece.shape[0] // BLOCK
        store[place : place + count] = piece[...].reshape(count, BLOCK, PAIR)
        place += count

    def take_query(own):
        wide_query[...] = widen(query_ref[:, head_columns(own, heads * PAIR)])

    each_head(heads, take_query)
    forward_head(
        slots, pl.program_id(0), index_ref, valid_ref, store, wide_query, wide_context, logsum_ref
    )

    def give_context(own):
        context_ref[:, head_columns(own)] = wide_context[:, BLOCK:]

    each_head(heads, give_context)


def backward_kernel(slots, heads, count, index_ref, valid_ref, query_ref, grad_ref, logsum_ref, *refs):
    pieces, refs = refs[:count], refs[count:]
    grad_pieces, joined_ref = refs[: count - 1], refs[count - 1]
    store, sums, both_rows, wide_grad = refs[count:]
    rows = query_ref.shape[0]
    blocks = rows // BLOCK
    head = pl.program_id(0)
    fill_store(store, pieces)
    sums[...] = jnp.zeros_like(sums)
    lane = lax.broadcasted_iota(jnp.int32, (BLOCK, PAIR), 1)

    def take_both(own):
        query = query_ref[:, head_columns(own, heads * PAIR)]
        both_rows[...] = jnp.concatenate([query, grad_ref[:, head_columns(own)]], axis=1)

    each_head(heads, take_both)

    def step(group, carry):
        ids = [group * UNROLL + unit for unit in range(UNROLL)]
        listed = [
            listed_blocks(index_ref, store, (head * blocks + block) * slots, slots)
            for block in ids
        ]
        lefts = []
        for block in ids:
            both = both_rows[block_rows(block), :]
            lefts.append(
                jnp.concatenate(
                    [
                        jnp.where(lane < BLOCK, both, 0).astype(bf16),
                        jnp.where(lane < BLOCK, 0, both).astype(bf16),
                    ],
                    axis=0,
                )
            )
        products = [contract(left, pairs, NT) for left, pairs in zip(lefts, listed)]
        mixes = []
        for block, product in zip(ids, products):
            score = mask_scores(product[:BLOCK], valid_ref, block)
            grad_prob = product[BLOCK:]
            logsum = jnp.concatenate([logsum_ref[block_rows(block), :]] * (slots // 2), axis=1)
            prob = jnp.exp(score - logsum)
            delta = jnp.sum(prob * grad_prob, axis=1, keepdims=True)
            grad_score = prob * (grad_prob - delta)
            mixes.append(jnp.concatenate([grad_score.astype(bf16), prob.astype(bf16)], axis=0))
        for block, mix, pairs in zip(ids, mixes, listed):
            wide_grad[block_rows(block), :] = contract(mix[:BLOCK], pairs, NN).astype(bf16)
        terms = [contract(mix, left, TN) for mix, left in zip(mixes, lefts)]
        for block, term in zip(ids, terms):
            base = (head * blocks + block) * slots
            for slot in range(slots):
                sums[block_rows(index_ref[base + slot]), :] += term[
                    slot * BLOCK : (slot + 1) * BLOCK
                ]
        return carry

    lax.fori_loop(0, blocks // UNROLL, step, 0)
    place = 0
    for grad_piece in grad_pieces:
        grad_piece[...] = sums[place : place + grad_piece.shape[0], :].astype(bf16)
        place += grad_piece.shape[0]

    def give_joined(own):
        joined_ref[:, own * PAIR : (own + 1) * PAIR] = sums[place:, :].astype(bf16)
        start = heads * PAIR + own * BLOCK
        joined_ref[:, start : start + BLOCK] = wide_grad[:, :BLOCK]

    each_head(heads, give_joined)


def lasting(microseconds):
    return pl.CostEstimate(
        flops=0, bytes_accessed=int(microseconds * 3.69e6), transcendentals=0
    )


def per_head(array):
    return pl.BlockSpec((array.shape[0], PAIR), lambda head, *_: (0, head))


def whole(array):
    return pl.BlockSpec(array.shape, lambda head, *_: (0, 0))


def attend_forward(index, valid, joined, pieces, heads, slots):
    rows = joined.shape[0]
    pieces = pieces + [joined]
    context = jax.ShapeDtypeStruct((rows, heads * BLOCK), bf16)
    stored = sum(piece.shape[0] for piece in pieces)
    logsum = jax.ShapeDtypeStruct((rows, heads * PAIR), f32)
    return pl.pallas_call(
        functools.partial(forward_kernel, slots, heads),
        grid_spec=pltpu.PrefetchScalarGridSpec(
            num_scalar_prefetch=2,
            grid=(heads,),
            in_specs=[whole(joined)] + [per_head(piece) for piece in pieces],
            out_specs=[whole(context), per_head(logsum)],
            scratch_shapes=[
                pltpu.VMEM((stored // BLOCK, BLOCK, PAIR), bf16),
                pltpu.VMEM((rows, PAIR), bf16),
                pltpu.VMEM((rows, PAIR), bf16),
            ],
        ),
        out_shape=[context, logsum],
        compiler_params=pltpu.CompilerParams(vmem_limit_bytes=40 * 2**20),
        cost_estimate=lasting(18),
    )(index, valid, joined, *pieces)


def attend_backward(index, valid, joined, grads, logsum, pieces, heads, slots):
    rows = joined.shape[0]
    pieces = pieces + [joined]
    stored = sum(piece.shape[0] for piece in pieces)
    piece_specs = [per_head(piece) for piece in pieces]
    return pl.pallas_call(
        functools.partial(backward_kernel, slots, heads, len(pieces)),
        grid_spec=pltpu.PrefetchScalarGridSpec(
            num_scalar_prefetch=2,
            grid=(heads,),
            in_specs=[whole(joined), whole(grads), per_head(logsum)] + piece_specs,
            out_specs=piece_specs[:-1] + [whole(joined)],
            scratch_shapes=[
                pltpu.VMEM((stored, PAIR), bf16),
                pltpu.VMEM((stored, PAIR), f32),
                pltpu.VMEM((rows, PAIR), bf16),
                pltpu.VMEM((rows, PAIR), bf16),
            ],
        ),
        out_shape=[jax.ShapeDtypeStruct(piece.shape, bf16) for piece in pieces],
        compiler_params=pltpu.CompilerParams(vmem_limit_bytes=50 * 2**20),
        cost_estimate=lasting(25),
    )(index, valid, joined, grads, logsum, *pieces)


def dense_kernel(core_ref, *refs):
    ins, (given_inner, given_outer, kept_inner, kept_outer, proj) = refs[:12], refs[12:]
    step = pl.program_id(0)
    half = pl.num_programs(0) // 2

    def term(first):
        total = contract(ins[first][...], ins[first + 2][...], TN)
        return (total + contract(ins[first + 1][...], ins[first + 3][...], TN)).astype(bf16)

    @pl.when(step < half)
    def _():
        given_inner[...] = term(0)
        given_outer[...] = term(4)

    @pl.when(step >= half)
    def _():
        kept_inner[...] = term(0)
        kept_outer[...] = term(4)

    @pl.when(step == 0)
    def _():
        proj[...] = term(8)


def dense_terms(core, units, rows):
    steps = 8
    hidden = units[0][0].shape[1]
    tile = hidden // steps
    width = rows[0][0].shape[1]

    def unit_tile(step, core_ref):
        owner = jnp.where(step < steps // 2, 1 - core_ref[0], core_ref[0])
        return (0, owner * (steps // 2) + step % (steps // 2))

    def whole_rows(array):
        return pl.BlockSpec(array.shape, lambda step, *_: (0, 0))

    ins, specs = [], []
    for place in range(3):
        for array in units[place]:
            ins.append(array)
            if place < 2:
                specs.append(pl.BlockSpec((array.shape[0], tile), unit_tile))
            else:
                specs.append(whole_rows(array))
        for array in rows[place]:
            ins.append(array)
            specs.append(whole_rows(array))
    half = jax.ShapeDtypeStruct((hidden // 2, width), bf16)
    proj = jax.ShapeDtypeStruct((units[2][0].shape[1], width), bf16)
    given = pl.BlockSpec((tile, width), lambda step, *_: (jnp.minimum(step, steps // 2 - 1), 0))
    kept = pl.BlockSpec((tile, width), lambda step, *_: (jnp.maximum(step - steps // 2, 0), 0))
    return pl.pallas_call(
        dense_kernel,
        grid_spec=pltpu.PrefetchScalarGridSpec(
            num_scalar_prefetch=1,
            grid=(steps,),
            in_specs=specs,
            out_specs=[given, given, kept, kept, whole_rows(proj)],
        ),
        out_shape=[half] * 4 + [proj],
        compiler_params=pltpu.CompilerParams(vmem_limit_bytes=40 * 2**20),
        cost_estimate=lasting(15),
    )(core.reshape(1), *ins)


def plane_exchange(values, split_axis, concat_axis):
    count = lax.axis_size(SEQ)
    groups = [list(range(place, count, 2)) for place in range(2)]
    return lax.all_to_all(
        values,
        SEQ,
        split_axis=split_axis,
        concat_axis=concat_axis,
        axis_index_groups=groups,
        tiled=True,
    )


def plane_gather(values):
    count = lax.axis_size(SEQ) // 2
    return plane_exchange(jnp.concatenate([values] * count, axis=0), 0, 0)


def core_swap(block):
    route = [(place, place ^ 1) for place in range(lax.axis_size(SEQ))]
    return lax.ppermute(block, SEQ, route)


def column_shift(block, step):
    count = lax.axis_size(TP)
    return lax.ppermute(block, TP, [(place, (place + step) % count) for place in range(count)])


def column_gather(values):
    count = lax.axis_size(TP)
    place = lax.axis_index(TP)
    spread = jnp.zeros((count,) + values.shape, values.dtype)
    spread = lax.dynamic_update_index_in_dim(spread, values, place, axis=0)
    for step in range(1, count):
        spread = lax.dynamic_update_index_in_dim(
            spread, column_shift(values, step), (place - step) % count, axis=0
        )
    return spread


def after(values, *earlier):
    return lax.optimization_barrier((values, earlier))[0]


def sum_parts(parts):
    total = parts[0].astype(f32)
    for place in range(1, len(parts)):
        total = total + parts[place].astype(f32)
    return total


def partner_of(place):
    return place + 1 - 2 * (place % 2)


def enter(neighbours):
    barrier = pltpu.get_barrier_semaphore()
    count = 0
    for exists, device in neighbours:

        @pl.when(exists)
        def _():
            pl.semaphore_signal(
                barrier, inc=1, device_id=device, device_id_type=pl.DeviceIdType.MESH
            )

        count = count + jnp.where(exists, 1, 0)
    pl.semaphore_wait(barrier, count)


def remote(source, target, send, receive, device):
    return pltpu.make_async_remote_copy(
        src_ref=source,
        dst_ref=target,
        send_sem=send,
        recv_sem=receive,
        device_id=device,
        device_id_type=pl.DeviceIdType.MESH,
    )


def plane_ids():
    seq_place = lax.axis_index(SEQ)
    chip, core = seq_place // 2, seq_place % 2
    beside = chip + 1 - 2 * (chip % 2)
    above = chip + 2 - 4 * (chip // 2)
    facing = 3 - chip
    return chip, core, beside, above, facing


def column_way(place, way, distance):
    return place - distance if way == 0 else place + distance


class ColumnSpread:

    def __init__(self, parts, own, near, far, other, keep_sem, along_sems, across_sems):
        self.parts, self.own, self.near, self.far = parts, own, near, far
        self.other, self.keep_sem = other, keep_sem
        self.along_sems, self.across_sems = along_sems, across_sems
        self.count = lax.axis_size(TP)
        self.place = lax.axis_index(TP)
        self.rows = own.shape[0] // parts

    def cut(self, part):
        return pl.ds(part * self.rows, self.rows)

    def block(self, way, distance, part):
        if distance == 0:
            return self.own.at[self.cut(part)]
        return self.near.at[column_way(self.place, way, distance), self.cut(part)]

    def along(self, way, distance, part):
        return remote(
            self.block(way, distance, part),
            self.near.at[column_way(self.place, way, distance), self.cut(part)],
            self.along_sems[0].at[way, distance, part],
            self.along_sems[1].at[way, distance, part],
            {TP: self.place + 1 if way == 0 else self.place - 1},
        )

    def landed(self, way, distance, part):
        block = self.near.at[column_way(self.place, way, distance), self.cut(part)]
        return remote(
            block,
            block,
            self.along_sems[0].at[way, distance, part],
            self.along_sems[1].at[way, distance - 1, part],
            self.other,
        )

    def across(self, way, distance, part):
        return remote(
            self.block(way, distance, part),
            self.far.at[column_way(self.place, way, distance), self.cut(part)],
            self.across_sems[0].at[way, distance, part],
            self.across_sems[1].at[way, distance, part],
            self.other,
        )

    def keep(self):
        return pltpu.make_async_copy(self.own, self.near.at[self.place], self.keep_sem)

    def goes_on(self, way):
        return self.place < self.count - 1 if way == 0 else self.place > 0

    def has_come(self, way, distance):
        if way == 0:
            return self.place >= distance
        return self.place + distance < self.count

    def start(self):
        for part in range(self.parts):
            for way in range(2):

                @pl.when(self.goes_on(way))
                def _():
                    self.along(way, 0, part).start()

        if self.far is not None:
            for part in range(self.parts):
                self.across(0, 0, part).start()
        self.keep().start()

    def step(self, distance, part):
        for way in range(2):

            @pl.when(self.has_come(way, distance))
            def _():
                self.landed(way, distance, part).wait_recv()
                if distance < self.count - 1:

                    @pl.when(self.goes_on(way))
                    def _():
                        self.along(way, distance, part).start()

                if self.far is not None:
                    self.across(way, distance, part).start()

    def finish(self):
        self.keep().wait()
        for part in range(self.parts):
            if self.far is not None:
                self.across(0, 0, part).wait()
            for way in range(2):

                @pl.when(self.goes_on(way))
                def _():
                    self.along(way, 0, part).wait_send()

        for distance in range(1, self.count):
            for part in range(self.parts):
                for way in range(2):

                    @pl.when(self.has_come(way, distance))
                    def _():
                        if distance < self.count - 1:

                            @pl.when(self.goes_on(way))
                            def _():
                                self.along(way, distance, part).wait_send()

                        if self.far is not None:
                            self.across(way, distance, part).wait()


class PlaneSpread:

    def __init__(self, own, out, sems):
        self.own, self.out = own, out
        self.send_row, self.recv_row, self.send_on, self.recv_on = sems
        self.chip, core, beside, above, self.facing = plane_ids()
        self.ways = ({SEQ: 2 * beside + core}, {SEQ: 2 * above + core})
        self.chips = (beside, above)

    def first(self, way, part):
        return remote(
            self.own(part),
            self.out(self.chip, part),
            self.send_row.at[way, part],
            self.recv_row.at[way, part],
            self.ways[way],
        )

    def second(self, way):
        return remote(
            self.out(self.chips[way], way),
            self.out(self.chips[way], way),
            self.send_on.at[way],
            self.recv_on.at[way],
            self.ways[1 - way],
        )

    def start(self):
        self.first(0, 0).start()
        self.first(1, 1).start()

    def forward(self):
        for way in range(2):
            self.first(way, way).wait_recv()
            self.second(way).start()
        for way in range(2):
            self.first(way, 1 - way).start()

    def arrive(self):
        for way in range(2):
            self.first(way, 1 - way).wait_recv()
        for way in range(2):
            self.second(way).wait_recv()

    def finish(self):
        for way in range(2):
            self.second(way).wait_send()
            for part in range(2):
                self.first(way, part).wait_send()


def plane_sems():
    dma = pltpu.SemaphoreType.DMA
    return [dma((2, 2)), dma((2, 2)), dma((2,)), dma((2,))]


def column_sems(parts):
    sems = pltpu.SemaphoreType.DMA((2, 4, parts))
    return [sems, sems, sems, sems]


def halves_of(own, out, keep_sem):
    half = own.shape[0] // 2
    chip = plane_ids()[0]
    return (
        lambda part: own.at[pl.ds(part * half, half)],
        lambda place, part: out.at[place, pl.ds(part * half, half)],
        pltpu.make_async_copy(own, out.at[chip], keep_sem),
    )


def neighbours(facing_too, column_too):
    chip, core, beside, above, facing = plane_ids()
    count = lax.axis_size(TP)
    place = lax.axis_index(TP)
    always = place >= 0
    devices = [(always, {SEQ: 2 * chip + 1 - core})]
    devices += [(always, {SEQ: 2 * beside + core}), (always, {SEQ: 2 * above + core})]
    if facing_too:
        devices.append((always, {SEQ: 2 * facing + core}))
    if column_too:
        for step in range(1, count):
            devices.append((always, {TP: lax.rem(place + step, count)}))
    else:
        devices.append((place < count - 1, {TP: place + 1}))
        devices.append((place > 0, {TP: place - 1}))
    return devices


def first_kernel(
    parts,
    own_ref,
    weight_ref,
    share_ref,
    random_ref,
    out_ref,
    spread_ref,
    column_ref,
    random_out_ref,
    randoms,
    own_sem,
    send_row,
    recv_row,
    send_on,
    recv_on,
    send_z,
    recv_z,
    send_far,
    recv_far,
    send_random,
    recv_random,
    send_column,
    recv_column,
    send_share,
    recv_share,
):
    chip, core, beside, above, facing = plane_ids()
    tp_count = lax.axis_size(TP)
    place = lax.axis_index(TP)
    other = {SEQ: 2 * chip + 1 - core}
    weight_rows = weight_ref.shape[0] // (2 * parts)
    column = [{TP: lax.rem(place + step, tp_count)} for step in range(1, tp_count)]
    enter(neighbours(True, True))
    own, out, keep_rows = halves_of(own_ref, out_ref, own_sem.at[0])
    rows = PlaneSpread(own, out, (send_row, recv_row, send_on, recv_on))
    shares = ColumnSpread(
        2, share_ref, column_ref, None, other, own_sem.at[2], (send_share, recv_share), None
    )

    def weight_cut(part, holder):
        return pl.ds((holder * parts + part) * weight_rows, weight_rows)

    def weight_along(source, way, part):
        at = weight_cut(part, core)
        return remote(
            source.at[at],
            spread_ref.at[at],
            send_z.at[way, part],
            recv_z.at[part],
            {TP: place + 1 if way == 0 else place - 1},
        )

    def weight_across(part):
        at = weight_cut(part, core)
        return remote(
            spread_ref.at[at], spread_ref.at[at], send_far.at[part], recv_far.at[part], other
        )

    def goes_on(way):
        if way == 0:
            return (place >= chip) & (place < tp_count - 1)
        return (place <= chip) & (place > 0)

    def random_to_holder(sender):
        return remote(
            random_ref,
            randoms.at[sender],
            send_random,
            recv_random.at[sender],
            {SEQ: 2 * place + core},
        )

    def random_along(step):
        return remote(
            randoms,
            random_out_ref,
            send_column.at[step],
            recv_column,
            column[step],
        )

    rows.start()

    @pl.when(place != chip)
    def _():
        random_to_holder(chip).start()

    for part in range(parts):
        for way in range(2):

            @pl.when((place == chip) & goes_on(way))
            def _():
                weight_along(weight_ref, way, part).start()

    shares.start()
    keep_rows.start()

    @pl.when(place == chip)
    def _():
        keep = pltpu.make_async_copy(weight_ref, spread_ref, own_sem.at[1])
        keep.start()
        keep.wait()
        randoms[chip] = random_ref[...]
        for step in range(1, tp_count):
            random_to_holder(lax.rem(chip + step, tp_count)).wait_recv()
        random_out_ref[...] = randoms[...]
        for step in range(tp_count - 1):
            random_along(step).start()

    rows.forward()
    for part in range(parts):

        @pl.when(place != chip)
        def _():
            weight_along(spread_ref, 0, part).wait_recv()
            for way in range(2):

                @pl.when(goes_on(way))
                def _():
                    weight_along(spread_ref, way, part).start()

            weight_across(part).start()

    for distance in range(1, tp_count):
        for part in range(2):
            shares.step(distance, part)
    rows.arrive()
    rows.finish()
    shares.finish()
    keep_rows.wait()

    @pl.when(place != chip)
    def _():
        random_to_holder(chip).wait_send()
        random_along(0).wait_recv()

    @pl.when(place == chip)
    def _():
        for step in range(tp_count - 1):
            random_along(step).wait_send()

    for part in range(parts):

        @pl.when(place != chip)
        def _():
            weight_across(part).wait()

        for way in range(2):

            @pl.when(goes_on(way))
            def _():
                weight_along(spread_ref, way, part).wait_send()


def first_exchange(own, weight, share, randoms, collective_id, parts=4):
    chips = lax.axis_size(SEQ) // 2
    count = lax.axis_size(TP)
    resident = pl.BlockSpec(memory_space=pltpu.VMEM)
    dma = pltpu.SemaphoreType.DMA
    return pl.pallas_call(
        functools.partial(first_kernel, parts),
        out_shape=[
            jax.ShapeDtypeStruct((chips,) + own.shape, own.dtype),
            jax.ShapeDtypeStruct(weight.shape, weight.dtype),
            jax.ShapeDtypeStruct((count,) + share.shape, share.dtype),
            jax.ShapeDtypeStruct((chips,) + randoms.shape, randoms.dtype),
        ],
        in_specs=[resident] * 4,
        out_specs=[resident] * 4,
        scratch_shapes=[pltpu.VMEM((chips,) + randoms.shape, randoms.dtype), dma((3,))]
        + plane_sems()
        + [
            dma((2, parts)),
            dma((parts,)),
            dma((parts,)),
            dma((parts,)),
            dma,
            dma((chips,)),
            dma((chips - 1,)),
            dma,
        ]
        + column_sems(2)[:2],
        compiler_params=pltpu.CompilerParams(
            collective_id=collective_id, has_side_effects=True, vmem_limit_bytes=32 * 2**20
        ),
        cost_estimate=lasting(30),
    )(own, weight, share, randoms)


class WeightSpread:

    def __init__(self, column, rows, out, keep_sem, cross_sems, plane_sems):
        self.out, self.cross_sems = out, cross_sems
        self.chip, self.core, self.beside, self.above, self.facing = plane_ids()
        self.other = {SEQ: 2 * self.chip + 1 - self.core}
        self.half = column.shape[0] // 2
        self.plane = PlaneSpread(
            lambda part: column.at[pl.ds(part * self.half, self.half), rows],
            lambda where, part: out.at[self.core, where, pl.ds(part * self.half, self.half)],
            plane_sems,
        )
        self.keep = pltpu.make_async_copy(
            column.at[:, rows], out.at[self.core, self.chip], keep_sem
        )

    def across(self, where, part):
        chip = (self.chip, self.beside, self.above, self.facing)[where]
        block = self.out.at[self.core, chip, pl.ds(part * self.half, self.half)]
        at = (where, part)
        return remote(
            block, block, self.cross_sems[0].at[at], self.cross_sems[1].at[at], self.other
        )

    def start(self):
        self.plane.start()
        self.keep.start()

    def forward(self):
        self.plane.forward()
        self.keep.wait()
        for where, part in ((0, 0), (0, 1), (1, 0), (2, 1)):
            self.across(where, part).start()

    def arrive(self):
        self.plane.arrive()
        for where, part in ((1, 1), (2, 0), (3, 0), (3, 1)):
            self.across(where, part).start()

    def finish(self):
        self.plane.finish()
        for where in range(4):
            for part in range(2):
                self.across(where, part).wait()


def weight_sems():
    dma = pltpu.SemaphoreType.DMA
    return [dma, dma((4, 2)), dma((4, 2))] + plane_sems()


def weight_shape(column, rows):
    tp_count, _, width = column.shape
    chips = lax.axis_size(SEQ) // 2
    return jax.ShapeDtypeStruct((2, chips, tp_count, rows[1] - rows[0], width), column.dtype)


def second_kernel(
    parts,
    rows,
    longs_ref,
    own_ref,
    column_ref,
    near_ref,
    far_ref,
    out_ref,
    weight_ref,
    keep_sem,
    *sems,
):
    chip, core = plane_ids()[:2]
    enter(neighbours(False, False))
    other = {SEQ: 2 * chip + 1 - core}
    longs = ColumnSpread(
        parts, longs_ref, near_ref, far_ref, other, keep_sem.at[0], sems[:2], sems[2:4]
    )
    own, out, keep_rows = halves_of(own_ref, out_ref, keep_sem.at[1])
    plane = PlaneSpread(own, out, sems[4:8])
    weight = WeightSpread(
        column_ref, pl.ds(rows[0], rows[1] - rows[0]), weight_ref, sems[8], sems[9:11], sems[11:15]
    )
    longs.start()
    plane.start()
    weight.start()
    keep_rows.start()
    for part in range(parts):
        longs.step(1, part)
    plane.forward()
    weight.forward()
    for part in range(parts):
        longs.step(2, part)
    plane.arrive()
    weight.arrive()
    for part in range(parts):
        longs.step(3, part)
    plane.finish()
    weight.finish()
    longs.finish()
    keep_rows.wait()


def second_exchange(longs, own, column, rows, collective_id, parts=2):
    chips = lax.axis_size(SEQ) // 2
    near = jax.ShapeDtypeStruct((lax.axis_size(TP),) + longs.shape, longs.dtype)
    resident = pl.BlockSpec(memory_space=pltpu.VMEM)
    return pl.pallas_call(
        functools.partial(second_kernel, parts, rows),
        out_shape=[
            near,
            near,
            jax.ShapeDtypeStruct((chips,) + own.shape, own.dtype),
            weight_shape(column, rows),
        ],
        in_specs=[resident] * 3,
        out_specs=[resident] * 4,
        scratch_shapes=[pltpu.SemaphoreType.DMA((2,))]
        + column_sems(parts)
        + plane_sems()
        + weight_sems(),
        compiler_params=pltpu.CompilerParams(
            collective_id=collective_id, has_side_effects=True, vmem_limit_bytes=48 * 2**20
        ),
        cost_estimate=lasting(58),
    )(longs, own, column)


def third_kernel(
    parts,
    cuts,
    slots,
    heads,
    index_ref,
    valid_ref,
    longs_ref,
    column_ref,
    joined_ref,
    *refs,
):
    count = len(cuts)
    pieces, refs = refs[:3], refs[3:]
    near_ref, far_ref, context_ref, logsum_ref, refs = refs[0], refs[1], refs[2], refs[3], refs[4:]
    outs, refs = refs[:count], refs[count:]
    stores, wide_query, wide_context, sent, refs = refs[:2], refs[2], refs[3], refs[4], refs[5:]
    load_sem, keep_sem, block_sems, sems = refs[0], refs[1], refs[2:4], refs[4:8]
    chip, core, beside, above, facing = plane_ids()
    enter(neighbours(True, False))
    other = {SEQ: 2 * chip + 1 - core}
    longs = ColumnSpread(
        parts, longs_ref, near_ref, far_ref, other, keep_sem, sems[:2], sems[2:4]
    )
    weights = []
    for index, (first, last) in enumerate(cuts):
        own = refs[8 + 7 * index : 15 + 7 * index]
        weights.append(
            WeightSpread(
                column_ref, pl.ds(first, last - first), outs[index], own[0], own[1:3], own[3:7]
            )
        )

    def loads(head):
        copies, place = [], 0
        for index, piece in enumerate(pieces):
            rows = piece.shape[0]
            copies.append(
                pltpu.make_async_copy(
                    piece.at[:, :, pl.ds(head * PAIR, PAIR)],
                    stores[head % 2].at[pl.ds(place, rows)],
                    load_sem.at[head, index],
                )
            )
            place += rows
        return copies

    def load(head):
        for copy in loads(head):
            copy.start()

    def work(head):
        for copy in loads(head):
            copy.wait()
        if head + 1 < heads:
            load(head + 1)
        wide_query[...] = widen(joined_ref[:, head_columns(head, heads * PAIR)])
        forward_head(
            slots,
            head,
            index_ref,
            valid_ref,
            stores[head % 2],
            wide_query,
            wide_context,
            logsum_ref.at[:, pl.ds(head * PAIR, PAIR)],
        )
        rows = sent.shape[1]
        for place in range(sent.shape[0]):
            sent[place, :, head_columns(head)] = wide_context[
                place * rows : (place + 1) * rows, BLOCK:
            ]

    def send_block(index):
        target = (beside, above, facing)[index]
        return remote(
            sent.at[target],
            context_ref.at[chip],
            block_sems[0].at[index],
            block_sems[1].at[index],
            {SEQ: 2 * target + core},
        )

    load(0)
    longs.start()
    for weight in weights:
        weight.start()
    work(0)
    for part in range(parts):
        longs.step(1, part)
    for weight in weights:
        weight.forward()
    work(1)
    for part in range(parts):
        longs.step(2, part)
    work(2)
    for index in range(3):
        send_block(index).start()
    context_ref[chip] = sent[chip]
    for weight in weights:
        weight.arrive()
    for part in range(parts):
        longs.step(3, part)
    longs.finish()
    for weight in weights:
        weight.finish()
    for index in range(3):
        send_block(index).wait()


def third_exchange(
    longs, column, index, valid, joined, pieces, cuts, heads, slots, collective_id, parts=2
):
    near = jax.ShapeDtypeStruct((column.shape[0],) + longs.shape, longs.dtype)
    chips = lax.axis_size(SEQ) // 2
    rows = joined.shape[0]
    stored = sum(piece.shape[0] for piece in pieces) + rows
    context = jax.ShapeDtypeStruct((chips, rows // chips, heads * BLOCK), joined.dtype)
    resident = pl.BlockSpec(memory_space=pltpu.VMEM)
    scalars = pl.BlockSpec(memory_space=pltpu.SMEM)
    anywhere = pl.BlockSpec(memory_space=pl.ANY)
    dma = pltpu.SemaphoreType.DMA
    sems = [sem for _ in cuts for sem in weight_sems()]
    return pl.pallas_call(
        functools.partial(third_kernel, parts, cuts, slots, heads),
        out_shape=[near, near, context, jax.ShapeDtypeStruct((rows, heads * PAIR), f32)]
        + [weight_shape(column, cut) for cut in cuts],
        in_specs=[scalars] * 2 + [resident] * 3 + [anywhere] * 3,
        out_specs=[resident] * (4 + len(cuts)),
        scratch_shapes=[
            pltpu.VMEM((stored // BLOCK, BLOCK, PAIR), bf16),
            pltpu.VMEM((stored // BLOCK, BLOCK, PAIR), bf16),
            pltpu.VMEM((rows, PAIR), bf16),
            pltpu.VMEM((rows, PAIR), bf16),
            pltpu.VMEM(context.shape, bf16),
            dma((heads, 3)),
            dma,
            dma((3,)),
            dma((3,)),
        ]
        + column_sems(parts)
        + sems,
        compiler_params=pltpu.CompilerParams(
            collective_id=collective_id, has_side_effects=True, vmem_limit_bytes=52 * 2**20
        ),
        cost_estimate=lasting(62),
    )(
        index,
        valid,
        longs,
        column,
        joined,
        *(piece.reshape(-1, BLOCK, piece.shape[1]) for piece in pieces + [joined]),
    )


class ColumnReduce:

    def __init__(self, parts, step_rows, sums, came, sems):
        self.parts, self.step_rows = parts, step_rows
        self.sums, self.came, self.sems = sums, came, sems
        self.count = lax.axis_size(TP)
        self.place = lax.axis_index(TP)
        self.rows = sums.shape[1] // parts
        self.order = []
        for step in range(self.count):
            for owner in (step, self.count - 1 - step):
                if owner not in self.order:
                    self.order.append(owner)

    def along(self, way, owner, part):
        at = pl.ds(part * self.rows, self.rows)
        return remote(
            self.sums.at[owner, at],
            self.came.at[way, owner, at],
            self.sems[0].at[way, owner, part],
            self.sems[1].at[way, owner, part],
            {TP: self.place - 1 if way == 0 else self.place + 1},
        )

    def add(self, owner, source, part):
        @pl.loop(0, self.rows // self.step_rows)
        def _(step):
            start = pl.multiple_of(part * self.rows + step * self.step_rows, self.step_rows)
            at = pl.ds(start, self.step_rows)
            total = self.sums[owner, at, :].astype(f32) + source[at, :].astype(f32)
            self.sums[owner, at, :] = total.astype(self.sums.dtype)

    def takes(self, way):
        return self.place < self.count - 1 if way == 0 else self.place > 0

    def passes(self, way, owner):
        return self.place > owner if way == 0 else self.place < owner

    def begin(self, owner, part):
        for way in range(2):

            @pl.when(self.passes(way, owner) & ~self.takes(way))
            def _():
                self.along(way, owner, part).start()

    def move(self, way, owner, part):
        @pl.when(self.passes(way, owner) & self.takes(way))
        def _():
            self.along(way, owner, part).wait_recv()
            self.add(owner, self.came.at[way, owner], part)
            self.along(way, owner, part).start()

    def end(self):
        for part in range(self.parts):
            for way in range(2):
                for owner in range(self.count):

                    @pl.when((self.place == owner) & self.takes(way))
                    def _():
                        self.along(way, owner, part).wait_recv()
                        self.add(owner, self.came.at[way, owner], part)

    def finish(self):
        for owner in range(self.count):
            for part in range(self.parts):
                for way in range(2):

                    @pl.when(self.passes(way, owner))
                    def _():
                        self.along(way, owner, part).wait_send()

    def give(self, out):
        for owner in range(self.count):

            @pl.when(self.place == owner)
            def _():
                out[...] = self.sums[owner]


class PlaneReduce:

    def __init__(self, step_rows, terms, out, buffers, sems):
        self.step_rows, self.terms, self.out = step_rows, terms, out
        self.came, self.facing_came, self.sent, self.last = buffers
        self.sems = sems
        self.chip, core, beside, above, self.facing = plane_ids()
        self.ways = ({SEQ: 2 * beside + core}, {SEQ: 2 * above + core})
        self.chips = (beside, above)
        self.half = terms.shape[1] // 2

    def copy(self, kind, way, source, target, device):
        return remote(
            source, target.at[way], self.sems[0].at[kind, way], self.sems[1].at[kind, way], device
        )

    def pieces(self, way):
        return pl.ds(way * self.half, self.half)

    def facing_term(self, way):
        source = self.terms.at[self.facing, self.pieces(way)]
        return self.copy(0, way, source, self.facing_came, self.ways[way])

    def near_term(self, way):
        source = self.terms.at[self.chips[way], self.pieces(way)]
        return self.copy(1, way, source, self.came, self.ways[way])

    def summed(self, way):
        return self.copy(2, way, self.sent.at[way], self.last, self.ways[1 - way])

    def each_step(self, work):
        steps = self.terms.shape[2] // self.step_rows

        @pl.loop(0, self.half * steps)
        def _(step):
            start = pl.multiple_of((step % steps) * self.step_rows, self.step_rows)
            work(step // steps, pl.ds(start, self.step_rows))

    def start(self):
        for way in range(2):
            self.facing_term(way).start()
        for way in range(2):
            self.near_term(way).start()

    def move(self):
        for way in range(2):
            self.facing_term(way).wait_recv()

            def add_term(piece, at):
                total = self.terms[self.chips[1 - way], way * self.half + piece, at, :].astype(f32)
                total = total + self.facing_came[way, piece, at, :].astype(f32)
                self.sent[way, piece, at, :] = total.astype(self.sent.dtype)

            self.each_step(add_term)
            self.summed(way).start()

    def end(self):
        for way in range(2):
            self.near_term(way).wait_recv()
            self.summed(way).wait_recv()

            def add_last(piece, at):
                total = self.terms[self.chip, way * self.half + piece, at, :].astype(f32)
                total = total + self.came[way, piece, at, :].astype(f32)
                total = total + self.last[way, piece, at, :].astype(f32)
                self.out[way * self.half + piece, at, :] = total.astype(self.out.dtype)

            self.each_step(add_last)

    def finish(self):
        for way in range(2):
            self.facing_term(way).wait_send()
            self.near_term(way).wait_send()
            self.summed(way).wait_send()


def reduce_scratch(shape, dtype):
    half = pltpu.VMEM((2, shape[1] // 2) + shape[2:], dtype)
    sems = pltpu.SemaphoreType.DMA((3, 2))
    return [half] * 4 + [sems, sems]


def fourth_kernel(parts, cuts, near_ref, far_ref, *refs):
    count = len(cuts) - 1
    terms, givens, refs = refs[:count], refs[count : 2 * count], refs[2 * count :]
    out_ref, dense_ref, sums, given, came, dense, more = refs[:7]
    load_sem, send_far, recv_far, send_z, recv_z = refs[7:12]
    buffers, sems = refs[12:16], refs[16:18]
    place = lax.axis_index(TP)
    chip, core = plane_ids()[:2]
    other = {SEQ: 2 * chip + 1 - core}
    loads = [pltpu.make_async_copy(near_ref, sums, load_sem.at[0])]
    for index in range(count):
        rows = pl.ds(cuts[index], cuts[index + 1] - cuts[index])
        loads.append(
            pltpu.make_async_copy(
                terms[index], dense.at[:, :, rows], load_sem.at[1 + 2 * index]
            )
        )
        loads.append(
            pltpu.make_async_copy(givens[index], more.at[:, :, rows], load_sem.at[2 + 2 * index])
        )
    for load in loads:
        load.start()
    enter(neighbours(False, False))
    step_rows = dense.shape[2] // 2
    column = ColumnReduce(parts, sums.shape[1] // parts // 2, sums, came, (send_z, recv_z))
    plane = PlaneReduce(step_rows, dense, dense_ref, buffers, sems)

    def across(owner):
        return remote(
            far_ref.at[owner], given.at[owner], send_far.at[owner], recv_far.at[owner], other
        )

    def move(steps):
        for part in range(parts):
            for way, owner in steps:
                column.move(way, owner, part)

    for owner in column.order:
        across(owner).start()
    for load in loads:
        load.wait()
    pieces, steps = dense.shape[1], dense.shape[2] // step_rows

    @pl.loop(0, dense.shape[0] * pieces * steps)
    def _(step):
        at = pl.ds(pl.multiple_of((step % steps) * step_rows, step_rows), step_rows)
        piece = (step // steps) % pieces
        where = step // (steps * pieces)
        total = dense[where, piece, at, :].astype(f32) + more[where, piece, at, :].astype(f32)
        dense[where, piece, at, :] = total.astype(dense.dtype)

    plane.start()
    for owner in column.order:
        across(owner).wait_recv()
        for part in range(parts):
            column.add(owner, given.at[owner], part)
            column.begin(owner, part)
    last = column.count - 1

    @pl.when(place == last - 1)
    def _():
        move([(0, 0)])

    @pl.when(place == 1)
    def _():
        move([(1, last)])

    plane.move()

    @pl.when(place == last - 1)
    def _():
        move([(0, 1), (1, last)])

    @pl.when(place == 1)
    def _():
        move([(1, last - 1), (0, 0)])

    column.end()
    column.give(out_ref)
    plane.end()
    column.finish()
    plane.finish()
    for owner in column.order:
        across(owner).wait_send()


def fourth_exchange(near, far, terms, givens, cuts, collective_id, parts=2):
    count = lax.axis_size(TP)
    block = near.shape[1:]
    chips = givens[0].shape[0]
    width = givens[0].shape[-1]
    dense = (chips, count, cuts[-1], width)
    resident = pl.BlockSpec(memory_space=pltpu.VMEM)
    anywhere = pl.BlockSpec(memory_space=pl.ANY)
    dma = pltpu.SemaphoreType.DMA
    pieces = len(cuts) - 1
    return pl.pallas_call(
        functools.partial(fourth_kernel, parts, cuts),
        out_shape=[
            jax.ShapeDtypeStruct(block, near.dtype),
            jax.ShapeDtypeStruct(dense[1:], near.dtype),
        ],
        in_specs=[anywhere, resident] + [anywhere] * (2 * pieces),
        out_specs=[resident] * 2,
        scratch_shapes=[
            pltpu.VMEM((count,) + block, near.dtype),
            pltpu.VMEM((count,) + block, near.dtype),
            pltpu.VMEM((2, count) + block, near.dtype),
            pltpu.VMEM(dense, near.dtype),
            pltpu.VMEM(dense, near.dtype),
            dma((1 + 2 * pieces,)),
            dma((count,)),
            dma((count,)),
            dma((2, count, parts)),
            dma((2, count, parts)),
        ]
        + reduce_scratch(dense, near.dtype),
        compiler_params=pltpu.CompilerParams(
            collective_id=collective_id, has_side_effects=True, vmem_limit_bytes=52 * 2**20
        ),
        cost_estimate=lasting(62),
    )(near, far, *terms, *givens)


def fifth_kernel(rows_ref, dense_ref, out_ref, own_ref, came, send_z, recv_z, *refs):
    buffers, sems = refs[:4], refs[4:6]
    count = lax.axis_size(TP)
    place = lax.axis_index(TP)
    enter(neighbours(False, True))
    plane = PlaneReduce(rows_ref.shape[2] // 2, rows_ref, out_ref, buffers, sems)

    def to_owner(step):
        owner = lax.rem(place + step, count)
        return remote(
            dense_ref.at[owner], came.at[step - 1], send_z.at[step], recv_z.at[step], {TP: owner}
        )

    plane.start()
    for step in range(1, count):
        to_owner(step).start()
    plane.move()
    plane.end()
    for step in range(1, count):
        to_owner(step).wait()

    step_rows = own_ref.shape[0] // 2

    @pl.loop(0, 2)
    def _(step):
        at = pl.ds(pl.multiple_of(step * step_rows, step_rows), step_rows)
        total = dense_ref[place, at, :].astype(f32)
        for other in range(count - 1):
            total = total + came[other, at, :].astype(f32)
        own_ref[at, :] = total.astype(own_ref.dtype)

    plane.finish()


def fifth_exchange(rows, dense, collective_id):
    count = lax.axis_size(TP)
    resident = pl.BlockSpec(memory_space=pltpu.VMEM)
    dma = pltpu.SemaphoreType.DMA
    return pl.pallas_call(
        fifth_kernel,
        out_shape=[
            jax.ShapeDtypeStruct(rows.shape[1:], f32),
            jax.ShapeDtypeStruct(dense.shape[1:], dense.dtype),
        ],
        in_specs=[resident] * 2,
        out_specs=[resident] * 2,
        scratch_shapes=[
            pltpu.VMEM((count - 1,) + dense.shape[1:], dense.dtype),
            dma((count,)),
            dma((count,)),
        ]
        + reduce_scratch(rows.shape, rows.dtype),
        compiler_params=pltpu.CompilerParams(
            collective_id=collective_id, has_side_effects=True, vmem_limit_bytes=48 * 2**20
        ),
        cost_estimate=lasting(30),
    )(rows, dense)


def sixth_kernel(
    parts,
    terms_ref,
    own_ref,
    rows_ref,
    out_ref,
    dense_ref,
    all_ref,
    sums,
    given,
    came,
    send_far,
    recv_far,
    send_z,
    recv_z,
    send_plane,
    recv_plane,
    send_on,
    send_back,
    recv_back,
    keep_sem,
    send_row,
    recv_row,
    send_next,
    recv_next,
    send_dense,
    recv_dense,
    column_came,
    plane_came,
    send_all,
    recv_all,
):
    chip, core, beside, above, facing = plane_ids()
    count = lax.axis_size(TP)
    place = lax.axis_index(TP)
    other = {SEQ: 2 * chip + 1 - core}
    ways = ({SEQ: 2 * beside + core}, {SEQ: 2 * above + core})
    rows = sums.shape[0]
    part_rows = rows // parts
    always = place >= 0
    holds = place == chip
    far_column = [
        (always, {SEQ: 2 * chip + 1 - core, TP: lax.rem(place + step, count)})
        for step in range(1, count)
    ]
    enter(neighbours(True, True) + far_column)
    half = own_ref.shape[0] // 2
    dense = PlaneSpread(
        lambda part: own_ref.at[pl.ds(part * half, half)],
        lambda where, part: dense_ref.at[where, core, pl.ds(part * half, half)],
        (send_row, recv_row, send_next, recv_next),
    )
    keep = pltpu.make_async_copy(own_ref, dense_ref.at[chip, core], keep_sem)

    def dense_across(where):
        block = dense_ref.at[(chip, beside, above, facing)[where], core]
        return remote(block, block, send_dense.at[where], recv_dense.at[where], other)

    mine = core * count + place

    def column_copy(index):
        peer = lax.rem(mine + index, 2 * count)
        return remote(
            rows_ref,
            column_came.at[mine],
            send_all.at[index],
            recv_all.at[index],
            {SEQ: 2 * chip + peer // count, TP: lax.rem(peer, count)},
        )

    def column_landed(index):
        sender = lax.rem(mine + 2 * count - index, 2 * count)
        block = column_came.at[sender]
        return remote(block, block, send_all.at[index], recv_all.at[index], other)

    def plane_copy(index):
        return remote(
            plane_came.at[chip],
            plane_came.at[chip],
            send_all.at[2 * count + index],
            recv_all.at[2 * count + index],
            {SEQ: 2 * (beside, above, facing)[index] + core},
        )

    dense.start()
    keep.start()
    column_came[mine] = rows_ref[...]
    for index in range(1, 2 * count):
        column_copy(index).start()

    def cut(part):
        return pl.ds(part * part_rows, part_rows)

    def own_cut(part):
        return pl.ds(pl.multiple_of(core * rows + part * part_rows, 16), part_rows)

    across = remote(
        terms_ref.at[pl.ds(pl.multiple_of((1 - core) * rows, 16), rows)], given, send_far, recv_far, other
    )
    across.start()

    def along(way, part):
        return remote(
            sums.at[cut(part)],
            came.at[way, cut(part)],
            send_z.at[way, part],
            recv_z.at[way, part],
            {TP: place - 1 if way == 0 else place + 1},
        )

    def add(source, part):
        total = sums[cut(part), :].astype(f32) + source[cut(part), :].astype(f32)
        sums[cut(part), :] = total.astype(sums.dtype)

    def to_plane(way, part):
        return remote(
            out_ref.at[own_cut(part)],
            out_ref.at[own_cut(part)],
            send_plane.at[way, part],
            recv_plane.at[part],
            ways[way],
        )

    def onward(part):
        return remote(
            out_ref.at[own_cut(part)],
            out_ref.at[own_cut(part)],
            send_on.at[part],
            recv_plane.at[part],
            ways[1 - part // (parts // 2)],
        )

    def back(part):
        return remote(
            out_ref.at[own_cut(part)],
            out_ref.at[own_cut(part)],
            send_back.at[part],
            recv_back.at[part],
            other,
        )

    across.wait_recv()
    keep.wait()
    dense_across(0).start()
    for part in range(parts):
        sums[cut(part), :] = terms_ref[own_cut(part), :]
        add(given, part)
        for way in range(2):
            passes = place > chip if way == 0 else place < chip
            takes = place < count - 1 if way == 0 else place > 0

            @pl.when(passes)
            def _():
                @pl.when(takes)
                def _():
                    along(way, part).wait_recv()
                    add(came.at[way], part)

                along(way, part).start()

    dense.forward()
    for part in range(parts):
        for way in range(2):
            takes = place < count - 1 if way == 0 else place > 0

            @pl.when(holds & takes)
            def _():
                along(way, part).wait_recv()
                add(came.at[way], part)

        @pl.when(holds)
        def _():
            out_ref[own_cut(part), :] = sums[cut(part), :]
            for way in range(2):
                to_plane(way, part).start()
            back(part).start()

    for index in range(1, 2 * count):
        column_landed(index).wait_recv()
    total = column_came[0]
    for index in range(1, 2 * count):
        total = total + column_came[index]
    plane_came[chip] = total
    for index in range(3):
        plane_copy(index).start()
    dense.arrive()
    for where in range(1, 4):
        dense_across(where).start()
    for part in range(parts):

        @pl.when(place != chip)
        def _():
            to_plane(0, part).wait_recv()

        @pl.when((beside if part < parts // 2 else above) == place)
        def _():
            onward(part).start()

        @pl.when(place != chip)
        def _():
            back(part).start()

    for index in range(1, 2 * count):
        column_copy(index).wait_send()
    for index in range(3):
        plane_copy(index).wait()
    total = plane_came[0]
    for index in range(1, plane_came.shape[0]):
        total = total + plane_came[index]
    all_ref[...] = total
    across.wait_send()
    dense.finish()
    for where in range(4):
        dense_across(where).wait()
    for part in range(parts):
        back(part).wait()

        @pl.when((beside if part < parts // 2 else above) == place)
        def _():
            onward(part).wait_send()

        for way in range(2):

            @pl.when(holds)
            def _():
                to_plane(way, part).wait_send()

            @pl.when(place > chip if way == 0 else place < chip)
            def _():
                along(way, part).wait_send()


def sixth_exchange(terms, own, small, collective_id):
    parts = 4
    chips = lax.axis_size(SEQ) // 2
    column = 2 * lax.axis_size(TP)
    rows = terms.shape[0] // 2
    half = (rows,) + terms.shape[1:]
    dma = pltpu.SemaphoreType.DMA
    resident = pl.BlockSpec(memory_space=pltpu.VMEM)
    return pl.pallas_call(
        functools.partial(sixth_kernel, parts),
        out_shape=[
            jax.ShapeDtypeStruct(terms.shape, terms.dtype),
            jax.ShapeDtypeStruct((chips, 2) + own.shape, own.dtype),
            jax.ShapeDtypeStruct(small.shape, small.dtype),
        ],
        in_specs=[resident] * 3,
        out_specs=[resident] * 3,
        scratch_shapes=[
            pltpu.VMEM(half, terms.dtype),
            pltpu.VMEM(half, terms.dtype),
            pltpu.VMEM((2,) + half, terms.dtype),
            dma,
            dma,
            dma((2, parts)),
            dma((2, parts)),
            dma((2, parts)),
            dma((parts,)),
            dma((parts,)),
            dma((parts,)),
            dma((parts,)),
            dma,
        ]
        + plane_sems()
        + [
            dma((4,)),
            dma((4,)),
            pltpu.VMEM((column,) + small.shape, small.dtype),
            pltpu.VMEM((chips,) + small.shape, small.dtype),
            dma((column + 3,)),
            dma((column + 3,)),
        ],
        compiler_params=pltpu.CompilerParams(
            collective_id=collective_id, has_side_effects=True, vmem_limit_bytes=32 * 2**20
        ),
        cost_estimate=lasting(35),
    )(terms, own, small)


def plane_applies(mesh, blocks, docs):
    seq_count, tp_count = mesh.shape[SEQ], mesh.shape[TP]
    groups = seq_count * tp_count
    return (
        tp_count == 4
        and seq_count == 2 * tp_count
        and blocks == groups * SHORT_BLK
        and 2 * tp_count * SHORT_BLK == LONG_BLK
        and blocks - SHORT_BLK * docs == 2 * (LONG_BLK - SHORT_BLK)
    )


class Micro:
    pass


def plane_body(
    tokens,
    doc_lengths,
    rand_blocks,
    query_weight,
    key_weight,
    value_weight,
    query_bias,
    value_bias,
    proj_weight,
    proj_bias,
    first_gain,
    first_bias,
    second_gain,
    second_bias,
    inner_weight,
    inner_bias,
    outer_weight,
    outer_bias,
    out_grad,
):
    micro_count, own_rows, model_width = tokens.shape
    seq_count = lax.axis_size(SEQ)
    tp_count = lax.axis_size(TP)
    chips = seq_count // 2
    seq_place = lax.axis_index(SEQ)
    tp_place = lax.axis_index(TP)
    chip = lax.shift_right_logical(seq_place, 1)
    core = seq_place & 1
    heads = rand_blocks.shape[2]
    rands = rand_blocks.shape[3]
    local_width = query_weight.shape[1]
    head_size = local_width // heads
    pair_width = heads * PAIR
    hidden_units = inner_weight.shape[1]
    classes = 2 * tp_count
    class_bits = classes.bit_length() - 1
    group_bits = SHORT_BLK.bit_length() - 1
    own_class = core * tp_count + tp_place
    long_docs = 2
    slots = 5 + rands
    group_rows = chips * own_rows
    score_scale = 1.0 / math.sqrt(head_size)

    def by_head(values):
        return values.reshape(values.shape[:-1] + (heads, -1))

    def side_by_side(first, second):
        paired = jnp.concatenate([by_head(first), by_head(second)], axis=-1)
        return paired.reshape(paired.shape[:-2] + (pair_width,))

    def low_half(wide):
        return by_head(wide)[..., :head_size].reshape(wide.shape[:-1] + (local_width,))

    def high_half(wide):
        return by_head(wide)[..., head_size:].reshape(wide.shape[:-1] + (local_width,))

    def slot_rows(values, slot):
        return values[slot * own_rows : (slot + 1) * own_rows]

    stage = [Micro() for _ in range(micro_count)]
    spare_rows = 128
    packed = jnp.concatenate([side_by_side(key_weight, value_weight), query_weight], axis=1)
    packed_bias = jnp.concatenate(
        [side_by_side(jnp.zeros_like(value_bias), value_bias), query_bias]
    )
    packed = jnp.concatenate([packed, packed_bias[None]], axis=0)
    packed = jnp.pad(packed, ((0, spare_rows - 1), (0, -packed.shape[1] % 128)))
    randoms = rand_blocks.reshape(-1)
    random_count = randoms.shape[0]
    randoms = jnp.pad(randoms, (0, -random_count % 1024)).reshape(-1, 128)
    for micro, held in enumerate(stage):
        held.inputs = tokens[micro].astype(f32)
        shifted, held.stats_one, held.inverse_one = layer_stats(
            held.inputs, first_gain, first_bias
        )
        held.low = shifted.astype(bf16)
    unit_cut = hidden_units // seq_count
    proj_cut = local_width // seq_count
    rest_rows = -(-(proj_cut + 1) // 16) * 16
    cuts = (0, rest_rows, rest_rows + unit_cut, rest_rows + 2 * unit_cut)

    def padded(row_values):
        return jnp.pad(row_values, [(0, 0)] * (row_values.ndim - 1) + [(0, model_width - unit_cut)])

    share = jnp.concatenate(
        [
            lax.dynamic_slice_in_dim(proj_weight, seq_place * proj_cut, proj_cut, axis=0),
            padded(lax.dynamic_slice_in_dim(inner_bias, seq_place * unit_cut, unit_cut)[None]),
            jnp.zeros((rest_rows - proj_cut - 1, model_width), bf16),
            lax.dynamic_slice_in_dim(inner_weight, seq_place * unit_cut, unit_cut, axis=1).T,
            lax.dynamic_slice_in_dim(outer_weight, seq_place * unit_cut, unit_cut, axis=0),
        ],
        axis=0,
    )
    one, packed, column, randoms = first_exchange(stage[0].low, packed, share, randoms, 1)
    stage[0].one = one.reshape(group_rows, model_width)
    pair_wide = packed[:model_width, :pair_width]
    pair_wide_bias = packed[model_width, :pair_width]
    query_part = packed[:model_width, pair_width : pair_width + local_width]
    query_part_bias = packed[model_width, pair_width : pair_width + local_width]
    joined_weight = jnp.concatenate([pair_wide, query_part * score_scale], axis=1)
    joined_bias = jnp.concatenate([pair_wide_bias, query_part_bias * score_scale])

    starts = jnp.cumsum(doc_lengths, axis=1) - doc_lengths
    is_long = doc_lengths == LONG_BLK
    long_firsts = jnp.min(jnp.where(is_long, starts, jnp.iinfo(jnp.int32).max), axis=1)
    long_lasts = jnp.max(jnp.where(is_long, starts, -1), axis=1)
    first_groups = lax.shift_right_logical(jnp.stack([long_firsts, long_lasts]), group_bits)
    own_groups = first_groups + ((own_class - first_groups) & (classes - 1))
    in_slot = lax.shift_right_logical(own_groups, class_bits)[:, :, None] == np.arange(chips)
    randoms = randoms.reshape(chips, -1)[:, :random_count]
    randoms = randoms.reshape(chips, micro_count, tp_count, SHORT_BLK, heads, rands)
    randoms = lax.dynamic_index_in_dim(randoms, tp_place, axis=2, keepdims=False)
    randoms = jnp.pad(randoms.transpose(1, 3, 0, 2, 4), [(0, 0)] * 4 + [(slots - rands, 0)])
    randoms = randoms.reshape(micro_count, -1)
    shape = (heads, chips, SHORT_BLK, slots)
    slot, block, entry = (part.reshape(-1) for part in np.indices(shape, np.int32)[1:])
    for micro, held in enumerate(stage):
        group = slot * classes + own_class
        number = group * SHORT_BLK + block
        in_long = [
            (number >= start) & (number < start + LONG_BLK)
            for start in (long_firsts[micro : micro + 1], long_lasts[micro : micro + 1])
        ]
        window_first = jnp.where(
            in_long[0],
            long_firsts[micro : micro + 1],
            jnp.where(in_long[1], long_lasts[micro : micro + 1], group * SHORT_BLK),
        )
        any_long = in_long[0] | in_long[1]
        window_final = window_first + jnp.where(any_long, LONG_BLK, SHORT_BLK)
        key = randoms[micro]
        for place, value in enumerate(
            (
                jnp.maximum(number - 1, window_first),
                jnp.minimum(number + 1, window_final - 1),
                number,
                window_first,
                window_first + 1,
            )
        ):
            key = jnp.where(entry == place, value, key)
        inside = key & (SHORT_BLK - 1)
        key_class = lax.shift_right_logical(key, group_bits) & (classes - 1)
        own_core = lax.shift_right_logical(key_class, class_bits - 1) == core
        piece = (key_class & (tp_count - 1)) + jnp.where(own_core, 0, tp_count)
        long_place = piece * long_docs + jnp.where(in_long[1], 1, 0)
        short_place = classes * long_docs + slot
        held.index = jnp.where(any_long, long_place, short_place) * SHORT_BLK + inside
        counts = jnp.where(entry == 0, number > window_first, number + 1 < window_final)
        counts = counts.astype(jnp.int32)[: chips * SHORT_BLK * slots]
        held.valid = counts.reshape(-1, slots)[:, :2].reshape(-1)
        held.in_slot = [in_slot[doc, micro].reshape(chips, 1, 1) for doc in range(long_docs)]

    def long_blocks(micro):
        held = stage[micro]
        held.joined = (contract(held.one, joined_weight, NN) + joined_bias).astype(bf16)
        parts = held.joined.reshape(chips, own_rows, -1)[:, :, :pair_width]
        longs = jnp.concatenate(
            [jnp.sum(jnp.where(chosen, parts, 0), axis=0) for chosen in held.in_slot], axis=0
        )
        return longs

    def keep_pieces(micro, near, far):
        stage[micro].pieces = [near.reshape(-1, pair_width), far.reshape(-1, pair_width)]

    def attend(micro):
        held = stage[micro]
        index = after(held.index, stage[micro - 1].grad_context_sent)
        held.context_sent, held.logsum = attend_forward(
            index, held.valid, held.joined, held.pieces, heads, slots
        )
        held.context = plane_exchange(held.context_sent, 0, 1)

    def feed_forward(micro):
        held = stage[micro]
        if micro:
            held.context = after(
                held.context, stage[micro - 1].long_sum_sent
            )
        hidden = held.inputs + contract(held.context, proj_full, NN) + proj_bias
        shifted, stats, inverse = layer_stats(hidden, second_gain, second_bias)
        held.two = shifted.astype(bf16)
        before = contract(held.two, inner_full, NT) + inner_bias_full
        held.active = gelu_exact(before).astype(bf16)
        result = hidden + contract(held.active, outer_full, NN) + outer_bias
        held.output = result.astype(bf16)
        held.grad_out = out_grad[micro]
        grad_float = held.grad_out.astype(f32)
        grad_active = contract(held.grad_out, outer_full, NT)
        held.grad_before = gelu_grad(before, grad_active).astype(bf16)
        grad_two = contract(held.grad_before, inner_full, NN)
        back, gain_sum, shift_sum = layer_back(grad_two, stats, inverse, second_gain)
        held.grad_hidden = grad_float + back
        held.branch = held.grad_hidden.astype(bf16)
        held.grad_context_sent = jnp.stack(
            [
                contract(
                    held.branch, proj_full[part * local_width : (part + 1) * local_width], NT
                ).astype(bf16)
                for part in range(chips)
            ]
        )
        held.grad_context = plane_exchange(held.grad_context_sent, 0, 0).reshape(
            group_rows, local_width
        )
        held.unit_sum = jnp.sum(held.grad_before.astype(f32), axis=0)
        held.row_sums = jnp.stack(
            [
                gain_sum,
                shift_sum,
                jnp.sum(held.branch.astype(f32), axis=0),
                jnp.sum(grad_float, axis=0),
            ]
        )

    def attend_back(micro, *earlier):
        held = stage[micro]
        near, far, held.grad_joined = attend_backward(
            held.index,
            held.valid,
            held.joined,
            after(held.grad_context, *earlier),
            held.logsum,
            held.pieces,
            heads,
            slots,
        )
        return near, far

    def input_rows(micro, long_sum):
        held = stage[micro]
        shape = (chips, own_rows, pair_width + local_width)
        lane = np.arange(shape[2], dtype=np.int32)
        joined = held.grad_joined.reshape(shape)
        for doc, chosen in enumerate(held.in_slot):
            long_part = jnp.pad(slot_rows(long_sum, doc), ((0, 0), (0, local_width)))
            joined = jnp.where(chosen & (lane < pair_width), long_part, joined)
        held.grad_joined = joined.reshape(group_rows, -1)
        rows = contract(held.grad_joined, joined_weight, NT)
        return rows.astype(bf16).reshape(chips, own_rows, model_width)

    def input_back(micro, grad_one):
        held = stage[micro]
        back, gain_sum, shift_sum = layer_back(
            grad_one, held.stats_one, held.inverse_one, first_gain
        )
        held.input_grad = held.grad_hidden + back
        held.first_sums = jnp.stack([gain_sum, shift_sum])

    longs = long_blocks(0)
    near, far, one, outer_full = second_exchange(longs, stage[1].low, column, cuts[2:4], 2)
    stage[1].one = one.reshape(group_rows, model_width)
    keep_pieces(0, near, far)
    longs = long_blocks(1)
    near, far, context, stage[0].logsum, rest, inner_full = third_exchange(
        longs,
        column,
        stage[0].index,
        stage[0].valid,
        stage[0].joined,
        stage[0].pieces,
        (cuts[0:2], cuts[1:3]),
        heads,
        slots,
        7,
    )
    keep_pieces(1, near, far)
    stage[0].context = context.transpose(1, 0, 2).reshape(own_rows, model_width)
    inner_full = inner_full.reshape(-1, model_width)
    outer_full = outer_full.reshape(-1, model_width)
    inner_bias_full = rest[:, :, :, proj_cut, :unit_cut].reshape(-1)
    proj_full = rest[:, :, :, :proj_cut].transpose(2, 1, 0, 3, 4)
    proj_full = proj_full.reshape(tp_count * local_width, model_width)
    feed_forward(0)
    attend(1)
    near, far = attend_back(0, stage[1].logsum, stage[1].context_sent)
    stage[0].long_sum_sent = sum_parts([near, core_swap(far)]).astype(bf16)
    long_sum = lax.psum_scatter(stage[0].long_sum_sent, TP, scatter_dimension=0, tiled=True)
    feed_forward(1)

    given_inner, given_outer, kept_inner, kept_outer, proj_part = dense_terms(
        after(core, stage[1].grad_context_sent),
        [[h.grad_before for h in stage], [h.active for h in stage], [h.context for h in stage]],
        [[h.two for h in stage], [h.grad_out for h in stage], [h.branch for h in stage]],
    )
    proj_part = proj_part.reshape(tp_count, chips, 2, proj_cut, model_width)
    unit_shape = (2, chips, tp_count)
    unit_sum = sum(h.unit_sum for h in stage).astype(bf16)
    rest_part = jnp.concatenate(
        [
            proj_part.transpose(2, 1, 0, 3, 4),
            padded(unit_sum.reshape(unit_shape + (1, unit_cut))),
            jnp.zeros(unit_shape + (rest_rows - proj_cut - 1, model_width), bf16),
        ],
        axis=3,
    )
    unit_shape = (chips, tp_count, -1, model_width)
    terms = [kept_inner.reshape(unit_shape), kept_outer.reshape(unit_shape)]
    givens = [core_swap(part.reshape(unit_shape)) for part in (given_inner, given_outer)]
    terms.append(lax.dynamic_index_in_dim(rest_part, core, axis=0, keepdims=False))
    givens.append(
        core_swap(lax.dynamic_index_in_dim(rest_part, 1 - core, axis=0, keepdims=False))
    )

    rows = input_rows(0, after(long_sum, kept_inner))
    grad_one = lax.psum_scatter(
        rows.reshape(group_rows, model_width),
        SEQ,
        scatter_dimension=0,
        axis_index_groups=[list(range(place, seq_count, 2)) for place in range(2)],
        tiled=True,
    )
    near, far = attend_back(1, rows)

    column_shape = (tp_count, long_docs * own_rows, pair_width)
    cuts = (0, unit_cut, 2 * unit_cut, 2 * unit_cut + rest_rows)
    row_shape = (chips, 2, own_rows // 2, model_width)
    long_sum, quarters = fourth_exchange(
        near.reshape(column_shape), far.reshape(column_shape), terms, givens, cuts, 3
    )
    rows = input_rows(1, long_sum)
    grad_one_now, own_sum = fifth_exchange(rows.reshape(row_shape), quarters, 4)
    input_back(0, after(grad_one, rows).astype(f32))
    input_back(1, grad_one_now.reshape(own_rows, model_width))

    ones = after([h.one for h in stage], grad_one_now)
    packed_sum = sum(contract(one, h.grad_joined, TN) for one, h in zip(ones, stage))
    packed_sum = jnp.pad(packed_sum, ((0, 0), (0, -packed_sum.shape[1] % 128))).astype(bf16)

    def own_columns(values):
        wide = jnp.zeros((chips, local_width), f32)
        return lax.dynamic_update_slice_in_dim(wide, values[None], chip, axis=0).reshape(-1)

    joined_sum = sum(jnp.sum(h.grad_joined.astype(f32), axis=0) for h in stage)
    packed_sum, dense_sum, all_rows = sixth_exchange(
        packed_sum,
        own_sum,
        jnp.concatenate(
            [
                sum(h.row_sums for h in stage),
                sum(h.first_sums for h in stage),
                own_columns(joined_sum[pair_width:] * score_scale)[None],
                own_columns(high_half(joined_sum[:pair_width]))[None],
            ],
            axis=0,
        ),
        6,
    )
    key_grad = low_half(packed_sum[:, :pair_width]).astype(f32)
    value_grad = high_half(packed_sum[:, :pair_width]).astype(f32)
    query_grad = packed_sum[:, pair_width : pair_width + local_width].astype(f32) * score_scale
    dense_sum = dense_sum.reshape(seq_count, -1, model_width).astype(f32)
    inner_weight_grad = dense_sum[:, :unit_cut].reshape(hidden_units, model_width).T
    outer_weight_grad = dense_sum[:, unit_cut : 2 * unit_cut].reshape(hidden_units, model_width)
    rest = dense_sum[:, 2 * unit_cut :]
    proj_weight_grad = rest[:, :proj_cut].reshape(local_width, model_width)
    inner_bias_grad = rest[:, proj_cut, :unit_cut].reshape(hidden_units)

    def my_columns(row):
        return lax.dynamic_slice_in_dim(row, tp_place * local_width, local_width)

    return (
        jnp.stack([h.output for h in stage]),
        jnp.stack([h.input_grad for h in stage]),
        query_grad,
        key_grad,
        value_grad,
        my_columns(all_rows[6]),
        my_columns(all_rows[7]),
        proj_weight_grad,
        all_rows[2],
        all_rows[4],
        all_rows[5],
        all_rows[0],
        all_rows[1],
        inner_weight_grad,
        inner_bias_grad,
        outer_weight_grad,
        all_rows[3],
    )


def general_body(
    tokens,
    doc_lengths,
    rand_blocks,
    query_weight,
    key_weight,
    value_weight,
    query_bias,
    value_bias,
    proj_weight,
    proj_bias,
    first_gain,
    first_bias,
    second_gain,
    second_bias,
    inner_weight,
    inner_bias,
    outer_weight,
    outer_bias,
    out_grad,
):
    micro_count, local_rows, model_width = tokens.shape
    seq_count = lax.axis_size(SEQ)
    tp_count = lax.axis_size(TP)
    seq_place = lax.axis_index(SEQ)
    tp_place = lax.axis_index(TP)
    block_dev = rand_blocks.shape[1]
    heads = rand_blocks.shape[2]
    local_width = query_weight.shape[1]
    head_size = local_width // heads
    hidden_units = inner_weight.shape[1]
    group_rows = block_dev * BLOCK
    reach_dev = (block_dev + LONG_BLK - 2) // block_dev
    window = 2 * reach_dev + 1
    score_scale = 1.0 / math.sqrt(head_size)
    lowest = (seq_place - reach_dev) * block_dev
    blocks = seq_place * block_dev + jnp.arange(block_dev, dtype=jnp.int32)

    held = jnp.concatenate([inner_weight.T, outer_weight, proj_weight, inner_bias[None]], axis=0)
    used_rows = held.shape[0]
    piece_rows = -(-used_rows // (16 * seq_count)) * 16
    held_rows = piece_rows * seq_count
    held = jnp.pad(held, ((0, held_rows - used_rows), (0, 0)))
    share = lax.dynamic_slice_in_dim(held, seq_place * piece_rows, piece_rows, axis=0)
    spread = lax.all_gather(share, (TP, SEQ), axis=0, tiled=True)
    spread = spread.reshape(tp_count, held_rows, model_width)
    cuts = [0, hidden_units, 2 * hidden_units, 2 * hidden_units + local_width, used_rows]
    inner_full = spread[:, cuts[0] : cuts[1]].reshape(-1, model_width)
    outer_full = spread[:, cuts[1] : cuts[2]].reshape(-1, model_width)
    proj_full = spread[:, cuts[2] : cuts[3]].reshape(-1, model_width)
    inner_bias_full = spread[:, cuts[3] : cuts[4]].reshape(-1)

    def by_head(weight):
        return weight.reshape(weight.shape[:-1] + (heads, head_size))

    def side_by_side(first, second):
        paired = jnp.concatenate([by_head(first), by_head(second)], axis=-1)
        return paired.reshape(paired.shape[:-2] + (heads * PAIR,))

    pair_wide = side_by_side(key_weight, value_weight)
    pair_wide_bias = side_by_side(jnp.zeros_like(value_bias), value_bias)

    stage = [Micro() for _ in range(micro_count)]
    for micro, held in enumerate(stage):
        inputs = tokens[micro].astype(f32)
        shifted, stats, inverse = layer_stats(inputs, first_gain, first_bias)
        held.inputs, held.stats_one, held.inverse_one = inputs, stats, inverse
        held.one = lax.all_gather(shifted.astype(bf16), TP, axis=0, tiled=True)

    for micro, held in enumerate(stage):
        one = held.one
        pair_rows = (contract(one, pair_wide, NN) + pair_wide_bias).astype(bf16)
        offsets = [offset for offset in range(-reach_dev, reach_dev + 1) if offset != 0]
        pieces = [from_behind(pair_rows, SEQ, -offset) for offset in offsets]
        queries = ((contract(one, query_weight, NN) + query_bias) * score_scale).astype(bf16)
        held.joined = jnp.concatenate([pair_rows, queries], axis=1)
        key_index, key_valid = block_keys(doc_lengths[micro], rand_blocks[micro], blocks)
        slots = key_index.shape[2]
        slot_index = jnp.clip(key_index - lowest, 0, window * block_dev - 1)
        piece = slot_index // block_dev
        piece = jnp.where(piece == reach_dev, 2 * reach_dev, piece - (piece > reach_dev))
        slot_index = piece * block_dev + slot_index % block_dev
        held.index = slot_index.transpose(1, 0, 2).reshape(-1)
        held.valid = key_valid.reshape(-1)
        held.pieces = pieces

    for held in stage:
        context, held.logsum = attend_forward(
            held.index,
            held.valid,
            held.joined,
            held.pieces,
            heads,
            slots,
        )
        held.context = lax.all_to_all(context, TP, split_axis=0, concat_axis=1, tiled=True)

    outputs = []
    for micro, held in enumerate(stage):
        context = held.context
        hidden = held.inputs + contract(context, proj_full, NN) + proj_bias
        shifted, stats, inverse = layer_stats(hidden, second_gain, second_bias)
        two = shifted.astype(bf16)
        before = contract(two, inner_full, NT) + inner_bias_full
        active = gelu_exact(before).astype(bf16)
        result = hidden + contract(active, outer_full, NN) + outer_bias
        outputs.append(result.astype(bf16))
        grad_out = out_grad[micro]
        grad_float = grad_out.astype(f32)
        grad_active = contract(grad_out, outer_full, NT)
        grad_before = gelu_grad(before, grad_active).astype(bf16)
        grad_two = contract(grad_before, inner_full, NN)
        back, gain_sum, shift_sum = layer_back(grad_two, stats, inverse, second_gain)
        grad_hidden = grad_float + back
        branch = grad_hidden.astype(bf16)
        grad_context = contract(branch, proj_full, NT).astype(bf16)
        held.grad_context = lax.all_to_all(
            grad_context, TP, split_axis=1, concat_axis=0, tiled=True
        )
        held.grad_hidden = grad_hidden
        held.dense = (two, grad_before, active, grad_out, context, branch)
        held.row_sums = (
            jnp.sum(grad_before.astype(f32), axis=0),
            gain_sum,
            shift_sum,
            jnp.sum(branch.astype(f32), axis=0),
            jnp.sum(grad_float, axis=0),
        )

    two, grad_before, active, grad_out, context, branch = (
        jnp.concatenate(group, axis=0) for group in zip(*(h.dense for h in stage))
    )
    inner_part = contract(grad_before, two, TN).astype(bf16)
    outer_part = contract(active, grad_out, TN).astype(bf16)
    proj_part = contract(context, branch, TN).astype(bf16)
    grad_rows = 2 * hidden_units + local_width
    grad_piece = -(-grad_rows // (16 * seq_count)) * 16
    grad_held = grad_piece * seq_count
    parts = jnp.concatenate(
        [
            inner_part.reshape(tp_count, hidden_units, model_width),
            outer_part.reshape(tp_count, hidden_units, model_width),
            proj_part.reshape(tp_count, local_width, model_width),
            jnp.zeros((tp_count, grad_held - grad_rows, model_width), bf16),
        ],
        axis=1,
    ).reshape(tp_count * grad_held, model_width)
    own_part = lax.psum_scatter(parts, (TP, SEQ), scatter_dimension=0, tiled=True)
    dense_sum = lax.all_gather(own_part, SEQ, axis=0, tiled=True).astype(f32)
    inner_weight_grad = dense_sum[cuts[0] : cuts[1]].T
    outer_weight_grad = dense_sum[cuts[1] : cuts[2]]
    proj_weight_grad = dense_sum[cuts[2] : cuts[3]]

    for held in stage:
        *grad_pieces, joined = attend_backward(
            held.index,
            held.valid,
            held.joined,
            held.grad_context,
            held.logsum,
            held.pieces,
            heads,
            slots,
        )
        pair_width = heads * PAIR
        returned = joined[:, :pair_width].astype(f32)
        held.grad_query = joined[:, pair_width:]
        for offset, grad_piece in zip(offsets, grad_pieces):
            returned = returned + from_behind(grad_piece, SEQ, offset).astype(f32)
        held.grad_pair = returned.astype(bf16)

    input_grads = []
    query_sum = pair_sum = 0.0
    query_bias_sum = pair_bias_sum = 0.0
    first_gain_sum = first_bias_sum = 0.0
    for held in stage:
        grad_query, grad_pair, one = held.grad_query, held.grad_pair, held.one
        rows = contract(grad_query, query_weight * score_scale, NT) + contract(grad_pair, pair_wide, NT)
        grad_one = lax.psum_scatter(
            rows.astype(bf16), TP, scatter_dimension=0, tiled=True
        ).astype(f32)
        query_sum = query_sum + contract(one, grad_query, TN)
        pair_sum = pair_sum + contract(one, grad_pair, TN)
        query_bias_sum = query_bias_sum + jnp.sum(grad_query.astype(f32), axis=0)
        pair_bias_sum = pair_bias_sum + jnp.sum(grad_pair.astype(f32), axis=0)
        back, gain_sum, shift_sum = layer_back(
            grad_one, held.stats_one, held.inverse_one, first_gain
        )
        first_gain_sum = first_gain_sum + gain_sum
        first_bias_sum = first_bias_sum + shift_sum
        input_grads.append(held.grad_hidden + back)

    def low_half(wide):
        return wide.reshape(wide.shape[:-1] + (heads, PAIR))[..., :head_size].reshape(
            wide.shape[:-1] + (local_width,)
        )

    def high_half(wide):
        return wide.reshape(wide.shape[:-1] + (heads, PAIR))[..., head_size:].reshape(
            wide.shape[:-1] + (local_width,)
        )

    query_grad, key_grad, value_grad = lax.psum(
        (query_sum * score_scale, low_half(pair_sum), high_half(pair_sum)), SEQ
    )
    inner_bias_sum, second_gain_sum, second_bias_sum, proj_bias_sum, outer_bias_sum = (
        sum(group) for group in zip(*(h.row_sums for h in stage))
    )

    def own_columns(values):
        wide = jnp.zeros((tp_count, local_width), f32)
        return lax.dynamic_update_slice_in_dim(wide, values[None], tp_place, axis=0).reshape(-1)

    early = lax.psum(
        jnp.concatenate(
            [
                inner_bias_sum,
                second_gain_sum,
                second_bias_sum,
                proj_bias_sum,
                outer_bias_sum,
            ]
        ),
        (SEQ, TP),
    )
    late = lax.psum(
        jnp.concatenate(
            [
                first_gain_sum,
                first_bias_sum,
                own_columns(query_bias_sum * score_scale),
                own_columns(high_half(pair_bias_sum)),
            ]
        ),
        (SEQ, TP),
    )
    inner_bias_all = early[: tp_count * hidden_units].reshape(tp_count, hidden_units)
    early_rows = early[tp_count * hidden_units :].reshape(-1, model_width)
    late_rows = late.reshape(-1, model_width)

    def my_columns(row):
        return lax.dynamic_slice_in_dim(row, tp_place * local_width, local_width)

    return (
        jnp.stack(outputs),
        jnp.stack(input_grads),
        query_grad,
        key_grad,
        value_grad,
        my_columns(late_rows[2]),
        my_columns(late_rows[3]),
        proj_weight_grad,
        early_rows[2],
        late_rows[0],
        late_rows[1],
        early_rows[0],
        early_rows[1],
        inner_weight_grad,
        lax.dynamic_index_in_dim(inner_bias_all, tp_place, axis=0, keepdims=False),
        outer_weight_grad,
        early_rows[3],
    )


def solution(mesh):
    def choose(tokens, doc_lengths, rand_blocks, *rest):
        blocks = rand_blocks.shape[1] * mesh.shape[SEQ]
        if plane_applies(mesh, blocks, doc_lengths.shape[1]):
            return plane_body(tokens, doc_lengths, rand_blocks, *rest)
        return general_body(tokens, doc_lengths, rand_blocks, *rest)

    return jax.shard_map(
        choose,
        mesh=mesh,
        in_specs=(
            P(None, (SEQ, TP), None),
            P(),
            P(None, SEQ, TP, None),
            P(None, TP),
            P(None, TP),
            P(None, TP),
            P(TP),
            P(TP),
            P(TP, None),
            P(),
            P(),
            P(),
            P(),
            P(),
            P(None, TP),
            P(TP),
            P(TP, None),
            P(),
            P(None, (SEQ, TP), None),
        ),
        out_specs=(
            P(None, (SEQ, TP), None),
            P(None, (SEQ, TP), None),
            P(None, TP),
            P(None, TP),
            P(None, TP),
            P(TP),
            P(TP),
            P(TP, None),
            P(),
            P(),
            P(),
            P(),
            P(),
            P(None, TP),
            P(TP),
            P(TP, None),
            P(),
        ),
        check_vma=False,
    )
```

```python
import functools
import math

import jax
import jax.numpy as jnp
import numpy as np
from jax import lax
from jax.experimental import pallas as pl
from jax.experimental.pallas import tpu as pltpu
from jax.sharding import PartitionSpec as P

BLOCK = 64
LONG_BLK = 64
SHORT_BLK = 8
PAIR = 2 * BLOCK
UNROLL = 8
SEQ = "seq"
TP = "tp"

NORM_EPS = 1e-05
MASKED = -1000000000.0

f32 = jnp.float32
bf16 = jnp.bfloat16

NN = (((1,), (0,)), ((), ()))
NT = (((1,), (1,)), ((), ()))
TN = (((0,), (0,)), ((), ()))


def contract(left, right, dims):
    return lax.dot_general(left, right, dims, preferred_element_type=f32)


def from_behind(block, axis, distance):
    devices = range(lax.axis_size(axis))
    route = [(i - distance, i) for i in devices if i - distance in devices]
    return lax.ppermute(block, axis, route)


def gelu_exact(values):
    return 0.5 * values * (1.0 + lax.erf(values / math.sqrt(2.0)))


def gelu_grad(values, grad_rows):
    _, pull_back = jax.vjp(gelu_exact, values)
    return pull_back(grad_rows)[0]


def layer_stats(values, norm_gain, norm_shift):
    row_mean = jnp.mean(values, axis=-1, keepdims=True)
    centred = values - row_mean
    inverse = lax.rsqrt(jnp.mean(centred * centred, axis=-1, keepdims=True) + NORM_EPS)
    normed = centred * inverse
    return (normed * norm_gain + norm_shift, normed, inverse)


def layer_back(grad_rows, normed, inverse, norm_gain):
    scaled = grad_rows * norm_gain
    inner_term = (
        scaled
        - jnp.mean(scaled, axis=-1, keepdims=True)
        - normed * jnp.mean(scaled * normed, axis=-1, keepdims=True)
    )
    return (inverse * inner_term, jnp.sum(grad_rows * normed, axis=0), jnp.sum(grad_rows, axis=0))


def block_keys(lengths, randoms, blocks):
    doc_ends = jnp.cumsum(lengths)
    doc_starts = doc_ends - lengths
    doc_owner = jnp.sum((blocks[:, None] >= doc_ends[None, :]).astype(jnp.int32), axis=1)
    doc_ids = jnp.arange(lengths.shape[0], dtype=jnp.int32)
    doc_hit = doc_owner[:, None] == doc_ids[None, :]
    doc_first = jnp.sum(jnp.where(doc_hit, doc_starts[None, :], 0), axis=1)
    doc_final = jnp.sum(jnp.where(doc_hit, doc_ends[None, :], 0), axis=1)
    fixed_keys = jnp.stack(
        [
            jnp.maximum(blocks - 1, doc_first),
            jnp.minimum(blocks + 1, doc_final - 1),
            blocks,
            doc_first,
            doc_first + 1,
        ],
        axis=1,
    )
    block_count = randoms.shape[0]
    head_count = randoms.shape[1]
    key_index = jnp.concatenate(
        [jnp.broadcast_to(fixed_keys[:, None, :], (block_count, head_count, 5)), randoms], axis=2
    )
    key_valid = jnp.stack([blocks > doc_first, blocks + 1 < doc_final], axis=1)
    return (key_index, key_valid.astype(jnp.int32))


def block_rows(block):
    return pl.ds(pl.multiple_of(block * BLOCK, BLOCK), BLOCK)


def listed_blocks(index_ref, store, base, slots):
    return jnp.concatenate(
        [store[block_rows(index_ref[base + slot]), :] for slot in range(slots)], axis=0
    )


def mask_scores(scores, valid_ref, block):
    lane = lax.broadcasted_iota(jnp.int32, (1, PAIR), 1)
    keep = jnp.where(lane < BLOCK, valid_ref[2 * block], valid_ref[2 * block + 1]) > 0
    return jnp.concatenate([jnp.where(keep, scores[:, :PAIR], MASKED), scores[:, PAIR:]], axis=1)


def fill_store(store, pieces):
    place = 0
    for piece in pieces:
        store[place : place + piece.shape[0], :] = piece[...]
        place += piece.shape[0]


def each_head(heads, work):
    for head in range(heads):

        @pl.when(pl.program_id(0) == head)
        def _():
            work(head)


def head_columns(head, first=0):
    return slice(first + head * BLOCK, first + (head + 1) * BLOCK)


def forward_head(slots, head, index_ref, valid_ref, store, wide_query, wide_context, logsum_ref):
    blocks = wide_query.shape[0] // BLOCK

    def step(group, carry):
        ids = [group * UNROLL + unit for unit in range(UNROLL)]
        listed = []
        for block in ids:
            first = (head * blocks + block) * slots
            listed.append(
                jnp.concatenate([store[index_ref[first + slot]] for slot in range(slots)], axis=0)
            )
        scores = [
            mask_scores(contract(wide_query[block_rows(block), :], pairs, NT), valid_ref, block)
            for block, pairs in zip(ids, listed)
        ]
        probs = []
        for block, score in zip(ids, scores):
            top = jnp.max(score, axis=1, keepdims=True)
            raised = jnp.exp(score - top)
            total = jnp.sum(raised, axis=1, keepdims=True)
            probs.append((raised * (1.0 / total)).astype(bf16))
            logsum_ref[block_rows(block), :] = jnp.broadcast_to(
                top + jnp.log(total), (BLOCK, PAIR)
            )
        for block, prob, pairs in zip(ids, probs, listed):
            wide_context[block_rows(block), :] = contract(prob, pairs, NN).astype(bf16)
        return carry

    lax.fori_loop(0, blocks // UNROLL, step, 0)


def widen(query):
    return jnp.concatenate([query, jnp.zeros_like(query)], axis=1)


def forward_kernel(slots, heads, index_ref, valid_ref, query_ref, *refs):
    *pieces, context_ref, logsum_ref, store, wide_query, wide_context = refs
    place = 0
    for piece in pieces:
        count = piece.shape[0] // BLOCK
        store[place : place + count] = piece[...].reshape(count, BLOCK, PAIR)
        place += count

    def take_query(own):
        wide_query[...] = widen(query_ref[:, head_columns(own, heads * PAIR)])

    each_head(heads, take_query)
    forward_head(
        slots, pl.program_id(0), index_ref, valid_ref, store, wide_query, wide_context, logsum_ref
    )

    def give_context(own):
        context_ref[:, head_columns(own)] = wide_context[:, BLOCK:]

    each_head(heads, give_context)


def backward_kernel(slots, heads, count, index_ref, valid_ref, query_ref, grad_ref, logsum_ref, *refs):
    pieces, refs = refs[:count], refs[count:]
    grad_pieces, joined_ref = refs[: count - 1], refs[count - 1]
    store, sums, both_rows, wide_grad = refs[count:]
    rows = query_ref.shape[0]
    blocks = rows // BLOCK
    head = pl.program_id(0)
    fill_store(store, pieces)
    sums[...] = jnp.zeros_like(sums)
    lane = lax.broadcasted_iota(jnp.int32, (BLOCK, PAIR), 1)

    def take_both(own):
        query = query_ref[:, head_columns(own, heads * PAIR)]
        both_rows[...] = jnp.concatenate([query, grad_ref[:, head_columns(own)]], axis=1)

    each_head(heads, take_both)

    def step(group, carry):
        ids = [group * UNROLL + unit for unit in range(UNROLL)]
        listed = [
            listed_blocks(index_ref, store, (head * blocks + block) * slots, slots)
            for block in ids
        ]
        lefts = []
        for block in ids:
            both = both_rows[block_rows(block), :]
            lefts.append(
                jnp.concatenate(
                    [
                        jnp.where(lane < BLOCK, both, 0).astype(bf16),
                        jnp.where(lane < BLOCK, 0, both).astype(bf16),
                    ],
                    axis=0,
                )
            )
        products = [contract(left, pairs, NT) for left, pairs in zip(lefts, listed)]
        mixes = []
        for block, product in zip(ids, products):
            score = mask_scores(product[:BLOCK], valid_ref, block)
            grad_prob = product[BLOCK:]
            logsum = jnp.concatenate([logsum_ref[block_rows(block), :]] * (slots // 2), axis=1)
            prob = jnp.exp(score - logsum)
            delta = jnp.sum(prob * grad_prob, axis=1, keepdims=True)
            grad_score = prob * (grad_prob - delta)
            mixes.append(jnp.concatenate([grad_score.astype(bf16), prob.astype(bf16)], axis=0))
        for block, mix, pairs in zip(ids, mixes, listed):
            wide_grad[block_rows(block), :] = contract(mix[:BLOCK], pairs, NN).astype(bf16)
        terms = [contract(mix, left, TN) for mix, left in zip(mixes, lefts)]
        for block, term in zip(ids, terms):
            base = (head * blocks + block) * slots
            for slot in range(slots):
                sums[block_rows(index_ref[base + slot]), :] += term[
                    slot * BLOCK : (slot + 1) * BLOCK
                ]
        return carry

    lax.fori_loop(0, blocks // UNROLL, step, 0)
    place = 0
    for grad_piece in grad_pieces:
        grad_piece[...] = sums[place : place + grad_piece.shape[0], :].astype(bf16)
        place += grad_piece.shape[0]

    def give_joined(own):
        joined_ref[:, own * PAIR : (own + 1) * PAIR] = sums[place:, :].astype(bf16)
        start = heads * PAIR + own * BLOCK
        joined_ref[:, start : start + BLOCK] = wide_grad[:, :BLOCK]

    each_head(heads, give_joined)


def lasting(microseconds):
    return pl.CostEstimate(
        flops=0, bytes_accessed=int(microseconds * 3.69e6), transcendentals=0
    )


def per_head(array):
    return pl.BlockSpec((array.shape[0], PAIR), lambda head, *_: (0, head))


def whole(array):
    return pl.BlockSpec(array.shape, lambda head, *_: (0, 0))


def attend_forward(index, valid, joined, pieces, heads, slots):
    rows = joined.shape[0]
    pieces = pieces + [joined]
    context = jax.ShapeDtypeStruct((rows, heads * BLOCK), bf16)
    stored = sum(piece.shape[0] for piece in pieces)
    logsum = jax.ShapeDtypeStruct((rows, heads * PAIR), f32)
    return pl.pallas_call(
        functools.partial(forward_kernel, slots, heads),
        grid_spec=pltpu.PrefetchScalarGridSpec(
            num_scalar_prefetch=2,
            grid=(heads,),
            in_specs=[whole(joined)] + [per_head(piece) for piece in pieces],
            out_specs=[whole(context), per_head(logsum)],
            scratch_shapes=[
                pltpu.VMEM((stored // BLOCK, BLOCK, PAIR), bf16),
                pltpu.VMEM((rows, PAIR), bf16),
                pltpu.VMEM((rows, PAIR), bf16),
            ],
        ),
        out_shape=[context, logsum],
        compiler_params=pltpu.CompilerParams(vmem_limit_bytes=40 * 2**20),
        cost_estimate=lasting(18),
    )(index, valid, joined, *pieces)


def attend_backward(index, valid, joined, grads, logsum, pieces, heads, slots):
    rows = joined.shape[0]
    pieces = pieces + [joined]
    stored = sum(piece.shape[0] for piece in pieces)
    piece_specs = [per_head(piece) for piece in pieces]
    return pl.pallas_call(
        functools.partial(backward_kernel, slots, heads, len(pieces)),
        grid_spec=pltpu.PrefetchScalarGridSpec(
            num_scalar_prefetch=2,
            grid=(heads,),
            in_specs=[whole(joined), whole(grads), per_head(logsum)] + piece_specs,
            out_specs=piece_specs[:-1] + [whole(joined)],
            scratch_shapes=[
                pltpu.VMEM((stored, PAIR), bf16),
                pltpu.VMEM((stored, PAIR), f32),
                pltpu.VMEM((rows, PAIR), bf16),
                pltpu.VMEM((rows, PAIR), bf16),
            ],
        ),
        out_shape=[jax.ShapeDtypeStruct(piece.shape, bf16) for piece in pieces],
        compiler_params=pltpu.CompilerParams(vmem_limit_bytes=50 * 2**20),
        cost_estimate=lasting(25),
    )(index, valid, joined, grads, logsum, *pieces)


def dense_kernel(core_ref, *refs):
    ins, (given_inner, given_outer, kept_inner, kept_outer, proj) = refs[:12], refs[12:]
    step = pl.program_id(0)
    half = pl.num_programs(0) // 2

    def term(first):
        total = contract(ins[first][...], ins[first + 2][...], TN)
        return (total + contract(ins[first + 1][...], ins[first + 3][...], TN)).astype(bf16)

    @pl.when(step < half)
    def _():
        given_inner[...] = term(0)
        given_outer[...] = term(4)

    @pl.when(step >= half)
    def _():
        kept_inner[...] = term(0)
        kept_outer[...] = term(4)

    @pl.when(step == 0)
    def _():
        proj[...] = term(8)


def dense_terms(core, units, rows):
    steps = 8
    hidden = units[0][0].shape[1]
    tile = hidden // steps
    width = rows[0][0].shape[1]

    def unit_tile(step, core_ref):
        owner = jnp.where(step < steps // 2, 1 - core_ref[0], core_ref[0])
        return (0, owner * (steps // 2) + step % (steps // 2))

    def whole_rows(array):
        return pl.BlockSpec(array.shape, lambda step, *_: (0, 0))

    ins, specs = [], []
    for place in range(3):
        for array in units[place]:
            ins.append(array)
            if place < 2:
                specs.append(pl.BlockSpec((array.shape[0], tile), unit_tile))
            else:
                specs.append(whole_rows(array))
        for array in rows[place]:
            ins.append(array)
            specs.append(whole_rows(array))
    half = jax.ShapeDtypeStruct((hidden // 2, width), bf16)
    proj = jax.ShapeDtypeStruct((units[2][0].shape[1], width), bf16)
    given = pl.BlockSpec((tile, width), lambda step, *_: (jnp.minimum(step, steps // 2 - 1), 0))
    kept = pl.BlockSpec((tile, width), lambda step, *_: (jnp.maximum(step - steps // 2, 0), 0))
    return pl.pallas_call(
        dense_kernel,
        grid_spec=pltpu.PrefetchScalarGridSpec(
            num_scalar_prefetch=1,
            grid=(steps,),
            in_specs=specs,
            out_specs=[given, given, kept, kept, whole_rows(proj)],
        ),
        out_shape=[half] * 4 + [proj],
        compiler_params=pltpu.CompilerParams(vmem_limit_bytes=40 * 2**20),
        cost_estimate=lasting(15),
    )(core.reshape(1), *ins)


def plane_exchange(values, split_axis, concat_axis):
    count = lax.axis_size(SEQ)
    groups = [list(range(place, count, 2)) for place in range(2)]
    return lax.all_to_all(
        values,
        SEQ,
        split_axis=split_axis,
        concat_axis=concat_axis,
        axis_index_groups=groups,
        tiled=True,
    )


def plane_gather(values):
    count = lax.axis_size(SEQ) // 2
    return plane_exchange(jnp.concatenate([values] * count, axis=0), 0, 0)


def core_swap(block):
    route = [(place, place ^ 1) for place in range(lax.axis_size(SEQ))]
    return lax.ppermute(block, SEQ, route)


def column_shift(block, step):
    count = lax.axis_size(TP)
    return lax.ppermute(block, TP, [(place, (place + step) % count) for place in range(count)])


def column_gather(values):
    count = lax.axis_size(TP)
    place = lax.axis_index(TP)
    spread = jnp.zeros((count,) + values.shape, values.dtype)
    spread = lax.dynamic_update_index_in_dim(spread, values, place, axis=0)
    for step in range(1, count):
        spread = lax.dynamic_update_index_in_dim(
            spread, column_shift(values, step), (place - step) % count, axis=0
        )
    return spread


def after(values, *earlier):
    return lax.optimization_barrier((values, earlier))[0]


def sum_parts(parts):
    total = parts[0].astype(f32)
    for place in range(1, len(parts)):
        total = total + parts[place].astype(f32)
    return total


def partner_of(place):
    return place + 1 - 2 * (place % 2)


def enter(neighbours):
    barrier = pltpu.get_barrier_semaphore()
    count = 0
    for exists, device in neighbours:

        @pl.when(exists)
        def _():
            pl.semaphore_signal(
                barrier, inc=1, device_id=device, device_id_type=pl.DeviceIdType.MESH
            )

        count = count + jnp.where(exists, 1, 0)
    pl.semaphore_wait(barrier, count)


def remote(source, target, send, receive, device):
    return pltpu.make_async_remote_copy(
        src_ref=source,
        dst_ref=target,
        send_sem=send,
        recv_sem=receive,
        device_id=device,
        device_id_type=pl.DeviceIdType.MESH,
    )


def plane_ids():
    seq_place = lax.axis_index(SEQ)
    chip, core = seq_place // 2, seq_place % 2
    beside = chip + 1 - 2 * (chip % 2)
    above = chip + 2 - 4 * (chip // 2)
    facing = 3 - chip
    return chip, core, beside, above, facing


def column_way(place, way, distance):
    return place - distance if way == 0 else place + distance


class ColumnSpread:

    def __init__(self, parts, own, near, far, other, keep_sem, along_sems, across_sems):
        self.parts, self.own, self.near, self.far = parts, own, near, far
        self.other, self.keep_sem = other, keep_sem
        self.along_sems, self.across_sems = along_sems, across_sems
        self.count = lax.axis_size(TP)
        self.place = lax.axis_index(TP)
        self.rows = own.shape[0] // parts

    def cut(self, part):
        return pl.ds(part * self.rows, self.rows)

    def block(self, way, distance, part):
        if distance == 0:
            return self.own.at[self.cut(part)]
        return self.near.at[column_way(self.place, way, distance), self.cut(part)]

    def along(self, way, distance, part):
        return remote(
            self.block(way, distance, part),
            self.near.at[column_way(self.place, way, distance), self.cut(part)],
            self.along_sems[0].at[way, distance, part],
            self.along_sems[1].at[way, distance, part],
            {TP: self.place + 1 if way == 0 else self.place - 1},
        )

    def landed(self, way, distance, part):
        block = self.near.at[column_way(self.place, way, distance), self.cut(part)]
        return remote(
            block,
            block,
            self.along_sems[0].at[way, distance, part],
            self.along_sems[1].at[way, distance - 1, part],
            self.other,
        )

    def across(self, way, distance, part):
        return remote(
            self.block(way, distance, part),
            self.far.at[column_way(self.place, way, distance), self.cut(part)],
            self.across_sems[0].at[way, distance, part],
            self.across_sems[1].at[way, distance, part],
            self.other,
        )

    def keep(self):
        return pltpu.make_async_copy(self.own, self.near.at[self.place], self.keep_sem)

    def goes_on(self, way):
        return self.place < self.count - 1 if way == 0 else self.place > 0

    def has_come(self, way, distance):
        if way == 0:
            return self.place >= distance
        return self.place + distance < self.count

    def start(self):
        for part in range(self.parts):
            for way in range(2):

                @pl.when(self.goes_on(way))
                def _():
                    self.along(way, 0, part).start()

        if self.far is not None:
            for part in range(self.parts):
                self.across(0, 0, part).start()
        self.keep().start()

    def step(self, distance, part):
        for way in range(2):

            @pl.when(self.has_come(way, distance))
            def _():
                self.landed(way, distance, part).wait_recv()
                if distance < self.count - 1:

                    @pl.when(self.goes_on(way))
                    def _():
                        self.along(way, distance, part).start()

                if self.far is not None:
                    self.across(way, distance, part).start()

    def finish(self):
        self.keep().wait()
        for part in range(self.parts):
            if self.far is not None:
                self.across(0, 0, part).wait()
            for way in range(2):

                @pl.when(self.goes_on(way))
                def _():
                    self.along(way, 0, part).wait_send()

        for distance in range(1, self.count):
            for part in range(self.parts):
                for way in range(2):

                    @pl.when(self.has_come(way, distance))
                    def _():
                        if distance < self.count - 1:

                            @pl.when(self.goes_on(way))
                            def _():
                                self.along(way, distance, part).wait_send()

                        if self.far is not None:
                            self.across(way, distance, part).wait()


class PlaneSpread:

    def __init__(self, own, out, sems):
        self.own, self.out = own, out
        self.send_row, self.recv_row, self.send_on, self.recv_on = sems
        self.chip, core, beside, above, self.facing = plane_ids()
        self.ways = ({SEQ: 2 * beside + core}, {SEQ: 2 * above + core})
        self.chips = (beside, above)

    def first(self, way, part):
        return remote(
            self.own(part),
            self.out(self.chip, part),
            self.send_row.at[way, part],
            self.recv_row.at[way, part],
            self.ways[way],
        )

    def second(self, way):
        return remote(
            self.out(self.chips[way], way),
            self.out(self.chips[way], way),
            self.send_on.at[way],
            self.recv_on.at[way],
            self.ways[1 - way],
        )

    def start(self):
        self.first(0, 0).start()
        self.first(1, 1).start()

    def forward(self):
        for way in range(2):
            self.first(way, way).wait_recv()
            self.second(way).start()
        for way in range(2):
            self.first(way, 1 - way).start()

    def arrive(self):
        for way in range(2):
            self.first(way, 1 - way).wait_recv()
        for way in range(2):
            self.second(way).wait_recv()

    def finish(self):
        for way in range(2):
            self.second(way).wait_send()
            for part in range(2):
                self.first(way, part).wait_send()


def plane_sems():
    dma = pltpu.SemaphoreType.DMA
    return [dma((2, 2)), dma((2, 2)), dma((2,)), dma((2,))]


def column_sems(parts):
    sems = pltpu.SemaphoreType.DMA((2, 4, parts))
    return [sems, sems, sems, sems]


def halves_of(own, out, keep_sem):
    half = own.shape[0] // 2
    chip = plane_ids()[0]
    return (
        lambda part: own.at[pl.ds(part * half, half)],
        lambda place, part: out.at[place, pl.ds(part * half, half)],
        pltpu.make_async_copy(own, out.at[chip], keep_sem),
    )


def neighbours(facing_too, column_too):
    chip, core, beside, above, facing = plane_ids()
    count = lax.axis_size(TP)
    place = lax.axis_index(TP)
    always = place >= 0
    devices = [(always, {SEQ: 2 * chip + 1 - core})]
    devices += [(always, {SEQ: 2 * beside + core}), (always, {SEQ: 2 * above + core})]
    if facing_too:
        devices.append((always, {SEQ: 2 * facing + core}))
    if column_too:
        for step in range(1, count):
            devices.append((always, {TP: lax.rem(place + step, count)}))
    else:
        devices.append((place < count - 1, {TP: place + 1}))
        devices.append((place > 0, {TP: place - 1}))
    return devices


def first_kernel(
    parts,
    own_ref,
    weight_ref,
    share_ref,
    random_ref,
    out_ref,
    spread_ref,
    column_ref,
    random_out_ref,
    randoms,
    own_sem,
    send_row,
    recv_row,
    send_on,
    recv_on,
    send_z,
    recv_z,
    send_far,
    recv_far,
    send_random,
    recv_random,
    send_column,
    recv_column,
    send_share,
    recv_share,
):
    chip, core, beside, above, facing = plane_ids()
    tp_count = lax.axis_size(TP)
    place = lax.axis_index(TP)
    other = {SEQ: 2 * chip + 1 - core}
    weight_rows = weight_ref.shape[0] // (2 * parts)
    column = [{TP: lax.rem(place + step, tp_count)} for step in range(1, tp_count)]
    enter(neighbours(True, True))
    own, out, keep_rows = halves_of(own_ref, out_ref, own_sem.at[0])
    rows = PlaneSpread(own, out, (send_row, recv_row, send_on, recv_on))
    shares = ColumnSpread(
        2, share_ref, column_ref, None, other, own_sem.at[2], (send_share, recv_share), None
    )

    def weight_cut(part, holder):
        return pl.ds((holder * parts + part) * weight_rows, weight_rows)

    def weight_along(source, way, part):
        at = weight_cut(part, core)
        return remote(
            source.at[at],
            spread_ref.at[at],
            send_z.at[way, part],
            recv_z.at[part],
            {TP: place + 1 if way == 0 else place - 1},
        )

    def weight_across(part):
        at = weight_cut(part, core)
        return remote(
            spread_ref.at[at], spread_ref.at[at], send_far.at[part], recv_far.at[part], other
        )

    def goes_on(way):
        if way == 0:
            return (place >= chip) & (place < tp_count - 1)
        return (place <= chip) & (place > 0)

    def random_to_holder(sender):
        return remote(
            random_ref,
            randoms.at[sender],
            send_random,
            recv_random.at[sender],
            {SEQ: 2 * place + core},
        )

    def random_along(step):
        return remote(
            randoms,
            random_out_ref,
            send_column.at[step],
            recv_column,
            column[step],
        )

    rows.start()

    @pl.when(place != chip)
    def _():
        random_to_holder(chip).start()

    for part in range(parts):
        for way in range(2):

            @pl.when((place == chip) & goes_on(way))
            def _():
                weight_along(weight_ref, way, part).start()

    shares.start()
    keep_rows.start()

    @pl.when(place == chip)
    def _():
        keep = pltpu.make_async_copy(weight_ref, spread_ref, own_sem.at[1])
        keep.start()
        keep.wait()
        randoms[chip] = random_ref[...]
        for step in range(1, tp_count):
            random_to_holder(lax.rem(chip + step, tp_count)).wait_recv()
        random_out_ref[...] = randoms[...]
        for step in range(tp_count - 1):
            random_along(step).start()

    rows.forward()
    for part in range(parts):

        @pl.when(place != chip)
        def _():
            weight_along(spread_ref, 0, part).wait_recv()
            for way in range(2):

                @pl.when(goes_on(way))
                def _():
                    weight_along(spread_ref, way, part).start()

            weight_across(part).start()

    for distance in range(1, tp_count):
        for part in range(2):
            shares.step(distance, part)
    rows.arrive()
    rows.finish()
    shares.finish()
    keep_rows.wait()

    @pl.when(place != chip)
    def _():
        random_to_holder(chip).wait_send()
        random_along(0).wait_recv()

    @pl.when(place == chip)
    def _():
        for step in range(tp_count - 1):
            random_along(step).wait_send()

    for part in range(parts):

        @pl.when(place != chip)
        def _():
            weight_across(part).wait()

        for way in range(2):

            @pl.when(goes_on(way))
            def _():
                weight_along(spread_ref, way, part).wait_send()


def first_exchange(own, weight, share, randoms, collective_id, parts=4):
    chips = lax.axis_size(SEQ) // 2
    count = lax.axis_size(TP)
    resident = pl.BlockSpec(memory_space=pltpu.VMEM)
    dma = pltpu.SemaphoreType.DMA
    return pl.pallas_call(
        functools.partial(first_kernel, parts),
        out_shape=[
            jax.ShapeDtypeStruct((chips,) + own.shape, own.dtype),
            jax.ShapeDtypeStruct(weight.shape, weight.dtype),
            jax.ShapeDtypeStruct((count,) + share.shape, share.dtype),
            jax.ShapeDtypeStruct((chips,) + randoms.shape, randoms.dtype),
        ],
        in_specs=[resident] * 4,
        out_specs=[resident] * 4,
        scratch_shapes=[pltpu.VMEM((chips,) + randoms.shape, randoms.dtype), dma((3,))]
        + plane_sems()
        + [
            dma((2, parts)),
            dma((parts,)),
            dma((parts,)),
            dma((parts,)),
            dma,
            dma((chips,)),
            dma((chips - 1,)),
            dma,
        ]
        + column_sems(2)[:2],
        compiler_params=pltpu.CompilerParams(
            collective_id=collective_id, has_side_effects=True, vmem_limit_bytes=32 * 2**20
        ),
        cost_estimate=lasting(30),
    )(own, weight, share, randoms)


class WeightSpread:

    def __init__(self, column, rows, out, keep_sem, cross_sems, plane_sems):
        self.out, self.cross_sems = out, cross_sems
        self.chip, self.core, self.beside, self.above, self.facing = plane_ids()
        self.other = {SEQ: 2 * self.chip + 1 - self.core}
        self.half = column.shape[0] // 2
        self.plane = PlaneSpread(
            lambda part: column.at[pl.ds(part * self.half, self.half), rows],
            lambda where, part: out.at[self.core, where, pl.ds(part * self.half, self.half)],
            plane_sems,
        )
        self.keep = pltpu.make_async_copy(
            column.at[:, rows], out.at[self.core, self.chip], keep_sem
        )

    def across(self, where, part):
        chip = (self.chip, self.beside, self.above, self.facing)[where]
        block = self.out.at[self.core, chip, pl.ds(part * self.half, self.half)]
        at = (where, part)
        return remote(
            block, block, self.cross_sems[0].at[at], self.cross_sems[1].at[at], self.other
        )

    def start(self):
        self.plane.start()
        self.keep.start()

    def forward(self):
        self.plane.forward()
        self.keep.wait()
        for where, part in ((0, 0), (0, 1), (1, 0), (2, 1)):
            self.across(where, part).start()

    def arrive(self):
        self.plane.arrive()
        for where, part in ((1, 1), (2, 0), (3, 0), (3, 1)):
            self.across(where, part).start()

    def finish(self):
        self.plane.finish()
        for where in range(4):
            for part in range(2):
                self.across(where, part).wait()


def weight_sems():
    dma = pltpu.SemaphoreType.DMA
    return [dma, dma((4, 2)), dma((4, 2))] + plane_sems()


def weight_shape(column, rows):
    tp_count, _, width = column.shape
    chips = lax.axis_size(SEQ) // 2
    return jax.ShapeDtypeStruct((2, chips, tp_count, rows[1] - rows[0], width), column.dtype)


def second_kernel(
    parts,
    rows,
    longs_ref,
    own_ref,
    column_ref,
    near_ref,
    far_ref,
    out_ref,
    weight_ref,
    keep_sem,
    *sems,
):
    chip, core = plane_ids()[:2]
    enter(neighbours(False, False))
    other = {SEQ: 2 * chip + 1 - core}
    longs = ColumnSpread(
        parts, longs_ref, near_ref, far_ref, other, keep_sem.at[0], sems[:2], sems[2:4]
    )
    own, out, keep_rows = halves_of(own_ref, out_ref, keep_sem.at[1])
    plane = PlaneSpread(own, out, sems[4:8])
    weight = WeightSpread(
        column_ref, pl.ds(rows[0], rows[1] - rows[0]), weight_ref, sems[8], sems[9:11], sems[11:15]
    )
    longs.start()
    plane.start()
    weight.start()
    keep_rows.start()
    for part in range(parts):
        longs.step(1, part)
    plane.forward()
    weight.forward()
    for part in range(parts):
        longs.step(2, part)
    plane.arrive()
    weight.arrive()
    for part in range(parts):
        longs.step(3, part)
    plane.finish()
    weight.finish()
    longs.finish()
    keep_rows.wait()


def second_exchange(longs, own, column, rows, collective_id, parts=2):
    chips = lax.axis_size(SEQ) // 2
    near = jax.ShapeDtypeStruct((lax.axis_size(TP),) + longs.shape, longs.dtype)
    resident = pl.BlockSpec(memory_space=pltpu.VMEM)
    return pl.pallas_call(
        functools.partial(second_kernel, parts, rows),
        out_shape=[
            near,
            near,
            jax.ShapeDtypeStruct((chips,) + own.shape, own.dtype),
            weight_shape(column, rows),
        ],
        in_specs=[resident] * 3,
        out_specs=[resident] * 4,
        scratch_shapes=[pltpu.SemaphoreType.DMA((2,))]
        + column_sems(parts)
        + plane_sems()
        + weight_sems(),
        compiler_params=pltpu.CompilerParams(
            collective_id=collective_id, has_side_effects=True, vmem_limit_bytes=48 * 2**20
        ),
        cost_estimate=lasting(58),
    )(longs, own, column)


def third_kernel(
    parts,
    cuts,
    slots,
    heads,
    index_ref,
    valid_ref,
    longs_ref,
    column_ref,
    joined_ref,
    *refs,
):
    count = len(cuts)
    pieces, refs = refs[:3], refs[3:]
    near_ref, far_ref, context_ref, logsum_ref, refs = refs[0], refs[1], refs[2], refs[3], refs[4:]
    outs, refs = refs[:count], refs[count:]
    stores, wide_query, wide_context, sent, refs = refs[:2], refs[2], refs[3], refs[4], refs[5:]
    load_sem, keep_sem, block_sems, sems = refs[0], refs[1], refs[2:4], refs[4:8]
    chip, core, beside, above, facing = plane_ids()
    enter(neighbours(True, False))
    other = {SEQ: 2 * chip + 1 - core}
    longs = ColumnSpread(
        parts, longs_ref, near_ref, far_ref, other, keep_sem, sems[:2], sems[2:4]
    )
    weights = []
    for index, (first, last) in enumerate(cuts):
        own = refs[8 + 7 * index : 15 + 7 * index]
        weights.append(
            WeightSpread(
                column_ref, pl.ds(first, last - first), outs[index], own[0], own[1:3], own[3:7]
            )
        )

    def loads(head):
        copies, place = [], 0
        for index, piece in enumerate(pieces):
            rows = piece.shape[0]
            copies.append(
                pltpu.make_async_copy(
                    piece.at[:, :, pl.ds(head * PAIR, PAIR)],
                    stores[head % 2].at[pl.ds(place, rows)],
                    load_sem.at[head, index],
                )
            )
            place += rows
        return copies

    def load(head):
        for copy in loads(head):
            copy.start()

    def work(head):
        for copy in loads(head):
            copy.wait()
        if head + 1 < heads:
            load(head + 1)
        wide_query[...] = widen(joined_ref[:, head_columns(head, heads * PAIR)])
        forward_head(
            slots,
            head,
            index_ref,
            valid_ref,
            stores[head % 2],
            wide_query,
            wide_context,
            logsum_ref.at[:, pl.ds(head * PAIR, PAIR)],
        )
        rows = sent.shape[1]
        for place in range(sent.shape[0]):
            sent[place, :, head_columns(head)] = wide_context[
                place * rows : (place + 1) * rows, BLOCK:
            ]

    def send_block(index):
        target = (beside, above, facing)[index]
        return remote(
            sent.at[target],
            context_ref.at[chip],
            block_sems[0].at[index],
            block_sems[1].at[index],
            {SEQ: 2 * target + core},
        )

    load(0)
    longs.start()
    for weight in weights:
        weight.start()
    work(0)
    for part in range(parts):
        longs.step(1, part)
    for weight in weights:
        weight.forward()
    work(1)
    for part in range(parts):
        longs.step(2, part)
    work(2)
    for index in range(3):
        send_block(index).start()
    context_ref[chip] = sent[chip]
    for weight in weights:
        weight.arrive()
    for part in range(parts):
        longs.step(3, part)
    longs.finish()
    for weight in weights:
        weight.finish()
    for index in range(3):
        send_block(index).wait()


def third_exchange(
    longs, column, index, valid, joined, pieces, cuts, heads, slots, collective_id, parts=2
):
    near = jax.ShapeDtypeStruct((column.shape[0],) + longs.shape, longs.dtype)
    chips = lax.axis_size(SEQ) // 2
    rows = joined.shape[0]
    stored = sum(piece.shape[0] for piece in pieces) + rows
    context = jax.ShapeDtypeStruct((chips, rows // chips, heads * BLOCK), joined.dtype)
    resident = pl.BlockSpec(memory_space=pltpu.VMEM)
    scalars = pl.BlockSpec(memory_space=pltpu.SMEM)
    anywhere = pl.BlockSpec(memory_space=pl.ANY)
    dma = pltpu.SemaphoreType.DMA
    sems = [sem for _ in cuts for sem in weight_sems()]
    return pl.pallas_call(
        functools.partial(third_kernel, parts, cuts, slots, heads),
        out_shape=[near, near, context, jax.ShapeDtypeStruct((rows, heads * PAIR), f32)]
        + [weight_shape(column, cut) for cut in cuts],
        in_specs=[scalars] * 2 + [resident] * 3 + [anywhere] * 3,
        out_specs=[resident] * (4 + len(cuts)),
        scratch_shapes=[
            pltpu.VMEM((stored // BLOCK, BLOCK, PAIR), bf16),
            pltpu.VMEM((stored // BLOCK, BLOCK, PAIR), bf16),
            pltpu.VMEM((rows, PAIR), bf16),
            pltpu.VMEM((rows, PAIR), bf16),
            pltpu.VMEM(context.shape, bf16),
            dma((heads, 3)),
            dma,
            dma((3,)),
            dma((3,)),
        ]
        + column_sems(parts)
        + sems,
        compiler_params=pltpu.CompilerParams(
            collective_id=collective_id, has_side_effects=True, vmem_limit_bytes=52 * 2**20
        ),
        cost_estimate=lasting(62),
    )(
        index,
        valid,
        longs,
        column,
        joined,
        *(piece.reshape(-1, BLOCK, piece.shape[1]) for piece in pieces + [joined]),
    )


class ColumnReduce:

    def __init__(self, parts, step_rows, sums, came, sems):
        self.parts, self.step_rows = parts, step_rows
        self.sums, self.came, self.sems = sums, came, sems
        self.count = lax.axis_size(TP)
        self.place = lax.axis_index(TP)
        self.rows = sums.shape[1] // parts
        self.order = []
        for step in range(self.count):
            for owner in (step, self.count - 1 - step):
                if owner not in self.order:
                    self.order.append(owner)

    def along(self, way, owner, part):
        at = pl.ds(part * self.rows, self.rows)
        return remote(
            self.sums.at[owner, at],
            self.came.at[way, owner, at],
            self.sems[0].at[way, owner, part],
            self.sems[1].at[way, owner, part],
            {TP: self.place - 1 if way == 0 else self.place + 1},
        )

    def add(self, owner, source, part):
        @pl.loop(0, self.rows // self.step_rows)
        def _(step):
            start = pl.multiple_of(part * self.rows + step * self.step_rows, self.step_rows)
            at = pl.ds(start, self.step_rows)
            total = self.sums[owner, at, :].astype(f32) + source[at, :].astype(f32)
            self.sums[owner, at, :] = total.astype(self.sums.dtype)

    def takes(self, way):
        return self.place < self.count - 1 if way == 0 else self.place > 0

    def passes(self, way, owner):
        return self.place > owner if way == 0 else self.place < owner

    def begin(self, owner, part):
        for way in range(2):

            @pl.when(self.passes(way, owner) & ~self.takes(way))
            def _():
                self.along(way, owner, part).start()

    def move(self, way, owner, part):
        @pl.when(self.passes(way, owner) & self.takes(way))
        def _():
            self.along(way, owner, part).wait_recv()
            self.add(owner, self.came.at[way, owner], part)
            self.along(way, owner, part).start()

    def end(self):
        for part in range(self.parts):
            for way in range(2):
                for owner in range(self.count):

                    @pl.when((self.place == owner) & self.takes(way))
                    def _():
                        self.along(way, owner, part).wait_recv()
                        self.add(owner, self.came.at[way, owner], part)

    def finish(self):
        for owner in range(self.count):
            for part in range(self.parts):
                for way in range(2):

                    @pl.when(self.passes(way, owner))
                    def _():
                        self.along(way, owner, part).wait_send()

    def give(self, out):
        for owner in range(self.count):

            @pl.when(self.place == owner)
            def _():
                out[...] = self.sums[owner]


class PlaneReduce:

    def __init__(self, step_rows, terms, out, buffers, sems):
        self.step_rows, self.terms, self.out = step_rows, terms, out
        self.came, self.facing_came, self.sent, self.last = buffers
        self.sems = sems
        self.chip, core, beside, above, self.facing = plane_ids()
        self.ways = ({SEQ: 2 * beside + core}, {SEQ: 2 * above + core})
        self.chips = (beside, above)
        self.half = terms.shape[1] // 2

    def copy(self, kind, way, source, target, device):
        return remote(
            source, target.at[way], self.sems[0].at[kind, way], self.sems[1].at[kind, way], device
        )

    def pieces(self, way):
        return pl.ds(way * self.half, self.half)

    def facing_term(self, way):
        source = self.terms.at[self.facing, self.pieces(way)]
        return self.copy(0, way, source, self.facing_came, self.ways[way])

    def near_term(self, way):
        source = self.terms.at[self.chips[way], self.pieces(way)]
        return self.copy(1, way, source, self.came, self.ways[way])

    def summed(self, way):
        return self.copy(2, way, self.sent.at[way], self.last, self.ways[1 - way])

    def each_step(self, work):
        steps = self.terms.shape[2] // self.step_rows

        @pl.loop(0, self.half * steps)
        def _(step):
            start = pl.multiple_of((step % steps) * self.step_rows, self.step_rows)
            work(step // steps, pl.ds(start, self.step_rows))

    def start(self):
        for way in range(2):
            self.facing_term(way).start()
        for way in range(2):
            self.near_term(way).start()

    def move(self):
        for way in range(2):
            self.facing_term(way).wait_recv()

            def add_term(piece, at):
                total = self.terms[self.chips[1 - way], way * self.half + piece, at, :].astype(f32)
                total = total + self.facing_came[way, piece, at, :].astype(f32)
                self.sent[way, piece, at, :] = total.astype(self.sent.dtype)

            self.each_step(add_term)
            self.summed(way).start()

    def end(self):
        for way in range(2):
            self.near_term(way).wait_recv()
            self.summed(way).wait_recv()

            def add_last(piece, at):
                total = self.terms[self.chip, way * self.half + piece, at, :].astype(f32)
                total = total + self.came[way, piece, at, :].astype(f32)
                total = total + self.last[way, piece, at, :].astype(f32)
                self.out[way * self.half + piece, at, :] = total.astype(self.out.dtype)

            self.each_step(add_last)

    def finish(self):
        for way in range(2):
            self.facing_term(way).wait_send()
            self.near_term(way).wait_send()
            self.summed(way).wait_send()


def reduce_scratch(shape, dtype):
    half = pltpu.VMEM((2, shape[1] // 2) + shape[2:], dtype)
    sems = pltpu.SemaphoreType.DMA((3, 2))
    return [half] * 4 + [sems, sems]


def fourth_kernel(parts, cuts, near_ref, far_ref, *refs):
    count = len(cuts) - 1
    terms, givens, refs = refs[:count], refs[count : 2 * count], refs[2 * count :]
    out_ref, dense_ref, sums, given, came, dense, more = refs[:7]
    load_sem, send_far, recv_far, send_z, recv_z = refs[7:12]
    buffers, sems = refs[12:16], refs[16:18]
    place = lax.axis_index(TP)
    chip, core = plane_ids()[:2]
    other = {SEQ: 2 * chip + 1 - core}
    loads = [pltpu.make_async_copy(near_ref, sums, load_sem.at[0])]
    for index in range(count):
        rows = pl.ds(cuts[index], cuts[index + 1] - cuts[index])
        loads.append(
            pltpu.make_async_copy(
                terms[index], dense.at[:, :, rows], load_sem.at[1 + 2 * index]
            )
        )
        loads.append(
            pltpu.make_async_copy(givens[index], more.at[:, :, rows], load_sem.at[2 + 2 * index])
        )
    for load in loads:
        load.start()
    enter(neighbours(False, False))
    step_rows = dense.shape[2] // 2
    column = ColumnReduce(parts, sums.shape[1] // parts // 2, sums, came, (send_z, recv_z))
    plane = PlaneReduce(step_rows, dense, dense_ref, buffers, sems)

    def across(owner):
        return remote(
            far_ref.at[owner], given.at[owner], send_far.at[owner], recv_far.at[owner], other
        )

    def move(steps):
        for part in range(parts):
            for way, owner in steps:
                column.move(way, owner, part)

    for owner in column.order:
        across(owner).start()
    for load in loads:
        load.wait()
    pieces, steps = dense.shape[1], dense.shape[2] // step_rows

    @pl.loop(0, dense.shape[0] * pieces * steps)
    def _(step):
        at = pl.ds(pl.multiple_of((step % steps) * step_rows, step_rows), step_rows)
        piece = (step // steps) % pieces
        where = step // (steps * pieces)
        total = dense[where, piece, at, :].astype(f32) + more[where, piece, at, :].astype(f32)
        dense[where, piece, at, :] = total.astype(dense.dtype)

    plane.start()
    for owner in column.order:
        across(owner).wait_recv()
        for part in range(parts):
            column.add(owner, given.at[owner], part)
            column.begin(owner, part)
    last = column.count - 1

    @pl.when(place == last - 1)
    def _():
        move([(0, 0)])

    @pl.when(place == 1)
    def _():
        move([(1, last)])

    plane.move()

    @pl.when(place == last - 1)
    def _():
        move([(0, 1), (1, last)])

    @pl.when(place == 1)
    def _():
        move([(1, last - 1), (0, 0)])

    column.end()
    column.give(out_ref)
    plane.end()
    column.finish()
    plane.finish()
    for owner in column.order:
        across(owner).wait_send()


def fourth_exchange(near, far, terms, givens, cuts, collective_id, parts=2):
    count = lax.axis_size(TP)
    block = near.shape[1:]
    chips = givens[0].shape[0]
    width = givens[0].shape[-1]
    dense = (chips, count, cuts[-1], width)
    resident = pl.BlockSpec(memory_space=pltpu.VMEM)
    anywhere = pl.BlockSpec(memory_space=pl.ANY)
    dma = pltpu.SemaphoreType.DMA
    pieces = len(cuts) - 1
    return pl.pallas_call(
        functools.partial(fourth_kernel, parts, cuts),
        out_shape=[
            jax.ShapeDtypeStruct(block, near.dtype),
            jax.ShapeDtypeStruct(dense[1:], near.dtype),
        ],
        in_specs=[anywhere, resident] + [anywhere] * (2 * pieces),
        out_specs=[resident] * 2,
        scratch_shapes=[
            pltpu.VMEM((count,) + block, near.dtype),
            pltpu.VMEM((count,) + block, near.dtype),
            pltpu.VMEM((2, count) + block, near.dtype),
            pltpu.VMEM(dense, near.dtype),
            pltpu.VMEM(dense, near.dtype),
            dma((1 + 2 * pieces,)),
            dma((count,)),
            dma((count,)),
            dma((2, count, parts)),
            dma((2, count, parts)),
        ]
        + reduce_scratch(dense, near.dtype),
        compiler_params=pltpu.CompilerParams(
            collective_id=collective_id, has_side_effects=True, vmem_limit_bytes=52 * 2**20
        ),
        cost_estimate=lasting(62),
    )(near, far, *terms, *givens)


def fifth_kernel(rows_ref, dense_ref, out_ref, own_ref, came, send_z, recv_z, *refs):
    buffers, sems = refs[:4], refs[4:6]
    count = lax.axis_size(TP)
    place = lax.axis_index(TP)
    enter(neighbours(False, True))
    plane = PlaneReduce(rows_ref.shape[2] // 2, rows_ref, out_ref, buffers, sems)

    def to_owner(step):
        owner = lax.rem(place + step, count)
        return remote(
            dense_ref.at[owner], came.at[step - 1], send_z.at[step], recv_z.at[step], {TP: owner}
        )

    plane.start()
    for step in range(1, count):
        to_owner(step).start()
    plane.move()
    plane.end()
    for step in range(1, count):
        to_owner(step).wait()

    step_rows = own_ref.shape[0] // 2

    @pl.loop(0, 2)
    def _(step):
        at = pl.ds(pl.multiple_of(step * step_rows, step_rows), step_rows)
        total = dense_ref[place, at, :].astype(f32)
        for other in range(count - 1):
            total = total + came[other, at, :].astype(f32)
        own_ref[at, :] = total.astype(own_ref.dtype)

    plane.finish()


def fifth_exchange(rows, dense, collective_id):
    count = lax.axis_size(TP)
    resident = pl.BlockSpec(memory_space=pltpu.VMEM)
    dma = pltpu.SemaphoreType.DMA
    return pl.pallas_call(
        fifth_kernel,
        out_shape=[
            jax.ShapeDtypeStruct(rows.shape[1:], f32),
            jax.ShapeDtypeStruct(dense.shape[1:], dense.dtype),
        ],
        in_specs=[resident] * 2,
        out_specs=[resident] * 2,
        scratch_shapes=[
            pltpu.VMEM((count - 1,) + dense.shape[1:], dense.dtype),
            dma((count,)),
            dma((count,)),
        ]
        + reduce_scratch(rows.shape, rows.dtype),
        compiler_params=pltpu.CompilerParams(
            collective_id=collective_id, has_side_effects=True, vmem_limit_bytes=48 * 2**20
        ),
        cost_estimate=lasting(30),
    )(rows, dense)


def sixth_kernel(
    parts,
    terms_ref,
    own_ref,
    rows_ref,
    out_ref,
    dense_ref,
    all_ref,
    sums,
    given,
    came,
    send_far,
    recv_far,
    send_z,
    recv_z,
    send_plane,
    recv_plane,
    send_on,
    send_back,
    recv_back,
    keep_sem,
    send_row,
    recv_row,
    send_next,
    recv_next,
    send_dense,
    recv_dense,
    column_came,
    plane_came,
    send_all,
    recv_all,
):
    chip, core, beside, above, facing = plane_ids()
    count = lax.axis_size(TP)
    place = lax.axis_index(TP)
    other = {SEQ: 2 * chip + 1 - core}
    ways = ({SEQ: 2 * beside + core}, {SEQ: 2 * above + core})
    rows = sums.shape[0]
    part_rows = rows // parts
    always = place >= 0
    holds = place == chip
    far_column = [
        (always, {SEQ: 2 * chip + 1 - core, TP: lax.rem(place + step, count)})
        for step in range(1, count)
    ]
    enter(neighbours(True, True) + far_column)
    half = own_ref.shape[0] // 2
    dense = PlaneSpread(
        lambda part: own_ref.at[pl.ds(part * half, half)],
        lambda where, part: dense_ref.at[where, core, pl.ds(part * half, half)],
        (send_row, recv_row, send_next, recv_next),
    )
    keep = pltpu.make_async_copy(own_ref, dense_ref.at[chip, core], keep_sem)

    def dense_across(where):
        block = dense_ref.at[(chip, beside, above, facing)[where], core]
        return remote(block, block, send_dense.at[where], recv_dense.at[where], other)

    mine = core * count + place

    def column_copy(index):
        peer = lax.rem(mine + index, 2 * count)
        return remote(
            rows_ref,
            column_came.at[mine],
            send_all.at[index],
            recv_all.at[index],
            {SEQ: 2 * chip + peer // count, TP: lax.rem(peer, count)},
        )

    def column_landed(index):
        sender = lax.rem(mine + 2 * count - index, 2 * count)
        block = column_came.at[sender]
        return remote(block, block, send_all.at[index], recv_all.at[index], other)

    def plane_copy(index):
        return remote(
            plane_came.at[chip],
            plane_came.at[chip],
            send_all.at[2 * count + index],
            recv_all.at[2 * count + index],
            {SEQ: 2 * (beside, above, facing)[index] + core},
        )

    dense.start()
    keep.start()
    column_came[mine] = rows_ref[...]
    for index in range(1, 2 * count):
        column_copy(index).start()

    def cut(part):
        return pl.ds(part * part_rows, part_rows)

    def own_cut(part):
        return pl.ds(pl.multiple_of(core * rows + part * part_rows, 16), part_rows)

    across = remote(
        terms_ref.at[pl.ds(pl.multiple_of((1 - core) * rows, 16), rows)], given, send_far, recv_far, other
    )
    across.start()

    def along(way, part):
        return remote(
            sums.at[cut(part)],
            came.at[way, cut(part)],
            send_z.at[way, part],
            recv_z.at[way, part],
            {TP: place - 1 if way == 0 else place + 1},
        )

    def add(source, part):
        total = sums[cut(part), :].astype(f32) + source[cut(part), :].astype(f32)
        sums[cut(part), :] = total.astype(sums.dtype)

    def to_plane(way, part):
        return remote(
            out_ref.at[own_cut(part)],
            out_ref.at[own_cut(part)],
            send_plane.at[way, part],
            recv_plane.at[part],
            ways[way],
        )

    def onward(part):
        return remote(
            out_ref.at[own_cut(part)],
            out_ref.at[own_cut(part)],
            send_on.at[part],
            recv_plane.at[part],
            ways[1 - part // (parts // 2)],
        )

    def back(part):
        return remote(
            out_ref.at[own_cut(part)],
            out_ref.at[own_cut(part)],
            send_back.at[part],
            recv_back.at[part],
            other,
        )

    across.wait_recv()
    keep.wait()
    dense_across(0).start()
    for part in range(parts):
        sums[cut(part), :] = terms_ref[own_cut(part), :]
        add(given, part)
        for way in range(2):
            passes = place > chip if way == 0 else place < chip
            takes = place < count - 1 if way == 0 else place > 0

            @pl.when(passes)
            def _():
                @pl.when(takes)
                def _():
                    along(way, part).wait_recv()
                    add(came.at[way], part)

                along(way, part).start()

    dense.forward()
    for part in range(parts):
        for way in range(2):
            takes = place < count - 1 if way == 0 else place > 0

            @pl.when(holds & takes)
            def _():
                along(way, part).wait_recv()
                add(came.at[way], part)

        @pl.when(holds)
        def _():
            out_ref[own_cut(part), :] = sums[cut(part), :]
            for way in range(2):
                to_plane(way, part).start()
            back(part).start()

    for index in range(1, 2 * count):
        column_landed(index).wait_recv()
    total = column_came[0]
    for index in range(1, 2 * count):
        total = total + column_came[index]
    plane_came[chip] = total
    for index in range(3):
        plane_copy(index).start()
    dense.arrive()
    for where in range(1, 4):
        dense_across(where).start()
    for part in range(parts):

        @pl.when(place != chip)
        def _():
            to_plane(0, part).wait_recv()

        @pl.when((beside if part < parts // 2 else above) == place)
        def _():
            onward(part).start()

        @pl.when(place != chip)
        def _():
            back(part).start()

    for index in range(1, 2 * count):
        column_copy(index).wait_send()
    for index in range(3):
        plane_copy(index).wait()
    total = plane_came[0]
    for index in range(1, plane_came.shape[0]):
        total = total + plane_came[index]
    all_ref[...] = total
    across.wait_send()
    dense.finish()
    for where in range(4):
        dense_across(where).wait()
    for part in range(parts):
        back(part).wait()

        @pl.when((beside if part < parts // 2 else above) == place)
        def _():
            onward(part).wait_send()

        for way in range(2):

            @pl.when(holds)
            def _():
                to_plane(way, part).wait_send()

            @pl.when(place > chip if way == 0 else place < chip)
            def _():
                along(way, part).wait_send()


def sixth_exchange(terms, own, small, collective_id):
    parts = 4
    chips = lax.axis_size(SEQ) // 2
    column = 2 * lax.axis_size(TP)
    rows = terms.shape[0] // 2
    half = (rows,) + terms.shape[1:]
    dma = pltpu.SemaphoreType.DMA
    resident = pl.BlockSpec(memory_space=pltpu.VMEM)
    return pl.pallas_call(
        functools.partial(sixth_kernel, parts),
        out_shape=[
            jax.ShapeDtypeStruct(terms.shape, terms.dtype),
            jax.ShapeDtypeStruct((chips, 2) + own.shape, own.dtype),
            jax.ShapeDtypeStruct(small.shape, small.dtype),
        ],
        in_specs=[resident] * 3,
        out_specs=[resident] * 3,
        scratch_shapes=[
            pltpu.VMEM(half, terms.dtype),
            pltpu.VMEM(half, terms.dtype),
            pltpu.VMEM((2,) + half, terms.dtype),
            dma,
            dma,
            dma((2, parts)),
            dma((2, parts)),
            dma((2, parts)),
            dma((parts,)),
            dma((parts,)),
            dma((parts,)),
            dma((parts,)),
            dma,
        ]
        + plane_sems()
        + [
            dma((4,)),
            dma((4,)),
            pltpu.VMEM((column,) + small.shape, small.dtype),
            pltpu.VMEM((chips,) + small.shape, small.dtype),
            dma((column + 3,)),
            dma((column + 3,)),
        ],
        compiler_params=pltpu.CompilerParams(
            collective_id=collective_id, has_side_effects=True, vmem_limit_bytes=32 * 2**20
        ),
        cost_estimate=lasting(35),
    )(terms, own, small)


def plane_applies(mesh, blocks, docs):
    seq_count, tp_count = mesh.shape[SEQ], mesh.shape[TP]
    groups = seq_count * tp_count
    return (
        tp_count == 4
        and seq_count == 2 * tp_count
        and blocks == groups * SHORT_BLK
        and 2 * tp_count * SHORT_BLK == LONG_BLK
        and blocks - SHORT_BLK * docs == 2 * (LONG_BLK - SHORT_BLK)
    )


class Micro:
    pass


def plane_body(
    tokens,
    doc_lengths,
    rand_blocks,
    query_weight,
    key_weight,
    value_weight,
    query_bias,
    value_bias,
    proj_weight,
    proj_bias,
    first_gain,
    first_bias,
    second_gain,
    second_bias,
    inner_weight,
    inner_bias,
    outer_weight,
    outer_bias,
    out_grad,
):
    micro_count, own_rows, model_width = tokens.shape
    seq_count = lax.axis_size(SEQ)
    tp_count = lax.axis_size(TP)
    chips = seq_count // 2
    seq_place = lax.axis_index(SEQ)
    tp_place = lax.axis_index(TP)
    chip = lax.shift_right_logical(seq_place, 1)
    core = seq_place & 1
    heads = rand_blocks.shape[2]
    rands = rand_blocks.shape[3]
    local_width = query_weight.shape[1]
    head_size = local_width // heads
    pair_width = heads * PAIR
    hidden_units = inner_weight.shape[1]
    classes = 2 * tp_count
    class_bits = classes.bit_length() - 1
    group_bits = SHORT_BLK.bit_length() - 1
    own_class = core * tp_count + tp_place
    long_docs = 2
    slots = 5 + rands
    group_rows = chips * own_rows
    score_scale = 1.0 / math.sqrt(head_size)

    def by_head(values):
        return values.reshape(values.shape[:-1] + (heads, -1))

    def side_by_side(first, second):
        paired = jnp.concatenate([by_head(first), by_head(second)], axis=-1)
        return paired.reshape(paired.shape[:-2] + (pair_width,))

    def low_half(wide):
        return by_head(wide)[..., :head_size].reshape(wide.shape[:-1] + (local_width,))

    def high_half(wide):
        return by_head(wide)[..., head_size:].reshape(wide.shape[:-1] + (local_width,))

    def slot_rows(values, slot):
        return values[slot * own_rows : (slot + 1) * own_rows]

    stage = [Micro() for _ in range(micro_count)]
    spare_rows = 128
    packed = jnp.concatenate([side_by_side(key_weight, value_weight), query_weight], axis=1)
    packed_bias = jnp.concatenate(
        [side_by_side(jnp.zeros_like(value_bias), value_bias), query_bias]
    )
    packed = jnp.concatenate([packed, packed_bias[None]], axis=0)
    packed = jnp.pad(packed, ((0, spare_rows - 1), (0, -packed.shape[1] % 128)))
    randoms = rand_blocks.reshape(-1)
    random_count = randoms.shape[0]
    randoms = jnp.pad(randoms, (0, -random_count % 1024)).reshape(-1, 128)
    for micro, held in enumerate(stage):
        held.inputs = tokens[micro].astype(f32)
        shifted, held.stats_one, held.inverse_one = layer_stats(
            held.inputs, first_gain, first_bias
        )
        held.low = shifted.astype(bf16)
    unit_cut = hidden_units // seq_count
    proj_cut = local_width // seq_count
    rest_rows = -(-(proj_cut + 1) // 16) * 16
    cuts = (0, rest_rows, rest_rows + unit_cut, rest_rows + 2 * unit_cut)

    def padded(row_values):
        return jnp.pad(row_values, [(0, 0)] * (row_values.ndim - 1) + [(0, model_width - unit_cut)])

    share = jnp.concatenate(
        [
            lax.dynamic_slice_in_dim(proj_weight, seq_place * proj_cut, proj_cut, axis=0),
            padded(lax.dynamic_slice_in_dim(inner_bias, seq_place * unit_cut, unit_cut)[None]),
            jnp.zeros((rest_rows - proj_cut - 1, model_width), bf16),
            lax.dynamic_slice_in_dim(inner_weight, seq_place * unit_cut, unit_cut, axis=1).T,
            lax.dynamic_slice_in_dim(outer_weight, seq_place * unit_cut, unit_cut, axis=0),
        ],
        axis=0,
    )
    one, packed, column, randoms = first_exchange(stage[0].low, packed, share, randoms, 1)
    stage[0].one = one.reshape(group_rows, model_width)
    pair_wide = packed[:model_width, :pair_width]
    pair_wide_bias = packed[model_width, :pair_width]
    query_part = packed[:model_width, pair_width : pair_width + local_width]
    query_part_bias = packed[model_width, pair_width : pair_width + local_width]
    joined_weight = jnp.concatenate([pair_wide, query_part * score_scale], axis=1)
    joined_bias = jnp.concatenate([pair_wide_bias, query_part_bias * score_scale])

    starts = jnp.cumsum(doc_lengths, axis=1) - doc_lengths
    is_long = doc_lengths == LONG_BLK
    long_firsts = jnp.min(jnp.where(is_long, starts, jnp.iinfo(jnp.int32).max), axis=1)
    long_lasts = jnp.max(jnp.where(is_long, starts, -1), axis=1)
    first_groups = lax.shift_right_logical(jnp.stack([long_firsts, long_lasts]), group_bits)
    own_groups = first_groups + ((own_class - first_groups) & (classes - 1))
    in_slot = lax.shift_right_logical(own_groups, class_bits)[:, :, None] == np.arange(chips)
    randoms = randoms.reshape(chips, -1)[:, :random_count]
    randoms = randoms.reshape(chips, micro_count, tp_count, SHORT_BLK, heads, rands)
    randoms = lax.dynamic_index_in_dim(randoms, tp_place, axis=2, keepdims=False)
    randoms = jnp.pad(randoms.transpose(1, 3, 0, 2, 4), [(0, 0)] * 4 + [(slots - rands, 0)])
    randoms = randoms.reshape(micro_count, -1)
    shape = (heads, chips, SHORT_BLK, slots)
    slot, block, entry = (part.reshape(-1) for part in np.indices(shape, np.int32)[1:])
    for micro, held in enumerate(stage):
        group = slot * classes + own_class
        number = group * SHORT_BLK + block
        in_long = [
            (number >= start) & (number < start + LONG_BLK)
            for start in (long_firsts[micro : micro + 1], long_lasts[micro : micro + 1])
        ]
        window_first = jnp.where(
            in_long[0],
            long_firsts[micro : micro + 1],
            jnp.where(in_long[1], long_lasts[micro : micro + 1], group * SHORT_BLK),
        )
        any_long = in_long[0] | in_long[1]
        window_final = window_first + jnp.where(any_long, LONG_BLK, SHORT_BLK)
        key = randoms[micro]
        for place, value in enumerate(
            (
                jnp.maximum(number - 1, window_first),
                jnp.minimum(number + 1, window_final - 1),
                number,
                window_first,
                window_first + 1,
            )
        ):
            key = jnp.where(entry == place, value, key)
        inside = key & (SHORT_BLK - 1)
        key_class = lax.shift_right_logical(key, group_bits) & (classes - 1)
        own_core = lax.shift_right_logical(key_class, class_bits - 1) == core
        piece = (key_class & (tp_count - 1)) + jnp.where(own_core, 0, tp_count)
        long_place = piece * long_docs + jnp.where(in_long[1], 1, 0)
        short_place = classes * long_docs + slot
        held.index = jnp.where(any_long, long_place, short_place) * SHORT_BLK + inside
        counts = jnp.where(entry == 0, number > window_first, number + 1 < window_final)
        counts = counts.astype(jnp.int32)[: chips * SHORT_BLK * slots]
        held.valid = counts.reshape(-1, slots)[:, :2].reshape(-1)
        held.in_slot = [in_slot[doc, micro].reshape(chips, 1, 1) for doc in range(long_docs)]

    def long_blocks(micro):
        held = stage[micro]
        held.joined = (contract(held.one, joined_weight, NN) + joined_bias).astype(bf16)
        parts = held.joined.reshape(chips, own_rows, -1)[:, :, :pair_width]
        longs = jnp.concatenate(
            [jnp.sum(jnp.where(chosen, parts, 0), axis=0) for chosen in held.in_slot], axis=0
        )
        return longs

    def keep_pieces(micro, near, far):
        stage[micro].pieces = [near.reshape(-1, pair_width), far.reshape(-1, pair_width)]

    def attend(micro):
        held = stage[micro]
        index = after(held.index, stage[micro - 1].grad_context_sent)
        held.context_sent, held.logsum = attend_forward(
            index, held.valid, held.joined, held.pieces, heads, slots
        )
        held.context = plane_exchange(held.context_sent, 0, 1)

    def feed_forward(micro):
        held = stage[micro]
        if micro:
            held.context = after(
                held.context, stage[micro - 1].long_sum_sent
            )
        hidden = held.inputs + contract(held.context, proj_full, NN) + proj_bias
        shifted, stats, inverse = layer_stats(hidden, second_gain, second_bias)
        held.two = shifted.astype(bf16)
        before = contract(held.two, inner_full, NT) + inner_bias_full
        held.active = gelu_exact(before).astype(bf16)
        result = hidden + contract(held.active, outer_full, NN) + outer_bias
        held.output = result.astype(bf16)
        held.grad_out = out_grad[micro]
        grad_float = held.grad_out.astype(f32)
        grad_active = contract(held.grad_out, outer_full, NT)
        held.grad_before = gelu_grad(before, grad_active).astype(bf16)
        grad_two = contract(held.grad_before, inner_full, NN)
        back, gain_sum, shift_sum = layer_back(grad_two, stats, inverse, second_gain)
        held.grad_hidden = grad_float + back
        held.branch = held.grad_hidden.astype(bf16)
        held.grad_context_sent = jnp.stack(
            [
                contract(
                    held.branch, proj_full[part * local_width : (part + 1) * local_width], NT
                ).astype(bf16)
                for part in range(chips)
            ]
        )
        held.grad_context = plane_exchange(held.grad_context_sent, 0, 0).reshape(
            group_rows, local_width
        )
        held.unit_sum = jnp.sum(held.grad_before.astype(f32), axis=0)
        held.row_sums = jnp.stack(
            [
                gain_sum,
                shift_sum,
                jnp.sum(held.branch.astype(f32), axis=0),
                jnp.sum(grad_float, axis=0),
            ]
        )

    def attend_back(micro, *earlier):
        held = stage[micro]
        near, far, held.grad_joined = attend_backward(
            held.index,
            held.valid,
            held.joined,
            after(held.grad_context, *earlier),
            held.logsum,
            held.pieces,
            heads,
            slots,
        )
        return near, far

    def input_rows(micro, long_sum):
        held = stage[micro]
        shape = (chips, own_rows, pair_width + local_width)
        lane = np.arange(shape[2], dtype=np.int32)
        joined = held.grad_joined.reshape(shape)
        for doc, chosen in enumerate(held.in_slot):
            long_part = jnp.pad(slot_rows(long_sum, doc), ((0, 0), (0, local_width)))
            joined = jnp.where(chosen & (lane < pair_width), long_part, joined)
        held.grad_joined = joined.reshape(group_rows, -1)
        rows = contract(held.grad_joined, joined_weight, NT)
        return rows.astype(bf16).reshape(chips, own_rows, model_width)

    def input_back(micro, grad_one):
        held = stage[micro]
        back, gain_sum, shift_sum = layer_back(
            grad_one, held.stats_one, held.inverse_one, first_gain
        )
        held.input_grad = held.grad_hidden + back
        held.first_sums = jnp.stack([gain_sum, shift_sum])

    longs = long_blocks(0)
    near, far, one, outer_full = second_exchange(longs, stage[1].low, column, cuts[2:4], 2)
    stage[1].one = one.reshape(group_rows, model_width)
    keep_pieces(0, near, far)
    longs = long_blocks(1)
    near, far, context, stage[0].logsum, rest, inner_full = third_exchange(
        longs,
        column,
        stage[0].index,
        stage[0].valid,
        stage[0].joined,
        stage[0].pieces,
        (cuts[0:2], cuts[1:3]),
        heads,
        slots,
        7,
    )
    keep_pieces(1, near, far)
    stage[0].context = context.transpose(1, 0, 2).reshape(own_rows, model_width)
    inner_full = inner_full.reshape(-1, model_width)
    outer_full = outer_full.reshape(-1, model_width)
    inner_bias_full = rest[:, :, :, proj_cut, :unit_cut].reshape(-1)
    proj_full = rest[:, :, :, :proj_cut].transpose(2, 1, 0, 3, 4)
    proj_full = proj_full.reshape(tp_count * local_width, model_width)
    feed_forward(0)
    attend(1)
    near, far = attend_back(0, stage[1].logsum, stage[1].context_sent)
    stage[0].long_sum_sent = sum_parts([near, core_swap(far)]).astype(bf16)
    long_sum = lax.psum_scatter(stage[0].long_sum_sent, TP, scatter_dimension=0, tiled=True)
    feed_forward(1)

    given_inner, given_outer, kept_inner, kept_outer, proj_part = dense_terms(
        after(core, stage[1].grad_context_sent),
        [[h.grad_before for h in stage], [h.active for h in stage], [h.context for h in stage]],
        [[h.two for h in stage], [h.grad_out for h in stage], [h.branch for h in stage]],
    )
    proj_part = proj_part.reshape(tp_count, chips, 2, proj_cut, model_width)
    unit_shape = (2, chips, tp_count)
    unit_sum = sum(h.unit_sum for h in stage).astype(bf16)
    rest_part = jnp.concatenate(
        [
            proj_part.transpose(2, 1, 0, 3, 4),
            padded(unit_sum.reshape(unit_shape + (1, unit_cut))),
            jnp.zeros(unit_shape + (rest_rows - proj_cut - 1, model_width), bf16),
        ],
        axis=3,
    )
    unit_shape = (chips, tp_count, -1, model_width)
    terms = [kept_inner.reshape(unit_shape), kept_outer.reshape(unit_shape)]
    givens = [core_swap(part.reshape(unit_shape)) for part in (given_inner, given_outer)]
    terms.append(lax.dynamic_index_in_dim(rest_part, core, axis=0, keepdims=False))
    givens.append(
        core_swap(lax.dynamic_index_in_dim(rest_part, 1 - core, axis=0, keepdims=False))
    )

    rows = input_rows(0, after(long_sum, kept_inner))
    grad_one = lax.psum_scatter(
        rows.reshape(group_rows, model_width),
        SEQ,
        scatter_dimension=0,
        axis_index_groups=[list(range(place, seq_count, 2)) for place in range(2)],
        tiled=True,
    )
    near, far = attend_back(1, rows)

    column_shape = (tp_count, long_docs * own_rows, pair_width)
    cuts = (0, unit_cut, 2 * unit_cut, 2 * unit_cut + rest_rows)
    row_shape = (chips, 2, own_rows // 2, model_width)
    long_sum, quarters = fourth_exchange(
        near.reshape(column_shape), far.reshape(column_shape), terms, givens, cuts, 3
    )
    rows = input_rows(1, long_sum)
    grad_one_now, own_sum = fifth_exchange(rows.reshape(row_shape), quarters, 4)
    input_back(0, after(grad_one, rows).astype(f32))
    input_back(1, grad_one_now.reshape(own_rows, model_width))

    ones = after([h.one for h in stage], grad_one_now)
    packed_sum = sum(contract(one, h.grad_joined, TN) for one, h in zip(ones, stage))
    packed_sum = jnp.pad(packed_sum, ((0, 0), (0, -packed_sum.shape[1] % 128))).astype(bf16)

    def own_columns(values):
        wide = jnp.zeros((chips, local_width), f32)
        return lax.dynamic_update_slice_in_dim(wide, values[None], chip, axis=0).reshape(-1)

    joined_sum = sum(jnp.sum(h.grad_joined.astype(f32), axis=0) for h in stage)
    packed_sum, dense_sum, all_rows = sixth_exchange(
        packed_sum,
        own_sum,
        jnp.concatenate(
            [
                sum(h.row_sums for h in stage),
                sum(h.first_sums for h in stage),
                own_columns(joined_sum[pair_width:] * score_scale)[None],
                own_columns(high_half(joined_sum[:pair_width]))[None],
            ],
            axis=0,
        ),
        6,
    )
    key_grad = low_half(packed_sum[:, :pair_width]).astype(f32)
    value_grad = high_half(packed_sum[:, :pair_width]).astype(f32)
    query_grad = packed_sum[:, pair_width : pair_width + local_width].astype(f32) * score_scale
    dense_sum = dense_sum.reshape(seq_count, -1, model_width).astype(f32)
    inner_weight_grad = dense_sum[:, :unit_cut].reshape(hidden_units, model_width).T
    outer_weight_grad = dense_sum[:, unit_cut : 2 * unit_cut].reshape(hidden_units, model_width)
    rest = dense_sum[:, 2 * unit_cut :]
    proj_weight_grad = rest[:, :proj_cut].reshape(local_width, model_width)
    inner_bias_grad = rest[:, proj_cut, :unit_cut].reshape(hidden_units)

    def my_columns(row):
        return lax.dynamic_slice_in_dim(row, tp_place * local_width, local_width)

    return (
        jnp.stack([h.output for h in stage]),
        jnp.stack([h.input_grad for h in stage]),
        query_grad,
        key_grad,
        value_grad,
        my_columns(all_rows[6]),
        my_columns(all_rows[7]),
        proj_weight_grad,
        all_rows[2],
        all_rows[4],
        all_rows[5],
        all_rows[0],
        all_rows[1],
        inner_weight_grad,
        inner_bias_grad,
        outer_weight_grad,
        all_rows[3],
    )


def general_body(
    tokens,
    doc_lengths,
    rand_blocks,
    query_weight,
    key_weight,
    value_weight,
    query_bias,
    value_bias,
    proj_weight,
    proj_bias,
    first_gain,
    first_bias,
    second_gain,
    second_bias,
    inner_weight,
    inner_bias,
    outer_weight,
    outer_bias,
    out_grad,
):
    micro_count, local_rows, model_width = tokens.shape
    seq_count = lax.axis_size(SEQ)
    tp_count = lax.axis_size(TP)
    seq_place = lax.axis_index(SEQ)
    tp_place = lax.axis_index(TP)
    block_dev = rand_blocks.shape[1]
    heads = rand_blocks.shape[2]
    local_width = query_weight.shape[1]
    head_size = local_width // heads
    hidden_units = inner_weight.shape[1]
    group_rows = block_dev * BLOCK
    reach_dev = (block_dev + LONG_BLK - 2) // block_dev
    window = 2 * reach_dev + 1
    score_scale = 1.0 / math.sqrt(head_size)
    lowest = (seq_place - reach_dev) * block_dev
    blocks = seq_place * block_dev + jnp.arange(block_dev, dtype=jnp.int32)

    held = jnp.concatenate([inner_weight.T, outer_weight, proj_weight, inner_bias[None]], axis=0)
    used_rows = held.shape[0]
    piece_rows = -(-used_rows // (16 * seq_count)) * 16
    held_rows = piece_rows * seq_count
    held = jnp.pad(held, ((0, held_rows - used_rows), (0, 0)))
    share = lax.dynamic_slice_in_dim(held, seq_place * piece_rows, piece_rows, axis=0)
    spread = lax.all_gather(share, (TP, SEQ), axis=0, tiled=True)
    spread = spread.reshape(tp_count, held_rows, model_width)
    cuts = [0, hidden_units, 2 * hidden_units, 2 * hidden_units + local_width, used_rows]
    inner_full = spread[:, cuts[0] : cuts[1]].reshape(-1, model_width)
    outer_full = spread[:, cuts[1] : cuts[2]].reshape(-1, model_width)
    proj_full = spread[:, cuts[2] : cuts[3]].reshape(-1, model_width)
    inner_bias_full = spread[:, cuts[3] : cuts[4]].reshape(-1)

    def by_head(weight):
        return weight.reshape(weight.shape[:-1] + (heads, head_size))

    def side_by_side(first, second):
        paired = jnp.concatenate([by_head(first), by_head(second)], axis=-1)
        return paired.reshape(paired.shape[:-2] + (heads * PAIR,))

    pair_wide = side_by_side(key_weight, value_weight)
    pair_wide_bias = side_by_side(jnp.zeros_like(value_bias), value_bias)

    stage = [Micro() for _ in range(micro_count)]
    for micro, held in enumerate(stage):
        inputs = tokens[micro].astype(f32)
        shifted, stats, inverse = layer_stats(inputs, first_gain, first_bias)
        held.inputs, held.stats_one, held.inverse_one = inputs, stats, inverse
        held.one = lax.all_gather(shifted.astype(bf16), TP, axis=0, tiled=True)

    for micro, held in enumerate(stage):
        one = held.one
        pair_rows = (contract(one, pair_wide, NN) + pair_wide_bias).astype(bf16)
        offsets = [offset for offset in range(-reach_dev, reach_dev + 1) if offset != 0]
        pieces = [from_behind(pair_rows, SEQ, -offset) for offset in offsets]
        queries = ((contract(one, query_weight, NN) + query_bias) * score_scale).astype(bf16)
        held.joined = jnp.concatenate([pair_rows, queries], axis=1)
        key_index, key_valid = block_keys(doc_lengths[micro], rand_blocks[micro], blocks)
        slots = key_index.shape[2]
        slot_index = jnp.clip(key_index - lowest, 0, window * block_dev - 1)
        piece = slot_index // block_dev
        piece = jnp.where(piece == reach_dev, 2 * reach_dev, piece - (piece > reach_dev))
        slot_index = piece * block_dev + slot_index % block_dev
        held.index = slot_index.transpose(1, 0, 2).reshape(-1)
        held.valid = key_valid.reshape(-1)
        held.pieces = pieces

    for held in stage:
        context, held.logsum = attend_forward(
            held.index,
            held.valid,
            held.joined,
            held.pieces,
            heads,
            slots,
        )
        held.context = lax.all_to_all(context, TP, split_axis=0, concat_axis=1, tiled=True)

    outputs = []
    for micro, held in enumerate(stage):
        context = held.context
        hidden = held.inputs + contract(context, proj_full, NN) + proj_bias
        shifted, stats, inverse = layer_stats(hidden, second_gain, second_bias)
        two = shifted.astype(bf16)
        before = contract(two, inner_full, NT) + inner_bias_full
        active = gelu_exact(before).astype(bf16)
        result = hidden + contract(active, outer_full, NN) + outer_bias
        outputs.append(result.astype(bf16))
        grad_out = out_grad[micro]
        grad_float = grad_out.astype(f32)
        grad_active = contract(grad_out, outer_full, NT)
        grad_before = gelu_grad(before, grad_active).astype(bf16)
        grad_two = contract(grad_before, inner_full, NN)
        back, gain_sum, shift_sum = layer_back(grad_two, stats, inverse, second_gain)
        grad_hidden = grad_float + back
        branch = grad_hidden.astype(bf16)
        grad_context = contract(branch, proj_full, NT).astype(bf16)
        held.grad_context = lax.all_to_all(
            grad_context, TP, split_axis=1, concat_axis=0, tiled=True
        )
        held.grad_hidden = grad_hidden
        held.dense = (two, grad_before, active, grad_out, context, branch)
        held.row_sums = (
            jnp.sum(grad_before.astype(f32), axis=0),
            gain_sum,
            shift_sum,
            jnp.sum(branch.astype(f32), axis=0),
            jnp.sum(grad_float, axis=0),
        )

    two, grad_before, active, grad_out, context, branch = (
        jnp.concatenate(group, axis=0) for group in zip(*(h.dense for h in stage))
    )
    inner_part = contract(grad_before, two, TN).astype(bf16)
    outer_part = contract(active, grad_out, TN).astype(bf16)
    proj_part = contract(context, branch, TN).astype(bf16)
    grad_rows = 2 * hidden_units + local_width
    grad_piece = -(-grad_rows // (16 * seq_count)) * 16
    grad_held = grad_piece * seq_count
    parts = jnp.concatenate(
        [
            inner_part.reshape(tp_count, hidden_units, model_width),
            outer_part.reshape(tp_count, hidden_units, model_width),
            proj_part.reshape(tp_count, local_width, model_width),
            jnp.zeros((tp_count, grad_held - grad_rows, model_width), bf16),
        ],
        axis=1,
    ).reshape(tp_count * grad_held, model_width)
    own_part = lax.psum_scatter(parts, (TP, SEQ), scatter_dimension=0, tiled=True)
    dense_sum = lax.all_gather(own_part, SEQ, axis=0, tiled=True).astype(f32)
    inner_weight_grad = dense_sum[cuts[0] : cuts[1]].T
    outer_weight_grad = dense_sum[cuts[1] : cuts[2]]
    proj_weight_grad = dense_sum[cuts[2] : cuts[3]]

    for held in stage:
        *grad_pieces, joined = attend_backward(
            held.index,
            held.valid,
            held.joined,
            held.grad_context,
            held.logsum,
            held.pieces,
            heads,
            slots,
        )
        pair_width = heads * PAIR
        returned = joined[:, :pair_width].astype(f32)
        held.grad_query = joined[:, pair_width:]
        for offset, grad_piece in zip(offsets, grad_pieces):
            returned = returned + from_behind(grad_piece, SEQ, offset).astype(f32)
        held.grad_pair = returned.astype(bf16)

    input_grads = []
    query_sum = pair_sum = 0.0
    query_bias_sum = pair_bias_sum = 0.0
    first_gain_sum = first_bias_sum = 0.0
    for held in stage:
        grad_query, grad_pair, one = held.grad_query, held.grad_pair, held.one
        rows = contract(grad_query, query_weight * score_scale, NT) + contract(grad_pair, pair_wide, NT)
        grad_one = lax.psum_scatter(
            rows.astype(bf16), TP, scatter_dimension=0, tiled=True
        ).astype(f32)
        query_sum = query_sum + contract(one, grad_query, TN)
        pair_sum = pair_sum + contract(one, grad_pair, TN)
        query_bias_sum = query_bias_sum + jnp.sum(grad_query.astype(f32), axis=0)
        pair_bias_sum = pair_bias_sum + jnp.sum(grad_pair.astype(f32), axis=0)
        back, gain_sum, shift_sum = layer_back(
            grad_one, held.stats_one, held.inverse_one, first_gain
        )
        first_gain_sum = first_gain_sum + gain_sum
        first_bias_sum = first_bias_sum + shift_sum
        input_grads.append(held.grad_hidden + back)

    def low_half(wide):
        return wide.reshape(wide.shape[:-1] + (heads, PAIR))[..., :head_size].reshape(
            wide.shape[:-1] + (local_width,)
        )

    def high_half(wide):
        return wide.reshape(wide.shape[:-1] + (heads, PAIR))[..., head_size:].reshape(
            wide.shape[:-1] + (local_width,)
        )

    query_grad, key_grad, value_grad = lax.psum(
        (query_sum * score_scale, low_half(pair_sum), high_half(pair_sum)), SEQ
    )
    inner_bias_sum, second_gain_sum, second_bias_sum, proj_bias_sum, outer_bias_sum = (
        sum(group) for group in zip(*(h.row_sums for h in stage))
    )

    def own_columns(values):
        wide = jnp.zeros((tp_count, local_width), f32)
        return lax.dynamic_update_slice_in_dim(wide, values[None], tp_place, axis=0).reshape(-1)

    early = lax.psum(
        jnp.concatenate(
            [
                inner_bias_sum,
                second_gain_sum,
                second_bias_sum,
                proj_bias_sum,
                outer_bias_sum,
            ]
        ),
        (SEQ, TP),
    )
    late = lax.psum(
        jnp.concatenate(
            [
                first_gain_sum,
                first_bias_sum,
                own_columns(query_bias_sum * score_scale),
                own_columns(high_half(pair_bias_sum)),
            ]
        ),
        (SEQ, TP),
    )
    inner_bias_all = early[: tp_count * hidden_units].reshape(tp_count, hidden_units)
    early_rows = early[tp_count * hidden_units :].reshape(-1, model_width)
    late_rows = late.reshape(-1, model_width)

    def my_columns(row):
        return lax.dynamic_slice_in_dim(row, tp_place * local_width, local_width)

    return (
        jnp.stack(outputs),
        jnp.stack(input_grads),
        query_grad,
        key_grad,
        value_grad,
        my_columns(late_rows[2]),
        my_columns(late_rows[3]),
        proj_weight_grad,
        early_rows[2],
        late_rows[0],
        late_rows[1],
        early_rows[0],
        early_rows[1],
        inner_weight_grad,
        lax.dynamic_index_in_dim(inner_bias_all, tp_place, axis=0, keepdims=False),
        outer_weight_grad,
        early_rows[3],
    )


def solution(mesh):
    def choose(tokens, doc_lengths, rand_blocks, *rest):
        blocks = rand_blocks.shape[1] * mesh.shape[SEQ]
        if plane_applies(mesh, blocks, doc_lengths.shape[1]):
            return plane_body(tokens, doc_lengths, rand_blocks, *rest)
        return general_body(tokens, doc_lengths, rand_blocks, *rest)

    return jax.shard_map(
        choose,
        mesh=mesh,
        in_specs=(
            P(None, (SEQ, TP), None),
            P(),
            P(None, SEQ, TP, None),
            P(None, TP),
            P(None, TP),
            P(None, TP),
            P(TP),
            P(TP),
            P(TP, None),
            P(),
            P(),
            P(),
            P(),
            P(),
            P(None, TP),
            P(TP),
            P(TP, None),
            P(),
            P(None, (SEQ, TP), None),
        ),
        out_specs=(
            P(None, (SEQ, TP), None),
            P(None, (SEQ, TP), None),
            P(None, TP),
            P(None, TP),
            P(None, TP),
            P(TP),
            P(TP),
            P(TP, None),
            P(),
            P(),
            P(),
            P(),
            P(),
            P(None, TP),
            P(TP),
            P(TP, None),
            P(),
        ),
        check_vma=False,
    )
```
